32 devices in a mesh: section: 2 (over core), dp: 4 (over z), mp: 4 (over y, x).
Axes of the slice: x: 2, y: 2, z: 4, core: 2. Of those that a mesh axis runs over, the one named last changes fastest.
Arguments:
- patches: bfloat16 [64, 16, 1024], P('mp', 'dp'), may hold values from -6 to 6
- counts: int32 [16], P('dp'), may hold values from 35 to 63
- patch_index: int32 [64, 16], P('mp', 'dp'), may hold values from 0 to 195, as said below
- scale_level: int32 [16], P('dp'), may hold values from 0 to 7
- enc_gain_one: bfloat16 [1024], replicated, may hold values from 0.25 to 1.75
- enc_qkv: bfloat16 [1024, 3, 1024], P(None, None, 'mp'), may hold values from -0.1875 to 0.1875
- enc_out: bfloat16 [1024, 1024], P(None, 'mp'), may hold values from -0.5 to 0.5
- enc_gain_two: bfloat16 [1024], replicated, may hold values from 0.25 to 1.75
- enc_up: bfloat16 [1024, 4096], P(None, 'mp'), may hold values from -0.1875 to 0.1875
- enc_down: bfloat16 [1024, 4096], P(None, 'mp'), may hold values from -0.09375 to 0.09375
- w_proj: bfloat16 [1024, 512], replicated, may hold values from -0.1875 to 0.1875
- mask_token: bfloat16 [512], replicated, may hold values from -4 to 4
- pos_table: bfloat16 [8, 196, 512], replicated, may hold values from -1 to 1
- dec_gain_one: bfloat16 [512], replicated, may hold values from 0.25 to 1.75
- dec_qkv: bfloat16 [512, 3, 512], P(None, None, 'mp'), may hold values from -0.25 to 0.25
- dec_out: bfloat16 [512, 512], P(None, 'mp'), may hold values from -1 to 1
- dec_gain_two: bfloat16 [512], replicated, may hold values from 0.25 to 1.75
- dec_up: bfloat16 [512, 2048], P(None, 'mp'), may hold values from -0.25 to 0.25
- dec_down: bfloat16 [512, 2048], P(None, 'mp'), may hold values from -0.125 to 0.125
- decoded_grad: bfloat16 [196, 16, 512], P('mp', 'dp'), may hold values from -6 to 6
Outputs:
- decoded: float32 [196, 16, 512], P(None, 'dp', ('section', 'mp'))
- patches_grad: float32 [64, 16, 1024], P(None, 'dp', ('section', 'mp'))
- enc_qkv_grad: float32 [1024, 3, 1024], P(('section', 'dp'), None, 'mp')
- enc_out_grad: float32 [1024, 1024], P(('section', 'dp'), 'mp')
- enc_up_grad: float32 [1024, 4096], P(('section', 'dp'), 'mp')
- enc_down_grad: float32 [1024, 4096], P(('section', 'dp'), 'mp')
- dec_qkv_grad: float32 [512, 3, 512], P(('section', 'dp'), None, 'mp')
- dec_out_grad: float32 [512, 512], P(('section', 'dp'), 'mp')
- dec_up_grad: float32 [512, 2048], P(('section', 'dp'), 'mp')
- dec_down_grad: float32 [512, 2048], P(('section', 'dp'), 'mp')
- proj_grad: float32 [1024, 512], replicated
- enc_gain_one_grad: float32 [1024], replicated
- enc_gain_two_grad: float32 [1024], replicated
- dec_gain_one_grad: float32 [512], replicated
- dec_gain_two_grad: float32 [512], replicated
- mask_token_grad: float32 [512], replicated
The draws below stay inside these ranges and needn't reach their ends.
Inputs may be any that keep to these rules, and one draw needn't show every extreme that they name: `patch_index`: within each image the 64 entries are distinct patch numbers; slots at or past the image's count are padding.
All inputs are finite; a program needn't handle non-finite values.
Results may differ from the reference program's by a relative error of at most 0.035.
Values may be sent and summed in bfloat16 or wider, within the bound.
A program may use at most 320 MiB of HBM per device.

```python
import math
import jax
import jax.numpy as jnp
from jax import lax

D = 1024
HEADS = 16
MLP = 4096
DEC = 512
DEC_HEADS = 16
DEC_MLP = 2048
GRID = 196
SLOT = 64
LEVELS = 8
IMAGES = 16
N_DP = 4


def draw_patch_index(key, part):
    key = jax.random.fold_in(key, 11)
    image_keys = jax.random.split(key, IMAGES)
    chosen = jax.vmap(lambda single: jax.random.permutation(single, GRID)[:SLOT])(image_keys)
    return jnp.transpose(chosen).astype(jnp.int32)


def place_ends(drawn, rng, low, high):
    index_at = [jax.random.randint(jax.random.fold_in(rng, axis), (), 0, length) for axis, length in enumerate(drawn.shape)]
    main_axis = drawn.shape.index(max(drawn.shape))
    neighbour = index_at[:main_axis] + [(index_at[main_axis] + 1) % drawn.shape[main_axis]] + index_at[main_axis + 1:]
    return drawn.at[tuple(index_at)].set(low).at[tuple(neighbour)].set(high)


def level_of(key, shape, pieces, low, largest):
    gain = 1.0
    for axis_at, shards_of in pieces:
        draws = jax.random.uniform(jax.random.fold_in(jax.random.fold_in(key, 6), axis_at), (shards_of,), jnp.float32, low / len(pieces), largest / len(pieces))
        gain = gain * jnp.repeat(jnp.exp(draws), shape[axis_at] // shards_of).reshape((-1,) + (1,) * (len(shape) - 1 - axis_at))
    return gain


def scatter_about(key, dims, width, limit, shards=(), kind=jnp.bfloat16):
    array = width * jax.random.normal(key, dims, jnp.float32)
    if shards:
        array = array * level_of(key, dims, shards, -0.22, 0.18)
    return jnp.clip(array, -limit, limit).astype(kind)


def setup_inputs(seed: int = 0) -> dict:
    seeds = jax.random.split(jax.random.key(seed), 21)
    return {
        "patches": scatter_about(seeds[0], (SLOT, IMAGES, D), 1.0, 6.0, ((0, 4), (1, 4))),
        "counts": place_ends(jax.random.randint(seeds[1], (IMAGES,), SLOT * 35 // 64, SLOT * 63 // 64 + 1), jax.random.fold_in(seeds[1], 1), SLOT * 35 // 64, (SLOT * 63 // 64 + 1) - 1).astype(jnp.int32),
        "patch_index": draw_patch_index(jax.random.fold_in(seeds[20], 71), 0),
        "scale_level": place_ends(jax.random.randint(seeds[3], (IMAGES,), 0, LEVELS), jax.random.fold_in(seeds[3], 1), 0, LEVELS - 1).astype(jnp.int32),
        "enc_gain_one": jnp.clip(1.0 + 0.15 * jax.random.normal(seeds[4], (D,), jnp.float32), 0.25, 1.75).astype(jnp.bfloat16),
        "enc_qkv": scatter_about(seeds[5], (D, 3, D), D ** -0.5, 0.1875, ((2, 4),)),
        "enc_out": scatter_about(seeds[6], (D, D), (D // 8) ** -0.5, 0.5, ((1, 4),)),
        "enc_gain_two": jnp.clip(1.0 + 0.15 * jax.random.normal(seeds[7], (D,), jnp.float32), 0.25, 1.75).astype(jnp.bfloat16),
        "enc_up": scatter_about(seeds[8], (D, MLP), D ** -0.5, 0.1875, ((1, 4),)),
        "enc_down": scatter_about(seeds[9], (D, MLP), MLP ** -0.5, 0.09375, ((1, 4),)),
        "w_proj": scatter_about(seeds[10], (D, DEC), D ** -0.5, 0.1875),
        "mask_token": scatter_about(seeds[11], (DEC,), 1.0, 4.0),
        "pos_table": jnp.clip(jax.random.uniform(seeds[12], (LEVELS, GRID, DEC), jnp.float32, -1.0, 1.0), -1.0, 1.0).astype(jnp.bfloat16),
        "dec_gain_one": jnp.clip(1.0 + 0.15 * jax.random.normal(seeds[13], (DEC,), jnp.float32), 0.25, 1.75).astype(jnp.bfloat16),
        "dec_qkv": scatter_about(seeds[14], (DEC, 3, DEC), DEC ** -0.5, 0.25, ((2, 4),)),
        "dec_out": scatter_about(seeds[15], (DEC, DEC), (DEC // 16) ** -0.5, 1.0, ((1, 4),)),
        "dec_gain_two": jnp.clip(1.0 + 0.15 * jax.random.normal(seeds[16], (DEC,), jnp.float32), 0.25, 1.75).astype(jnp.bfloat16),
        "dec_up": scatter_about(seeds[17], (DEC, DEC_MLP), DEC ** -0.5, 0.25, ((1, 4),)),
        "dec_down": scatter_about(seeds[18], (DEC, DEC_MLP), DEC_MLP ** -0.5, 0.125, ((1, 4),)),
        "decoded_grad": scatter_about(seeds[19], (GRID, IMAGES, DEC), 1.0, 6.0, ((0, 4), (1, 4))),
    }


@jax.custom_vjp
def low(v):
    return lax.optimization_barrier(v.astype(jnp.bfloat16)).astype(jnp.float32)

@jax.custom_vjp
def low_back(v):
    return v

def low_keep(v):
    return (low(v), None)

def low_pass(kept, grad):
    return (grad,)

def back_keep(v):
    return (v, None)

def back_low(kept, grad):
    return (low(grad),)
low.defvjp(low_keep, low_pass)
low_back.defvjp(back_keep, back_low)
eps = 1e-06
precise = lax.Precision.HIGHEST

def layer_norm(values, gain_vec):
    average = lax.optimization_barrier(jnp.mean(values, axis=-1, keepdims=True))
    centered = values - average
    variance = lax.optimization_barrier(jnp.mean(centered * centered, axis=-1, keepdims=True))
    return centered * lax.rsqrt(variance + eps) * gain_vec

def layer_block(values, visible, weights, head_count):
    gain_one, w_qkv, w_out, gain_two, w_up, w_down = weights
    length = values.shape[0]
    images_in = values.shape[1]
    feature_width = values.shape[2]
    head_size = feature_width // head_count
    normed = low(layer_norm(values, gain_one))
    qkv_rows = low_back(low(jnp.einsum('sbw,wcf->sbcf', normed, w_qkv, precision=precise)))
    heads_view = qkv_rows.reshape(length, images_in, 3, head_count, head_size)
    scores = jnp.einsum('sbhe,tbhe->bhst', heads_view[:, :, 0], heads_view[:, :, 1], precision=precise)
    scores = low_back(scores * (1.0 / math.sqrt(head_size)))
    scores = jnp.where(visible[:, None, None, :], scores, -1e+30)
    probability = jax.nn.softmax(scores, axis=-1)
    context = jnp.einsum('bhst,tbhe->sbhe', low(probability), heads_view[:, :, 2], precision=precise)
    context = low_back(low(context.reshape(length, images_in, feature_width)))
    mixed_rows = low_back(jnp.einsum('sbf,wf->sbw', context, w_out, precision=precise))
    middle = values + mixed_rows
    normed_two = low(layer_norm(middle, gain_two))
    upper_in = low_back(jnp.einsum('sbw,wf->sbf', normed_two, w_up, precision=precise))
    hidden = low(jax.nn.gelu(upper_in, approximate=False))
    down_out = low_back(jnp.einsum('sbf,wf->sbw', hidden, w_down, precision=precise))
    return middle + down_out

def decoder_order(tensor):
    extent = tensor.shape
    per_device = IMAGES // N_DP
    splitted = tensor.reshape((extent[0], N_DP, per_device // N_DP, N_DP) + extent[2:])
    return jnp.moveaxis(splitted, 3, 1).reshape(extent)

def grouped(tensor, group_size):
    extent = tensor.shape
    splitted = tensor.reshape((extent[0], extent[1] // group_size, group_size) + extent[2:])
    return jnp.moveaxis(splitted, 1, 0)

def ungrouped(tensor):
    reordered = jnp.moveaxis(tensor, 0, 1)
    extent = reordered.shape
    return reordered.reshape((extent[0], extent[1] * extent[2]) + extent[3:])

def reference(patches, counts, patch_index, scale_level, enc_gain_one, enc_qkv, enc_out, enc_gain_two, enc_up, enc_down, w_proj, mask_token, pos_table, dec_gain_one, dec_qkv, dec_out, dec_gain_two, dec_up, dec_down, decoded_grad):
    group_size = 16
    visible = jnp.arange(SLOT, dtype=jnp.int32)[:, None] < counts[None, :]
    index_grid = decoder_order(patch_index)
    visible_grid = decoder_order(visible)
    level_grid = decoder_order(scale_level[None, :])[0]
    table_full = pos_table.astype(jnp.float32)
    patch_ids = jnp.arange(GRID, dtype=jnp.int32)
    all_visible = jnp.ones((group_size, GRID), dtype=bool)

    def forward(values, enc_weights, proj_weight, token_vec, dec_weights):

        def encode_group(bundle):
            block_out = layer_block(bundle[0], jnp.transpose(bundle[1]), enc_weights, HEADS)
            return low_back(low(jnp.einsum('sbw,wf->sbf', low(block_out), proj_weight, precision=precise)))
        sent_rows = ungrouped(lax.map(jax.checkpoint(encode_group), (grouped(values, group_size), grouped(visible, group_size))))
        sent_grid = decoder_order(sent_rows)

        def decode_group(bundle):
            rows_sent, index_rows, visible_rows, levels = bundle
            onehot = jnp.where(visible_rows[:, :, None] & (index_rows[:, :, None] == patch_ids[None, None, :]), 1.0, 0.0).astype(jnp.float32)
            placed = jnp.einsum('sbp,sbf->pbf', onehot, rows_sent, precision=precise)
            covered = jnp.transpose(lax.optimization_barrier(jnp.sum(onehot, axis=0)))
            position = jnp.transpose(table_full[levels], (1, 0, 2))
            grid_values = placed + (1.0 - covered)[:, :, None] * token_vec + position
            return layer_block(grid_values, all_visible, dec_weights, DEC_HEADS)
        bundles = (grouped(sent_grid, group_size), grouped(index_grid, group_size), grouped(visible_grid, group_size), level_grid.reshape(-1, group_size))
        return ungrouped(lax.map(jax.checkpoint(decode_group), bundles))
    enc_weights = tuple((weight.astype(jnp.float32) for weight in (enc_gain_one, enc_qkv, enc_out, enc_gain_two, enc_up, enc_down)))
    dec_weights = tuple((weight.astype(jnp.float32) for weight in (dec_gain_one, dec_qkv, dec_out, dec_gain_two, dec_up, dec_down)))
    decoded, pullback = jax.vjp(forward, patches.astype(jnp.float32), enc_weights, w_proj.astype(jnp.float32), mask_token.astype(jnp.float32), dec_weights)
    grad_values, grad_enc, grad_proj, grad_token, grad_dec = pullback(decoded_grad.astype(jnp.float32))
    return (decoded, grad_values, grad_enc[1], grad_enc[2], grad_enc[4], grad_enc[5], grad_dec[1], grad_dec[2], grad_dec[4], grad_dec[5], grad_proj, grad_enc[0], grad_enc[3], grad_dec[0], grad_dec[3], grad_token)
```

```python
import functools
import math

import jax
import jax.numpy as jnp
from jax import lax
from jax.experimental import pallas as pl
from jax.experimental.pallas import tpu as pltpu
from jax.sharding import PartitionSpec as P

HEAD = 64
DEC_HEAD = 32


eps = 1e-06


def norm_rows(values):
    average = jnp.mean(values, axis=-1, keepdims=True)
    centered = values - average
    variance = jnp.mean(centered * centered, axis=-1, keepdims=True)
    inverse = lax.rsqrt(variance + eps)
    return (centered * inverse, inverse)


def norm_back(normal, inverse, gain_vec, gradient):
    weighted = gradient * gain_vec
    first_term = jnp.mean(weighted, axis=-1, keepdims=True)
    second_term = jnp.mean(weighted * normal, axis=-1, keepdims=True)
    return (
        inverse * (weighted - first_term - normal * second_term),
        jnp.sum(gradient * normal, axis=(0, 1)),
    )


def spread(values):
    return lax.all_gather(values, "mp", axis=0, tiled=True)


def collect(values):
    return lax.psum_scatter(values, "mp", scatter_dimension=0, tiled=True)


def spare_of(work):
    return lambda: jax.tree.map(jnp.zeros_like, work())


def head_view(qkv_rows, head_size):
    return qkv_rows.reshape(
        qkv_rows.shape[0], qkv_rows.shape[1], 3, qkv_rows.shape[3] // head_size, head_size
    )


def score_rows(queries, key_rows, visible, head_size):
    scores = jnp.einsum(
        "sbhe,tbhe->bhst", queries, key_rows, preferred_element_type=jnp.float32
    ) * (1.0 / math.sqrt(head_size))
    return jnp.where(visible[:, None, None, :], scores, -1e30)


def attend(qkv_rows, visible, head_size):
    heads_view = head_view(qkv_rows, head_size)
    scores = score_rows(heads_view[:, :, 0], heads_view[:, :, 1], visible, head_size)
    highest = jnp.max(scores, axis=-1, keepdims=True)
    weights = jnp.exp(scores - highest)
    denominator = jnp.sum(weights, axis=-1, keepdims=True)
    probability = (weights / denominator).astype(jnp.bfloat16)
    context = jnp.einsum(
        "bhst,tbhe->sbhe", probability, heads_view[:, :, 2], preferred_element_type=jnp.float32
    )
    context = context.reshape(qkv_rows.shape[0], qkv_rows.shape[1], qkv_rows.shape[3]).astype(
        jnp.bfloat16
    )
    return (context, highest + jnp.log(denominator))


def attend_back(qkv_rows, visible, logsum, grad_context, head_size):
    heads_view = head_view(qkv_rows, head_size)
    queries = heads_view[:, :, 0]
    key_rows = heads_view[:, :, 1]
    value_rows = heads_view[:, :, 2]
    probability = jnp.exp(score_rows(queries, key_rows, visible, head_size) - logsum)
    grad_heads = grad_context.reshape(queries.shape)
    grad_values = jnp.einsum(
        "bhst,sbhe->tbhe",
        probability.astype(jnp.bfloat16),
        grad_heads,
        preferred_element_type=jnp.float32,
    )
    grad_probs = jnp.einsum(
        "sbhe,tbhe->bhst", grad_heads, value_rows, preferred_element_type=jnp.float32
    )
    row_inner = jnp.sum(grad_probs * probability, axis=-1, keepdims=True)
    grad_scores = (probability * (grad_probs - row_inner)).astype(jnp.bfloat16)
    score_scale = 1.0 / math.sqrt(head_size)
    grad_queries = (
        jnp.einsum("bhst,tbhe->sbhe", grad_scores, key_rows, preferred_element_type=jnp.float32)
        * score_scale
    )
    grad_keys = (
        jnp.einsum("bhst,sbhe->tbhe", grad_scores, queries, preferred_element_type=jnp.float32)
        * score_scale
    )
    stacked = jnp.stack([grad_queries, grad_keys, grad_values], axis=2)
    return stacked.reshape(qkv_rows.shape).astype(jnp.bfloat16)


def attention_local(normed_one, visible, w_qkv, w_out, head_size):
    qkv_rows = jnp.einsum(
        "sbw,wcf->sbcf", normed_one, w_qkv, preferred_element_type=jnp.float32
    ).astype(jnp.bfloat16)
    context, logsum = attend(qkv_rows, visible, head_size)
    mixed_terms = jnp.einsum("sbf,wf->sbw", context, w_out, preferred_element_type=jnp.float32)
    return (qkv_rows, context, logsum, mixed_terms)


def feed_local(normed_two, w_up, w_down):
    upper_in = jnp.einsum("sbw,wf->sbf", normed_two, w_up, preferred_element_type=jnp.float32)
    hidden = jax.nn.gelu(upper_in, approximate=False).astype(jnp.bfloat16)
    return (upper_in, jnp.einsum("sbf,wf->sbw", hidden, w_down, preferred_element_type=jnp.float32))


def feed_back_local(grad_full, normed_two, upper_in, w_up, w_down):
    value_out, gelu_pull = jax.vjp(
        lambda argument: jax.nn.gelu(argument, approximate=False), upper_in
    )
    hidden = value_out.astype(jnp.bfloat16)
    grad_down_w = jnp.einsum("sbw,sbf->wf", grad_full, hidden, preferred_element_type=jnp.float32)
    grad_hidden = jnp.einsum("sbw,wf->sbf", grad_full, w_down, preferred_element_type=jnp.float32)
    grad_upper = gelu_pull(grad_hidden)[0].astype(jnp.bfloat16)
    grad_up_w = jnp.einsum(
        "sbw,sbf->wf", normed_two, grad_upper, preferred_element_type=jnp.float32
    )
    grad_terms = jnp.einsum("sbf,wf->sbw", grad_upper, w_up, preferred_element_type=jnp.float32)
    return (grad_up_w, grad_down_w, grad_terms)


def attention_back_local(
    grad_full, qkv_rows, context, logsum, visible, normed_one, w_qkv, w_out, head_size
):
    grad_out_w = jnp.einsum("sbw,sbf->wf", grad_full, context, preferred_element_type=jnp.float32)
    grad_context = jnp.einsum(
        "sbw,wf->sbf", grad_full, w_out, preferred_element_type=jnp.float32
    ).astype(jnp.bfloat16)
    grad_qkv = attend_back(qkv_rows, visible, logsum, grad_context, head_size)
    grad_qkv_w = jnp.einsum(
        "sbw,sbcf->wcf", normed_one, grad_qkv, preferred_element_type=jnp.float32
    )
    grad_normed = jnp.einsum("sbcf,wcf->sbw", grad_qkv, w_qkv, preferred_element_type=jnp.float32)
    return (grad_qkv_w, grad_out_w, grad_normed)


def on_device(
    patches,
    counts,
    patch_index,
    scale_level,
    enc_gain_one,
    enc_qkv,
    enc_out,
    enc_gain_two,
    enc_up,
    enc_down,
    w_proj,
    mask_token,
    pos_table,
    dec_gain_one,
    dec_qkv,
    dec_out,
    dec_gain_two,
    dec_up,
    dec_down,
    decoded_grad,
):
    data_ways = lax.axis_size("dp")
    model_ways = lax.axis_size("mp")
    slot_rows = patches.shape[0]
    images = patches.shape[1]
    grid_rows = decoded_grad.shape[0]
    dec_width = decoded_grad.shape[2]
    slot_count = slot_rows * model_ways
    grid_count = grid_rows * model_ways
    per_peer = images // data_ways
    slot_start = lax.axis_index("mp") * slot_rows
    grid_start = lax.axis_index("mp") * grid_rows
    is_encoder = lax.axis_index("section") == 0
    visible = jnp.arange(slot_count, dtype=jnp.int32)[None, :] < counts[:, None]
    all_visible = jnp.ones((images, grid_count), dtype=bool)
    enc_g1 = enc_gain_one.astype(jnp.float32)
    enc_g2 = enc_gain_two.astype(jnp.float32)
    dec_g1 = dec_gain_one.astype(jnp.float32)
    dec_g2 = dec_gain_two.astype(jnp.float32)
    token_vec = mask_token.astype(jnp.float32)

    def on_encoder(work):
        return lax.cond(is_encoder, work, spare_of(work))

    def on_decoder(work):
        return lax.cond(is_encoder, spare_of(work), work)

    full_in = spread(patches)

    def enc_attention():
        normal_one, inverse_one = norm_rows(full_in.astype(jnp.float32))
        normed_one = (normal_one * enc_g1).astype(jnp.bfloat16)
        return attention_local(normed_one, visible, enc_qkv, enc_out, HEAD)

    enc_qkv_rows, enc_context, enc_logsum, enc_mixed_terms = on_encoder(enc_attention)
    enc_middle = patches.astype(jnp.float32) + collect(enc_mixed_terms)
    enc_normal_two, enc_inverse_two = norm_rows(enc_middle)
    enc_normed_two = spread((enc_normal_two * enc_g2).astype(jnp.bfloat16))
    enc_upper, enc_down_terms = on_encoder(lambda: feed_local(enc_normed_two, enc_up, enc_down))
    enc_out_low = (enc_middle + collect(enc_down_terms)).astype(jnp.bfloat16)

    def enc_send():
        sent_rows = jnp.einsum(
            "sbw,wf->sbf", enc_out_low, w_proj, preferred_element_type=jnp.float32
        ).astype(jnp.bfloat16)
        live_slot = (slot_start + jnp.arange(slot_rows, dtype=jnp.int32))[:, None] < counts[None, :]
        sent_index = jnp.where(live_slot, patch_index, grid_count)
        packed = (
            sent_rows.reshape(slot_rows, per_peer, data_ways, dec_width),
            sent_index.reshape(slot_rows, per_peer, data_ways),
            scale_level.reshape(1, per_peer, data_ways),
        )
        packed = tuple(
            (jnp.concatenate([jnp.zeros_like(member), member], axis=2) for member in packed)
        )
        return packed

    packed = on_encoder(enc_send)
    received = (
        lax.all_to_all(packed[0], ("section", "dp"), split_axis=2, concat_axis=1, tiled=True),
        lax.all_to_all(packed[1], ("section", "dp"), split_axis=2, concat_axis=1, tiled=True),
        lax.all_to_all(packed[2], ("section", "dp"), split_axis=2, concat_axis=1, tiled=True),
    )
    arrived = (received[0][:, :images, 0], received[1][:, :images, 0], received[2][0, :images, 0])
    arrived_rows, arrived_index, arrived_level = arrived

    def make_onehot():
        return (
            arrived_index[:, :, None] == jnp.arange(grid_count, dtype=jnp.int32)[None, None, :]
        ).astype(jnp.bfloat16)

    def dec_place():
        onehot_low = make_onehot()
        covered = jnp.transpose(jnp.sum(onehot_low.astype(jnp.float32), axis=0))
        placed = jnp.einsum(
            "sbp,sbf->pbf", onehot_low, arrived_rows, preferred_element_type=jnp.float32
        )
        return (placed - covered[:, :, None] * token_vec, covered)

    placed_terms, covered_terms = on_decoder(dec_place)
    placed_rows, covered_rows = collect((placed_terms, covered_terms))
    table_rows = lax.dynamic_slice_in_dim(pos_table, grid_start, grid_rows, 1)
    level_hot = (
        arrived_level[:, None] == jnp.arange(pos_table.shape[0], dtype=jnp.int32)[None, :]
    ).astype(jnp.bfloat16)
    position = jnp.einsum("bl,lpf->pbf", level_hot, table_rows, preferred_element_type=jnp.float32)
    grid_values = placed_rows + token_vec + position
    dec_normal_one, dec_inverse_one = norm_rows(grid_values)
    dec_normed_one = spread((dec_normal_one * dec_g1).astype(jnp.bfloat16))
    dec_qkv_rows, dec_context, dec_logsum, dec_mixed_terms = on_decoder(
        lambda: attention_local(dec_normed_one, all_visible, dec_qkv, dec_out, DEC_HEAD)
    )
    dec_middle = grid_values + collect(dec_mixed_terms)
    dec_normal_two, dec_inverse_two = norm_rows(dec_middle)
    dec_normed_two = spread((dec_normal_two * dec_g2).astype(jnp.bfloat16))

    def dec_feed():
        upper_in, down_terms = feed_local(dec_normed_two, dec_up, dec_down)
        own_rows = lax.dynamic_slice_in_dim(down_terms, grid_start, grid_rows, 0) + dec_middle
        return (upper_in, lax.dynamic_update_slice_in_dim(down_terms, own_rows, grid_start, 0))

    dec_upper, dec_summand = on_decoder(dec_feed)
    decoded = lax.psum_scatter(
        dec_summand.astype(jnp.bfloat16), ("section", "mp"), scatter_dimension=2, tiled=True
    ).astype(jnp.float32)
    dec_grad_full = spread(decoded_grad)
    dec_up_grad, dec_down_grad, dec_two_terms = on_decoder(
        lambda: feed_back_local(dec_grad_full, dec_normed_two, dec_upper, dec_up, dec_down)
    )
    dec_through, dec_gain_two_grad = norm_back(
        dec_normal_two, dec_inverse_two, dec_g2, collect(dec_two_terms)
    )
    dec_grad_middle = decoded_grad.astype(jnp.float32) + dec_through
    dec_middle_full = spread(dec_grad_middle.astype(jnp.bfloat16))
    dec_qkv_grad, dec_out_grad, dec_one_terms = on_decoder(
        lambda: attention_back_local(
            dec_middle_full,
            dec_qkv_rows,
            dec_context,
            dec_logsum,
            all_visible,
            dec_normed_one,
            dec_qkv,
            dec_out,
            DEC_HEAD,
        )
    )
    dec_inner, dec_gain_one_grad = norm_back(
        dec_normal_one, dec_inverse_one, dec_g1, collect(dec_one_terms)
    )
    grad_grid = dec_grad_middle + dec_inner
    grad_token = jnp.sum(grad_grid * (1.0 - covered_rows)[:, :, None], axis=(0, 1))
    grad_grid_full = spread(grad_grid.astype(jnp.bfloat16))

    def dec_return():
        grad_sent = jnp.einsum(
            "sbp,pbf->sbf", make_onehot(), grad_grid_full, preferred_element_type=jnp.float32
        ).astype(jnp.bfloat16)
        return jnp.concatenate([grad_sent, jnp.zeros_like(grad_sent)], axis=1)[:, :, None, :]

    back_rows = on_decoder(dec_return)
    returned = lax.all_to_all(
        back_rows, ("section", "dp"), split_axis=1, concat_axis=2, tiled=True
    )[:, :, data_ways:]
    grad_arrived = returned.reshape(slot_rows, images, dec_width)

    def enc_project_back():
        grad_proj_w = jnp.einsum(
            "sbw,sbf->wf", enc_out_low, grad_arrived, preferred_element_type=jnp.float32
        )
        grad_block = jnp.einsum(
            "sbf,wf->sbw", grad_arrived, w_proj, preferred_element_type=jnp.float32
        )
        return (grad_proj_w, grad_block)

    proj_grad, enc_grad_block = on_encoder(enc_project_back)
    enc_grad_full = spread(enc_grad_block.astype(jnp.bfloat16))
    enc_up_grad, enc_down_grad, enc_two_terms = on_encoder(
        lambda: feed_back_local(enc_grad_full, enc_normed_two, enc_upper, enc_up, enc_down)
    )
    enc_through, enc_gain_two_grad = norm_back(
        enc_normal_two, enc_inverse_two, enc_g2, collect(enc_two_terms)
    )
    enc_grad_middle = enc_grad_block + enc_through
    enc_middle_full = spread(enc_grad_middle.astype(jnp.bfloat16))

    def enc_attention_back():
        normal_one, inverse_one = norm_rows(full_in.astype(jnp.float32))
        normed_one = (normal_one * enc_g1).astype(jnp.bfloat16)
        grad_qkv_w, grad_out_w, grad_normed = attention_back_local(
            enc_middle_full,
            enc_qkv_rows,
            enc_context,
            enc_logsum,
            visible,
            normed_one,
            enc_qkv,
            enc_out,
            HEAD,
        )
        grad_inner, grad_gain_one = norm_back(normal_one, inverse_one, enc_g1, grad_normed)
        own_rows = lax.dynamic_slice_in_dim(grad_inner, slot_start, slot_rows, 0) + enc_grad_middle
        summand = lax.dynamic_update_slice_in_dim(grad_inner, own_rows, slot_start, 0)
        return (grad_qkv_w, grad_out_w, grad_gain_one, summand)

    enc_qkv_grad, enc_out_grad, enc_gain_one_grad, in_summand = on_encoder(enc_attention_back)
    patches_grad = lax.psum_scatter(
        in_summand.astype(jnp.bfloat16), ("section", "mp"), scatter_dimension=2, tiled=True
    ).astype(jnp.float32)
    enc_gain_two_grad = jnp.where(is_encoder, enc_gain_two_grad, 0.0)
    dec_gain_one_grad = jnp.where(is_encoder, 0.0, dec_gain_one_grad)
    dec_gain_two_grad = jnp.where(is_encoder, 0.0, dec_gain_two_grad)
    grad_token = jnp.where(is_encoder, 0.0, grad_token)
    sharded = (
        lax.psum_scatter(enc_qkv_grad, ("section", "dp"), scatter_dimension=0, tiled=True),
        lax.psum_scatter(enc_out_grad, ("section", "dp"), scatter_dimension=0, tiled=True),
        lax.psum_scatter(enc_up_grad, ("section", "dp"), scatter_dimension=0, tiled=True),
        lax.psum_scatter(enc_down_grad, ("section", "dp"), scatter_dimension=0, tiled=True),
        lax.psum_scatter(dec_qkv_grad, ("section", "dp"), scatter_dimension=0, tiled=True),
        lax.psum_scatter(dec_out_grad, ("section", "dp"), scatter_dimension=0, tiled=True),
        lax.psum_scatter(dec_up_grad, ("section", "dp"), scatter_dimension=0, tiled=True),
        lax.psum_scatter(dec_down_grad, ("section", "dp"), scatter_dimension=0, tiled=True),
    )
    shared = lax.psum(
        (
            proj_grad,
            enc_gain_one_grad,
            enc_gain_two_grad,
            dec_gain_one_grad,
            dec_gain_two_grad,
            grad_token,
        ),
        ("section", "dp", "mp"),
    )
    return (
        decoded,
        patches_grad,
        sharded[0],
        sharded[1],
        sharded[2],
        sharded[3],
        sharded[4],
        sharded[5],
        sharded[6],
        sharded[7],
        shared[0],
        shared[1],
        shared[2],
        shared[3],
        shared[4],
        shared[5],
    )


def placed_on(mesh, body):
    placed = (
        P("mp", "dp", None),
        P("dp"),
        P("mp", "dp"),
        P("dp"),
        P(),
        P(None, None, "mp"),
        P(None, "mp"),
        P(),
        P(None, "mp"),
        P(None, "mp"),
        P(),
        P(),
        P(),
        P(),
        P(None, None, "mp"),
        P(None, "mp"),
        P(),
        P(None, "mp"),
        P(None, "mp"),
        P("mp", "dp", None),
    )
    return jax.shard_map(
        body,
        mesh=mesh,
        in_specs=placed,
        out_specs=(
            P(None, "dp", ("section", "mp")),
            P(None, "dp", ("section", "mp")),
            P(("section", "dp"), None, "mp"),
            P(("section", "dp"), "mp"),
            P(("section", "dp"), "mp"),
            P(("section", "dp"), "mp"),
            P(("section", "dp"), None, "mp"),
            P(("section", "dp"), "mp"),
            P(("section", "dp"), "mp"),
            P(("section", "dp"), "mp"),
            P(),
            P(),
            P(),
            P(),
            P(),
            P(),
        ),
        check_vma=False,
    )


MESH = pl.DeviceIdType.MESH
F32 = jnp.float32
BF16 = jnp.bfloat16
WAYS = 4
PAIR = 2
SLOTS = 64
SHARD = 16
PATCHES = 49
ROWS = 64
WIDTH = 1024
DEC_WIDTH = 512
HEADS_HERE = 4
COPIES = 192


def dot(left, right, left_dim, right_dim):
    return lax.dot_general(
        left, right, (((left_dim,), (right_dim,)), ((), ())), preferred_element_type=F32
    )


def rows_back(normal, inverse, gain, gradient):
    weighted = gradient * gain
    first = jnp.mean(weighted, axis=-1, keepdims=True)
    second = jnp.mean(weighted * normal, axis=-1, keepdims=True)
    return inverse * (weighted - first - normal * second)


def gelu_both(upper):
    phi = 0.5 * (1.0 + lax.erf(upper * math.sqrt(0.5)))
    density = jnp.exp(-0.5 * upper * upper) * (1.0 / math.sqrt(2.0 * math.pi))
    return upper * phi, phi + upper * density


def head_mask(width, head, kind):
    lane = lax.broadcasted_iota(jnp.int32, (1, width), 1)
    return [
        ((lane >= h * head) & (lane < (h + 1) * head)).astype(F32).astype(kind)
        for h in range(HEADS_HERE)
    ]


def stack_heads(values, masks):
    return jnp.concatenate([values * mask for mask in masks], axis=0)


def fold_heads(stacked, masks, rows):
    total = None
    for h, mask in enumerate(masks):
        part = stacked[h * rows : (h + 1) * rows] * mask
        total = part if total is None else total + part
    return total


def attention(qkv, keep, rows, width, head, scale):
    low = head_mask(width, head, BF16)
    wide = head_mask(width, head, F32)
    queries = stack_heads(qkv[:, :width], low)
    scores = dot(queries, qkv[:, width : 2 * width], 1, 1) * scale
    scores = jnp.where(keep, scores, -1e30)
    weights = jnp.exp(scores - jnp.max(scores, axis=-1, keepdims=True))
    probs = weights / jnp.sum(weights, axis=-1, keepdims=True)
    mixed = dot(probs.astype(BF16), qkv[:, 2 * width :], 1, 0)
    return probs, fold_heads(mixed, wide, rows).astype(BF16)


def attention_back(qkv, probs, grad_context, rows, width, head, scale):
    low = head_mask(width, head, BF16)
    wide = head_mask(width, head, F32)
    queries = stack_heads(qkv[:, :width], low)
    grads = stack_heads(grad_context, low)
    grad_probs = dot(grads, qkv[:, 2 * width :], 1, 1)
    inner = jnp.sum(grad_probs * probs, axis=-1, keepdims=True)
    grad_scores = (probs * (grad_probs - inner)).astype(BF16)
    grad_queries = fold_heads(dot(grad_scores, qkv[:, width : 2 * width], 1, 0), wide, rows) * scale
    grad_keys = dot(grad_scores, queries, 0, 0) * scale
    grad_values = dot(probs.astype(BF16), grads, 0, 0)
    return jnp.concatenate([grad_queries, grad_keys, grad_values], axis=1).astype(BF16)


IN_NAMES = [
    "xs",
    "info",
    "keep",
    "gains",
    "dgrad",
    "w_qkv",
    "w_out",
    "w_up",
    "w_down",
    "w_proj",
    "table",
    "d_qkv",
    "d_out",
    "d_up",
    "d_down",
]
OUT_NAMES = [
    "o_dec",
    "o_pat",
    "o_qkv",
    "o_out",
    "o_up",
    "o_down",
    "o_dqkv",
    "o_dout",
    "o_dup",
    "o_ddown",
    "o_proj",
    "o_vec",
]
LOADED = dict(
    w_qkv=(WIDTH, 768),
    w_out=(WIDTH, 256),
    w_up=(WIDTH, 1024),
    w_down=(WIDTH, 1024),
    w_proj=(WIDTH, DEC_WIDTH),
    table=(8, 256, DEC_WIDTH),
    d_qkv=(DEC_WIDTH, 384),
    d_out=(DEC_WIDTH, 128),
    d_up=(DEC_WIDTH, 512),
    d_down=(DEC_WIDTH, 512),
)
BUFFERS = dict(
    xf=((2, 64, 1024), BF16),
    qkv=((2, 64, 768), BF16),
    probs=((2, 256, 64), F32),
    s1=((2, 64, 1024), BF16),
    r1=((3, 2, 16, 1024), BF16),
    mid=((2, 16, 1024), F32),
    n2=((2, 64, 1024), BF16),
    gp=((128, 1024), F32),
    s2=((2, 64, 1024), BF16),
    r2=((3, 2, 16, 1024), BF16),
    eo=((2, 16, 1024), BF16),
    eom=((2, 64, 256), BF16),
    sent=((2, 16, 512), BF16),
    arr=((2, 64, 512), BF16),
    meta=((2, 4, 8, 128), jnp.int32),
    dgf=((2, 256, 512), BF16),
    hot=((2, 256, 64), BF16),
    free=((2, 256, 1), F32),
    grid=((2, 256, 512), F32),
    dn1=((512, 512), BF16),
    dqkv=((512, 384), BF16),
    dprobs=((2, 1024, 256), F32),
    dctx=((512, 128), BF16),
    s3=((2, 256, 512), BF16),
    r3=((3, 2, 64, 512), BF16),
    dmid=((2, 64, 512), F32),
    dn2=((2, 256, 512), BF16),
    dhid=((512, 512), BF16),
    dgh=((512, 512), F32),
    dgu=((512, 512), BF16),
    s4=((2, 256, 512), BF16),
    r4=((3, 2, 64, 512), BF16),
    ds=((8, 256, 128), BF16),
    dr=((8, 256, 128), BF16),
    dgm=((2, 256, 512), BF16),
    dgq=((512, 384), BF16),
    s5=((2, 64, 512), BF16),
    r5=((3, 2, 16, 512), BF16),
    sg=((2, 16, 512), BF16),
    sgf=((2, 64, 512), BF16),
    wds=((256, 1536), BF16),
    wdr=((256, 1536), BF16),
    wdo=((256, 1536), F32),
    wzs=((4, 64, 1536), BF16),
    wzr=((3, 64, 1536), BF16),
    s6=((2, 64, 1024), BF16),
    r6=((3, 2, 16, 1024), BF16),
    gy=((128, 1024), BF16),
    gyo=((2, 16, 512), BF16),
    gm=((2, 64, 1024), BF16),
    fs=((8, 128, 128), BF16),
    fr=((8, 128, 128), BF16),
    hz=((4, 128, 1024), BF16),
    cz=((4, 128, 256), BF16),
    uz=((4, 128, 1024), BF16),
    qz=((4, 128, 768), BF16),
    xb=((4, 2, 4, 128, 128), BF16),
    xz=((4, 4, 2, 128, 128), BF16),
    wes=((128, 3072), BF16),
    wer=((128, 3072), BF16),
    ps=((2, 128, 512), BF16),
    pr=((128, 512), BF16),
    po=((128, 512), F32),
    pzs=((4, 32, 512), BF16),
    pzr=((3, 32, 512), BF16),
    pz=((4, 32, 512), BF16),
    pa=((4, 2, 128, 512), BF16),
    vec=((8, 512), F32),
    vr=((8, 8, 512), F32),
    vz=((4, 8, 512), F32),
)


class Refs:
    pass


def kernel(*refs):
    r = Refs()
    names = IN_NAMES + OUT_NAMES + list(BUFFERS) + ["v_" + n for n in LOADED]
    for name, ref in zip(names, refs):
        setattr(r, name, ref)
    load_sem, send_sem, recv_sem = refs[len(names) :]
    s, d, m = (lax.axis_index(a) for a in ("section", "dp", "mp"))
    used = [0]
    started = []

    def take(count):
        used[0] += count
        return used[0] - count

    def copy(src, dst, device, at, land=None):
        return pltpu.make_async_remote_copy(
            src_ref=src,
            dst_ref=dst,
            send_sem=send_sem.at[at],
            recv_sem=recv_sem.at[at if land is None else land],
            device_id=device,
            device_id_type=MESH,
        )

    def send(src, dst, device):
        made = copy(src, dst, device, take(1))
        made.start()
        started.append(made)
        return made

    def arrive(copies):
        for made in copies:
            made.wait_recv()

    def model(k):
        return lax.rem(m + k, WAYS)

    def data(k):
        return lax.rem(d + k, WAYS)

    def gather(ref, rows):
        own = ref.at[:, pl.ds(pl.multiple_of(m * rows, rows), rows)]
        return [send(own, own, {"mp": model(k)}) for k in (1, 2, 3)]

    def scatter(src, dst, rows):
        copies = []
        for k in (1, 2, 3):
            to = model(k)
            part = src.at[:, pl.ds(pl.multiple_of(to * rows, rows), rows)]
            copies.append(send(part, dst.at[k - 1], {"mp": to}))
        return copies

    def summed(src, dst, rows):
        total = src[:, pl.ds(pl.multiple_of(m * rows, rows), rows), :].astype(F32)
        for k in range(3):
            total = total + dst[k].astype(F32)
        return total

    def along(ref):
        return [send(ref.at[d], ref.at[d], {"dp": data(k)}) for k in (1, 2, 3)]

    def cuts(which, values):
        for block in range(8):
            r.xb[which, block // 4, block % 4] = values[:, block * 128 : (block + 1) * 128]
        r.xz[which, d] = r.xb[which, :, d]
        return [
            send(r.xb.at[which, :, data(k)], r.xz.at[which, d], {"dp": data(k)}) for k in (1, 2, 3)
        ]

    plane = [(a, k) for a in (0, 1) for k in range(4) if (a, k) != (0, 0)]

    def to_plane(a, k):
        return {"section": lax.rem(s + a, 2), "mp": model(k)}

    half = d // 2
    place = lax.rem(d, 2)

    def across(i, k):
        return {"section": half, "dp": 2 * s + i, "mp": model(k)}

    def mine(i):
        return (half == s) & (2 * s + i == d)

    def exchange(src_of, dst_of, own):
        at = take(8)
        for i in range(PAIR):
            for k in range(4):
                made = copy(
                    src_of(i), dst_of(place, m), across(i, k), at + 4 * i + k, at + 4 * place + k
                )
                if k:
                    made.start()
                else:
                    pl.when(jnp.logical_not(mine(i)))(made.start)
                    pl.when(mine(i))(functools.partial(own, i))

        def landed():
            for i in range(PAIR):
                for k in range(4):
                    made = copy(src_of(i), dst_of(i, model(4 - k)), across(i, k), at + 4 * i + k)
                    if k:
                        made.wait_recv()
                    else:
                        pl.when(jnp.logical_not(mine(i)))(made.wait_recv)

        def left():
            for i in range(PAIR):
                for k in range(4):
                    made = copy(src_of(i), dst_of(place, m), across(i, k), at + 4 * i + k)
                    if k:
                        made.wait_send()
                    else:
                        pl.when(jnp.logical_not(mine(i)))(made.wait_send)

        return landed, left

    loads = {}
    for at, name in enumerate(LOADED):
        loads[name] = pltpu.make_async_copy(
            getattr(r, name), getattr(r, "v_" + name), load_sem.at[at]
        )
        loads[name].start()

    barrier = pltpu.get_barrier_semaphore()
    for a, k in plane:
        pl.semaphore_signal(barrier, inc=1, device_id=to_plane(a, k), device_id_type=MESH)
    for k in (1, 2, 3):
        pl.semaphore_signal(barrier, inc=1, device_id={"dp": data(k)}, device_id_type=MESH)
    for i in range(PAIR):
        for k in range(4):
            signal = functools.partial(
                pl.semaphore_signal, barrier, inc=1, device_id=across(i, k), device_id_type=MESH
            )
            if k:
                signal()
            else:
                pl.when(jnp.logical_not(mine(i)))(signal)
    pl.semaphore_wait(barrier, 7 + 3 + 8 - (half == s).astype(jnp.int32))

    gain = [r.gains[i : i + 1, :] for i in range(5)]
    e_g1, e_g2 = gain[0], gain[1]
    d_g1, d_g2, token = (g[:, :DEC_WIDTH] for g in gain[2:5])

    own16 = pl.ds(pl.multiple_of(m * SHARD, SHARD), SHARD)
    own64 = pl.ds(pl.multiple_of(m * ROWS, ROWS), ROWS)
    r.xf[:, own16, :] = r.xs[...]
    got = gather(r.xf, SHARD)

    def own_info(i):
        r.meta[place, m] = r.info[i]

    info_landed, info_left = exchange(
        lambda i: r.info.at[i], lambda i, at: r.meta.at[i, at], own_info
    )
    r.dgf[:, own64, :] = r.dgrad[...]
    got_dg = gather(r.dgf, ROWS)
    arrive(got)
    normal, _ = norm_rows(r.xf[...].reshape(128, WIDTH).astype(F32))
    normed = (normal * e_g1).astype(BF16)
    loads["w_qkv"].wait()
    qkv = dot(normed, r.v_w_qkv[...], 1, 0).astype(BF16)
    contexts = []
    for i in range(PAIR):
        part = qkv[i * 64 : (i + 1) * 64]
        r.qkv[i] = part
        keep = r.keep[i, 0:1, 0:64] > 0.0
        probs, context = attention(part, keep, 64, 256, HEAD, 1.0 / math.sqrt(HEAD))
        r.probs[i] = probs
        contexts.append(context)
    context = jnp.concatenate(contexts, axis=0)
    loads["w_out"].wait()
    r.s1[...] = dot(context, r.v_w_out[...], 1, 1).astype(BF16).reshape(2, 64, WIDTH)
    got = scatter(r.s1, r.r1, SHARD)
    r.cz[d] = context
    got_c = along(r.cz)
    got_x1 = cuts(0, normed)

    info_landed()
    loads["table"].wait()
    row = lax.broadcasted_iota(jnp.int32, (256, 1), 0)
    real = (lax.rem(row, ROWS) < PATCHES).astype(F32)
    for i in range(PAIR):
        facts = r.meta[i, 0] + r.meta[i, 1] + r.meta[i, 2] + r.meta[i, 3]
        index = facts[0:1, 0:64]
        hot = (lax.broadcasted_iota(jnp.int32, (256, 64), 0) == index).astype(F32)
        free = real - jnp.sum(hot, axis=1, keepdims=True)
        r.hot[i] = hot.astype(BF16)
        r.free[i] = free
        r.grid[i] = free * token
        level = facts[1:2, 0:1]

        def add_level(l, carry):
            chosen = (level == l).astype(F32)
            r.grid[i] += chosen * r.v_table[l].astype(F32)
            return carry

        lax.fori_loop(0, 8, add_level, 0)

    arrive(got)
    middle = r.xs[...].astype(F32) + summed(r.s1, r.r1, SHARD)
    r.mid[...] = middle
    normal, _ = norm_rows(middle)
    r.n2[:, own16, :] = (normal * e_g2).astype(BF16)
    got = gather(r.n2, SHARD)
    arrive(got_dg)
    loads["d_down"].wait()
    r.dgh[...] = dot(r.dgf[...].reshape(512, 512), r.v_d_down[...], 1, 0)
    loads["w_up"].wait()
    loads["w_down"].wait()
    arrive(got)
    normed = r.n2[...].reshape(128, WIDTH)
    hidden, slope = gelu_both(dot(normed, r.v_w_up[...], 1, 0))
    r.gp[...] = slope
    hidden = hidden.astype(BF16)
    r.s2[...] = dot(hidden, r.v_w_down[...], 1, 1).astype(BF16).reshape(2, 64, WIDTH)
    got = scatter(r.s2, r.r2, SHARD)
    r.hz[d] = hidden
    got_h = along(r.hz)
    got_x2 = cuts(1, normed)
    loads["w_proj"].wait()
    arrive(got)
    out_low = (r.mid[...] + summed(r.s2, r.r2, SHARD)).astype(BF16)
    r.eo[...] = out_low
    r.sent[...] = (
        dot(out_low.reshape(32, WIDTH), r.v_w_proj[...], 1, 0).astype(BF16).reshape(2, 16, 512)
    )

    def own_sent(i):
        r.arr[place, own16, :] = r.sent[i]

    def slot_rows(ref):
        return lambda i, at: ref.at[i, pl.ds(pl.multiple_of(at * SHARD, SHARD), SHARD)]

    sent_landed, sent_left = exchange(lambda i: r.sent.at[i], slot_rows(r.arr), own_sent)
    r.eom[:, own16, :] = r.eo[:, :, pl.ds(pl.multiple_of(m * 256, 256), 256)]
    got_eo = []
    for k in (1, 2, 3):
        columns = pl.ds(pl.multiple_of(model(k) * 256, 256), 256)
        got_eo.append(send(r.eo.at[:, :, columns], r.eom.at[:, own16], {"mp": model(k)}))

    loads["d_qkv"].wait()
    loads["d_out"].wait()
    sent_landed()
    cols = lax.broadcasted_iota(jnp.int32, (1, 256), 1)
    d_keep = lax.rem(cols, ROWS) < PATCHES
    d_scale = 1.0 / math.sqrt(DEC_HEAD)
    for i in range(PAIR):
        values = r.grid[i] + dot(r.hot[i], r.arr[i], 1, 0)
        r.grid[i] = values
        normal, _ = norm_rows(values)
        normed = (normal * d_g1).astype(BF16)
        at = slice(i * 256, (i + 1) * 256)
        r.dn1[at, :] = normed
        part = dot(normed, r.v_d_qkv[...], 1, 0).astype(BF16)
        r.dqkv[at, :] = part
        probs, context = attention(part, d_keep, 256, 128, DEC_HEAD, d_scale)
        r.dprobs[i] = probs
        r.dctx[at, :] = context
        r.s3[i] = dot(context, r.v_d_out[...], 1, 1).astype(BF16)
    got = scatter(r.s3, r.r3, ROWS)
    loads["d_up"].wait()
    arrive(got)
    middle = r.grid[:, own64, :] + summed(r.s3, r.r3, ROWS)
    r.dmid[...] = middle
    normal, _ = norm_rows(middle)
    r.dn2[:, own64, :] = (normal * d_g2).astype(BF16)
    got = gather(r.dn2, ROWS)
    arrive(got)
    hidden, slope = gelu_both(dot(r.dn2[...].reshape(512, 512), r.v_d_up[...], 1, 0))
    grad_upper = (r.dgh[...] * slope).astype(BF16)
    r.dhid[...] = hidden.astype(BF16)
    r.dgu[...] = grad_upper

    r.s4[...] = dot(grad_upper, r.v_d_up[...], 1, 1).astype(BF16).reshape(2, 256, 512)
    got = scatter(r.s4, r.r4, ROWS)
    r.grid_out = dot(r.dhid[...], r.v_d_down[...], 1, 1).reshape(2, 256, 512)
    shard = lax.broadcasted_iota(jnp.int32, (256, 1), 0) // ROWS
    here = (shard == m).astype(F32)
    parts = []
    for i in range(PAIR):
        whole = jnp.concatenate([r.dmid[i]] * 4, axis=0)
        parts.append((r.grid_out[i] + whole * here).astype(F32))
    for block in range(8):
        at = slice(block * 64, (block + 1) * 64)
        r.ds[block] = jnp.concatenate([parts[0][:, at], parts[1][:, at]], axis=1).astype(BF16)
    rank = s * 4 + m
    got_dec = []
    for a, k in plane:
        to = lax.rem(s + a, 2) * 4 + model(k)
        got_dec.append(send(r.ds.at[to], r.dr.at[rank], to_plane(a, k)))
    r.dr[rank] = r.ds[rank]

    def dec_weights(left, right, first, size):
        for a in (0, 1):
            rows = pl.ds(pl.multiple_of(lax.rem(s + a, 2) * 256, 256), 256)
            value = dot(left[:, rows], right[...], 0, 0)
            if a == 0:
                r.wdo[:, first : first + size] = value
            else:
                r.wds[:, first : first + size] = value.astype(BF16)

    flat = lambda ref, rows, width: ref.reshape(rows, width)
    dec_weights(flat(r.dn2, 512, 512), r.dgu, 512, 512)
    arrive(got)
    total = summed(r.s4, r.r4, ROWS)
    normal, inverse = norm_rows(r.dmid[...])
    grad = r.dgrad[...].astype(F32) + rows_back(normal, inverse, d_g2, total)
    r.vec[...] = jnp.zeros((8, 512), F32)
    r.vec[5:6, :] = jnp.sum((total * normal).reshape(128, 512), axis=0, keepdims=True)
    r.dgm[:, own64, :] = grad.astype(BF16)
    got = gather(r.dgm, ROWS)
    dec_weights(flat(r.dgf, 512, 512), r.dhid, 1024, 512)
    arrive(got)
    gain_sum = jnp.zeros((1, 512), F32)
    token_sum = jnp.zeros((1, 512), F32)
    for i in range(PAIR):
        at = slice(i * 256, (i + 1) * 256)
        grad_low = r.dgm[i]
        grad_context = dot(grad_low, r.v_d_out[...], 1, 0).astype(BF16)
        part = attention_back(
            r.dqkv[at, :], r.dprobs[i], grad_context, 256, 128, DEC_HEAD, d_scale
        )
        r.dgq[at, :] = part
        terms = dot(part, r.v_d_qkv[...], 1, 1)
        normal, inverse = norm_rows(r.grid[i])
        gain_sum += jnp.sum(terms * normal, axis=0, keepdims=True)
        back = rows_back(normal, inverse, d_g1, terms) + 0.25 * grad_low.astype(F32)
        token_sum += jnp.sum(back * r.free[i], axis=0, keepdims=True)
        r.s5[i] = dot(r.hot[i], back.astype(BF16), 0, 0).astype(BF16)
    got = scatter(r.s5, r.r5, SHARD)
    r.vec[4:5, :] = gain_sum
    r.vec[6:7, :] = token_sum
    dec_weights(flat(r.dgm, 512, 512), r.dctx, 384, 128)
    dec_weights(r.dn1, r.dgq, 0, 384)
    got_wd = [send(r.wds, r.wdr, to_plane(1, 0))]
    arrive(got)
    r.sg[...] = summed(r.s5, r.r5, SHARD).astype(BF16)

    def own_back(i):
        r.sgf[place, own16, :] = r.sg[i]

    back_landed, back_left = exchange(lambda i: r.sg.at[i], slot_rows(r.sgf), own_back)
    arrive(got_dec)
    for a in (0, 1):
        total = r.dr[4 * a].astype(F32)
        for k in (1, 2, 3):
            total = total + r.dr[4 * a + k].astype(F32)
        r.o_dec[a] = total
    arrive(got_wd)
    for block in range(4):
        at = slice(block * 64, (block + 1) * 64)
        r.wdo[at, :] = r.wdo[at, :] + r.wdr[at, :].astype(F32)
        r.wzs[block] = r.wdo[at, :].astype(BF16)
    got_wz = [
        send(r.wzs.at[data(k)], r.wzr.at[k - 1], {"dp": data(k)}) for k in (1, 2, 3)
    ]

    back_landed()
    grad_sent = r.sgf[...].reshape(128, 512)
    grad_low = dot(grad_sent, r.v_w_proj[...], 1, 1).astype(BF16)
    r.gy[...] = grad_low
    grad_upper = (dot(grad_low, r.v_w_down[...], 1, 0) * r.gp[...]).astype(BF16)
    r.s6[...] = dot(grad_upper, r.v_w_up[...], 1, 1).astype(BF16).reshape(2, 64, WIDTH)
    got = scatter(r.s6, r.r6, SHARD)
    r.uz[d] = grad_upper
    got_u = along(r.uz)
    got_x3 = cuts(2, grad_low)
    arrive(got_eo)
    product = dot(r.eom[...].reshape(128, 256), grad_sent, 0, 0)
    for a in (0, 1):
        r.ps[a] = product[a * 128 : (a + 1) * 128].astype(BF16)
    other = lax.rem(s + 1, 2)
    got_p = [send(r.ps.at[other], r.pr, to_plane(1, 0))]
    arrive(got)
    total = summed(r.s6, r.r6, SHARD)
    normal, inverse = norm_rows(r.mid[...])
    own_sent_grad = r.sgf[:, own16, :].reshape(32, 512)
    own_grad = dot(own_sent_grad, r.v_w_proj[...], 1, 1).reshape(2, 16, WIDTH)
    grad = own_grad + rows_back(normal, inverse, e_g2, total)
    r.gm[:, own16, :] = grad.astype(BF16)
    got = gather(r.gm, SHARD)
    gain_two = jnp.sum((total * normal).reshape(32, WIDTH), axis=0, keepdims=True)
    r.vec[2:3, :] = gain_two[:, :512]
    r.vec[3:4, :] = gain_two[:, 512:]

    arrive(got_p)
    kept = r.ps[s].astype(F32) + r.pr[...].astype(F32)
    r.po[...] = kept
    for block in range(4):
        r.pzs[block] = kept[block * 32 : (block + 1) * 32].astype(BF16)
    got_pz = [send(r.pzs.at[data(k)], r.pzr.at[k - 1], {"dp": data(k)}) for k in (1, 2, 3)]

    arrive(got)
    grad_low = r.gm[...].reshape(128, WIDTH)
    grad_context = dot(grad_low, r.v_w_out[...], 1, 0).astype(BF16)
    parts = []
    for i in range(PAIR):
        parts.append(
            attention_back(
                r.qkv[i],
                r.probs[i],
                grad_context[i * 64 : (i + 1) * 64],
                64,
                256,
                HEAD,
                1.0 / math.sqrt(HEAD),
            )
        )
    part = jnp.concatenate(parts, axis=0)
    r.qz[d] = part
    got_q = along(r.qz)
    got_x4 = cuts(3, grad_low)
    terms = dot(part, r.v_w_qkv[...], 1, 1)
    normal, inverse = norm_rows(r.xf[...].reshape(128, WIDTH).astype(F32))
    gain_one = jnp.sum(terms * normal, axis=0, keepdims=True)
    r.vec[0:1, :] = gain_one[:, :512]
    r.vec[1:2, :] = gain_one[:, 512:]
    back = rows_back(normal, inverse, e_g1, terms) + 0.25 * grad_low.astype(F32)
    for block in range(8):
        r.fs[block] = back[:, block * 128 : (block + 1) * 128].astype(BF16)
    got_f = []
    for a, k in plane:
        to = lax.rem(s + a, 2) * 4 + model(k)
        got_f.append(send(r.fs.at[to], r.fr.at[rank], to_plane(a, k)))
    r.fr[rank] = r.fs[rank]
    r.vr[rank] = r.vec[...]
    got_v = [send(r.vec, r.vr.at[rank], to_plane(a, k)) for a, k in plane]

    arrive(got_pz)
    mine32 = pl.ds(pl.multiple_of(d * 32, 32), 32)
    total = r.po[mine32, :]
    for k in range(3):
        total = total + r.pzr[k].astype(F32)
    r.pz[d] = total.astype(BF16)
    got_pg = along(r.pz)

    def enc_weights(which, right, first, size, out):
        lefts = [
            r.xz[which, :, lax.rem(s + a, 2), :, :].reshape(512, 128) for a in (0, 1)
        ]
        value = right[...].reshape(512, size)
        r.wes[:, first : first + size] = dot(lefts[1], value, 0, 0).astype(BF16)
        made = send(
            r.wes.at[:, first : first + size], r.wer.at[:, first : first + size], to_plane(1, 0)
        )
        out[...] = dot(lefts[0], value, 0, 0)
        return made

    arrive(got_h)
    arrive(got_x3)
    got_w = [enc_weights(2, r.hz, 2048, 1024, r.o_down)]
    arrive(got_x2)
    arrive(got_u)
    got_w.append(enc_weights(1, r.uz, 1024, 1024, r.o_up))
    arrive(got_wz)
    total = r.wdo[pl.ds(pl.multiple_of(d * 64, 64), 64), :]
    for k in range(3):
        total = total + r.wzr[k].astype(F32)
    r.o_dqkv[...] = total[:, :384]
    r.o_dout[...] = total[:, 384:512]
    r.o_dup[...] = total[:, 512:1024]
    r.o_ddown[...] = total[:, 1024:]
    arrive(got_v)
    total = r.vr[0]
    for k in range(1, 8):
        total = total + r.vr[k]
    r.vz[d] = total
    got_vz = along(r.vz)
    arrive(got_pg)
    r.pa[m, s] = r.pz[...].reshape(128, 512)
    got_pa = [send(r.pa.at[m, s], r.pa.at[m, s], {"mp": model(k)}) for k in (1, 2, 3)]
    arrive(got_f)
    for a in (0, 1):
        total = r.fr[4 * a].astype(F32)
        for k in (1, 2, 3):
            total = total + r.fr[4 * a + k].astype(F32)
        r.o_pat[a] = total
    arrive(got_pa)
    got_ps = [send(r.pa.at[:, s], r.pa.at[:, s], to_plane(1, 0))]
    arrive(got_c)
    arrive(got_x4)
    got_w.append(enc_weights(3, r.cz, 768, 256, r.o_out))
    arrive(got_x1)
    arrive(got_q)
    got_w.append(enc_weights(0, r.qz, 0, 768, r.o_qkv))
    arrive(got_vz)
    r.o_vec[...] = r.vz[0] + r.vz[1] + r.vz[2] + r.vz[3]
    arrive(got_ps)
    for a in range(4):
        for b in range(2):
            at = a * 256 + b * 128
            r.o_proj[at : at + 128, :] = r.pa[a, b].astype(F32)
    firsts = [(2048, 1024, r.o_down), (1024, 1024, r.o_up), (768, 256, r.o_out), (0, 768, r.o_qkv)]
    for made, (first, size, out) in zip(got_w, firsts):
        made.wait_recv()
        out[...] += r.wer[:, first : first + size].astype(F32)
    for made in started:
        made.wait_send()
    for leave in (info_left, sent_left, back_left):
        leave()
    assert used[0] <= COPIES


def with_kernel(
    patches,
    counts,
    patch_index,
    scale_level,
    enc_gain_one,
    enc_qkv,
    enc_out,
    enc_gain_two,
    enc_up,
    enc_down,
    w_proj,
    mask_token,
    pos_table,
    dec_gain_one,
    dec_qkv,
    dec_out,
    dec_gain_two,
    dec_up,
    dec_down,
    decoded_grad,
):
    s, m = lax.axis_index("section"), lax.axis_index("mp")

    def own_pair(values, axis):
        return lax.dynamic_slice_in_dim(values, PAIR * s, PAIR, axis)

    rows = jnp.swapaxes(own_pair(patches, 1), 0, 1)
    grads = jnp.swapaxes(own_pair(decoded_grad, 1), 0, 1)
    grads = jnp.pad(grads, ((0, 0), (0, ROWS - PATCHES), (0, 0)))
    seen = own_pair(counts, 0)
    keep = (jnp.arange(128, dtype=jnp.int32)[None, :] < seen[:, None]).astype(F32)
    keep = jnp.broadcast_to(keep[:, None, :], (PAIR, 8, 128))
    index = jnp.swapaxes(own_pair(patch_index, 1), 0, 1)
    grid_row = (index // PATCHES) * ROWS + index % PATCHES
    slot = m * SHARD + jnp.arange(SHARD, dtype=jnp.int32)
    grid_row = jnp.where(slot[None, :] < seen[:, None], grid_row, -1)
    lanes = jnp.zeros((PAIR, 128), jnp.int32)
    lanes = lax.dynamic_update_slice(lanes, grid_row, (0, m * SHARD))
    level = jnp.where(m == 0, own_pair(scale_level, 0), 0)
    info = jnp.concatenate(
        [
            lanes[:, None, :],
            jnp.broadcast_to(level[:, None, None], (PAIR, 1, 128)),
            jnp.zeros((PAIR, 6, 128), jnp.int32),
        ],
        axis=1,
    )
    wide = lambda v: jnp.pad(v.astype(F32), (0, WIDTH - v.shape[0]))[None, :]
    gains = jnp.concatenate(
        [wide(v) for v in (enc_gain_one, enc_gain_two, dec_gain_one, dec_gain_two, mask_token)]
        + [jnp.zeros((3, WIDTH), F32)],
        axis=0,
    )
    table = pos_table.reshape(8, WAYS, PATCHES, DEC_WIDTH)
    table = jnp.pad(table, ((0, 0), (0, 0), (0, ROWS - PATCHES), (0, 0))).reshape(8, 256, DEC_WIDTH)
    inputs = (
        rows,
        info,
        keep,
        gains,
        grads,
        enc_qkv.reshape(WIDTH, 768),
        enc_out,
        enc_up,
        enc_down,
        w_proj,
        table,
        dec_qkv.reshape(DEC_WIDTH, 384),
        dec_out,
        dec_up,
        dec_down,
    )
    shapes = (
        (2, 256, 128),
        (2, 128, 128),
        (128, 768),
        (128, 256),
        (128, 1024),
        (128, 1024),
        (64, 384),
        (64, 128),
        (64, 512),
        (64, 512),
        (1024, 512),
        (8, 512),
    )
    vmem = pl.BlockSpec(memory_space=pltpu.VMEM)
    outs = pl.pallas_call(
        kernel,
        out_shape=[jax.ShapeDtypeStruct(shape, F32) for shape in shapes],
        in_specs=[vmem] * 5 + [pl.BlockSpec(memory_space=pl.ANY)] * 10,
        out_specs=[vmem] * len(shapes),
        scratch_shapes=[pltpu.VMEM(shape, kind) for shape, kind in BUFFERS.values()]
        + [pltpu.VMEM(shape, BF16) for shape in LOADED.values()]
        + [
            pltpu.SemaphoreType.DMA((len(LOADED),)),
            pltpu.SemaphoreType.DMA((COPIES,)),
            pltpu.SemaphoreType.DMA((COPIES,)),
        ],
        compiler_params=pltpu.CompilerParams(
            collective_id=0, has_side_effects=True, vmem_limit_bytes=60 * 2**20
        ),
        name="layer_pair",
    )(*inputs)
    dec, pat, qkv, out, up, down, dqkv, dout, dup, ddown, proj, vec = outs
    dec = dec.reshape(2, WAYS, ROWS, PAIR, 64)[:, :, :PATCHES]
    dec = jnp.transpose(dec, (1, 2, 0, 3, 4)).reshape(WAYS * PATCHES, 4, 64)
    pat = jnp.transpose(pat.reshape(2, PAIR, SLOTS, 128), (2, 0, 1, 3)).reshape(SLOTS, 4, 128)
    return (
        dec,
        pat,
        qkv.reshape(128, 3, 256),
        out,
        up,
        down,
        dqkv.reshape(64, 3, 128),
        dout,
        dup,
        ddown,
        proj,
        vec[0:2].reshape(WIDTH),
        vec[2:4].reshape(WIDTH),
        vec[4],
        vec[5],
        vec[6],
    )


def fits_kernel(mesh, shapes):
    ways = (mesh.shape["section"], mesh.shape["dp"], mesh.shape["mp"])
    wanted = {0: (64, 16, 1024), 5: (1024, 3, 1024), 8: (1024, 4096), 10: (1024, 512)}
    wanted.update({12: (8, 196, 512), 14: (512, 3, 512), 17: (512, 2048), 19: (196, 16, 512)})
    return ways == (2, 4, 4) and all(shapes[i] == shape for i, shape in wanted.items())


def solution(mesh):
    def program(*arrays):
        shapes = [array.shape for array in arrays]
        body = with_kernel if fits_kernel(mesh, shapes) else on_device
        return placed_on(mesh, body)(*arrays)

    return program
```

```python
import functools
import math

import jax
import jax.numpy as jnp
from jax import lax
from jax.experimental import pallas as pl
from jax.experimental.pallas import tpu as pltpu
from jax.sharding import PartitionSpec as P

HEAD = 64
DEC_HEAD = 32


eps = 1e-06


def norm_rows(values):
    average = jnp.mean(values, axis=-1, keepdims=True)
    centered = values - average
    variance = jnp.mean(centered * centered, axis=-1, keepdims=True)
    inverse = lax.rsqrt(variance + eps)
    return (centered * inverse, inverse)


def norm_back(normal, inverse, gain_vec, gradient):
    weighted = gradient * gain_vec
    first_term = jnp.mean(weighted, axis=-1, keepdims=True)
    second_term = jnp.mean(weighted * normal, axis=-1, keepdims=True)
    return (
        inverse * (weighted - first_term - normal * second_term),
        jnp.sum(gradient * normal, axis=(0, 1)),
    )


def spread(values):
    return lax.all_gather(values, "mp", axis=0, tiled=True)


def collect(values):
    return lax.psum_scatter(values, "mp", scatter_dimension=0, tiled=True)


def spare_of(work):
    return lambda: jax.tree.map(jnp.zeros_like, work())


def head_view(qkv_rows, head_size):
    return qkv_rows.reshape(
        qkv_rows.shape[0], qkv_rows.shape[1], 3, qkv_rows.shape[3] // head_size, head_size
    )


def score_rows(queries, key_rows, visible, head_size):
    scores = jnp.einsum(
        "sbhe,tbhe->bhst", queries, key_rows, preferred_element_type=jnp.float32
    ) * (1.0 / math.sqrt(head_size))
    return jnp.where(visible[:, None, None, :], scores, -1e30)


def attend(qkv_rows, visible, head_size):
    heads_view = head_view(qkv_rows, head_size)
    scores = score_rows(heads_view[:, :, 0], heads_view[:, :, 1], visible, head_size)
    highest = jnp.max(scores, axis=-1, keepdims=True)
    weights = jnp.exp(scores - highest)
    denominator = jnp.sum(weights, axis=-1, keepdims=True)
    probability = (weights / denominator).astype(jnp.bfloat16)
    context = jnp.einsum(
        "bhst,tbhe->sbhe", probability, heads_view[:, :, 2], preferred_element_type=jnp.float32
    )
    context = context.reshape(qkv_rows.shape[0], qkv_rows.shape[1], qkv_rows.shape[3]).astype(
        jnp.bfloat16
    )
    return (context, highest + jnp.log(denominator))


def attend_back(qkv_rows, visible, logsum, grad_context, head_size):
    heads_view = head_view(qkv_rows, head_size)
    queries = heads_view[:, :, 0]
    key_rows = heads_view[:, :, 1]
    value_rows = heads_view[:, :, 2]
    probability = jnp.exp(score_rows(queries, key_rows, visible, head_size) - logsum)
    grad_heads = grad_context.reshape(queries.shape)
    grad_values = jnp.einsum(
        "bhst,sbhe->tbhe",
        probability.astype(jnp.bfloat16),
        grad_heads,
        preferred_element_type=jnp.float32,
    )
    grad_probs = jnp.einsum(
        "sbhe,tbhe->bhst", grad_heads, value_rows, preferred_element_type=jnp.float32
    )
    row_inner = jnp.sum(grad_probs * probability, axis=-1, keepdims=True)
    grad_scores = (probability * (grad_probs - row_inner)).astype(jnp.bfloat16)
    score_scale = 1.0 / math.sqrt(head_size)
    grad_queries = (
        jnp.einsum("bhst,tbhe->sbhe", grad_scores, key_rows, preferred_element_type=jnp.float32)
        * score_scale
    )
    grad_keys = (
        jnp.einsum("bhst,sbhe->tbhe", grad_scores, queries, preferred_element_type=jnp.float32)
        * score_scale
    )
    stacked = jnp.stack([grad_queries, grad_keys, grad_values], axis=2)
    return stacked.reshape(qkv_rows.shape).astype(jnp.bfloat16)


def attention_local(normed_one, visible, w_qkv, w_out, head_size):
    qkv_rows = jnp.einsum(
        "sbw,wcf->sbcf", normed_one, w_qkv, preferred_element_type=jnp.float32
    ).astype(jnp.bfloat16)
    context, logsum = attend(qkv_rows, visible, head_size)
    mixed_terms = jnp.einsum("sbf,wf->sbw", context, w_out, preferred_element_type=jnp.float32)
    return (qkv_rows, context, logsum, mixed_terms)


def feed_local(normed_two, w_up, w_down):
    upper_in = jnp.einsum("sbw,wf->sbf", normed_two, w_up, preferred_element_type=jnp.float32)
    hidden = jax.nn.gelu(upper_in, approximate=False).astype(jnp.bfloat16)
    return (upper_in, jnp.einsum("sbf,wf->sbw", hidden, w_down, preferred_element_type=jnp.float32))


def feed_back_local(grad_full, normed_two, upper_in, w_up, w_down):
    value_out, gelu_pull = jax.vjp(
        lambda argument: jax.nn.gelu(argument, approximate=False), upper_in
    )
    hidden = value_out.astype(jnp.bfloat16)
    grad_down_w = jnp.einsum("sbw,sbf->wf", grad_full, hidden, preferred_element_type=jnp.float32)
    grad_hidden = jnp.einsum("sbw,wf->sbf", grad_full, w_down, preferred_element_type=jnp.float32)
    grad_upper = gelu_pull(grad_hidden)[0].astype(jnp.bfloat16)
    grad_up_w = jnp.einsum(
        "sbw,sbf->wf", normed_two, grad_upper, preferred_element_type=jnp.float32
    )
    grad_terms = jnp.einsum("sbf,wf->sbw", grad_upper, w_up, preferred_element_type=jnp.float32)
    return (grad_up_w, grad_down_w, grad_terms)


def attention_back_local(
    grad_full, qkv_rows, context, logsum, visible, normed_one, w_qkv, w_out, head_size
):
    grad_out_w = jnp.einsum("sbw,sbf->wf", grad_full, context, preferred_element_type=jnp.float32)
    grad_context = jnp.einsum(
        "sbw,wf->sbf", grad_full, w_out, preferred_element_type=jnp.float32
    ).astype(jnp.bfloat16)
    grad_qkv = attend_back(qkv_rows, visible, logsum, grad_context, head_size)
    grad_qkv_w = jnp.einsum(
        "sbw,sbcf->wcf", normed_one, grad_qkv, preferred_element_type=jnp.float32
    )
    grad_normed = jnp.einsum("sbcf,wcf->sbw", grad_qkv, w_qkv, preferred_element_type=jnp.float32)
    return (grad_qkv_w, grad_out_w, grad_normed)


def on_device(
    patches,
    counts,
    patch_index,
    scale_level,
    enc_gain_one,
    enc_qkv,
    enc_out,
    enc_gain_two,
    enc_up,
    enc_down,
    w_proj,
    mask_token,
    pos_table,
    dec_gain_one,
    dec_qkv,
    dec_out,
    dec_gain_two,
    dec_up,
    dec_down,
    decoded_grad,
):
    data_ways = lax.axis_size("dp")
    model_ways = lax.axis_size("mp")
    slot_rows = patches.shape[0]
    images = patches.shape[1]
    grid_rows = decoded_grad.shape[0]
    dec_width = decoded_grad.shape[2]
    slot_count = slot_rows * model_ways
    grid_count = grid_rows * model_ways
    per_peer = images // data_ways
    slot_start = lax.axis_index("mp") * slot_rows
    grid_start = lax.axis_index("mp") * grid_rows
    is_encoder = lax.axis_index("section") == 0
    visible = jnp.arange(slot_count, dtype=jnp.int32)[None, :] < counts[:, None]
    all_visible = jnp.ones((images, grid_count), dtype=bool)
    enc_g1 = enc_gain_one.astype(jnp.float32)
    enc_g2 = enc_gain_two.astype(jnp.float32)
    dec_g1 = dec_gain_one.astype(jnp.float32)
    dec_g2 = dec_gain_two.astype(jnp.float32)
    token_vec = mask_token.astype(jnp.float32)

    def on_encoder(work):
        return lax.cond(is_encoder, work, spare_of(work))

    def on_decoder(work):
        return lax.cond(is_encoder, spare_of(work), work)

    full_in = spread(patches)

    def enc_attention():
        normal_one, inverse_one = norm_rows(full_in.astype(jnp.float32))
        normed_one = (normal_one * enc_g1).astype(jnp.bfloat16)
        return attention_local(normed_one, visible, enc_qkv, enc_out, HEAD)

    enc_qkv_rows, enc_context, enc_logsum, enc_mixed_terms = on_encoder(enc_attention)
    enc_middle = patches.astype(jnp.float32) + collect(enc_mixed_terms)
    enc_normal_two, enc_inverse_two = norm_rows(enc_middle)
    enc_normed_two = spread((enc_normal_two * enc_g2).astype(jnp.bfloat16))
    enc_upper, enc_down_terms = on_encoder(lambda: feed_local(enc_normed_two, enc_up, enc_down))
    enc_out_low = (enc_middle + collect(enc_down_terms)).astype(jnp.bfloat16)

    def enc_send():
        sent_rows = jnp.einsum(
            "sbw,wf->sbf", enc_out_low, w_proj, preferred_element_type=jnp.float32
        ).astype(jnp.bfloat16)
        live_slot = (slot_start + jnp.arange(slot_rows, dtype=jnp.int32))[:, None] < counts[None, :]
        sent_index = jnp.where(live_slot, patch_index, grid_count)
        packed = (
            sent_rows.reshape(slot_rows, per_peer, data_ways, dec_width),
            sent_index.reshape(slot_rows, per_peer, data_ways),
            scale_level.reshape(1, per_peer, data_ways),
        )
        packed = tuple(
            (jnp.concatenate([jnp.zeros_like(member), member], axis=2) for member in packed)
        )
        return packed

    packed = on_encoder(enc_send)
    received = (
        lax.all_to_all(packed[0], ("section", "dp"), split_axis=2, concat_axis=1, tiled=True),
        lax.all_to_all(packed[1], ("section", "dp"), split_axis=2, concat_axis=1, tiled=True),
        lax.all_to_all(packed[2], ("section", "dp"), split_axis=2, concat_axis=1, tiled=True),
    )
    arrived = (received[0][:, :images, 0], received[1][:, :images, 0], received[2][0, :images, 0])
    arrived_rows, arrived_index, arrived_level = arrived

    def make_onehot():
        return (
            arrived_index[:, :, None] == jnp.arange(grid_count, dtype=jnp.int32)[None, None, :]
        ).astype(jnp.bfloat16)

    def dec_place():
        onehot_low = make_onehot()
        covered = jnp.transpose(jnp.sum(onehot_low.astype(jnp.float32), axis=0))
        placed = jnp.einsum(
            "sbp,sbf->pbf", onehot_low, arrived_rows, preferred_element_type=jnp.float32
        )
        return (placed - covered[:, :, None] * token_vec, covered)

    placed_terms, covered_terms = on_decoder(dec_place)
    placed_rows, covered_rows = collect((placed_terms, covered_terms))
    table_rows = lax.dynamic_slice_in_dim(pos_table, grid_start, grid_rows, 1)
    level_hot = (
        arrived_level[:, None] == jnp.arange(pos_table.shape[0], dtype=jnp.int32)[None, :]
    ).astype(jnp.bfloat16)
    position = jnp.einsum("bl,lpf->pbf", level_hot, table_rows, preferred_element_type=jnp.float32)
    grid_values = placed_rows + token_vec + position
    dec_normal_one, dec_inverse_one = norm_rows(grid_values)
    dec_normed_one = spread((dec_normal_one * dec_g1).astype(jnp.bfloat16))
    dec_qkv_rows, dec_context, dec_logsum, dec_mixed_terms = on_decoder(
        lambda: attention_local(dec_normed_one, all_visible, dec_qkv, dec_out, DEC_HEAD)
    )
    dec_middle = grid_values + collect(dec_mixed_terms)
    dec_normal_two, dec_inverse_two = norm_rows(dec_middle)
    dec_normed_two = spread((dec_normal_two * dec_g2).astype(jnp.bfloat16))

    def dec_feed():
        upper_in, down_terms = feed_local(dec_normed_two, dec_up, dec_down)
        own_rows = lax.dynamic_slice_in_dim(down_terms, grid_start, grid_rows, 0) + dec_middle
        return (upper_in, lax.dynamic_update_slice_in_dim(down_terms, own_rows, grid_start, 0))

    dec_upper, dec_summand = on_decoder(dec_feed)
    decoded = lax.psum_scatter(
        dec_summand.astype(jnp.bfloat16), ("section", "mp"), scatter_dimension=2, tiled=True
    ).astype(jnp.float32)
    dec_grad_full = spread(decoded_grad)
    dec_up_grad, dec_down_grad, dec_two_terms = on_decoder(
        lambda: feed_back_local(dec_grad_full, dec_normed_two, dec_upper, dec_up, dec_down)
    )
    dec_through, dec_gain_two_grad = norm_back(
        dec_normal_two, dec_inverse_two, dec_g2, collect(dec_two_terms)
    )
    dec_grad_middle = decoded_grad.astype(jnp.float32) + dec_through
    dec_middle_full = spread(dec_grad_middle.astype(jnp.bfloat16))
    dec_qkv_grad, dec_out_grad, dec_one_terms = on_decoder(
        lambda: attention_back_local(
            dec_middle_full,
            dec_qkv_rows,
            dec_context,
            dec_logsum,
            all_visible,
            dec_normed_one,
            dec_qkv,
            dec_out,
            DEC_HEAD,
        )
    )
    dec_inner, dec_gain_one_grad = norm_back(
        dec_normal_one, dec_inverse_one, dec_g1, collect(dec_one_terms)
    )
    grad_grid = dec_grad_middle + dec_inner
    grad_token = jnp.sum(grad_grid * (1.0 - covered_rows)[:, :, None], axis=(0, 1))
    grad_grid_full = spread(grad_grid.astype(jnp.bfloat16))

    def dec_return():
        grad_sent = jnp.einsum(
            "sbp,pbf->sbf", make_onehot(), grad_grid_full, preferred_element_type=jnp.float32
        ).astype(jnp.bfloat16)
        return jnp.concatenate([grad_sent, jnp.zeros_like(grad_sent)], axis=1)[:, :, None, :]

    back_rows = on_decoder(dec_return)
    returned = lax.all_to_all(
        back_rows, ("section", "dp"), split_axis=1, concat_axis=2, tiled=True
    )[:, :, data_ways:]
    grad_arrived = returned.reshape(slot_rows, images, dec_width)

    def enc_project_back():
        grad_proj_w = jnp.einsum(
            "sbw,sbf->wf", enc_out_low, grad_arrived, preferred_element_type=jnp.float32
        )
        grad_block = jnp.einsum(
            "sbf,wf->sbw", grad_arrived, w_proj, preferred_element_type=jnp.float32
        )
        return (grad_proj_w, grad_block)

    proj_grad, enc_grad_block = on_encoder(enc_project_back)
    enc_grad_full = spread(enc_grad_block.astype(jnp.bfloat16))
    enc_up_grad, enc_down_grad, enc_two_terms = on_encoder(
        lambda: feed_back_local(enc_grad_full, enc_normed_two, enc_upper, enc_up, enc_down)
    )
    enc_through, enc_gain_two_grad = norm_back(
        enc_normal_two, enc_inverse_two, enc_g2, collect(enc_two_terms)
    )
    enc_grad_middle = enc_grad_block + enc_through
    enc_middle_full = spread(enc_grad_middle.astype(jnp.bfloat16))

    def enc_attention_back():
        normal_one, inverse_one = norm_rows(full_in.astype(jnp.float32))
        normed_one = (normal_one * enc_g1).astype(jnp.bfloat16)
        grad_qkv_w, grad_out_w, grad_normed = attention_back_local(
            enc_middle_full,
            enc_qkv_rows,
            enc_context,
            enc_logsum,
            visible,
            normed_one,
            enc_qkv,
            enc_out,
            HEAD,
        )
        grad_inner, grad_gain_one = norm_back(normal_one, inverse_one, enc_g1, grad_normed)
        own_rows = lax.dynamic_slice_in_dim(grad_inner, slot_start, slot_rows, 0) + enc_grad_middle
        summand = lax.dynamic_update_slice_in_dim(grad_inner, own_rows, slot_start, 0)
        return (grad_qkv_w, grad_out_w, grad_gain_one, summand)

    enc_qkv_grad, enc_out_grad, enc_gain_one_grad, in_summand = on_encoder(enc_attention_back)
    patches_grad = lax.psum_scatter(
        in_summand.astype(jnp.bfloat16), ("section", "mp"), scatter_dimension=2, tiled=True
    ).astype(jnp.float32)
    enc_gain_two_grad = jnp.where(is_encoder, enc_gain_two_grad, 0.0)
    dec_gain_one_grad = jnp.where(is_encoder, 0.0, dec_gain_one_grad)
    dec_gain_two_grad = jnp.where(is_encoder, 0.0, dec_gain_two_grad)
    grad_token = jnp.where(is_encoder, 0.0, grad_token)
    sharded = (
        lax.psum_scatter(enc_qkv_grad, ("section", "dp"), scatter_dimension=0, tiled=True),
        lax.psum_scatter(enc_out_grad, ("section", "dp"), scatter_dimension=0, tiled=True),
        lax.psum_scatter(enc_up_grad, ("section", "dp"), scatter_dimension=0, tiled=True),
        lax.psum_scatter(enc_down_grad, ("section", "dp"), scatter_dimension=0, tiled=True),
        lax.psum_scatter(dec_qkv_grad, ("section", "dp"), scatter_dimension=0, tiled=True),
        lax.psum_scatter(dec_out_grad, ("section", "dp"), scatter_dimension=0, tiled=True),
        lax.psum_scatter(dec_up_grad, ("section", "dp"), scatter_dimension=0, tiled=True),
        lax.psum_scatter(dec_down_grad, ("section", "dp"), scatter_dimension=0, tiled=True),
    )
    shared = lax.psum(
        (
            proj_grad,
            enc_gain_one_grad,
            enc_gain_two_grad,
            dec_gain_one_grad,
            dec_gain_two_grad,
            grad_token,
        ),
        ("section", "dp", "mp"),
    )
    return (
        decoded,
        patches_grad,
        sharded[0],
        sharded[1],
        sharded[2],
        sharded[3],
        sharded[4],
        sharded[5],
        sharded[6],
        sharded[7],
        shared[0],
        shared[1],
        shared[2],
        shared[3],
        shared[4],
        shared[5],
    )


def placed_on(mesh, body):
    placed = (
        P("mp", "dp", None),
        P("dp"),
        P("mp", "dp"),
        P("dp"),
        P(),
        P(None, None, "mp"),
        P(None, "mp"),
        P(),
        P(None, "mp"),
        P(None, "mp"),
        P(),
        P(),
        P(),
        P(),
        P(None, None, "mp"),
        P(None, "mp"),
        P(),
        P(None, "mp"),
        P(None, "mp"),
        P("mp", "dp", None),
    )
    return jax.shard_map(
        body,
        mesh=mesh,
        in_specs=placed,
        out_specs=(
            P(None, "dp", ("section", "mp")),
            P(None, "dp", ("section", "mp")),
            P(("section", "dp"), None, "mp"),
            P(("section", "dp"), "mp"),
            P(("section", "dp"), "mp"),
            P(("section", "dp"), "mp"),
            P(("section", "dp"), None, "mp"),
            P(("section", "dp"), "mp"),
            P(("section", "dp"), "mp"),
            P(("section", "dp"), "mp"),
            P(),
            P(),
            P(),
            P(),
            P(),
            P(),
        ),
        check_vma=False,
    )


MESH = pl.DeviceIdType.MESH
F32 = jnp.float32
BF16 = jnp.bfloat16
WAYS = 4
PAIR = 2
SLOTS = 64
SHARD = 16
PATCHES = 49
ROWS = 64
WIDTH = 1024
DEC_WIDTH = 512
HEADS_HERE = 4
COPIES = 256


def dot(left, right, left_dim, right_dim):
    return lax.dot_general(
        left, right, (((left_dim,), (right_dim,)), ((), ())), preferred_element_type=F32
    )


def rows_back(normal, inverse, gain, gradient):
    weighted = gradient * gain
    first = jnp.mean(weighted, axis=-1, keepdims=True)
    second = jnp.mean(weighted * normal, axis=-1, keepdims=True)
    return inverse * (weighted - first - normal * second)


def gelu_both(upper):
    phi = 0.5 * (1.0 + lax.erf(upper * math.sqrt(0.5)))
    density = jnp.exp(-0.5 * upper * upper) * (1.0 / math.sqrt(2.0 * math.pi))
    return upper * phi, phi + upper * density


def head_mask(width, head, kind):
    lane = lax.broadcasted_iota(jnp.int32, (1, width), 1)
    return [
        ((lane >= h * head) & (lane < (h + 1) * head)).astype(F32).astype(kind)
        for h in range(HEADS_HERE)
    ]


def stack_heads(values, masks):
    return jnp.concatenate([values * mask for mask in masks], axis=0)


def fold_heads(stacked, masks, rows):
    total = None
    for h, mask in enumerate(masks):
        part = stacked[h * rows : (h + 1) * rows] * mask
        total = part if total is None else total + part
    return total


def attention(qkv, keep, rows, width, head, scale):
    low = head_mask(width, head, BF16)
    wide = head_mask(width, head, F32)
    queries = stack_heads(qkv[:, :width], low)
    scores = dot(queries, qkv[:, width : 2 * width], 1, 1) * scale
    scores = jnp.where(keep, scores, -1e30)
    weights = jnp.exp(scores - jnp.max(scores, axis=-1, keepdims=True))
    probs = weights / jnp.sum(weights, axis=-1, keepdims=True)
    mixed = dot(probs.astype(BF16), qkv[:, 2 * width :], 1, 0)
    return probs, fold_heads(mixed, wide, rows).astype(BF16)


def attention_back(qkv, probs, grad_context, rows, width, head, scale):
    low = head_mask(width, head, BF16)
    wide = head_mask(width, head, F32)
    queries = stack_heads(qkv[:, :width], low)
    grads = stack_heads(grad_context, low)
    grad_probs = dot(grads, qkv[:, 2 * width :], 1, 1)
    inner = jnp.sum(grad_probs * probs, axis=-1, keepdims=True)
    grad_scores = (probs * (grad_probs - inner)).astype(BF16)
    grad_queries = fold_heads(dot(grad_scores, qkv[:, width : 2 * width], 1, 0), wide, rows) * scale
    grad_keys = dot(grad_scores, queries, 0, 0) * scale
    grad_values = dot(probs.astype(BF16), grads, 0, 0)
    return jnp.concatenate([grad_queries, grad_keys, grad_values], axis=1).astype(BF16)


IN_NAMES = [
    "xs",
    "info",
    "keep",
    "gains",
    "dgrad",
    "w_qkv",
    "w_out",
    "w_up",
    "w_down",
    "w_proj",
    "table",
    "d_qkv",
    "d_out",
    "d_up",
    "d_down",
]
OUT_NAMES = [
    "o_dec",
    "o_pat",
    "o_qkv",
    "o_out",
    "o_up",
    "o_down",
    "o_dqkv",
    "o_dout",
    "o_dup",
    "o_ddown",
    "o_proj",
    "o_vec",
]
LOADED = dict(
    w_qkv=(WIDTH, 768),
    w_out=(WIDTH, 256),
    w_up=(WIDTH, 1024),
    w_down=(WIDTH, 1024),
    w_proj=(WIDTH, DEC_WIDTH),
    table=(8, 256, DEC_WIDTH),
    d_qkv=(DEC_WIDTH, 384),
    d_out=(DEC_WIDTH, 128),
    d_up=(DEC_WIDTH, 512),
    d_down=(DEC_WIDTH, 512),
)
BUFFERS = dict(
    xf=((2, 64, 1024), BF16),
    qkv=((2, 64, 768), BF16),
    probs=((2, 256, 64), F32),
    s1=((2, 64, 1024), BF16),
    r1=((2, 3, 16, 1024), BF16),
    mid=((2, 16, 1024), F32),
    n2=((2, 64, 1024), BF16),
    gp=((2, 64, 1024), F32),
    s2=((2, 64, 1024), BF16),
    r2=((2, 3, 16, 1024), BF16),
    eo=((2, 16, 1024), BF16),
    sent=((2, 16, 512), BF16),
    arr=((2, 64, 512), BF16),
    meta=((2, 4, 8, 128), jnp.int32),
    dgf=((2, 256, 512), BF16),
    hot=((2, 256, 64), BF16),
    free=((2, 256, 1), F32),
    grid=((2, 256, 512), F32),
    dn1=((512, 512), BF16),
    dqkv=((512, 384), BF16),
    dprobs=((2, 1024, 256), F32),
    dctx=((512, 128), BF16),
    s3=((2, 256, 512), BF16),
    r3=((2, 3, 64, 512), BF16),
    dmid=((2, 64, 512), F32),
    dn2=((2, 256, 512), BF16),
    dhid=((512, 512), BF16),
    dgh=((512, 512), F32),
    dgu=((512, 512), BF16),
    s4=((2, 256, 512), BF16),
    r4=((2, 3, 64, 512), BF16),
    ds=((8, 256, 128), BF16),
    dr=((8, 256, 128), BF16),
    dgm=((2, 256, 512), BF16),
    dgq=((512, 384), BF16),
    s5=((2, 64, 512), BF16),
    r5=((2, 3, 16, 512), BF16),
    sg=((2, 16, 512), BF16),
    w1s=((256, 1024), BF16),
    w1r=((256, 1024), BF16),
    w1o=((256, 1024), F32),
    z1s=((4, 64, 1024), BF16),
    z1r=((3, 64, 1024), BF16),
    w2s=((256, 512), BF16),
    w2r=((256, 512), BF16),
    w2o=((256, 512), F32),
    z2s=((4, 64, 512), BF16),
    z2r=((3, 64, 512), BF16),
    s6=((2, 64, 1024), BF16),
    r6=((2, 3, 16, 1024), BF16),
    gm=((2, 64, 1024), BF16),
    fs=((8, 2, 64, 128), BF16),
    fr=((8, 2, 64, 128), BF16),
    cz=((4, 2, 64, 256), BF16),
    uz=((4, 2, 64, 1024), BF16),
    qz=((4, 2, 64, 768), BF16),
    ez=((4, 2, 64, 256), BF16),
    sz=((4, 2, 4, 16, 512), BF16),
    xb=((3, 2, 4, 2, 64, 128), BF16),
    xz=((3, 4, 2, 2, 64, 128), BF16),
    ha=((512, 1024), BF16),
    ga=((512, 1024), BF16),
    wes=((128, 3072), BF16),
    wer=((128, 3072), BF16),
    ps=((256, 512), BF16),
    pr=((256, 512), BF16),
    pa=((4, 2, 128, 512), BF16),
    vec=((8, 512), F32),
    vr=((8, 8, 512), F32),
    vz=((4, 8, 512), F32),
)


class Refs:
    pass


def kernel(*refs):
    r = Refs()
    names = IN_NAMES + OUT_NAMES + list(BUFFERS) + ["v_" + n for n in LOADED]
    for name, ref in zip(names, refs):
        setattr(r, name, ref)
    load_sem, send_sem, recv_sem = refs[len(names) :]
    s, d, m = (lax.axis_index(a) for a in ("section", "dp", "mp"))
    used = [0]
    started = []

    def take(count):
        used[0] += count
        return used[0] - count

    def copy(src, dst, device, at, land=None):
        return pltpu.make_async_remote_copy(
            src_ref=src,
            dst_ref=dst,
            send_sem=send_sem.at[at],
            recv_sem=recv_sem.at[at if land is None else land],
            device_id=device,
            device_id_type=MESH,
        )

    def send(src, dst, device):
        made = copy(src, dst, device, take(1))
        made.start()
        started.append(made)
        return made

    def arrive(copies):
        for made in copies:
            made.wait_recv()

    def model(k):
        return lax.rem(m + k, WAYS)

    def data(k):
        return lax.rem(d + k, WAYS)

    def gather(ref, rows):
        own = ref.at[pl.ds(pl.multiple_of(m * rows, rows), rows)]
        return [send(own, own, {"mp": model(k)}) for k in (1, 2, 3)]

    def gather_all(ref, rows):
        own = ref.at[:, pl.ds(pl.multiple_of(m * rows, rows), rows)]
        return [send(own, own, {"mp": model(k)}) for k in (1, 2, 3)]

    def scatter(src, dst, rows):
        copies = []
        for k in (1, 2, 3):
            to = model(k)
            part = src.at[pl.ds(pl.multiple_of(to * rows, rows), rows)]
            copies.append(send(part, dst.at[k - 1], {"mp": to}))
        return copies

    def summed(src, dst, rows):
        total = src[pl.ds(pl.multiple_of(m * rows, rows), rows), :].astype(F32)
        for k in range(3):
            total = total + dst[k].astype(F32)
        return total

    def along(ref):
        return [send(ref.at[d], ref.at[d], {"dp": data(k)}) for k in (1, 2, 3)]

    def cuts(which, values):
        for i, value in enumerate(values):
            for block in range(8):
                at = slice(block * 128, (block + 1) * 128)
                r.xb[which, block // 4, block % 4, i] = value[:, at]
        r.xz[which, d] = r.xb[which, :, d]
        return [
            send(r.xb.at[which, :, data(k)], r.xz.at[which, d], {"dp": data(k)}) for k in (1, 2, 3)
        ]

    plane = [(a, k) for a in (0, 1) for k in range(4) if (a, k) != (0, 0)]

    def to_plane(a, k):
        return {"section": lax.rem(s + a, 2), "mp": model(k)}

    half = d // 2
    place = lax.rem(d, 2)

    def across(i, k):
        return {"section": half, "dp": 2 * s + i, "mp": model(k)}

    def mine(i):
        return (half == s) & (2 * s + i == d)

    def to_dp():
        return sending[0] if sending else d

    sending = []

    class exchange:
        def __init__(self, src_of, dst_of, own):
            self.src_of, self.dst_of, self.own = src_of, dst_of, own
            self.at = take(8)

        def out(self, i, k):
            sending.append(2 * s + i)
            land = self.dst_of(place, m)
            sending.clear()
            at = self.at
            return copy(self.src_of(i), land, across(i, k), at + 4 * i + k, at + 4 * place + k)

        def come(self, i, k):
            at = self.at + 4 * i + k
            return copy(self.src_of(i), self.dst_of(i, model(4 - k)), across(i, k), at)

        def start(self, i):
            for k in (1, 2, 3):
                self.out(i, k).start()
            pl.when(jnp.logical_not(mine(i)))(self.out(i, 0).start)
            pl.when(mine(i))(functools.partial(self.own, i))

        def landed(self, i):
            pl.when(jnp.logical_not(mine(i)))(self.come(i, 0).wait_recv)
            for k in (1, 2, 3):
                self.come(i, k).wait_recv()

        def left(self):
            for i in range(PAIR):
                for k in (1, 2, 3):
                    self.out(i, k).wait_send()
                pl.when(jnp.logical_not(mine(i)))(self.out(i, 0).wait_send)

    def slot_rows(ref):
        return lambda i, at: ref.at[i, pl.ds(pl.multiple_of(at * SHARD, SHARD), SHARD)]

    def put_info(i):
        r.meta[place, m] = r.info[i]

    def put_rows(ref):
        def put(i):
            ref[place, pl.ds(pl.multiple_of(m * SHARD, SHARD), SHARD), :] = r.sent[i]

        return put

    loads = {}
    for at, name in enumerate(LOADED):
        loads[name] = pltpu.make_async_copy(
            getattr(r, name), getattr(r, "v_" + name), load_sem.at[at]
        )
        loads[name].start()

    barrier = pltpu.get_barrier_semaphore()
    for a, k in plane:
        pl.semaphore_signal(barrier, inc=1, device_id=to_plane(a, k), device_id_type=MESH)
    for k in (1, 2, 3):
        pl.semaphore_signal(barrier, inc=1, device_id={"dp": data(k)}, device_id_type=MESH)
    for i in range(PAIR):
        for k in range(4):
            signal = functools.partial(
                pl.semaphore_signal, barrier, inc=1, device_id=across(i, k), device_id_type=MESH
            )
            if k:
                signal()
            else:
                pl.when(jnp.logical_not(mine(i)))(signal)
    pl.semaphore_wait(barrier, 7 + 3 + 8 - (half == s).astype(jnp.int32))

    gain = [r.gains[i : i + 1, :] for i in range(5)]
    e_g1, e_g2 = gain[0], gain[1]
    d_g1, d_g2, token = (g[:, :DEC_WIDTH] for g in gain[2:5])

    own16 = pl.ds(pl.multiple_of(m * SHARD, SHARD), SHARD)
    own64 = pl.ds(pl.multiple_of(m * ROWS, ROWS), ROWS)
    e_scale = 1.0 / math.sqrt(HEAD)
    d_scale = 1.0 / math.sqrt(DEC_HEAD)
    other = lax.rem(s + 1, 2)
    rank = s * 4 + m
    pair = range(PAIR)

    r.xf[:, own16, :] = r.xs[...]
    got = [gather(r.xf.at[i], SHARD) for i in pair]
    info = exchange(lambda i: r.info.at[i], lambda i, at: r.meta.at[i, at], put_info)
    for i in pair:
        info.start(i)
    r.dgf[:, own64, :] = r.dgrad[...]
    loads["w_qkv"].wait()
    loads["w_out"].wait()
    sent_on = []
    contexts, normeds = [], []
    for i in pair:
        arrive(got[i])
        normal, _ = norm_rows(r.xf[i].astype(F32))
        normed = (normal * e_g1).astype(BF16)
        part = dot(normed, r.v_w_qkv[...], 1, 0).astype(BF16)
        r.qkv[i] = part
        keep = r.keep[i, 0:1, 0:64] > 0.0
        probs, context = attention(part, keep, 64, 256, HEAD, e_scale)
        r.probs[i] = probs
        r.s1[i] = dot(context, r.v_w_out[...], 1, 1).astype(BF16)
        sent_on.append(scatter(r.s1.at[i], r.r1.at[i], SHARD))
        r.cz[d, i] = context
        normeds.append(normed)
    got_c = along(r.cz)
    got_x1 = cuts(0, normeds)
    got_dg = gather_all(r.dgf, ROWS)

    loads["table"].wait()
    row = lax.broadcasted_iota(jnp.int32, (256, 1), 0)
    real = (lax.rem(row, ROWS) < PATCHES).astype(F32)
    for i in pair:
        info.landed(i)
        facts = r.meta[i, 0] + r.meta[i, 1] + r.meta[i, 2] + r.meta[i, 3]
        index = facts[0:1, 0:64]
        hot = (lax.broadcasted_iota(jnp.int32, (256, 64), 0) == index).astype(F32)
        free = real - jnp.sum(hot, axis=1, keepdims=True)
        r.hot[i] = hot.astype(BF16)
        r.free[i] = free
        r.grid[i] = free * token
        level = facts[1:2, 0:1]

        def add_level(l, carry):
            chosen = (level == l).astype(F32)
            r.grid[i] += chosen * r.v_table[l].astype(F32)
            return carry

        lax.fori_loop(0, 8, add_level, 0)

    got = []
    for i in pair:
        arrive(sent_on[i])
        middle = r.xs[i].astype(F32) + summed(r.s1.at[i], r.r1.at[i], SHARD)
        r.mid[i] = middle
        normal, _ = norm_rows(middle)
        r.n2[i, own16, :] = (normal * e_g2).astype(BF16)
        got.append(gather(r.n2.at[i], SHARD))
    loads["w_up"].wait()
    loads["w_down"].wait()
    loads["w_proj"].wait()
    sent_on = []
    for i in pair:
        arrive(got[i])
        upper = dot(r.n2[i], r.v_w_up[...], 1, 0)
        r.uz[d, i] = upper.astype(BF16)
        hidden, slope = gelu_both(upper)
        r.gp[i] = slope
        r.s2[i] = dot(hidden.astype(BF16), r.v_w_down[...], 1, 1).astype(BF16)
        sent_on.append(scatter(r.s2.at[i], r.r2.at[i], SHARD))
    arrive(got_dg)
    loads["d_down"].wait()
    r.dgh[...] = dot(r.dgf[...].reshape(512, 512), r.v_d_down[...], 1, 0)
    sent = exchange(lambda i: r.sent.at[i], slot_rows(r.arr), put_rows(r.arr))
    for i in pair:
        arrive(sent_on[i])
        out_low = (r.mid[i] + summed(r.s2.at[i], r.r2.at[i], SHARD)).astype(BF16)
        r.eo[i] = out_low
        r.sent[i] = dot(out_low, r.v_w_proj[...], 1, 0).astype(BF16)
        sent.start(i)
    r.ez[d, :, own16] = r.eo[:, :, pl.ds(pl.multiple_of(m * 256, 256), 256)]
    got_eo = []
    for k in (1, 2, 3):
        columns = pl.ds(pl.multiple_of(model(k) * 256, 256), 256)
        got_eo.append(send(r.eo.at[:, :, columns], r.ez.at[d, :, own16], {"mp": model(k)}))

    loads["d_qkv"].wait()
    loads["d_out"].wait()
    loads["d_up"].wait()
    cols = lax.broadcasted_iota(jnp.int32, (1, 256), 1)
    d_keep = lax.rem(cols, ROWS) < PATCHES
    sent_on = []
    for i in pair:
        sent.landed(i)
        values = r.grid[i] + dot(r.hot[i], r.arr[i], 1, 0)
        r.grid[i] = values
        normal, _ = norm_rows(values)
        normed = (normal * d_g1).astype(BF16)
        at = slice(i * 256, (i + 1) * 256)
        r.dn1[at, :] = normed
        part = dot(normed, r.v_d_qkv[...], 1, 0).astype(BF16)
        r.dqkv[at, :] = part
        probs, context = attention(part, d_keep, 256, 128, DEC_HEAD, d_scale)
        r.dprobs[i] = probs
        r.dctx[at, :] = context
        r.s3[i] = dot(context, r.v_d_out[...], 1, 1).astype(BF16)
        sent_on.append(scatter(r.s3.at[i], r.r3.at[i], ROWS))
    got_u = along(r.uz)
    got_x2 = cuts(1, [r.n2[0], r.n2[1]])
    arrive(got_eo)
    got_ez = along(r.ez)
    got = []
    for i in pair:
        arrive(sent_on[i])
        middle = r.grid[i, own64, :] + summed(r.s3.at[i], r.r3.at[i], ROWS)
        r.dmid[i] = middle
        normal, _ = norm_rows(middle)
        r.dn2[i, own64, :] = (normal * d_g2).astype(BF16)
        got.append(gather(r.dn2.at[i], ROWS))
    sent_on = []
    for i in pair:
        arrive(got[i])
        at = slice(i * 256, (i + 1) * 256)
        hidden, slope = gelu_both(dot(r.dn2[i], r.v_d_up[...], 1, 0))
        grad_upper = (r.dgh[at, :] * slope).astype(BF16)
        r.dhid[at, :] = hidden.astype(BF16)
        r.dgu[at, :] = grad_upper
        r.s4[i] = dot(grad_upper, r.v_d_up[...], 1, 1).astype(BF16)
        sent_on.append(scatter(r.s4.at[i], r.r4.at[i], ROWS))

    def dec_weights(left, right, own, away, first):
        size = right.shape[1]
        for a in (0, 1):
            rows = pl.ds(pl.multiple_of(lax.rem(s + a, 2) * 256, 256), 256)
            value = dot(left[:, rows], right[...], 0, 0)
            if a == 0:
                own[:, first : first + size] = value
            else:
                away[:, first : first + size] = value.astype(BF16)

    def dec_sums(own, arrived, away, landing):
        for block in range(4):
            at = slice(block * 64, (block + 1) * 64)
            own[at, :] = own[at, :] + arrived[at, :].astype(F32)
            away[block] = own[at, :].astype(BF16)
        return [send(away.at[data(k)], landing.at[k - 1], {"dp": data(k)}) for k in (1, 2, 3)]

    dec_weights(r.dn2.reshape(512, 512), r.dgu, r.w1o, r.w1s, 0)
    dec_weights(r.dgf.reshape(512, 512), r.dhid, r.w1o, r.w1s, 512)
    got_w1 = [send(r.w1s, r.w1r, to_plane(1, 0))]
    r.vec[...] = jnp.zeros((8, 512), F32)
    got = []
    gain_sum = jnp.zeros((1, 512), F32)
    for i in pair:
        arrive(sent_on[i])
        total = summed(r.s4.at[i], r.r4.at[i], ROWS)
        normal, inverse = norm_rows(r.dmid[i])
        grad = r.dgrad[i].astype(F32) + rows_back(normal, inverse, d_g2, total)
        gain_sum += jnp.sum(total * normal, axis=0, keepdims=True)
        r.dgm[i, own64, :] = grad.astype(BF16)
        got.append(gather(r.dgm.at[i], ROWS))
    r.vec[5:6, :] = gain_sum
    shard = lax.broadcasted_iota(jnp.int32, (256, 1), 0) // ROWS
    here = (shard == m).astype(F32)
    parts = []
    for i in pair:
        whole = jnp.concatenate([r.dmid[i]] * 4, axis=0)
        value = dot(r.dhid[i * 256 : (i + 1) * 256, :], r.v_d_down[...], 1, 1)
        parts.append(value + whole * here)
    for block in range(8):
        at = slice(block * 64, (block + 1) * 64)
        r.ds[block] = jnp.concatenate([parts[0][:, at], parts[1][:, at]], axis=1).astype(BF16)
    got_dec = []
    for a, k in plane:
        to = lax.rem(s + a, 2) * 4 + model(k)
        got_dec.append(send(r.ds.at[to], r.dr.at[rank], to_plane(a, k)))
    r.dr[rank] = r.ds[rank]
    arrive(got_w1)
    got_z1 = dec_sums(r.w1o, r.w1r, r.z1s, r.z1r)

    gain_sum = jnp.zeros((1, 512), F32)
    token_sum = jnp.zeros((1, 512), F32)
    sent_on = []
    for i in pair:
        arrive(got[i])
        at = slice(i * 256, (i + 1) * 256)
        grad_low = r.dgm[i]
        grad_context = dot(grad_low, r.v_d_out[...], 1, 0).astype(BF16)
        part = attention_back(
            r.dqkv[at, :], r.dprobs[i], grad_context, 256, 128, DEC_HEAD, d_scale
        )
        r.dgq[at, :] = part
        terms = dot(part, r.v_d_qkv[...], 1, 1)
        normal, inverse = norm_rows(r.grid[i])
        gain_sum += jnp.sum(terms * normal, axis=0, keepdims=True)
        back = rows_back(normal, inverse, d_g1, terms) + 0.25 * grad_low.astype(F32)
        token_sum += jnp.sum(back * r.free[i], axis=0, keepdims=True)
        r.s5[i] = dot(r.hot[i], back.astype(BF16), 0, 0).astype(BF16)
        sent_on.append(scatter(r.s5.at[i], r.r5.at[i], SHARD))
    r.vec[4:5, :] = gain_sum
    r.vec[6:7, :] = token_sum

    def put_back(i):
        r.sz[d, place, m] = r.sg[i]

    back = exchange(
        lambda i: r.sg.at[i], lambda i, at: r.sz.at[to_dp(), i, at], put_back
    )
    for i in pair:
        arrive(sent_on[i])
        r.sg[i] = summed(r.s5.at[i], r.r5.at[i], SHARD).astype(BF16)
        back.start(i)
    dec_weights(r.dn1, r.dgq, r.w2o, r.w2s, 0)
    dec_weights(r.dgm.reshape(512, 512), r.dctx, r.w2o, r.w2s, 384)
    got_w2 = [send(r.w2s, r.w2r, to_plane(1, 0))]

    sent_on = []
    for i in pair:
        back.landed(i)
        grad_low = dot(r.sz[d, i].reshape(64, 512), r.v_w_proj[...], 1, 1).astype(BF16)
        grad_upper = (dot(grad_low, r.v_w_down[...], 1, 0) * r.gp[i]).astype(BF16)
        r.s6[i] = dot(grad_upper, r.v_w_up[...], 1, 1).astype(BF16)
        sent_on.append(scatter(r.s6.at[i], r.r6.at[i], SHARD))
    got_sz = [
        send(r.sz.at[d, :, m], r.sz.at[d, :, m], {"dp": data(k)}) for k in (1, 2, 3)
    ]
    arrive(got_w2)
    got_z2 = dec_sums(r.w2o, r.w2r, r.z2s, r.z2r)
    got = []
    gain_two = jnp.zeros((1, WIDTH), F32)
    for i in pair:
        arrive(sent_on[i])
        total = summed(r.s6.at[i], r.r6.at[i], SHARD)
        normal, inverse = norm_rows(r.mid[i])
        own_grad = dot(r.sz[d, i, m], r.v_w_proj[...], 1, 1)
        grad = own_grad + rows_back(normal, inverse, e_g2, total)
        gain_two += jnp.sum(total * normal, axis=0, keepdims=True)
        r.gm[i, own16, :] = grad.astype(BF16)
        got.append(gather(r.gm.at[i], SHARD))
    r.vec[2:3, :] = gain_two[:, :512]
    r.vec[3:4, :] = gain_two[:, 512:]
    arrive(got_sz)
    got_sm = []
    for k in (1, 2, 3):
        for j in (1, 2, 3):
            part = r.sz.at[data(k), :, m]
            got_sm.append(send(part, r.sz.at[data(k), :, m], {"mp": model(j)}))
    gain_one = jnp.zeros((1, WIDTH), F32)
    got_f, got_q = [], []
    for i in pair:
        arrive(got[i])
        grad_low = r.gm[i]
        grad_context = dot(grad_low, r.v_w_out[...], 1, 0).astype(BF16)
        part = attention_back(r.qkv[i], r.probs[i], grad_context, 64, 256, HEAD, e_scale)
        r.qz[d, i] = part
        got_q += [send(r.qz.at[d, i], r.qz.at[d, i], {"dp": data(k)}) for k in (1, 2, 3)]
        terms = dot(part, r.v_w_qkv[...], 1, 1)
        normal, inverse = norm_rows(r.xf[i].astype(F32))
        gain_one += jnp.sum(terms * normal, axis=0, keepdims=True)
        grad = rows_back(normal, inverse, e_g1, terms) + 0.25 * grad_low.astype(F32)
        for block in range(8):
            r.fs[block, i] = grad[:, block * 128 : (block + 1) * 128].astype(BF16)
        for a, k in plane:
            to = lax.rem(s + a, 2) * 4 + model(k)
            got_f.append(send(r.fs.at[to, i], r.fr.at[rank, i], to_plane(a, k)))
        r.fr[rank, i] = r.fs[rank, i]
    got_x4 = cuts(2, [r.gm[0], r.gm[1]])
    r.vec[0:1, :] = gain_one[:, :512]
    r.vec[1:2, :] = gain_one[:, 512:]
    r.vr[rank] = r.vec[...]
    got_v = [send(r.vec, r.vr.at[rank], to_plane(a, k)) for a, k in plane]

    def enc_weights(lefts, value, first, out):
        size = value.shape[1]
        r.wes[:, first : first + size] = dot(lefts[1], value, 0, 0).astype(BF16)
        made = send(
            r.wes.at[:, first : first + size], r.wer.at[:, first : first + size], to_plane(1, 0)
        )
        out[...] = dot(lefts[0], value, 0, 0)
        return made

    def cut_rows(which):
        return [r.xz[which, :, lax.rem(s + a, 2)].reshape(512, 128) for a in (0, 1)]

    arrive(got_u)
    hidden, slope = gelu_both(r.uz[...].reshape(512, WIDTH).astype(F32))
    r.ha[...] = hidden.astype(BF16)
    arrive(got_sm)
    grad_all = r.sz[...].reshape(512, 512)
    r.ga[...] = dot(grad_all, r.v_w_proj[...], 1, 1).astype(BF16)
    grad_upper = (dot(r.ga[...], r.v_w_down[...], 1, 0) * slope).astype(BF16)
    lefts = []
    for a in (0, 1):
        block = lax.rem(s + a, 2) * 4 + d
        lefts.append(r.ga[:, pl.ds(pl.multiple_of(block * 128, 128), 128)])
    got_w = [enc_weights(lefts, r.ha[...], 2048, r.o_down)]
    arrive(got_x2)
    got_w.append(enc_weights(cut_rows(1), grad_upper, 1024, r.o_up))

    arrive(got_ez)
    r.ps[...] = dot(r.ez[...].reshape(512, 256), grad_all, 0, 0).astype(BF16)
    got_p = [send(r.ps, r.pr, to_plane(1, 0))]
    arrive(got_z1)
    mine64 = pl.ds(pl.multiple_of(d * 64, 64), 64)
    total = r.w1o[mine64, :]
    for k in range(3):
        total = total + r.z1r[k].astype(F32)
    r.o_dup[...] = total[:, :512]
    r.o_ddown[...] = total[:, 512:]
    arrive(got_z2)
    total = r.w2o[mine64, :]
    for k in range(3):
        total = total + r.z2r[k].astype(F32)
    r.o_dqkv[...] = total[:, :384]
    r.o_dout[...] = total[:, 384:]
    arrive(got_p)
    half_rows = pl.ds(pl.multiple_of(s * 128, 128), 128)
    r.pa[m, s] = (r.ps[half_rows, :].astype(F32) + r.pr[half_rows, :].astype(F32)).astype(BF16)
    got_pa = [send(r.pa.at[m, s], r.pa.at[m, s], {"mp": model(k)}) for k in (1, 2, 3)]
    arrive(got_v)
    total = r.vr[0]
    for k in range(1, 8):
        total = total + r.vr[k]
    r.vz[d] = total
    got_vz = along(r.vz)
    arrive(got_dec)
    for a in (0, 1):
        total = r.dr[4 * a].astype(F32)
        for k in (1, 2, 3):
            total = total + r.dr[4 * a + k].astype(F32)
        r.o_dec[a] = total
    arrive(got_f)
    for a in (0, 1):
        total = r.fr[4 * a].astype(F32)
        for k in (1, 2, 3):
            total = total + r.fr[4 * a + k].astype(F32)
        r.o_pat[a] = total.reshape(128, 128)
    arrive(got_pa)
    got_ps = [send(r.pa.at[:, s], r.pa.at[:, s], to_plane(1, 0))]
    arrive(got_c)
    arrive(got_x4)
    got_w.append(enc_weights(cut_rows(2), r.cz[...].reshape(512, 256), 768, r.o_out))
    arrive(got_x1)
    arrive(got_q)
    got_w.append(enc_weights(cut_rows(0), r.qz[...].reshape(512, 768), 0, r.o_qkv))
    arrive(got_vz)
    r.o_vec[...] = r.vz[0] + r.vz[1] + r.vz[2] + r.vz[3]
    arrive(got_ps)
    for a in range(4):
        for b in range(2):
            at = a * 256 + b * 128
            r.o_proj[at : at + 128, :] = r.pa[a, b].astype(F32)
    firsts = [(2048, 1024, r.o_down), (1024, 1024, r.o_up), (768, 256, r.o_out), (0, 768, r.o_qkv)]
    for made, (first, size, out) in zip(got_w, firsts):
        made.wait_recv()
        out[...] += r.wer[:, first : first + size].astype(F32)
    for made in started:
        made.wait_send()
    for leave in (info, sent, back):
        leave.left()
    assert used[0] <= COPIES


def with_kernel(
    patches,
    counts,
    patch_index,
    scale_level,
    enc_gain_one,
    enc_qkv,
    enc_out,
    enc_gain_two,
    enc_up,
    enc_down,
    w_proj,
    mask_token,
    pos_table,
    dec_gain_one,
    dec_qkv,
    dec_out,
    dec_gain_two,
    dec_up,
    dec_down,
    decoded_grad,
):
    s, m = lax.axis_index("section"), lax.axis_index("mp")

    def own_pair(values, axis):
        return lax.dynamic_slice_in_dim(values, PAIR * s, PAIR, axis)

    rows = jnp.swapaxes(own_pair(patches, 1), 0, 1)
    grads = jnp.swapaxes(own_pair(decoded_grad, 1), 0, 1)
    grads = jnp.pad(grads, ((0, 0), (0, ROWS - PATCHES), (0, 0)))
    seen = own_pair(counts, 0)
    keep = (jnp.arange(128, dtype=jnp.int32)[None, :] < seen[:, None]).astype(F32)
    keep = jnp.broadcast_to(keep[:, None, :], (PAIR, 8, 128))
    index = jnp.swapaxes(own_pair(patch_index, 1), 0, 1)
    grid_row = (index // PATCHES) * ROWS + index % PATCHES
    slot = m * SHARD + jnp.arange(SHARD, dtype=jnp.int32)
    grid_row = jnp.where(slot[None, :] < seen[:, None], grid_row, -1)
    lanes = jnp.zeros((PAIR, 128), jnp.int32)
    lanes = lax.dynamic_update_slice(lanes, grid_row, (0, m * SHARD))
    level = jnp.where(m == 0, own_pair(scale_level, 0), 0)
    info = jnp.concatenate(
        [
            lanes[:, None, :],
            jnp.broadcast_to(level[:, None, None], (PAIR, 1, 128)),
            jnp.zeros((PAIR, 6, 128), jnp.int32),
        ],
        axis=1,
    )
    wide = lambda v: jnp.pad(v.astype(F32), (0, WIDTH - v.shape[0]))[None, :]
    gains = jnp.concatenate(
        [wide(v) for v in (enc_gain_one, enc_gain_two, dec_gain_one, dec_gain_two, mask_token)]
        + [jnp.zeros((3, WIDTH), F32)],
        axis=0,
    )
    table = pos_table.reshape(8, WAYS, PATCHES, DEC_WIDTH)
    table = jnp.pad(table, ((0, 0), (0, 0), (0, ROWS - PATCHES), (0, 0))).reshape(8, 256, DEC_WIDTH)
    inputs = (
        rows,
        info,
        keep,
        gains,
        grads,
        enc_qkv.reshape(WIDTH, 768),
        enc_out,
        enc_up,
        enc_down,
        w_proj,
        table,
        dec_qkv.reshape(DEC_WIDTH, 384),
        dec_out,
        dec_up,
        dec_down,
    )
    shapes = (
        (2, 256, 128),
        (2, 128, 128),
        (128, 768),
        (128, 256),
        (128, 1024),
        (128, 1024),
        (64, 384),
        (64, 128),
        (64, 512),
        (64, 512),
        (1024, 512),
        (8, 512),
    )
    vmem = pl.BlockSpec(memory_space=pltpu.VMEM)
    outs = pl.pallas_call(
        kernel,
        out_shape=[jax.ShapeDtypeStruct(shape, F32) for shape in shapes],
        in_specs=[vmem] * 5 + [pl.BlockSpec(memory_space=pl.ANY)] * 10,
        out_specs=[vmem] * len(shapes),
        scratch_shapes=[pltpu.VMEM(shape, kind) for shape, kind in BUFFERS.values()]
        + [pltpu.VMEM(shape, BF16) for shape in LOADED.values()]
        + [
            pltpu.SemaphoreType.DMA((len(LOADED),)),
            pltpu.SemaphoreType.DMA((COPIES,)),
            pltpu.SemaphoreType.DMA((COPIES,)),
        ],
        compiler_params=pltpu.CompilerParams(
            collective_id=0, has_side_effects=True, vmem_limit_bytes=60 * 2**20
        ),
        name="layer_pair",
    )(*inputs)
    dec, pat, qkv, out, up, down, dqkv, dout, dup, ddown, proj, vec = outs
    dec = dec.reshape(2, WAYS, ROWS, PAIR, 64)[:, :, :PATCHES]
    dec = jnp.transpose(dec, (1, 2, 0, 3, 4)).reshape(WAYS * PATCHES, 4, 64)
    pat = jnp.transpose(pat.reshape(2, PAIR, SLOTS, 128), (2, 0, 1, 3)).reshape(SLOTS, 4, 128)
    return (
        dec,
        pat,
        qkv.reshape(128, 3, 256),
        out,
        up,
        down,
        dqkv.reshape(64, 3, 128),
        dout,
        dup,
        ddown,
        proj,
        vec[0:2].reshape(WIDTH),
        vec[2:4].reshape(WIDTH),
        vec[4],
        vec[5],
        vec[6],
    )


def fits_kernel(mesh, shapes):
    ways = (mesh.shape["section"], mesh.shape["dp"], mesh.shape["mp"])
    wanted = {0: (64, 16, 1024), 5: (1024, 3, 1024), 8: (1024, 4096), 10: (1024, 512)}
    wanted.update({12: (8, 196, 512), 14: (512, 3, 512), 17: (512, 2048), 19: (196, 16, 512)})
    return ways == (2, 4, 4) and all(shapes[i] == shape for i, shape in wanted.items())


def solution(mesh):
    def program(*arrays):
        shapes = [array.shape for array in arrays]
        body = with_kernel if fits_kernel(mesh, shapes) else on_device
        return placed_on(mesh, body)(*arrays)

    return program
```

```python
import functools
import math

import jax
import jax.numpy as jnp
from jax import lax
from jax.experimental import pallas as pl
from jax.experimental.pallas import tpu as pltpu
from jax.sharding import PartitionSpec as P

HEAD = 64
DEC_HEAD = 32


eps = 1e-06


def norm_rows(values):
    average = jnp.mean(values, axis=-1, keepdims=True)
    centered = values - average
    variance = jnp.mean(centered * centered, axis=-1, keepdims=True)
    inverse = lax.rsqrt(variance + eps)
    return (centered * inverse, inverse)


def norm_back(normal, inverse, gain_vec, gradient):
    weighted = gradient * gain_vec
    first_term = jnp.mean(weighted, axis=-1, keepdims=True)
    second_term = jnp.mean(weighted * normal, axis=-1, keepdims=True)
    return (
        inverse * (weighted - first_term - normal * second_term),
        jnp.sum(gradient * normal, axis=(0, 1)),
    )


def spread(values):
    return lax.all_gather(values, "mp", axis=0, tiled=True)


def collect(values):
    return lax.psum_scatter(values, "mp", scatter_dimension=0, tiled=True)


def spare_of(work):
    return lambda: jax.tree.map(jnp.zeros_like, work())


def head_view(qkv_rows, head_size):
    return qkv_rows.reshape(
        qkv_rows.shape[0], qkv_rows.shape[1], 3, qkv_rows.shape[3] // head_size, head_size
    )


def score_rows(queries, key_rows, visible, head_size):
    scores = jnp.einsum(
        "sbhe,tbhe->bhst", queries, key_rows, preferred_element_type=jnp.float32
    ) * (1.0 / math.sqrt(head_size))
    return jnp.where(visible[:, None, None, :], scores, -1e30)


def attend(qkv_rows, visible, head_size):
    heads_view = head_view(qkv_rows, head_size)
    scores = score_rows(heads_view[:, :, 0], heads_view[:, :, 1], visible, head_size)
    highest = jnp.max(scores, axis=-1, keepdims=True)
    weights = jnp.exp(scores - highest)
    denominator = jnp.sum(weights, axis=-1, keepdims=True)
    probability = (weights / denominator).astype(jnp.bfloat16)
    context = jnp.einsum(
        "bhst,tbhe->sbhe", probability, heads_view[:, :, 2], preferred_element_type=jnp.float32
    )
    context = context.reshape(qkv_rows.shape[0], qkv_rows.shape[1], qkv_rows.shape[3]).astype(
        jnp.bfloat16
    )
    return (context, highest + jnp.log(denominator))


def attend_back(qkv_rows, visible, logsum, grad_context, head_size):
    heads_view = head_view(qkv_rows, head_size)
    queries = heads_view[:, :, 0]
    key_rows = heads_view[:, :, 1]
    value_rows = heads_view[:, :, 2]
    probability = jnp.exp(score_rows(queries, key_rows, visible, head_size) - logsum)
    grad_heads = grad_context.reshape(queries.shape)
    grad_values = jnp.einsum(
        "bhst,sbhe->tbhe",
        probability.astype(jnp.bfloat16),
        grad_heads,
        preferred_element_type=jnp.float32,
    )
    grad_probs = jnp.einsum(
        "sbhe,tbhe->bhst", grad_heads, value_rows, preferred_element_type=jnp.float32
    )
    row_inner = jnp.sum(grad_probs * probability, axis=-1, keepdims=True)
    grad_scores = (probability * (grad_probs - row_inner)).astype(jnp.bfloat16)
    score_scale = 1.0 / math.sqrt(head_size)
    grad_queries = (
        jnp.einsum("bhst,tbhe->sbhe", grad_scores, key_rows, preferred_element_type=jnp.float32)
        * score_scale
    )
    grad_keys = (
        jnp.einsum("bhst,sbhe->tbhe", grad_scores, queries, preferred_element_type=jnp.float32)
        * score_scale
    )
    stacked = jnp.stack([grad_queries, grad_keys, grad_values], axis=2)
    return stacked.reshape(qkv_rows.shape).astype(jnp.bfloat16)


def attention_local(normed_one, visible, w_qkv, w_out, head_size):
    qkv_rows = jnp.einsum(
        "sbw,wcf->sbcf", normed_one, w_qkv, preferred_element_type=jnp.float32
    ).astype(jnp.bfloat16)
    context, logsum = attend(qkv_rows, visible, head_size)
    mixed_terms = jnp.einsum("sbf,wf->sbw", context, w_out, preferred_element_type=jnp.float32)
    return (qkv_rows, context, logsum, mixed_terms)


def feed_local(normed_two, w_up, w_down):
    upper_in = jnp.einsum("sbw,wf->sbf", normed_two, w_up, preferred_element_type=jnp.float32)
    hidden = jax.nn.gelu(upper_in, approximate=False).astype(jnp.bfloat16)
    return (upper_in, jnp.einsum("sbf,wf->sbw", hidden, w_down, preferred_element_type=jnp.float32))


def feed_back_local(grad_full, normed_two, upper_in, w_up, w_down):
    value_out, gelu_pull = jax.vjp(
        lambda argument: jax.nn.gelu(argument, approximate=False), upper_in
    )
    hidden = value_out.astype(jnp.bfloat16)
    grad_down_w = jnp.einsum("sbw,sbf->wf", grad_full, hidden, preferred_element_type=jnp.float32)
    grad_hidden = jnp.einsum("sbw,wf->sbf", grad_full, w_down, preferred_element_type=jnp.float32)
    grad_upper = gelu_pull(grad_hidden)[0].astype(jnp.bfloat16)
    grad_up_w = jnp.einsum(
        "sbw,sbf->wf", normed_two, grad_upper, preferred_element_type=jnp.float32
    )
    grad_terms = jnp.einsum("sbf,wf->sbw", grad_upper, w_up, preferred_element_type=jnp.float32)
    return (grad_up_w, grad_down_w, grad_terms)


def attention_back_local(
    grad_full, qkv_rows, context, logsum, visible, normed_one, w_qkv, w_out, head_size
):
    grad_out_w = jnp.einsum("sbw,sbf->wf", grad_full, context, preferred_element_type=jnp.float32)
    grad_context = jnp.einsum(
        "sbw,wf->sbf", grad_full, w_out, preferred_element_type=jnp.float32
    ).astype(jnp.bfloat16)
    grad_qkv = attend_back(qkv_rows, visible, logsum, grad_context, head_size)
    grad_qkv_w = jnp.einsum(
        "sbw,sbcf->wcf", normed_one, grad_qkv, preferred_element_type=jnp.float32
    )
    grad_normed = jnp.einsum("sbcf,wcf->sbw", grad_qkv, w_qkv, preferred_element_type=jnp.float32)
    return (grad_qkv_w, grad_out_w, grad_normed)


def on_device(
    patches,
    counts,
    patch_index,
    scale_level,
    enc_gain_one,
    enc_qkv,
    enc_out,
    enc_gain_two,
    enc_up,
    enc_down,
    w_proj,
    mask_token,
    pos_table,
    dec_gain_one,
    dec_qkv,
    dec_out,
    dec_gain_two,
    dec_up,
    dec_down,
    decoded_grad,
):
    data_ways = lax.axis_size("dp")
    model_ways = lax.axis_size("mp")
    slot_rows = patches.shape[0]
    images = patches.shape[1]
    grid_rows = decoded_grad.shape[0]
    dec_width = decoded_grad.shape[2]
    slot_count = slot_rows * model_ways
    grid_count = grid_rows * model_ways
    per_peer = images // data_ways
    slot_start = lax.axis_index("mp") * slot_rows
    grid_start = lax.axis_index("mp") * grid_rows
    is_encoder = lax.axis_index("section") == 0
    visible = jnp.arange(slot_count, dtype=jnp.int32)[None, :] < counts[:, None]
    all_visible = jnp.ones((images, grid_count), dtype=bool)
    enc_g1 = enc_gain_one.astype(jnp.float32)
    enc_g2 = enc_gain_two.astype(jnp.float32)
    dec_g1 = dec_gain_one.astype(jnp.float32)
    dec_g2 = dec_gain_two.astype(jnp.float32)
    token_vec = mask_token.astype(jnp.float32)

    def on_encoder(work):
        return lax.cond(is_encoder, work, spare_of(work))

    def on_decoder(work):
        return lax.cond(is_encoder, spare_of(work), work)

    full_in = spread(patches)

    def enc_attention():
        normal_one, inverse_one = norm_rows(full_in.astype(jnp.float32))
        normed_one = (normal_one * enc_g1).astype(jnp.bfloat16)
        return attention_local(normed_one, visible, enc_qkv, enc_out, HEAD)

    enc_qkv_rows, enc_context, enc_logsum, enc_mixed_terms = on_encoder(enc_attention)
    enc_middle = patches.astype(jnp.float32) + collect(enc_mixed_terms)
    enc_normal_two, enc_inverse_two = norm_rows(enc_middle)
    enc_normed_two = spread((enc_normal_two * enc_g2).astype(jnp.bfloat16))
    enc_upper, enc_down_terms = on_encoder(lambda: feed_local(enc_normed_two, enc_up, enc_down))
    enc_out_low = (enc_middle + collect(enc_down_terms)).astype(jnp.bfloat16)

    def enc_send():
        sent_rows = jnp.einsum(
            "sbw,wf->sbf", enc_out_low, w_proj, preferred_element_type=jnp.float32
        ).astype(jnp.bfloat16)
        live_slot = (slot_start + jnp.arange(slot_rows, dtype=jnp.int32))[:, None] < counts[None, :]
        sent_index = jnp.where(live_slot, patch_index, grid_count)
        packed = (
            sent_rows.reshape(slot_rows, per_peer, data_ways, dec_width),
            sent_index.reshape(slot_rows, per_peer, data_ways),
            scale_level.reshape(1, per_peer, data_ways),
        )
        packed = tuple(
            (jnp.concatenate([jnp.zeros_like(member), member], axis=2) for member in packed)
        )
        return packed

    packed = on_encoder(enc_send)
    received = (
        lax.all_to_all(packed[0], ("section", "dp"), split_axis=2, concat_axis=1, tiled=True),
        lax.all_to_all(packed[1], ("section", "dp"), split_axis=2, concat_axis=1, tiled=True),
        lax.all_to_all(packed[2], ("section", "dp"), split_axis=2, concat_axis=1, tiled=True),
    )
    arrived = (received[0][:, :images, 0], received[1][:, :images, 0], received[2][0, :images, 0])
    arrived_rows, arrived_index, arrived_level = arrived

    def make_onehot():
        return (
            arrived_index[:, :, None] == jnp.arange(grid_count, dtype=jnp.int32)[None, None, :]
        ).astype(jnp.bfloat16)

    def dec_place():
        onehot_low = make_onehot()
        covered = jnp.transpose(jnp.sum(onehot_low.astype(jnp.float32), axis=0))
        placed = jnp.einsum(
            "sbp,sbf->pbf", onehot_low, arrived_rows, preferred_element_type=jnp.float32
        )
        return (placed - covered[:, :, None] * token_vec, covered)

    placed_terms, covered_terms = on_decoder(dec_place)
    placed_rows, covered_rows = collect((placed_terms, covered_terms))
    table_rows = lax.dynamic_slice_in_dim(pos_table, grid_start, grid_rows, 1)
    level_hot = (
        arrived_level[:, None] == jnp.arange(pos_table.shape[0], dtype=jnp.int32)[None, :]
    ).astype(jnp.bfloat16)
    position = jnp.einsum("bl,lpf->pbf", level_hot, table_rows, preferred_element_type=jnp.float32)
    grid_values = placed_rows + token_vec + position
    dec_normal_one, dec_inverse_one = norm_rows(grid_values)
    dec_normed_one = spread((dec_normal_one * dec_g1).astype(jnp.bfloat16))
    dec_qkv_rows, dec_context, dec_logsum, dec_mixed_terms = on_decoder(
        lambda: attention_local(dec_normed_one, all_visible, dec_qkv, dec_out, DEC_HEAD)
    )
    dec_middle = grid_values + collect(dec_mixed_terms)
    dec_normal_two, dec_inverse_two = norm_rows(dec_middle)
    dec_normed_two = spread((dec_normal_two * dec_g2).astype(jnp.bfloat16))

    def dec_feed():
        upper_in, down_terms = feed_local(dec_normed_two, dec_up, dec_down)
        own_rows = lax.dynamic_slice_in_dim(down_terms, grid_start, grid_rows, 0) + dec_middle
        return (upper_in, lax.dynamic_update_slice_in_dim(down_terms, own_rows, grid_start, 0))

    dec_upper, dec_summand = on_decoder(dec_feed)
    decoded = lax.psum_scatter(
        dec_summand.astype(jnp.bfloat16), ("section", "mp"), scatter_dimension=2, tiled=True
    ).astype(jnp.float32)
    dec_grad_full = spread(decoded_grad)
    dec_up_grad, dec_down_grad, dec_two_terms = on_decoder(
        lambda: feed_back_local(dec_grad_full, dec_normed_two, dec_upper, dec_up, dec_down)
    )
    dec_through, dec_gain_two_grad = norm_back(
        dec_normal_two, dec_inverse_two, dec_g2, collect(dec_two_terms)
    )
    dec_grad_middle = decoded_grad.astype(jnp.float32) + dec_through
    dec_middle_full = spread(dec_grad_middle.astype(jnp.bfloat16))
    dec_qkv_grad, dec_out_grad, dec_one_terms = on_decoder(
        lambda: attention_back_local(
            dec_middle_full,
            dec_qkv_rows,
            dec_context,
            dec_logsum,
            all_visible,
            dec_normed_one,
            dec_qkv,
            dec_out,
            DEC_HEAD,
        )
    )
    dec_inner, dec_gain_one_grad = norm_back(
        dec_normal_one, dec_inverse_one, dec_g1, collect(dec_one_terms)
    )
    grad_grid = dec_grad_middle + dec_inner
    grad_token = jnp.sum(grad_grid * (1.0 - covered_rows)[:, :, None], axis=(0, 1))
    grad_grid_full = spread(grad_grid.astype(jnp.bfloat16))

    def dec_return():
        grad_sent = jnp.einsum(
            "sbp,pbf->sbf", make_onehot(), grad_grid_full, preferred_element_type=jnp.float32
        ).astype(jnp.bfloat16)
        return jnp.concatenate([grad_sent, jnp.zeros_like(grad_sent)], axis=1)[:, :, None, :]

    back_rows = on_decoder(dec_return)
    returned = lax.all_to_all(
        back_rows, ("section", "dp"), split_axis=1, concat_axis=2, tiled=True
    )[:, :, data_ways:]
    grad_arrived = returned.reshape(slot_rows, images, dec_width)

    def enc_project_back():
        grad_proj_w = jnp.einsum(
            "sbw,sbf->wf", enc_out_low, grad_arrived, preferred_element_type=jnp.float32
        )
        grad_block = jnp.einsum(
            "sbf,wf->sbw", grad_arrived, w_proj, preferred_element_type=jnp.float32
        )
        return (grad_proj_w, grad_block)

    proj_grad, enc_grad_block = on_encoder(enc_project_back)
    enc_grad_full = spread(enc_grad_block.astype(jnp.bfloat16))
    enc_up_grad, enc_down_grad, enc_two_terms = on_encoder(
        lambda: feed_back_local(enc_grad_full, enc_normed_two, enc_upper, enc_up, enc_down)
    )
    enc_through, enc_gain_two_grad = norm_back(
        enc_normal_two, enc_inverse_two, enc_g2, collect(enc_two_terms)
    )
    enc_grad_middle = enc_grad_block + enc_through
    enc_middle_full = spread(enc_grad_middle.astype(jnp.bfloat16))

    def enc_attention_back():
        normal_one, inverse_one = norm_rows(full_in.astype(jnp.float32))
        normed_one = (normal_one * enc_g1).astype(jnp.bfloat16)
        grad_qkv_w, grad_out_w, grad_normed = attention_back_local(
            enc_middle_full,
            enc_qkv_rows,
            enc_context,
            enc_logsum,
            visible,
            normed_one,
            enc_qkv,
            enc_out,
            HEAD,
        )
        grad_inner, grad_gain_one = norm_back(normal_one, inverse_one, enc_g1, grad_normed)
        own_rows = lax.dynamic_slice_in_dim(grad_inner, slot_start, slot_rows, 0) + enc_grad_middle
        summand = lax.dynamic_update_slice_in_dim(grad_inner, own_rows, slot_start, 0)
        return (grad_qkv_w, grad_out_w, grad_gain_one, summand)

    enc_qkv_grad, enc_out_grad, enc_gain_one_grad, in_summand = on_encoder(enc_attention_back)
    patches_grad = lax.psum_scatter(
        in_summand.astype(jnp.bfloat16), ("section", "mp"), scatter_dimension=2, tiled=True
    ).astype(jnp.float32)
    enc_gain_two_grad = jnp.where(is_encoder, enc_gain_two_grad, 0.0)
    dec_gain_one_grad = jnp.where(is_encoder, 0.0, dec_gain_one_grad)
    dec_gain_two_grad = jnp.where(is_encoder, 0.0, dec_gain_two_grad)
    grad_token = jnp.where(is_encoder, 0.0, grad_token)
    sharded = (
        lax.psum_scatter(enc_qkv_grad, ("section", "dp"), scatter_dimension=0, tiled=True),
        lax.psum_scatter(enc_out_grad, ("section", "dp"), scatter_dimension=0, tiled=True),
        lax.psum_scatter(enc_up_grad, ("section", "dp"), scatter_dimension=0, tiled=True),
        lax.psum_scatter(enc_down_grad, ("section", "dp"), scatter_dimension=0, tiled=True),
        lax.psum_scatter(dec_qkv_grad, ("section", "dp"), scatter_dimension=0, tiled=True),
        lax.psum_scatter(dec_out_grad, ("section", "dp"), scatter_dimension=0, tiled=True),
        lax.psum_scatter(dec_up_grad, ("section", "dp"), scatter_dimension=0, tiled=True),
        lax.psum_scatter(dec_down_grad, ("section", "dp"), scatter_dimension=0, tiled=True),
    )
    shared = lax.psum(
        (
            proj_grad,
            enc_gain_one_grad,
            enc_gain_two_grad,
            dec_gain_one_grad,
            dec_gain_two_grad,
            grad_token,
        ),
        ("section", "dp", "mp"),
    )
    return (
        decoded,
        patches_grad,
        sharded[0],
        sharded[1],
        sharded[2],
        sharded[3],
        sharded[4],
        sharded[5],
        sharded[6],
        sharded[7],
        shared[0],
        shared[1],
        shared[2],
        shared[3],
        shared[4],
        shared[5],
    )


def placed_on(mesh, body):
    placed = (
        P("mp", "dp", None),
        P("dp"),
        P("mp", "dp"),
        P("dp"),
        P(),
        P(None, None, "mp"),
        P(None, "mp"),
        P(),
        P(None, "mp"),
        P(None, "mp"),
        P(),
        P(),
        P(),
        P(),
        P(None, None, "mp"),
        P(None, "mp"),
        P(),
        P(None, "mp"),
        P(None, "mp"),
        P("mp", "dp", None),
    )
    return jax.shard_map(
        body,
        mesh=mesh,
        in_specs=placed,
        out_specs=(
            P(None, "dp", ("section", "mp")),
            P(None, "dp", ("section", "mp")),
            P(("section", "dp"), None, "mp"),
            P(("section", "dp"), "mp"),
            P(("section", "dp"), "mp"),
            P(("section", "dp"), "mp"),
            P(("section", "dp"), None, "mp"),
            P(("section", "dp"), "mp"),
            P(("section", "dp"), "mp"),
            P(("section", "dp"), "mp"),
            P(),
            P(),
            P(),
            P(),
            P(),
            P(),
        ),
        check_vma=False,
    )


MESH = pl.DeviceIdType.MESH
F32 = jnp.float32
BF16 = jnp.bfloat16
WAYS = 4
PAIR = 2
SLOTS = 64
SHARD = 16
PATCHES = 49
ROWS = 64
WIDTH = 1024
DEC_WIDTH = 512
HEADS_HERE = 4
COPIES = 256


def padded_row(patch):
    shard = sum((patch >= k * PATCHES).astype(jnp.int32) for k in (1, 2, 3))
    return patch + (ROWS - PATCHES) * shard


def dot(left, right, left_dim, right_dim):
    return lax.dot_general(
        left, right, (((left_dim,), (right_dim,)), ((), ())), preferred_element_type=F32
    )


def rows_back(normal, inverse, gain, gradient):
    weighted = gradient * gain
    first = jnp.mean(weighted, axis=-1, keepdims=True)
    second = jnp.mean(weighted * normal, axis=-1, keepdims=True)
    return inverse * (weighted - first - normal * second)


def gelu_both(upper):
    phi = 0.5 * (1.0 + lax.erf(upper * math.sqrt(0.5)))
    density = jnp.exp(-0.5 * upper * upper) * (1.0 / math.sqrt(2.0 * math.pi))
    return upper * phi, phi + upper * density


def head_mask(width, head, kind):
    lane = lax.broadcasted_iota(jnp.int32, (1, width), 1)
    return [
        ((lane >= h * head) & (lane < (h + 1) * head)).astype(F32).astype(kind)
        for h in range(HEADS_HERE)
    ]


def stack_heads(values, masks):
    return jnp.concatenate([values * mask for mask in masks], axis=0)


def fold_heads(stacked, masks, rows):
    total = None
    for h, mask in enumerate(masks):
        part = stacked[h * rows : (h + 1) * rows] * mask
        total = part if total is None else total + part
    return total


def attention(qkv, keep, rows, width, head, scale):
    low = head_mask(width, head, BF16)
    wide = head_mask(width, head, F32)
    queries = stack_heads(qkv[:, :width], low)
    scores = dot(queries, qkv[:, width : 2 * width], 1, 1) * scale
    scores = jnp.where(keep, scores, -1e30)
    weights = jnp.exp(scores - jnp.max(scores, axis=-1, keepdims=True))
    probs = weights / jnp.sum(weights, axis=-1, keepdims=True)
    mixed = dot(probs.astype(BF16), qkv[:, 2 * width :], 1, 0)
    return probs, fold_heads(mixed, wide, rows).astype(BF16)


def attention_back(qkv, probs, grad_context, rows, width, head, scale):
    low = head_mask(width, head, BF16)
    wide = head_mask(width, head, F32)
    queries = stack_heads(qkv[:, :width], low)
    grads = stack_heads(grad_context, low)
    grad_probs = dot(grads, qkv[:, 2 * width :], 1, 1)
    inner = jnp.sum(grad_probs * probs, axis=-1, keepdims=True)
    grad_scores = (probs * (grad_probs - inner)).astype(BF16)
    grad_queries = fold_heads(dot(grad_scores, qkv[:, width : 2 * width], 1, 0), wide, rows) * scale
    grad_keys = dot(grad_scores, queries, 0, 0) * scale
    grad_values = dot(probs.astype(BF16), grads, 0, 0)
    return jnp.concatenate([grad_queries, grad_keys, grad_values], axis=1).astype(BF16)


IN_NAMES = [
    "xs",
    "counts",
    "index",
    "levels",
    "g1",
    "g2",
    "g3",
    "g4",
    "g5",
    "dgrad",
    "w_qkv",
    "w_out",
    "w_up",
    "w_down",
    "w_proj",
    "table",
    "d_qkv",
    "d_out",
    "d_up",
    "d_down",
]
OUT_NAMES = [
    "o_dec",
    "o_pat",
    "o_qkv",
    "o_out",
    "o_up",
    "o_down",
    "o_dqkv",
    "o_dout",
    "o_dup",
    "o_ddown",
    "o_proj",
    "o_v1",
    "o_v2",
    "o_v3",
    "o_v4",
    "o_v5",
]
LOADED = dict(
    w_qkv=(WIDTH, 768),
    w_out=(WIDTH, 256),
    w_up=(WIDTH, 1024),
    w_down=(WIDTH, 1024),
    w_proj=(WIDTH, DEC_WIDTH),
    table=(196, 8, DEC_WIDTH),
    d_qkv=(DEC_WIDTH, 384),
    d_out=(DEC_WIDTH, 128),
    d_up=(DEC_WIDTH, 512),
    d_down=(DEC_WIDTH, 512),
)
STORED = dict(
    o_dec=(4, 64, 196),
    o_qkv=(3, 128, 256),
    o_out=(128, 256),
    o_up=(128, 1024),
    o_down=(128, 1024),
    o_dqkv=(3, 64, 128),
    o_dout=(64, 128),
    o_dup=(64, 512),
    o_ddown=(64, 512),
    o_proj=(1024, 512),
)
BUFFERS = dict(
    info=((2, 8, 128), jnp.int32),
    flat=((1568, 512), BF16),
    xf=((2, 64, 1024), BF16),
    qkv=((2, 64, 768), BF16),
    probs=((2, 256, 64), F32),
    s1=((2, 64, 1024), BF16),
    r1=((2, 3, 16, 1024), BF16),
    mid=((2, 16, 1024), F32),
    n2=((2, 64, 1024), BF16),
    gp=((2, 64, 1024), F32),
    s2=((2, 64, 1024), BF16),
    r2=((2, 3, 16, 1024), BF16),
    eo=((2, 16, 1024), BF16),
    sent=((2, 16, 512), BF16),
    arr=((2, 64, 512), BF16),
    meta=((2, 4, 8, 128), jnp.int32),
    dgf=((2, 256, 512), BF16),
    hot=((2, 256, 64), BF16),
    free=((2, 256, 1), F32),
    grid=((2, 256, 512), F32),
    dn1=((512, 512), BF16),
    dqkv=((512, 384), BF16),
    dprobs=((2, 1024, 256), F32),
    dctx=((512, 128), BF16),
    s3=((2, 256, 512), BF16),
    r3=((2, 3, 64, 512), BF16),
    dmid=((2, 64, 512), F32),
    dn2=((2, 256, 512), BF16),
    dhid=((512, 512), BF16),
    dgh=((512, 512), F32),
    dgu=((512, 512), BF16),
    s4=((2, 256, 512), BF16),
    r4=((2, 3, 64, 512), BF16),
    ds=((8, 256, 128), BF16),
    dr=((8, 256, 128), BF16),
    dgm=((2, 256, 512), BF16),
    dgq=((512, 384), BF16),
    s5=((2, 64, 512), BF16),
    r5=((2, 3, 16, 512), BF16),
    sg=((2, 16, 512), BF16),
    w1s=((256, 1024), BF16),
    w1r=((256, 1024), BF16),
    w1o=((256, 1024), F32),
    z1s=((4, 64, 1024), BF16),
    z1r=((3, 64, 1024), BF16),
    w2s=((256, 512), BF16),
    w2r=((256, 512), BF16),
    w2o=((256, 512), F32),
    z2s=((4, 64, 512), BF16),
    z2r=((3, 64, 512), BF16),
    s6=((2, 64, 1024), BF16),
    r6=((2, 3, 16, 1024), BF16),
    gm=((2, 64, 1024), BF16),
    fs=((8, 2, 64, 128), BF16),
    fr=((8, 2, 64, 128), BF16),
    cz=((4, 2, 64, 256), BF16),
    uz=((4, 2, 64, 1024), BF16),
    qz=((4, 2, 64, 768), BF16),
    ez=((4, 2, 64, 256), BF16),
    sz=((4, 2, 4, 16, 512), BF16),
    xb=((3, 2, 4, 2, 64, 128), BF16),
    xz=((3, 4, 2, 2, 64, 128), BF16),
    ha=((512, 1024), BF16),
    ga=((512, 1024), BF16),
    wes=((128, 3072), BF16),
    wer=((128, 3072), BF16),
    own_qkv=((128, 768), F32),
    ps=((256, 512), BF16),
    pr=((256, 512), BF16),
    pa=((4, 2, 128, 512), BF16),
    vec=((8, 512), F32),
    vr=((8, 8, 512), F32),
    vz=((4, 8, 512), F32),
)


class Refs:
    pass


def kernel(*refs):
    r = Refs()
    names = IN_NAMES + OUT_NAMES + list(BUFFERS) + ["v_" + n for n in (*LOADED, *STORED)]
    for name, ref in zip(names, refs):
        setattr(r, name, ref)
    load_sem, store_sem, send_sem, recv_sem = refs[len(names) :]
    s, d, m = (lax.axis_index(a) for a in ("section", "dp", "mp"))
    used = [0]
    started = []

    def take(count):
        used[0] += count
        return used[0] - count

    def copy(src, dst, device, at, land=None):
        return pltpu.make_async_remote_copy(
            src_ref=src,
            dst_ref=dst,
            send_sem=send_sem.at[at],
            recv_sem=recv_sem.at[at if land is None else land],
            device_id=device,
            device_id_type=MESH,
        )

    def send(src, dst, device):
        made = copy(src, dst, device, take(1))
        made.start()
        started.append(made)
        return made

    def arrive(copies):
        for made in copies:
            made.wait_recv()

    def model(k):
        return lax.rem(m + k, WAYS)

    def data(k):
        return lax.rem(d + k, WAYS)

    def gather(ref, rows):
        own = ref.at[pl.ds(pl.multiple_of(m * rows, rows), rows)]
        return [send(own, own, {"mp": model(k)}) for k in (1, 2, 3)]

    def gather_all(ref, rows):
        own = ref.at[:, pl.ds(pl.multiple_of(m * rows, rows), rows)]
        return [send(own, own, {"mp": model(k)}) for k in (1, 2, 3)]

    def scatter(src, dst, rows):
        copies = []
        for k in (1, 2, 3):
            to = model(k)
            part = src.at[pl.ds(pl.multiple_of(to * rows, rows), rows)]
            copies.append(send(part, dst.at[k - 1], {"mp": to}))
        return copies

    def summed(src, dst, rows):
        total = src[pl.ds(pl.multiple_of(m * rows, rows), rows), :].astype(F32)
        for k in range(3):
            total = total + dst[k].astype(F32)
        return total

    def along(ref):
        return [send(ref.at[d], ref.at[d], {"dp": data(k)}) for k in (1, 2, 3)]

    def cuts(which, values):
        for i, value in enumerate(values):
            for block in range(8):
                at = slice(block * 128, (block + 1) * 128)
                r.xb[which, block // 4, block % 4, i] = value[:, at]
        r.xz[which, d] = r.xb[which, :, d]
        return [
            send(r.xb.at[which, :, data(k)], r.xz.at[which, d], {"dp": data(k)}) for k in (1, 2, 3)
        ]

    plane = [(a, k) for a in (0, 1) for k in range(4) if (a, k) != (0, 0)]

    def to_plane(a, k):
        return {"section": lax.rem(s + a, 2), "mp": model(k)}

    half = d // 2
    place = lax.rem(d, 2)

    def across(i, k):
        return {"section": half, "dp": 2 * s + i, "mp": model(k)}

    def mine(i):
        return (half == s) & (2 * s + i == d)

    def to_dp():
        return sending[0] if sending else d

    sending = []

    class exchange:
        def __init__(self, src_of, dst_of, own):
            self.src_of, self.dst_of, self.own = src_of, dst_of, own
            self.at = take(8)

        def out(self, i, k):
            sending.append(2 * s + i)
            land = self.dst_of(place, m)
            sending.clear()
            at = self.at
            return copy(self.src_of(i), land, across(i, k), at + 4 * i + k, at + 4 * place + k)

        def come(self, i, k):
            at = self.at + 4 * i + k
            return copy(self.src_of(i), self.dst_of(i, model(4 - k)), across(i, k), at)

        def start(self, i):
            for k in (1, 2, 3):
                self.out(i, k).start()
            pl.when(jnp.logical_not(mine(i)))(self.out(i, 0).start)
            pl.when(mine(i))(functools.partial(self.own, i))

        def landed(self, i):
            pl.when(jnp.logical_not(mine(i)))(self.come(i, 0).wait_recv)
            for k in (1, 2, 3):
                self.come(i, k).wait_recv()

        def left(self):
            for i in range(PAIR):
                for k in (1, 2, 3):
                    self.out(i, k).wait_send()
                pl.when(jnp.logical_not(mine(i)))(self.out(i, 0).wait_send)

    def slot_rows(ref):
        return lambda i, at: ref.at[i, pl.ds(pl.multiple_of(at * SHARD, SHARD), SHARD)]

    def put_info(i):
        r.meta[place, m] = r.info[i]

    def put_rows(ref):
        def put(i):
            ref[place, pl.ds(pl.multiple_of(m * SHARD, SHARD), SHARD), :] = r.sent[i]

        return put

    loads = {}

    def load(name, parts):
        src, dst = getattr(r, name), getattr(r, "v_" + name)
        if not parts:
            return [(src, dst)]
        width = dst.shape[1] // parts
        return [(src.at[c], dst.at[:, c * width : (c + 1) * width]) for c in range(parts)]

    at = 0
    for name in LOADED:
        loads[name] = []
        for src, dst in load(name, 3 if name in ("w_qkv", "d_qkv") else 0):
            loads[name].append(pltpu.make_async_copy(src, dst, load_sem.at[at]))
            at += 1
        for made in loads[name]:
            made.start()

    def loaded(*which):
        for name in which:
            for made in loads[name]:
                made.wait()

    stores = []

    def store(*which):
        for name in which:
            at = list(STORED).index(name)
            made = pltpu.make_async_copy(getattr(r, "v_" + name), getattr(r, name), store_sem.at[at])
            made.start()
            stores.append(made)

    barrier = pltpu.get_barrier_semaphore()
    for a, k in plane:
        pl.semaphore_signal(barrier, inc=1, device_id=to_plane(a, k), device_id_type=MESH)
    for k in (1, 2, 3):
        pl.semaphore_signal(barrier, inc=1, device_id={"dp": data(k)}, device_id_type=MESH)
    for i in range(PAIR):
        for k in range(4):
            signal = functools.partial(
                pl.semaphore_signal, barrier, inc=1, device_id=across(i, k), device_id_type=MESH
            )
            if k:
                signal()
            else:
                pl.when(jnp.logical_not(mine(i)))(signal)
    pl.semaphore_wait(barrier, 7 + 3 + 8 - (half == s).astype(jnp.int32))

    e_g1, e_g2 = (g[...].astype(F32).reshape(1, WIDTH) for g in (r.g1, r.g2))
    d_g1, d_g2, token = (g[...].astype(F32).reshape(1, DEC_WIDTH) for g in (r.g3, r.g4, r.g5))

    own16 = pl.ds(pl.multiple_of(m * SHARD, SHARD), SHARD)
    own64 = pl.ds(pl.multiple_of(m * ROWS, ROWS), ROWS)
    e_scale = 1.0 / math.sqrt(HEAD)
    d_scale = 1.0 / math.sqrt(DEC_HEAD)
    other = lax.rem(s + 1, 2)
    rank = s * 4 + m
    pair = range(PAIR)

    def own_images(ref):
        values = ref[...].astype(F32)
        return [jnp.where(s == 0, values[:, i], values[:, PAIR + i]) for i in pair]

    got = []
    for i, rows in enumerate(own_images(r.xs)):
        r.xf[i, own16, :] = rows.astype(BF16)
        got.append(gather(r.xf.at[i], SHARD))
    slot = m * SHARD + lax.broadcasted_iota(jnp.int32, (1, SHARD), 1)
    r.info[...] = jnp.zeros((2, 8, 128), jnp.int32)
    for i in pair:
        patch = r.index[pl.ds(PAIR * s + i, 1), :]
        live = slot < r.counts[PAIR * s + i]
        r.info[i, 0:1, 0:SHARD] = jnp.where(live, padded_row(patch), -1)
        r.info[i, 1:2, :] = jnp.zeros((1, 128), jnp.int32) + r.levels[PAIR * s + i]
    info = exchange(lambda i: r.info.at[i], lambda i, at: r.meta.at[i, at], put_info)
    for i in pair:
        info.start(i)
    for i, rows in enumerate(own_images(r.dgrad)):
        rows = jnp.concatenate([rows, jnp.zeros((ROWS - PATCHES, DEC_WIDTH), F32)], axis=0)
        r.dgf[i, own64, :] = rows.astype(BF16)
    loaded("w_qkv")
    loaded("w_out")
    sent_on = []
    contexts, normeds = [], []
    for i in pair:
        arrive(got[i])
        normal, _ = norm_rows(r.xf[i].astype(F32))
        normed = (normal * e_g1).astype(BF16)
        part = dot(normed, r.v_w_qkv[...], 1, 0).astype(BF16)
        r.qkv[i] = part
        keep = lax.broadcasted_iota(jnp.int32, (1, SLOTS), 1) < r.counts[PAIR * s + i]
        probs, context = attention(part, keep, 64, 256, HEAD, e_scale)
        r.probs[i] = probs
        r.s1[i] = dot(context, r.v_w_out[...], 1, 1).astype(BF16)
        sent_on.append(scatter(r.s1.at[i], r.r1.at[i], SHARD))
        r.cz[d, i] = context
        normeds.append(normed)
    got_c = along(r.cz)
    got_x1 = cuts(0, normeds)
    got_dg = gather_all(r.dgf, ROWS)

    row = lax.broadcasted_iota(jnp.int32, (256, 1), 0)
    is_real = lax.rem(row, ROWS) < PATCHES
    real = is_real.astype(F32)
    entry = jnp.where(is_real, (row - (ROWS - PATCHES) * (row // ROWS)) * 8, -8)

    def start_grid(i):
        info.landed(i)
        index = jnp.concatenate([r.meta[i, k, 0:1, 0:SHARD] for k in range(4)], axis=1)
        hot = (lax.broadcasted_iota(jnp.int32, (256, 64), 0) == index).astype(F32)
        free = real - jnp.sum(hot, axis=1, keepdims=True)
        r.hot[i] = hot.astype(BF16)
        r.free[i] = free
        level = r.meta[i, 0, 1:2, 0:1]
        chosen = lax.broadcasted_iota(jnp.int32, (256, 196 * 8), 1) == entry + level
        r.grid[i] = free * token + dot(chosen.astype(F32).astype(BF16), r.flat[...], 1, 0)

    loaded("table")
    r.flat[...] = r.v_table[...].astype(F32).reshape(196 * 8, DEC_WIDTH).astype(BF16)
    start_grid(0)

    got = []
    for i in pair:
        arrive(sent_on[i])
        middle = r.xf[i, own16, :].astype(F32) + summed(r.s1.at[i], r.r1.at[i], SHARD)
        r.mid[i] = middle
        normal, _ = norm_rows(middle)
        r.n2[i, own16, :] = (normal * e_g2).astype(BF16)
        got.append(gather(r.n2.at[i], SHARD))
    start_grid(1)
    loaded("w_up")
    loaded("w_down")
    loaded("w_proj")
    sent_on = []
    for i in pair:
        arrive(got[i])
        upper = dot(r.n2[i], r.v_w_up[...], 1, 0)
        r.uz[d, i] = upper.astype(BF16)
        hidden, slope = gelu_both(upper)
        r.gp[i] = slope
        r.s2[i] = dot(hidden.astype(BF16), r.v_w_down[...], 1, 1).astype(BF16)
        sent_on.append(scatter(r.s2.at[i], r.r2.at[i], SHARD))
    arrive(got_dg)
    loaded("d_down")
    r.dgh[...] = dot(r.dgf[...].reshape(512, 512), r.v_d_down[...], 1, 0)
    sent = exchange(lambda i: r.sent.at[i], slot_rows(r.arr), put_rows(r.arr))
    for i in pair:
        arrive(sent_on[i])
        out_low = (r.mid[i] + summed(r.s2.at[i], r.r2.at[i], SHARD)).astype(BF16)
        r.eo[i] = out_low
        r.sent[i] = dot(out_low, r.v_w_proj[...], 1, 0).astype(BF16)
        sent.start(i)
    r.ez[d, :, own16] = r.eo[:, :, pl.ds(pl.multiple_of(m * 256, 256), 256)]
    got_eo = []
    for k in (1, 2, 3):
        columns = pl.ds(pl.multiple_of(model(k) * 256, 256), 256)
        got_eo.append(send(r.eo.at[:, :, columns], r.ez.at[d, :, own16], {"mp": model(k)}))

    loaded("d_qkv")
    loaded("d_out")
    loaded("d_up")
    cols = lax.broadcasted_iota(jnp.int32, (1, 256), 1)
    d_keep = lax.rem(cols, ROWS) < PATCHES
    sent_on = []
    for i in pair:
        sent.landed(i)
        values = r.grid[i] + dot(r.hot[i], r.arr[i], 1, 0)
        r.grid[i] = values
        normal, _ = norm_rows(values)
        normed = (normal * d_g1).astype(BF16)
        at = slice(i * 256, (i + 1) * 256)
        r.dn1[at, :] = normed
        part = dot(normed, r.v_d_qkv[...], 1, 0).astype(BF16)
        r.dqkv[at, :] = part
        probs, context = attention(part, d_keep, 256, 128, DEC_HEAD, d_scale)
        r.dprobs[i] = probs
        r.dctx[at, :] = context
        r.s3[i] = dot(context, r.v_d_out[...], 1, 1).astype(BF16)
        sent_on.append(scatter(r.s3.at[i], r.r3.at[i], ROWS))
    got_u = along(r.uz)
    got_x2 = cuts(1, [r.n2[0], r.n2[1]])
    arrive(got_eo)
    got_ez = along(r.ez)
    got = []
    for i in pair:
        arrive(sent_on[i])
        middle = r.grid[i, own64, :] + summed(r.s3.at[i], r.r3.at[i], ROWS)
        r.dmid[i] = middle
        normal, _ = norm_rows(middle)
        r.dn2[i, own64, :] = (normal * d_g2).astype(BF16)
        got.append(gather(r.dn2.at[i], ROWS))
    sent_on = []
    for i in pair:
        arrive(got[i])
        at = slice(i * 256, (i + 1) * 256)
        hidden, slope = gelu_both(dot(r.dn2[i], r.v_d_up[...], 1, 0))
        grad_upper = (r.dgh[at, :] * slope).astype(BF16)
        r.dhid[at, :] = hidden.astype(BF16)
        r.dgu[at, :] = grad_upper
        r.s4[i] = dot(grad_upper, r.v_d_up[...], 1, 1).astype(BF16)
        sent_on.append(scatter(r.s4.at[i], r.r4.at[i], ROWS))

    def dec_weights(left, right, own, away, first):
        size = right.shape[1]
        for a in (0, 1):
            rows = pl.ds(pl.multiple_of(lax.rem(s + a, 2) * 256, 256), 256)
            value = dot(left[:, rows], right[...], 0, 0)
            if a == 0:
                own[:, first : first + size] = value
            else:
                away[:, first : first + size] = value.astype(BF16)

    def dec_sums(own, arrived, away, landing):
        for block in range(4):
            at = slice(block * 64, (block + 1) * 64)
            own[at, :] = own[at, :] + arrived[at, :].astype(F32)
            away[block] = own[at, :].astype(BF16)
        return [send(away.at[data(k)], landing.at[k - 1], {"dp": data(k)}) for k in (1, 2, 3)]

    dec_weights(r.dn2.reshape(512, 512), r.dgu, r.w1o, r.w1s, 0)
    dec_weights(r.dgf.reshape(512, 512), r.dhid, r.w1o, r.w1s, 512)
    got_w1 = [send(r.w1s, r.w1r, to_plane(1, 0))]
    r.vec[...] = jnp.zeros((8, 512), F32)
    got = []
    gain_sum = jnp.zeros((1, 512), F32)
    for i in pair:
        arrive(sent_on[i])
        total = summed(r.s4.at[i], r.r4.at[i], ROWS)
        normal, inverse = norm_rows(r.dmid[i])
        grad = r.dgf[i, own64, :].astype(F32) + rows_back(normal, inverse, d_g2, total)
        gain_sum += jnp.sum(total * normal, axis=0, keepdims=True)
        r.dgm[i, own64, :] = grad.astype(BF16)
        got.append(gather(r.dgm.at[i], ROWS))
    r.vec[5:6, :] = gain_sum
    shard = lax.broadcasted_iota(jnp.int32, (256, 1), 0) // ROWS
    here = (shard == m).astype(F32)
    parts = []
    for i in pair:
        whole = jnp.concatenate([r.dmid[i]] * 4, axis=0)
        value = dot(r.dhid[i * 256 : (i + 1) * 256, :], r.v_d_down[...], 1, 1)
        parts.append(value + whole * here)
    for block in range(8):
        at = slice(block * 64, (block + 1) * 64)
        r.ds[block] = jnp.concatenate([parts[0][:, at], parts[1][:, at]], axis=1).astype(BF16)
    got_dec = []
    for a, k in plane:
        to = lax.rem(s + a, 2) * 4 + model(k)
        got_dec.append(send(r.ds.at[to], r.dr.at[rank], to_plane(a, k)))
    r.dr[rank] = r.ds[rank]
    arrive(got_w1)
    got_z1 = dec_sums(r.w1o, r.w1r, r.z1s, r.z1r)

    gain_sum = jnp.zeros((1, 512), F32)
    token_sum = jnp.zeros((1, 512), F32)
    sent_on = []
    for i in pair:
        arrive(got[i])
        at = slice(i * 256, (i + 1) * 256)
        grad_low = r.dgm[i]
        grad_context = dot(grad_low, r.v_d_out[...], 1, 0).astype(BF16)
        part = attention_back(
            r.dqkv[at, :], r.dprobs[i], grad_context, 256, 128, DEC_HEAD, d_scale
        )
        r.dgq[at, :] = part
        terms = dot(part, r.v_d_qkv[...], 1, 1)
        normal, inverse = norm_rows(r.grid[i])
        gain_sum += jnp.sum(terms * normal, axis=0, keepdims=True)
        back = rows_back(normal, inverse, d_g1, terms) + 0.25 * grad_low.astype(F32)
        token_sum += jnp.sum(back * r.free[i], axis=0, keepdims=True)
        r.s5[i] = dot(r.hot[i], back.astype(BF16), 0, 0).astype(BF16)
        sent_on.append(scatter(r.s5.at[i], r.r5.at[i], SHARD))
    r.vec[4:5, :] = gain_sum
    r.vec[6:7, :] = token_sum

    def put_back(i):
        r.sz[d, place, m] = r.sg[i]

    back = exchange(
        lambda i: r.sg.at[i], lambda i, at: r.sz.at[to_dp(), i, at], put_back
    )
    for i in pair:
        arrive(sent_on[i])
        r.sg[i] = summed(r.s5.at[i], r.r5.at[i], SHARD).astype(BF16)
        back.start(i)
    dec_weights(r.dn1, r.dgq, r.w2o, r.w2s, 0)
    dec_weights(r.dgm.reshape(512, 512), r.dctx, r.w2o, r.w2s, 384)
    got_w2 = [send(r.w2s, r.w2r, to_plane(1, 0))]

    sent_on = []
    for i in pair:
        back.landed(i)
        grad_low = dot(r.sz[d, i].reshape(64, 512), r.v_w_proj[...], 1, 1).astype(BF16)
        grad_upper = (dot(grad_low, r.v_w_down[...], 1, 0) * r.gp[i]).astype(BF16)
        r.s6[i] = dot(grad_upper, r.v_w_up[...], 1, 1).astype(BF16)
        sent_on.append(scatter(r.s6.at[i], r.r6.at[i], SHARD))
    got_sz = [
        send(r.sz.at[d, :, m], r.sz.at[d, :, m], {"dp": data(k)}) for k in (1, 2, 3)
    ]
    arrive(got_w2)
    got_z2 = dec_sums(r.w2o, r.w2r, r.z2s, r.z2r)
    got = []
    gain_two = jnp.zeros((1, WIDTH), F32)
    for i in pair:
        arrive(sent_on[i])
        total = summed(r.s6.at[i], r.r6.at[i], SHARD)
        normal, inverse = norm_rows(r.mid[i])
        own_grad = dot(r.sz[d, i, m], r.v_w_proj[...], 1, 1)
        grad = own_grad + rows_back(normal, inverse, e_g2, total)
        gain_two += jnp.sum(total * normal, axis=0, keepdims=True)
        r.gm[i, own16, :] = grad.astype(BF16)
        got.append(gather(r.gm.at[i], SHARD))
    r.vec[2:3, :] = gain_two[:, :512]
    r.vec[3:4, :] = gain_two[:, 512:]
    arrive(got_sz)
    got_sm = []
    for k in (1, 2, 3):
        for j in (1, 2, 3):
            part = r.sz.at[data(k), :, m]
            got_sm.append(send(part, r.sz.at[data(k), :, m], {"mp": model(j)}))
    gain_one = jnp.zeros((1, WIDTH), F32)
    got_f, got_q = [], []
    for i in pair:
        arrive(got[i])
        grad_low = r.gm[i]
        grad_context = dot(grad_low, r.v_w_out[...], 1, 0).astype(BF16)
        part = attention_back(r.qkv[i], r.probs[i], grad_context, 64, 256, HEAD, e_scale)
        r.qz[d, i] = part
        got_q += [send(r.qz.at[d, i], r.qz.at[d, i], {"dp": data(k)}) for k in (1, 2, 3)]
        terms = dot(part, r.v_w_qkv[...], 1, 1)
        normal, inverse = norm_rows(r.xf[i].astype(F32))
        gain_one += jnp.sum(terms * normal, axis=0, keepdims=True)
        grad = rows_back(normal, inverse, e_g1, terms) + 0.25 * grad_low.astype(F32)
        for block in range(8):
            r.fs[block, i] = grad[:, block * 128 : (block + 1) * 128].astype(BF16)
        for a, k in plane:
            to = lax.rem(s + a, 2) * 4 + model(k)
            got_f.append(send(r.fs.at[to, i], r.fr.at[rank, i], to_plane(a, k)))
        r.fr[rank, i] = r.fs[rank, i]
    got_x4 = cuts(2, [r.gm[0], r.gm[1]])
    r.vec[0:1, :] = gain_one[:, :512]
    r.vec[1:2, :] = gain_one[:, 512:]
    r.vr[rank] = r.vec[...]
    got_v = [send(r.vec, r.vr.at[rank], to_plane(a, k)) for a, k in plane]

    def enc_weights(lefts, value, first, out):
        size = value.shape[1]
        r.wes[:, first : first + size] = dot(lefts[1], value, 0, 0).astype(BF16)
        made = send(
            r.wes.at[:, first : first + size], r.wer.at[:, first : first + size], to_plane(1, 0)
        )
        out[...] = dot(lefts[0], value, 0, 0)
        return made

    def cut_rows(which):
        return [r.xz[which, :, lax.rem(s + a, 2)].reshape(512, 128) for a in (0, 1)]

    arrive(got_u)
    hidden, slope = gelu_both(r.uz[...].reshape(512, WIDTH).astype(F32))
    r.ha[...] = hidden.astype(BF16)
    arrive(got_sm)
    grad_all = r.sz[...].reshape(512, 512)
    r.ga[...] = dot(grad_all, r.v_w_proj[...], 1, 1).astype(BF16)
    grad_upper = (dot(r.ga[...], r.v_w_down[...], 1, 0) * slope).astype(BF16)
    lefts = []
    for a in (0, 1):
        block = lax.rem(s + a, 2) * 4 + d
        lefts.append(r.ga[:, pl.ds(pl.multiple_of(block * 128, 128), 128)])
    got_w = [enc_weights(lefts, r.ha[...], 2048, r.v_o_down)]
    arrive(got_x2)
    got_w.append(enc_weights(cut_rows(1), grad_upper, 1024, r.v_o_up))

    arrive(got_ez)
    r.ps[...] = dot(r.ez[...].reshape(512, 256), grad_all, 0, 0).astype(BF16)
    got_p = [send(r.ps, r.pr, to_plane(1, 0))]
    arrive(got_z1)
    mine64 = pl.ds(pl.multiple_of(d * 64, 64), 64)
    total = r.w1o[mine64, :]
    for k in range(3):
        total = total + r.z1r[k].astype(F32)
    r.v_o_dup[...] = total[:, :512]
    r.v_o_ddown[...] = total[:, 512:]
    store("o_dup", "o_ddown")
    arrive(got_z2)
    total = r.w2o[mine64, :]
    for k in range(3):
        total = total + r.z2r[k].astype(F32)
    for c in range(3):
        r.v_o_dqkv[c] = total[:, c * 128 : (c + 1) * 128]
    r.v_o_dout[...] = total[:, 384:]
    store("o_dqkv", "o_dout")
    arrive(got_p)
    half_rows = pl.ds(pl.multiple_of(s * 128, 128), 128)
    r.pa[m, s] = (r.ps[half_rows, :].astype(F32) + r.pr[half_rows, :].astype(F32)).astype(BF16)
    got_pa = [send(r.pa.at[m, s], r.pa.at[m, s], {"mp": model(k)}) for k in (1, 2, 3)]
    arrive(got_v)
    total = r.vr[0]
    for k in range(1, 8):
        total = total + r.vr[k]
    r.vz[d] = total
    got_vz = along(r.vz)
    arrive(got_dec)
    token_at = padded_row(lax.broadcasted_iota(jnp.int32, (1024, 196), 1))
    row_at = lax.rem(lax.broadcasted_iota(jnp.int32, (1024, 1), 0), 256)
    kept = (row_at == token_at).astype(F32).astype(BF16)
    for a in (0, 1):
        total = dot(r.dr[4 * a : 4 * a + 4].reshape(1024, 128), kept, 0, 0)
        for i in pair:
            r.v_o_dec[PAIR * a + i] = total[i * 64 : (i + 1) * 64]
    store("o_dec")
    arrive(got_f)
    for a in (0, 1):
        total = r.fr[4 * a].astype(F32)
        for k in (1, 2, 3):
            total = total + r.fr[4 * a + k].astype(F32)
        for i in pair:
            r.o_pat[:, PAIR * a + i, :] = total[i]
    arrive(got_pa)
    got_ps = [send(r.pa.at[:, s], r.pa.at[:, s], to_plane(1, 0))]
    arrive(got_c)
    arrive(got_x4)
    got_w.append(enc_weights(cut_rows(2), r.cz[...].reshape(512, 256), 768, r.v_o_out))
    arrive(got_x1)
    arrive(got_q)
    got_w.append(enc_weights(cut_rows(0), r.qz[...].reshape(512, 768), 0, r.own_qkv))
    arrive(got_ps)
    for a in range(4):
        for b in range(2):
            at = a * 256 + b * 128
            r.v_o_proj[at : at + 128, :] = r.pa[a, b].astype(F32)
    store("o_proj")
    arrive(got_vz)
    total = r.vz[0] + r.vz[1] + r.vz[2] + r.vz[3]
    r.o_v1[...] = jnp.concatenate([total[0:1], total[1:2]], axis=1).reshape(WIDTH)
    r.o_v2[...] = jnp.concatenate([total[2:3], total[3:4]], axis=1).reshape(WIDTH)
    for at, out in ((4, r.o_v3), (5, r.o_v4), (6, r.o_v5)):
        out[...] = total[at : at + 1].reshape(DEC_WIDTH)
    firsts = [(2048, 1024), (1024, 1024), (768, 256), (0, 768)]
    names = ["o_down", "o_up", "o_out", "o_qkv"]
    for made, (first, size), name in zip(got_w, firsts, names):
        made.wait_recv()
        more = r.wer[:, first : first + size].astype(F32)
        if name == "o_qkv":
            for c in range(3):
                at = slice(c * 256, (c + 1) * 256)
                r.v_o_qkv[c] = r.own_qkv[:, at] + more[:, at]
        else:
            out = getattr(r, "v_" + name)
            out[...] = out[...] + more
        store(name)
    for made in started:
        made.wait_send()
    for leave in (info, sent, back):
        leave.left()
    for made in stores:
        made.wait()
    assert used[0] <= COPIES


def with_kernel(
    patches,
    counts,
    patch_index,
    scale_level,
    enc_gain_one,
    enc_qkv,
    enc_out,
    enc_gain_two,
    enc_up,
    enc_down,
    w_proj,
    mask_token,
    pos_table,
    dec_gain_one,
    dec_qkv,
    dec_out,
    dec_gain_two,
    dec_up,
    dec_down,
    decoded_grad,
):
    inputs = (
        patches,
        counts,
        patch_index.T,
        scale_level,
        enc_gain_one,
        enc_gain_two,
        dec_gain_one,
        dec_gain_two,
        mask_token,
        decoded_grad,
        jnp.swapaxes(enc_qkv, 0, 1),
        enc_out,
        enc_up,
        enc_down,
        w_proj,
        jnp.swapaxes(pos_table, 0, 1),
        jnp.swapaxes(dec_qkv, 0, 1),
        dec_out,
        dec_up,
        dec_down,
    )
    shapes = dict(STORED, o_pat=(SLOTS, 4, 128), o_v1=(WIDTH,), o_v2=(WIDTH,))
    shapes.update(o_v3=(DEC_WIDTH,), o_v4=(DEC_WIDTH,), o_v5=(DEC_WIDTH,))
    shapes = [jax.ShapeDtypeStruct(shapes[name], F32) for name in OUT_NAMES]
    vmem = pl.BlockSpec(memory_space=pltpu.VMEM)
    smem = pl.BlockSpec(memory_space=pltpu.SMEM)
    hbm = pl.BlockSpec(memory_space=pl.ANY)
    outs = pl.pallas_call(
        kernel,
        out_shape=shapes,
        in_specs=[vmem, smem, vmem, smem] + [vmem] * 6 + [hbm] * len(LOADED),
        out_specs=[hbm if name in STORED else vmem for name in OUT_NAMES],
        scratch_shapes=[pltpu.VMEM(shape, kind) for shape, kind in BUFFERS.values()]
        + [pltpu.VMEM(shape, BF16) for shape in LOADED.values()]
        + [pltpu.VMEM(shape, F32) for shape in STORED.values()]
        + [
            pltpu.SemaphoreType.DMA((len(LOADED) + 4,)),
            pltpu.SemaphoreType.DMA((len(STORED),)),
            pltpu.SemaphoreType.DMA((COPIES,)),
            pltpu.SemaphoreType.DMA((COPIES,)),
        ],
        compiler_params=pltpu.CompilerParams(
            collective_id=0, has_side_effects=True, vmem_limit_bytes=60 * 2**20
        ),
        name="layer_pair",
    )(*inputs)
    outs = list(
        pl.pallas_call(
            hand_over,
            out_shape=shapes,
            in_specs=[hbm] * len(shapes),
            out_specs=[hbm] * len(shapes),
            scratch_shapes=[pltpu.VMEM(shape.shape, F32) for shape in shapes]
            + [pltpu.SemaphoreType.DMA((len(shapes),))] * 2,
            compiler_params=pltpu.CompilerParams(vmem_limit_bytes=60 * 2**20),
            name="hand_over",
        )(*outs)
    )
    outs[0] = jnp.transpose(outs[0], (2, 0, 1))
    outs[2] = jnp.swapaxes(outs[2], 0, 1)
    outs[6] = jnp.swapaxes(outs[6], 0, 1)
    return tuple(outs)


def hand_over(*refs):
    count = len(OUT_NAMES)
    given, returned, held = (refs[i * count : (i + 1) * count] for i in range(3))
    come, go = refs[3 * count :]
    arriving = [pltpu.make_async_copy(given[i], held[i], come.at[i]) for i in range(count)]
    leaving = [pltpu.make_async_copy(held[i], returned[i], go.at[i]) for i in range(count)]
    for made in arriving:
        made.start()
    for first, second in zip(arriving, leaving):
        first.wait()
        second.start()
    for made in leaving:
        made.wait()


def fits_kernel(mesh, shapes):
    ways = (mesh.shape["section"], mesh.shape["dp"], mesh.shape["mp"])
    wanted = {0: (64, 16, 1024), 5: (1024, 3, 1024), 8: (1024, 4096), 10: (1024, 512)}
    wanted.update({12: (8, 196, 512), 14: (512, 3, 512), 17: (512, 2048), 19: (196, 16, 512)})
    return ways == (2, 4, 4) and all(shapes[i] == shape for i, shape in wanted.items())


def solution(mesh):
    def program(*arrays):
        shapes = [array.shape for array in arrays]
        body = with_kernel if fits_kernel(mesh, shapes) else on_device
        return placed_on(mesh, body)(*arrays)

    return program
```

```python
import functools
import math

import jax
import jax.numpy as jnp
from jax import lax
from jax.experimental import pallas as pl
from jax.experimental.pallas import tpu as pltpu
from jax.sharding import PartitionSpec as P

HEAD = 64
DEC_HEAD = 32


eps = 1e-06


def norm_rows(values):
    average = jnp.mean(values, axis=-1, keepdims=True)
    centered = values - average
    variance = jnp.mean(centered * centered, axis=-1, keepdims=True)
    inverse = lax.rsqrt(variance + eps)
    return (centered * inverse, inverse)


def norm_back(normal, inverse, gain_vec, gradient):
    weighted = gradient * gain_vec
    first_term = jnp.mean(weighted, axis=-1, keepdims=True)
    second_term = jnp.mean(weighted * normal, axis=-1, keepdims=True)
    return (
        inverse * (weighted - first_term - normal * second_term),
        jnp.sum(gradient * normal, axis=(0, 1)),
    )


def spread(values):
    return lax.all_gather(values, "mp", axis=0, tiled=True)


def collect(values):
    return lax.psum_scatter(values, "mp", scatter_dimension=0, tiled=True)


def spare_of(work):
    return lambda: jax.tree.map(jnp.zeros_like, work())


def head_view(qkv_rows, head_size):
    return qkv_rows.reshape(
        qkv_rows.shape[0], qkv_rows.shape[1], 3, qkv_rows.shape[3] // head_size, head_size
    )


def score_rows(queries, key_rows, visible, head_size):
    scores = jnp.einsum(
        "sbhe,tbhe->bhst", queries, key_rows, preferred_element_type=jnp.float32
    ) * (1.0 / math.sqrt(head_size))
    return jnp.where(visible[:, None, None, :], scores, -1e30)


def attend(qkv_rows, visible, head_size):
    heads_view = head_view(qkv_rows, head_size)
    scores = score_rows(heads_view[:, :, 0], heads_view[:, :, 1], visible, head_size)
    highest = jnp.max(scores, axis=-1, keepdims=True)
    weights = jnp.exp(scores - highest)
    denominator = jnp.sum(weights, axis=-1, keepdims=True)
    probability = (weights / denominator).astype(jnp.bfloat16)
    context = jnp.einsum(
        "bhst,tbhe->sbhe", probability, heads_view[:, :, 2], preferred_element_type=jnp.float32
    )
    context = context.reshape(qkv_rows.shape[0], qkv_rows.shape[1], qkv_rows.shape[3]).astype(
        jnp.bfloat16
    )
    return (context, highest + jnp.log(denominator))


def attend_back(qkv_rows, visible, logsum, grad_context, head_size):
    heads_view = head_view(qkv_rows, head_size)
    queries = heads_view[:, :, 0]
    key_rows = heads_view[:, :, 1]
    value_rows = heads_view[:, :, 2]
    probability = jnp.exp(score_rows(queries, key_rows, visible, head_size) - logsum)
    grad_heads = grad_context.reshape(queries.shape)
    grad_values = jnp.einsum(
        "bhst,sbhe->tbhe",
        probability.astype(jnp.bfloat16),
        grad_heads,
        preferred_element_type=jnp.float32,
    )
    grad_probs = jnp.einsum(
        "sbhe,tbhe->bhst", grad_heads, value_rows, preferred_element_type=jnp.float32
    )
    row_inner = jnp.sum(grad_probs * probability, axis=-1, keepdims=True)
    grad_scores = (probability * (grad_probs - row_inner)).astype(jnp.bfloat16)
    score_scale = 1.0 / math.sqrt(head_size)
    grad_queries = (
        jnp.einsum("bhst,tbhe->sbhe", grad_scores, key_rows, preferred_element_type=jnp.float32)
        * score_scale
    )
    grad_keys = (
        jnp.einsum("bhst,sbhe->tbhe", grad_scores, queries, preferred_element_type=jnp.float32)
        * score_scale
    )
    stacked = jnp.stack([grad_queries, grad_keys, grad_values], axis=2)
    return stacked.reshape(qkv_rows.shape).astype(jnp.bfloat16)


def attention_local(normed_one, visible, w_qkv, w_out, head_size):
    qkv_rows = jnp.einsum(
        "sbw,wcf->sbcf", normed_one, w_qkv, preferred_element_type=jnp.float32
    ).astype(jnp.bfloat16)
    context, logsum = attend(qkv_rows, visible, head_size)
    mixed_terms = jnp.einsum("sbf,wf->sbw", context, w_out, preferred_element_type=jnp.float32)
    return (qkv_rows, context, logsum, mixed_terms)


def feed_local(normed_two, w_up, w_down):
    upper_in = jnp.einsum("sbw,wf->sbf", normed_two, w_up, preferred_element_type=jnp.float32)
    hidden = jax.nn.gelu(upper_in, approximate=False).astype(jnp.bfloat16)
    return (upper_in, jnp.einsum("sbf,wf->sbw", hidden, w_down, preferred_element_type=jnp.float32))


def feed_back_local(grad_full, normed_two, upper_in, w_up, w_down):
    value_out, gelu_pull = jax.vjp(
        lambda argument: jax.nn.gelu(argument, approximate=False), upper_in
    )
    hidden = value_out.astype(jnp.bfloat16)
    grad_down_w = jnp.einsum("sbw,sbf->wf", grad_full, hidden, preferred_element_type=jnp.float32)
    grad_hidden = jnp.einsum("sbw,wf->sbf", grad_full, w_down, preferred_element_type=jnp.float32)
    grad_upper = gelu_pull(grad_hidden)[0].astype(jnp.bfloat16)
    grad_up_w = jnp.einsum(
        "sbw,sbf->wf", normed_two, grad_upper, preferred_element_type=jnp.float32
    )
    grad_terms = jnp.einsum("sbf,wf->sbw", grad_upper, w_up, preferred_element_type=jnp.float32)
    return (grad_up_w, grad_down_w, grad_terms)


def attention_back_local(
    grad_full, qkv_rows, context, logsum, visible, normed_one, w_qkv, w_out, head_size
):
    grad_out_w = jnp.einsum("sbw,sbf->wf", grad_full, context, preferred_element_type=jnp.float32)
    grad_context = jnp.einsum(
        "sbw,wf->sbf", grad_full, w_out, preferred_element_type=jnp.float32
    ).astype(jnp.bfloat16)
    grad_qkv = attend_back(qkv_rows, visible, logsum, grad_context, head_size)
    grad_qkv_w = jnp.einsum(
        "sbw,sbcf->wcf", normed_one, grad_qkv, preferred_element_type=jnp.float32
    )
    grad_normed = jnp.einsum("sbcf,wcf->sbw", grad_qkv, w_qkv, preferred_element_type=jnp.float32)
    return (grad_qkv_w, grad_out_w, grad_normed)


def on_device(
    patches,
    counts,
    patch_index,
    scale_level,
    enc_gain_one,
    enc_qkv,
    enc_out,
    enc_gain_two,
    enc_up,
    enc_down,
    w_proj,
    mask_token,
    pos_table,
    dec_gain_one,
    dec_qkv,
    dec_out,
    dec_gain_two,
    dec_up,
    dec_down,
    decoded_grad,
):
    data_ways = lax.axis_size("dp")
    model_ways = lax.axis_size("mp")
    slot_rows = patches.shape[0]
    images = patches.shape[1]
    grid_rows = decoded_grad.shape[0]
    dec_width = decoded_grad.shape[2]
    slot_count = slot_rows * model_ways
    grid_count = grid_rows * model_ways
    per_peer = images // data_ways
    slot_start = lax.axis_index("mp") * slot_rows
    grid_start = lax.axis_index("mp") * grid_rows
    is_encoder = lax.axis_index("section") == 0
    visible = jnp.arange(slot_count, dtype=jnp.int32)[None, :] < counts[:, None]
    all_visible = jnp.ones((images, grid_count), dtype=bool)
    enc_g1 = enc_gain_one.astype(jnp.float32)
    enc_g2 = enc_gain_two.astype(jnp.float32)
    dec_g1 = dec_gain_one.astype(jnp.float32)
    dec_g2 = dec_gain_two.astype(jnp.float32)
    token_vec = mask_token.astype(jnp.float32)

    def on_encoder(work):
        return lax.cond(is_encoder, work, spare_of(work))

    def on_decoder(work):
        return lax.cond(is_encoder, spare_of(work), work)

    full_in = spread(patches)

    def enc_attention():
        normal_one, inverse_one = norm_rows(full_in.astype(jnp.float32))
        normed_one = (normal_one * enc_g1).astype(jnp.bfloat16)
        return attention_local(normed_one, visible, enc_qkv, enc_out, HEAD)

    enc_qkv_rows, enc_context, enc_logsum, enc_mixed_terms = on_encoder(enc_attention)
    enc_middle = patches.astype(jnp.float32) + collect(enc_mixed_terms)
    enc_normal_two, enc_inverse_two = norm_rows(enc_middle)
    enc_normed_two = spread((enc_normal_two * enc_g2).astype(jnp.bfloat16))
    enc_upper, enc_down_terms = on_encoder(lambda: feed_local(enc_normed_two, enc_up, enc_down))
    enc_out_low = (enc_middle + collect(enc_down_terms)).astype(jnp.bfloat16)

    def enc_send():
        sent_rows = jnp.einsum(
            "sbw,wf->sbf", enc_out_low, w_proj, preferred_element_type=jnp.float32
        ).astype(jnp.bfloat16)
        live_slot = (slot_start + jnp.arange(slot_rows, dtype=jnp.int32))[:, None] < counts[None, :]
        sent_index = jnp.where(live_slot, patch_index, grid_count)
        packed = (
            sent_rows.reshape(slot_rows, per_peer, data_ways, dec_width),
            sent_index.reshape(slot_rows, per_peer, data_ways),
            scale_level.reshape(1, per_peer, data_ways),
        )
        packed = tuple(
            (jnp.concatenate([jnp.zeros_like(member), member], axis=2) for member in packed)
        )
        return packed

    packed = on_encoder(enc_send)
    received = (
        lax.all_to_all(packed[0], ("section", "dp"), split_axis=2, concat_axis=1, tiled=True),
        lax.all_to_all(packed[1], ("section", "dp"), split_axis=2, concat_axis=1, tiled=True),
        lax.all_to_all(packed[2], ("section", "dp"), split_axis=2, concat_axis=1, tiled=True),
    )
    arrived = (received[0][:, :images, 0], received[1][:, :images, 0], received[2][0, :images, 0])
    arrived_rows, arrived_index, arrived_level = arrived

    def make_onehot():
        return (
            arrived_index[:, :, None] == jnp.arange(grid_count, dtype=jnp.int32)[None, None, :]
        ).astype(jnp.bfloat16)

    def dec_place():
        onehot_low = make_onehot()
        covered = jnp.transpose(jnp.sum(onehot_low.astype(jnp.float32), axis=0))
        placed = jnp.einsum(
            "sbp,sbf->pbf", onehot_low, arrived_rows, preferred_element_type=jnp.float32
        )
        return (placed - covered[:, :, None] * token_vec, covered)

    placed_terms, covered_terms = on_decoder(dec_place)
    placed_rows, covered_rows = collect((placed_terms, covered_terms))
    table_rows = lax.dynamic_slice_in_dim(pos_table, grid_start, grid_rows, 1)
    level_hot = (
        arrived_level[:, None] == jnp.arange(pos_table.shape[0], dtype=jnp.int32)[None, :]
    ).astype(jnp.bfloat16)
    position = jnp.einsum("bl,lpf->pbf", level_hot, table_rows, preferred_element_type=jnp.float32)
    grid_values = placed_rows + token_vec + position
    dec_normal_one, dec_inverse_one = norm_rows(grid_values)
    dec_normed_one = spread((dec_normal_one * dec_g1).astype(jnp.bfloat16))
    dec_qkv_rows, dec_context, dec_logsum, dec_mixed_terms = on_decoder(
        lambda: attention_local(dec_normed_one, all_visible, dec_qkv, dec_out, DEC_HEAD)
    )
    dec_middle = grid_values + collect(dec_mixed_terms)
    dec_normal_two, dec_inverse_two = norm_rows(dec_middle)
    dec_normed_two = spread((dec_normal_two * dec_g2).astype(jnp.bfloat16))

    def dec_feed():
        upper_in, down_terms = feed_local(dec_normed_two, dec_up, dec_down)
        own_rows = lax.dynamic_slice_in_dim(down_terms, grid_start, grid_rows, 0) + dec_middle
        return (upper_in, lax.dynamic_update_slice_in_dim(down_terms, own_rows, grid_start, 0))

    dec_upper, dec_summand = on_decoder(dec_feed)
    decoded = lax.psum_scatter(
        dec_summand.astype(jnp.bfloat16), ("section", "mp"), scatter_dimension=2, tiled=True
    ).astype(jnp.float32)
    dec_grad_full = spread(decoded_grad)
    dec_up_grad, dec_down_grad, dec_two_terms = on_decoder(
        lambda: feed_back_local(dec_grad_full, dec_normed_two, dec_upper, dec_up, dec_down)
    )
    dec_through, dec_gain_two_grad = norm_back(
        dec_normal_two, dec_inverse_two, dec_g2, collect(dec_two_terms)
    )
    dec_grad_middle = decoded_grad.astype(jnp.float32) + dec_through
    dec_middle_full = spread(dec_grad_middle.astype(jnp.bfloat16))
    dec_qkv_grad, dec_out_grad, dec_one_terms = on_decoder(
        lambda: attention_back_local(
            dec_middle_full,
            dec_qkv_rows,
            dec_context,
            dec_logsum,
            all_visible,
            dec_normed_one,
            dec_qkv,
            dec_out,
            DEC_HEAD,
        )
    )
    dec_inner, dec_gain_one_grad = norm_back(
        dec_normal_one, dec_inverse_one, dec_g1, collect(dec_one_terms)
    )
    grad_grid = dec_grad_middle + dec_inner
    grad_token = jnp.sum(grad_grid * (1.0 - covered_rows)[:, :, None], axis=(0, 1))
    grad_grid_full = spread(grad_grid.astype(jnp.bfloat16))

    def dec_return():
        grad_sent = jnp.einsum(
            "sbp,pbf->sbf", make_onehot(), grad_grid_full, preferred_element_type=jnp.float32
        ).astype(jnp.bfloat16)
        return jnp.concatenate([grad_sent, jnp.zeros_like(grad_sent)], axis=1)[:, :, None, :]

    back_rows = on_decoder(dec_return)
    returned = lax.all_to_all(
        back_rows, ("section", "dp"), split_axis=1, concat_axis=2, tiled=True
    )[:, :, data_ways:]
    grad_arrived = returned.reshape(slot_rows, images, dec_width)

    def enc_project_back():
        grad_proj_w = jnp.einsum(
            "sbw,sbf->wf", enc_out_low, grad_arrived, preferred_element_type=jnp.float32
        )
        grad_block = jnp.einsum(
            "sbf,wf->sbw", grad_arrived, w_proj, preferred_element_type=jnp.float32
        )
        return (grad_proj_w, grad_block)

    proj_grad, enc_grad_block = on_encoder(enc_project_back)
    enc_grad_full = spread(enc_grad_block.astype(jnp.bfloat16))
    enc_up_grad, enc_down_grad, enc_two_terms = on_encoder(
        lambda: feed_back_local(enc_grad_full, enc_normed_two, enc_upper, enc_up, enc_down)
    )
    enc_through, enc_gain_two_grad = norm_back(
        enc_normal_two, enc_inverse_two, enc_g2, collect(enc_two_terms)
    )
    enc_grad_middle = enc_grad_block + enc_through
    enc_middle_full = spread(enc_grad_middle.astype(jnp.bfloat16))

    def enc_attention_back():
        normal_one, inverse_one = norm_rows(full_in.astype(jnp.float32))
        normed_one = (normal_one * enc_g1).astype(jnp.bfloat16)
        grad_qkv_w, grad_out_w, grad_normed = attention_back_local(
            enc_middle_full,
            enc_qkv_rows,
            enc_context,
            enc_logsum,
            visible,
            normed_one,
            enc_qkv,
            enc_out,
            HEAD,
        )
        grad_inner, grad_gain_one = norm_back(normal_one, inverse_one, enc_g1, grad_normed)
        own_rows = lax.dynamic_slice_in_dim(grad_inner, slot_start, slot_rows, 0) + enc_grad_middle
        summand = lax.dynamic_update_slice_in_dim(grad_inner, own_rows, slot_start, 0)
        return (grad_qkv_w, grad_out_w, grad_gain_one, summand)

    enc_qkv_grad, enc_out_grad, enc_gain_one_grad, in_summand = on_encoder(enc_attention_back)
    patches_grad = lax.psum_scatter(
        in_summand.astype(jnp.bfloat16), ("section", "mp"), scatter_dimension=2, tiled=True
    ).astype(jnp.float32)
    enc_gain_two_grad = jnp.where(is_encoder, enc_gain_two_grad, 0.0)
    dec_gain_one_grad = jnp.where(is_encoder, 0.0, dec_gain_one_grad)
    dec_gain_two_grad = jnp.where(is_encoder, 0.0, dec_gain_two_grad)
    grad_token = jnp.where(is_encoder, 0.0, grad_token)
    sharded = (
        lax.psum_scatter(enc_qkv_grad, ("section", "dp"), scatter_dimension=0, tiled=True),
        lax.psum_scatter(enc_out_grad, ("section", "dp"), scatter_dimension=0, tiled=True),
        lax.psum_scatter(enc_up_grad, ("section", "dp"), scatter_dimension=0, tiled=True),
        lax.psum_scatter(enc_down_grad, ("section", "dp"), scatter_dimension=0, tiled=True),
        lax.psum_scatter(dec_qkv_grad, ("section", "dp"), scatter_dimension=0, tiled=True),
        lax.psum_scatter(dec_out_grad, ("section", "dp"), scatter_dimension=0, tiled=True),
        lax.psum_scatter(dec_up_grad, ("section", "dp"), scatter_dimension=0, tiled=True),
        lax.psum_scatter(dec_down_grad, ("section", "dp"), scatter_dimension=0, tiled=True),
    )
    shared = lax.psum(
        (
            proj_grad,
            enc_gain_one_grad,
            enc_gain_two_grad,
            dec_gain_one_grad,
            dec_gain_two_grad,
            grad_token,
        ),
        ("section", "dp", "mp"),
    )
    return (
        decoded,
        patches_grad,
        sharded[0],
        sharded[1],
        sharded[2],
        sharded[3],
        sharded[4],
        sharded[5],
        sharded[6],
        sharded[7],
        shared[0],
        shared[1],
        shared[2],
        shared[3],
        shared[4],
        shared[5],
    )


def placed_on(mesh, body):
    placed = (
        P("mp", "dp", None),
        P("dp"),
        P("mp", "dp"),
        P("dp"),
        P(),
        P(None, None, "mp"),
        P(None, "mp"),
        P(),
        P(None, "mp"),
        P(None, "mp"),
        P(),
        P(),
        P(),
        P(),
        P(None, None, "mp"),
        P(None, "mp"),
        P(),
        P(None, "mp"),
        P(None, "mp"),
        P("mp", "dp", None),
    )
    return jax.shard_map(
        body,
        mesh=mesh,
        in_specs=placed,
        out_specs=(
            P(None, "dp", ("section", "mp")),
            P(None, "dp", ("section", "mp")),
            P(("section", "dp"), None, "mp"),
            P(("section", "dp"), "mp"),
            P(("section", "dp"), "mp"),
            P(("section", "dp"), "mp"),
            P(("section", "dp"), None, "mp"),
            P(("section", "dp"), "mp"),
            P(("section", "dp"), "mp"),
            P(("section", "dp"), "mp"),
            P(),
            P(),
            P(),
            P(),
            P(),
            P(),
        ),
        check_vma=False,
    )


MESH = pl.DeviceIdType.MESH
F32 = jnp.float32
BF16 = jnp.bfloat16
WAYS = 4
PAIR = 2
SLOTS = 64
SHARD = 16
PATCHES = 49
ROWS = 64
WIDTH = 1024
DEC_WIDTH = 512
HEADS_HERE = 4
COPIES = 256


def padded_row(patch):
    shard = sum((patch >= k * PATCHES).astype(jnp.int32) for k in (1, 2, 3))
    return patch + (ROWS - PATCHES) * shard


def dot(left, right, left_dim, right_dim):
    return lax.dot_general(
        left, right, (((left_dim,), (right_dim,)), ((), ())), preferred_element_type=F32
    )


def rows_back(normal, inverse, gain, gradient):
    weighted = gradient * gain
    first = jnp.mean(weighted, axis=-1, keepdims=True)
    second = jnp.mean(weighted * normal, axis=-1, keepdims=True)
    return inverse * (weighted - first - normal * second)


def gelu_both(upper):
    phi = 0.5 * (1.0 + lax.erf(upper * math.sqrt(0.5)))
    density = jnp.exp(-0.5 * upper * upper) * (1.0 / math.sqrt(2.0 * math.pi))
    return upper * phi, phi + upper * density


def head_mask(width, head, kind):
    lane = lax.broadcasted_iota(jnp.int32, (1, width), 1)
    return [
        ((lane >= h * head) & (lane < (h + 1) * head)).astype(F32).astype(kind)
        for h in range(HEADS_HERE)
    ]


def stack_heads(values, masks):
    return jnp.concatenate([values * mask for mask in masks], axis=0)


def fold_heads(stacked, masks, rows):
    total = None
    for h, mask in enumerate(masks):
        part = stacked[h * rows : (h + 1) * rows] * mask
        total = part if total is None else total + part
    return total


def attention(qkv, keep, rows, width, head, scale):
    low = head_mask(width, head, BF16)
    wide = head_mask(width, head, F32)
    queries = stack_heads(qkv[:, :width], low)
    scores = dot(queries, qkv[:, width : 2 * width], 1, 1) * scale
    scores = jnp.where(keep, scores, -1e30)
    weights = jnp.exp(scores - jnp.max(scores, axis=-1, keepdims=True))
    probs = weights / jnp.sum(weights, axis=-1, keepdims=True)
    mixed = dot(probs.astype(BF16), qkv[:, 2 * width :], 1, 0)
    return probs, fold_heads(mixed, wide, rows).astype(BF16)


def attention_back(qkv, probs, grad_context, rows, width, head, scale):
    low = head_mask(width, head, BF16)
    wide = head_mask(width, head, F32)
    queries = stack_heads(qkv[:, :width], low)
    grads = stack_heads(grad_context, low)
    grad_probs = dot(grads, qkv[:, 2 * width :], 1, 1)
    inner = jnp.sum(grad_probs * probs, axis=-1, keepdims=True)
    grad_scores = (probs * (grad_probs - inner)).astype(BF16)
    grad_queries = fold_heads(dot(grad_scores, qkv[:, width : 2 * width], 1, 0), wide, rows) * scale
    grad_keys = dot(grad_scores, queries, 0, 0) * scale
    grad_values = dot(probs.astype(BF16), grads, 0, 0)
    return jnp.concatenate([grad_queries, grad_keys, grad_values], axis=1).astype(BF16)


IN_NAMES = [
    "xs",
    "counts",
    "index",
    "levels",
    "g1",
    "g2",
    "g3",
    "g4",
    "g5",
    "dgrad",
    "w_qkv",
    "w_out",
    "w_up",
    "w_down",
    "w_proj",
    "table",
    "d_qkv",
    "d_out",
    "d_up",
    "d_down",
]
OUT_NAMES = [
    "o_dec",
    "o_pat",
    "o_qkv",
    "o_out",
    "o_up",
    "o_down",
    "o_dqkv",
    "o_dout",
    "o_dup",
    "o_ddown",
    "o_proj",
    "o_v1",
    "o_v2",
    "o_v3",
    "o_v4",
    "o_v5",
]
LOADED = dict(
    w_qkv=(WIDTH, 768),
    w_out=(WIDTH, 256),
    w_up=(WIDTH, 1024),
    w_down=(WIDTH, 1024),
    w_proj=(WIDTH, DEC_WIDTH),
    table=(196, 8, DEC_WIDTH),
    d_qkv=(DEC_WIDTH, 384),
    d_out=(DEC_WIDTH, 128),
    d_up=(DEC_WIDTH, 512),
    d_down=(DEC_WIDTH, 512),
)
STORED = dict(
    o_dec=(4, 64, 196),
    o_qkv=(3, 128, 256),
    o_out=(128, 256),
    o_up=(128, 1024),
    o_down=(128, 1024),
    o_dqkv=(3, 64, 128),
    o_dout=(64, 128),
    o_dup=(64, 512),
    o_ddown=(64, 512),
    o_proj=(1024, 512),
)
BUFFERS = dict(
    info=((2, 8, 128), jnp.int32),
    flat=((1568, 512), BF16),
    xf=((2, 64, 1024), BF16),
    qkv=((2, 64, 768), BF16),
    probs=((2, 256, 64), F32),
    s1=((2, 64, 1024), BF16),
    r1=((2, 3, 16, 1024), BF16),
    mid=((2, 16, 1024), F32),
    n2=((2, 64, 1024), BF16),
    gp=((2, 64, 1024), F32),
    s2=((2, 64, 1024), BF16),
    r2=((2, 3, 16, 1024), BF16),
    eo=((2, 16, 1024), BF16),
    sent=((2, 16, 512), BF16),
    arr=((2, 64, 512), BF16),
    meta=((2, 4, 8, 128), jnp.int32),
    dgf=((2, 256, 512), BF16),
    hot=((2, 256, 64), BF16),
    free=((2, 256, 1), F32),
    grid=((2, 256, 512), F32),
    dn1=((512, 512), BF16),
    dqkv=((512, 384), BF16),
    dprobs=((2, 1024, 256), F32),
    dctx=((512, 128), BF16),
    s3=((2, 256, 512), BF16),
    r3=((2, 3, 64, 512), BF16),
    dmid=((2, 64, 512), F32),
    dn2=((2, 256, 512), BF16),
    dhid=((512, 512), BF16),
    dgh=((512, 512), F32),
    dgu=((512, 512), BF16),
    s4=((2, 256, 512), BF16),
    r4=((2, 3, 64, 512), BF16),
    ds=((8, 256, 128), BF16),
    dr=((8, 256, 128), BF16),
    dgm=((2, 256, 512), BF16),
    dgq=((512, 384), BF16),
    s5=((2, 64, 512), BF16),
    r5=((2, 3, 16, 512), BF16),
    sg=((2, 16, 512), BF16),
    w1s=((256, 1024), BF16),
    w1r=((256, 1024), BF16),
    w1o=((256, 1024), F32),
    z1s=((4, 64, 1024), BF16),
    z1r=((3, 64, 1024), BF16),
    w2s=((256, 512), BF16),
    w2r=((256, 512), BF16),
    w2o=((256, 512), F32),
    z2s=((4, 64, 512), BF16),
    z2r=((3, 64, 512), BF16),
    s6=((2, 64, 1024), BF16),
    r6=((2, 3, 16, 1024), BF16),
    gm=((2, 64, 1024), BF16),
    fs=((8, 2, 64, 128), BF16),
    fr=((8, 2, 64, 128), BF16),
    cz=((4, 2, 64, 256), BF16),
    nz=((4, 2, 4, 16, 1024), BF16),
    qz=((4, 2, 64, 768), BF16),
    ez=((4, 2, 64, 256), BF16),
    sz=((4, 2, 4, 16, 512), BF16),
    xb=((2, 2, 4, 2, 64, 128), BF16),
    xz=((2, 4, 2, 2, 64, 128), BF16),
    ha=((512, 1024), BF16),
    sa=((512, 1024), BF16),
    ga=((512, 1024), BF16),
    wes=((128, 3072), BF16),
    wer=((128, 3072), BF16),
    own_qkv=((128, 768), F32),
    ps=((256, 512), BF16),
    pr=((256, 512), BF16),
    pa=((4, 2, 128, 512), BF16),
    vec=((8, 512), F32),
    vr=((8, 8, 512), F32),
    vz=((4, 8, 512), F32),
)


class Refs:
    pass


def kernel(*refs):
    r = Refs()
    names = IN_NAMES + OUT_NAMES + list(BUFFERS) + ["v_" + n for n in (*LOADED, *STORED)]
    for name, ref in zip(names, refs):
        setattr(r, name, ref)
    load_sem, store_sem, send_sem, recv_sem = refs[len(names) :]
    s, d, m = (lax.axis_index(a) for a in ("section", "dp", "mp"))
    used = [0]
    started = []

    def take(count):
        used[0] += count
        return used[0] - count

    def copy(src, dst, device, at, land=None):
        return pltpu.make_async_remote_copy(
            src_ref=src,
            dst_ref=dst,
            send_sem=send_sem.at[at],
            recv_sem=recv_sem.at[at if land is None else land],
            device_id=device,
            device_id_type=MESH,
        )

    def send(src, dst, device):
        made = copy(src, dst, device, take(1))
        made.start()
        started.append(made)
        return made

    def arrive(copies):
        for made in copies:
            made.wait_recv()

    def model(k):
        return lax.rem(m + k, WAYS)

    def data(k):
        return lax.rem(d + k, WAYS)

    def gather(ref, rows):
        own = ref.at[pl.ds(pl.multiple_of(m * rows, rows), rows)]
        return [send(own, own, {"mp": model(k)}) for k in (1, 2, 3)]

    def scatter(src, dst, rows):
        copies = []
        for k in (1, 2, 3):
            to = model(k)
            part = src.at[pl.ds(pl.multiple_of(to * rows, rows), rows)]
            copies.append(send(part, dst.at[k - 1], {"mp": to}))
        return copies

    def summed(src, dst, rows):
        total = src[pl.ds(pl.multiple_of(m * rows, rows), rows), :].astype(F32)
        for k in range(3):
            total = total + dst[k].astype(F32)
        return total

    def relay(ref, i):
        copies = []
        for k in (1, 2, 3):
            part = ref.at[data(k), i, m]
            copies += [send(part, part, {"mp": model(j)}) for j in (1, 2, 3)]
        return copies

    def along(ref):
        return [send(ref.at[d], ref.at[d], {"dp": data(k)}) for k in (1, 2, 3)]

    def block_columns(which, values):
        for i, value in enumerate(values):
            for block in range(8):
                at = slice(block * 128, (block + 1) * 128)
                r.xb[which, block // 4, block % 4, i] = value[:, at]
        r.xz[which, d] = r.xb[which, :, d]

    def send_columns(which):
        return [
            send(r.xb.at[which, :, data(k)], r.xz.at[which, d], {"dp": data(k)}) for k in (1, 2, 3)
        ]

    plane = [(a, k) for a in (0, 1) for k in range(4) if (a, k) != (0, 0)]

    def to_plane(a, k):
        return {"section": lax.rem(s + a, 2), "mp": model(k)}

    half = d // 2
    place = lax.rem(d, 2)

    def across(i, k):
        return {"section": half, "dp": 2 * s + i, "mp": model(k)}

    def mine(i):
        return (half == s) & (2 * s + i == d)

    def to_dp():
        return sending[0] if sending else d

    sending = []

    class exchange:
        def __init__(self, src_of, dst_of, own):
            self.src_of, self.dst_of, self.own = src_of, dst_of, own
            self.at = take(8)

        def out(self, i, k):
            sending.append(2 * s + i)
            land = self.dst_of(place, m)
            sending.clear()
            at = self.at
            return copy(self.src_of(i), land, across(i, k), at + 4 * i + k, at + 4 * place + k)

        def come(self, i, k):
            at = self.at + 4 * i + k
            return copy(self.src_of(i), self.dst_of(i, model(4 - k)), across(i, k), at)

        def start(self, i):
            for k in (1, 2, 3):
                self.out(i, k).start()
            pl.when(jnp.logical_not(mine(i)))(self.out(i, 0).start)
            pl.when(mine(i))(functools.partial(self.own, i))

        def landed(self, i):
            pl.when(jnp.logical_not(mine(i)))(self.come(i, 0).wait_recv)
            for k in (1, 2, 3):
                self.come(i, k).wait_recv()

        def left(self):
            for i in range(PAIR):
                for k in (1, 2, 3):
                    self.out(i, k).wait_send()
                pl.when(jnp.logical_not(mine(i)))(self.out(i, 0).wait_send)

    def slot_rows(ref):
        return lambda i, at: ref.at[i, pl.ds(pl.multiple_of(at * SHARD, SHARD), SHARD)]

    def put_info(i):
        r.meta[place, m] = r.info[i]

    def put_rows(ref):
        def put(i):
            ref[place, pl.ds(pl.multiple_of(m * SHARD, SHARD), SHARD), :] = r.sent[i]

        return put

    loads = {}

    def load(name, parts):
        src, dst = getattr(r, name), getattr(r, "v_" + name)
        if not parts:
            return [(src, dst)]
        width = dst.shape[1] // parts
        return [(src.at[c], dst.at[:, c * width : (c + 1) * width]) for c in range(parts)]

    at = 0
    for name in LOADED:
        loads[name] = []
        for src, dst in load(name, 3 if name in ("w_qkv", "d_qkv") else 0):
            loads[name].append(pltpu.make_async_copy(src, dst, load_sem.at[at]))
            at += 1
        for made in loads[name]:
            made.start()

    def loaded(*which):
        for name in which:
            for made in loads[name]:
                made.wait()

    stores = []

    def store(*which):
        for name in which:
            at = list(STORED).index(name)
            made = pltpu.make_async_copy(getattr(r, "v_" + name), getattr(r, name), store_sem.at[at])
            made.start()
            stores.append(made)

    barrier = pltpu.get_barrier_semaphore()
    for a, k in plane:
        pl.semaphore_signal(barrier, inc=1, device_id=to_plane(a, k), device_id_type=MESH)
    for k in (1, 2, 3):
        pl.semaphore_signal(barrier, inc=1, device_id={"dp": data(k)}, device_id_type=MESH)
    for i in range(PAIR):
        for k in range(4):
            signal = functools.partial(
                pl.semaphore_signal, barrier, inc=1, device_id=across(i, k), device_id_type=MESH
            )
            if k:
                signal()
            else:
                pl.when(jnp.logical_not(mine(i)))(signal)
    pl.semaphore_wait(barrier, 7 + 3 + 8 - (half == s).astype(jnp.int32))

    e_g1, e_g2 = (g[...].astype(F32).reshape(1, WIDTH) for g in (r.g1, r.g2))
    d_g1, d_g2, token = (g[...].astype(F32).reshape(1, DEC_WIDTH) for g in (r.g3, r.g4, r.g5))

    own16 = pl.ds(pl.multiple_of(m * SHARD, SHARD), SHARD)
    own64 = pl.ds(pl.multiple_of(m * ROWS, ROWS), ROWS)
    e_scale = 1.0 / math.sqrt(HEAD)
    d_scale = 1.0 / math.sqrt(DEC_HEAD)
    other = lax.rem(s + 1, 2)
    rank = s * 4 + m
    pair = range(PAIR)

    def own_images(ref):
        values = ref[...].astype(F32)
        return [jnp.where(s == 0, values[:, i], values[:, PAIR + i]) for i in pair]

    got = []
    for i, rows in enumerate(own_images(r.xs)):
        r.xf[i, own16, :] = rows.astype(BF16)
        got.append(gather(r.xf.at[i], SHARD))
    slot = m * SHARD + lax.broadcasted_iota(jnp.int32, (1, SHARD), 1)
    r.info[...] = jnp.zeros((2, 8, 128), jnp.int32)
    for i in pair:
        patch = r.index[pl.ds(PAIR * s + i, 1), :]
        live = slot < r.counts[PAIR * s + i]
        r.info[i, 0:1, 0:SHARD] = jnp.where(live, padded_row(patch), -1)
        r.info[i, 1:2, :] = jnp.zeros((1, 128), jnp.int32) + r.levels[PAIR * s + i]
    info = exchange(lambda i: r.info.at[i], lambda i, at: r.meta.at[i, at], put_info)
    for i in pair:
        info.start(i)
    for i, rows in enumerate(own_images(r.dgrad)):
        rows = jnp.concatenate([rows, jnp.zeros((ROWS - PATCHES, DEC_WIDTH), F32)], axis=0)
        r.dgf[i, own64, :] = rows.astype(BF16)
    loaded("w_qkv")
    loaded("w_out")
    sent_on = []
    contexts, normeds = [], []
    for i in pair:
        arrive(got[i])
    got_dg = []
    for i in pair:
        got_dg += gather(r.dgf.at[i], ROWS)
        normal, _ = norm_rows(r.xf[i].astype(F32))
        normed = (normal * e_g1).astype(BF16)
        part = dot(normed, r.v_w_qkv[...], 1, 0).astype(BF16)
        r.qkv[i] = part
        keep = lax.broadcasted_iota(jnp.int32, (1, SLOTS), 1) < r.counts[PAIR * s + i]
        probs, context = attention(part, keep, 64, 256, HEAD, e_scale)
        r.probs[i] = probs
        r.s1[i] = dot(context, r.v_w_out[...], 1, 1).astype(BF16)
        sent_on.append(scatter(r.s1.at[i], r.r1.at[i], SHARD))
        r.cz[d, i] = context
        normeds.append(normed)
    block_columns(0, normeds)

    row = lax.broadcasted_iota(jnp.int32, (256, 1), 0)
    is_real = lax.rem(row, ROWS) < PATCHES
    real = is_real.astype(F32)
    entry = jnp.where(is_real, (row - (ROWS - PATCHES) * (row // ROWS)) * 8, -8)

    def start_grid(i):
        info.landed(i)
        index = jnp.concatenate([r.meta[i, k, 0:1, 0:SHARD] for k in range(4)], axis=1)
        hot = (lax.broadcasted_iota(jnp.int32, (256, 64), 0) == index).astype(F32)
        free = real - jnp.sum(hot, axis=1, keepdims=True)
        r.hot[i] = hot.astype(BF16)
        r.free[i] = free
        level = r.meta[i, 0, 1:2, 0:1]
        chosen = lax.broadcasted_iota(jnp.int32, (256, 196 * 8), 1) == entry + level
        r.grid[i] = free * token + dot(chosen.astype(F32).astype(BF16), r.flat[...], 1, 0)

    loaded("table")
    r.flat[...] = r.v_table[...].astype(F32).reshape(196 * 8, DEC_WIDTH).astype(BF16)
    start_grid(0)

    got = []
    for i in pair:
        arrive(sent_on[i])
        middle = r.xf[i, own16, :].astype(F32) + summed(r.s1.at[i], r.r1.at[i], SHARD)
        r.mid[i] = middle
        normal, _ = norm_rows(middle)
        r.n2[i, own16, :] = (normal * e_g2).astype(BF16)
        got.append(gather(r.n2.at[i], SHARD))
    got_nz = [
        send(r.n2.at[:, own16], r.nz.at[d, :, m], {"dp": data(k)}) for k in (1, 2, 3)
    ]
    start_grid(1)
    loaded("w_up")
    loaded("w_down")
    loaded("w_proj")
    sent_on = []
    for i in pair:
        arrive(got[i])
        upper = dot(r.n2[i], r.v_w_up[...], 1, 0)
        hidden, slope = gelu_both(upper)
        r.gp[i] = slope
        r.s2[i] = dot(hidden.astype(BF16), r.v_w_down[...], 1, 1).astype(BF16)
        sent_on.append(scatter(r.s2.at[i], r.r2.at[i], SHARD))
    arrive(got_dg)
    loaded("d_down")
    r.dgh[...] = dot(r.dgf[...].reshape(512, 512), r.v_d_down[...], 1, 0)
    sent = exchange(lambda i: r.sent.at[i], slot_rows(r.arr), put_rows(r.arr))
    for i in pair:
        arrive(sent_on[i])
        out_low = (r.mid[i] + summed(r.s2.at[i], r.r2.at[i], SHARD)).astype(BF16)
        r.eo[i] = out_low
        r.sent[i] = dot(out_low, r.v_w_proj[...], 1, 0).astype(BF16)
        sent.start(i)
    r.ez[d, :, own16] = r.eo[:, :, pl.ds(pl.multiple_of(m * 256, 256), 256)]
    got_eo = []
    for k in (1, 2, 3):
        columns = pl.ds(pl.multiple_of(model(k) * 256, 256), 256)
        got_eo.append(send(r.eo.at[:, :, columns], r.ez.at[d, :, own16], {"mp": model(k)}))

    loaded("d_qkv")
    loaded("d_out")
    loaded("d_up")
    cols = lax.broadcasted_iota(jnp.int32, (1, 256), 1)
    d_keep = lax.rem(cols, ROWS) < PATCHES
    sent_on = []
    for i in pair:
        sent.landed(i)
    arrive(got_nz)
    got_nm = []
    for i in pair:
        got_nm += relay(r.nz, i)
        values = r.grid[i] + dot(r.hot[i], r.arr[i], 1, 0)
        r.grid[i] = values
        normal, _ = norm_rows(values)
        normed = (normal * d_g1).astype(BF16)
        at = slice(i * 256, (i + 1) * 256)
        r.dn1[at, :] = normed
        part = dot(normed, r.v_d_qkv[...], 1, 0).astype(BF16)
        r.dqkv[at, :] = part
        probs, context = attention(part, d_keep, 256, 128, DEC_HEAD, d_scale)
        r.dprobs[i] = probs
        r.dctx[at, :] = context
        r.s3[i] = dot(context, r.v_d_out[...], 1, 1).astype(BF16)
        sent_on.append(scatter(r.s3.at[i], r.r3.at[i], ROWS))
    r.nz[d] = r.n2[...].reshape(2, 4, 16, WIDTH)
    arrive(got_eo)
    got_ez = along(r.ez)
    got_c = along(r.cz)
    got_x1 = send_columns(0)
    got = []
    for i in pair:
        arrive(sent_on[i])
        middle = r.grid[i, own64, :] + summed(r.s3.at[i], r.r3.at[i], ROWS)
        r.dmid[i] = middle
        normal, _ = norm_rows(middle)
        r.dn2[i, own64, :] = (normal * d_g2).astype(BF16)
        got.append(gather(r.dn2.at[i], ROWS))

    def upper_of(j):
        at = slice(j * 128, (j + 1) * 128)
        hidden, slope = gelu_both(dot(r.nz[j].reshape(128, WIDTH), r.v_w_up[...], 1, 0))
        r.ha[at, :] = hidden.astype(BF16)
        r.sa[at, :] = slope.astype(BF16)

    arrive(got_nm)
    upper_of(0)
    sent_on = []
    for i in pair:
        arrive(got[i])
        at = slice(i * 256, (i + 1) * 256)
        hidden, slope = gelu_both(dot(r.dn2[i], r.v_d_up[...], 1, 0))
        grad_upper = (r.dgh[at, :] * slope).astype(BF16)
        r.dhid[at, :] = hidden.astype(BF16)
        r.dgu[at, :] = grad_upper
        r.s4[i] = dot(grad_upper, r.v_d_up[...], 1, 1).astype(BF16)
        sent_on.append(scatter(r.s4.at[i], r.r4.at[i], ROWS))

    def dec_weights(left, right, own, away, first):
        size = right.shape[1]
        for a in (0, 1):
            rows = pl.ds(pl.multiple_of(lax.rem(s + a, 2) * 256, 256), 256)
            value = dot(left[:, rows], right[...], 0, 0)
            if a == 0:
                own[:, first : first + size] = value
            else:
                away[:, first : first + size] = value.astype(BF16)

    def dec_sums(own, arrived, away, landing):
        for block in range(4):
            at = slice(block * 64, (block + 1) * 64)
            own[at, :] = own[at, :] + arrived[at, :].astype(F32)
            away[block] = own[at, :].astype(BF16)
        return [send(away.at[data(k)], landing.at[k - 1], {"dp": data(k)}) for k in (1, 2, 3)]

    dec_weights(r.dn2.reshape(512, 512), r.dgu, r.w1o, r.w1s, 0)
    dec_weights(r.dgf.reshape(512, 512), r.dhid, r.w1o, r.w1s, 512)
    got_w1 = [send(r.w1s, r.w1r, to_plane(1, 0))]
    upper_of(1)
    r.vec[...] = jnp.zeros((8, 512), F32)
    got = []
    gain_sum = jnp.zeros((1, 512), F32)
    for i in pair:
        arrive(sent_on[i])
        total = summed(r.s4.at[i], r.r4.at[i], ROWS)
        normal, inverse = norm_rows(r.dmid[i])
        grad = r.dgf[i, own64, :].astype(F32) + rows_back(normal, inverse, d_g2, total)
        gain_sum += jnp.sum(total * normal, axis=0, keepdims=True)
        r.dgm[i, own64, :] = grad.astype(BF16)
        got.append(gather(r.dgm.at[i], ROWS))
    r.vec[5:6, :] = gain_sum
    shard = lax.broadcasted_iota(jnp.int32, (256, 1), 0) // ROWS
    here = (shard == m).astype(F32)
    parts = []
    for i in pair:
        whole = jnp.concatenate([r.dmid[i]] * 4, axis=0)
        value = dot(r.dhid[i * 256 : (i + 1) * 256, :], r.v_d_down[...], 1, 1)
        parts.append(value + whole * here)
    for block in range(8):
        at = slice(block * 64, (block + 1) * 64)
        r.ds[block] = jnp.concatenate([parts[0][:, at], parts[1][:, at]], axis=1).astype(BF16)
    upper_of(2)
    arrive(got_w1)
    got_z1 = dec_sums(r.w1o, r.w1r, r.z1s, r.z1r)

    gain_sum = jnp.zeros((1, 512), F32)
    token_sum = jnp.zeros((1, 512), F32)
    sent_on = []
    got_dec = []
    for i in pair:
        arrive(got[i])
        if i == 1:
            for a, k in plane:
                to = lax.rem(s + a, 2) * 4 + model(k)
                got_dec.append(send(r.ds.at[to], r.dr.at[rank], to_plane(a, k)))
            r.dr[rank] = r.ds[rank]
        at = slice(i * 256, (i + 1) * 256)
        grad_low = r.dgm[i]
        grad_context = dot(grad_low, r.v_d_out[...], 1, 0).astype(BF16)
        part = attention_back(
            r.dqkv[at, :], r.dprobs[i], grad_context, 256, 128, DEC_HEAD, d_scale
        )
        r.dgq[at, :] = part
        terms = dot(part, r.v_d_qkv[...], 1, 1)
        normal, inverse = norm_rows(r.grid[i])
        gain_sum += jnp.sum(terms * normal, axis=0, keepdims=True)
        back = rows_back(normal, inverse, d_g1, terms) + 0.25 * grad_low.astype(F32)
        token_sum += jnp.sum(back * r.free[i], axis=0, keepdims=True)
        r.s5[i] = dot(r.hot[i], back.astype(BF16), 0, 0).astype(BF16)
        sent_on.append(scatter(r.s5.at[i], r.r5.at[i], SHARD))
    r.vec[4:5, :] = gain_sum
    r.vec[6:7, :] = token_sum

    def put_back(i):
        r.sz[d, place, m] = r.sg[i]

    back = exchange(
        lambda i: r.sg.at[i], lambda i, at: r.sz.at[to_dp(), i, at], put_back
    )
    for i in pair:
        arrive(sent_on[i])
        r.sg[i] = summed(r.s5.at[i], r.r5.at[i], SHARD).astype(BF16)
        back.start(i)
    dec_weights(r.dn1, r.dgq, r.w2o, r.w2s, 0)
    dec_weights(r.dgm.reshape(512, 512), r.dctx, r.w2o, r.w2s, 384)
    got_w2 = [send(r.w2s, r.w2r, to_plane(1, 0))]
    upper_of(3)

    sent_on = []
    for i in pair:
        back.landed(i)
        grad_low = dot(r.sz[d, i].reshape(64, 512), r.v_w_proj[...], 1, 1).astype(BF16)
        grad_upper = (dot(grad_low, r.v_w_down[...], 1, 0) * r.gp[i]).astype(BF16)
        r.s6[i] = dot(grad_upper, r.v_w_up[...], 1, 1).astype(BF16)
        sent_on.append(scatter(r.s6.at[i], r.r6.at[i], SHARD))
    got_sz = [
        send(r.sz.at[d, :, m], r.sz.at[d, :, m], {"dp": data(k)}) for k in (1, 2, 3)
    ]
    arrive(got_w2)
    got_z2 = dec_sums(r.w2o, r.w2r, r.z2s, r.z2r)
    got = []
    gain_two = jnp.zeros((1, WIDTH), F32)
    for i in pair:
        arrive(sent_on[i])
        total = summed(r.s6.at[i], r.r6.at[i], SHARD)
        normal, inverse = norm_rows(r.mid[i])
        own_grad = dot(r.sz[d, i, m], r.v_w_proj[...], 1, 1)
        grad = own_grad + rows_back(normal, inverse, e_g2, total)
        gain_two += jnp.sum(total * normal, axis=0, keepdims=True)
        r.gm[i, own16, :] = grad.astype(BF16)
        got.append(gather(r.gm.at[i], SHARD))
    r.vec[2:3, :] = gain_two[:, :512]
    r.vec[3:4, :] = gain_two[:, 512:]
    arrive(got_sz)
    got_sm = relay(r.sz, 0) + relay(r.sz, 1)
    gain_one = jnp.zeros((1, WIDTH), F32)
    got_f, got_q = [], []
    for i in pair:
        arrive(got[i])
        if i == 1:
            block_columns(1, [r.gm[0], r.gm[1]])
            got_x4 = send_columns(1)
        grad_low = r.gm[i]
        grad_context = dot(grad_low, r.v_w_out[...], 1, 0).astype(BF16)
        part = attention_back(r.qkv[i], r.probs[i], grad_context, 64, 256, HEAD, e_scale)
        r.qz[d, i] = part
        got_q += [send(r.qz.at[d, i], r.qz.at[d, i], {"dp": data(k)}) for k in (1, 2, 3)]
        terms = dot(part, r.v_w_qkv[...], 1, 1)
        normal, inverse = norm_rows(r.xf[i].astype(F32))
        gain_one += jnp.sum(terms * normal, axis=0, keepdims=True)
        grad = rows_back(normal, inverse, e_g1, terms) + 0.25 * grad_low.astype(F32)
        for block in range(8):
            r.fs[block, i] = grad[:, block * 128 : (block + 1) * 128].astype(BF16)
        for a, k in plane:
            to = lax.rem(s + a, 2) * 4 + model(k)
            got_f.append(send(r.fs.at[to, i], r.fr.at[rank, i], to_plane(a, k)))
        r.fr[rank, i] = r.fs[rank, i]
    r.vec[0:1, :] = gain_one[:, :512]
    r.vec[1:2, :] = gain_one[:, 512:]
    r.vr[rank] = r.vec[...]
    got_v = [send(r.vec, r.vr.at[rank], to_plane(a, k)) for a, k in plane]

    def enc_weights(lefts, value, first, out):
        size = value.shape[1]
        r.wes[:, first : first + size] = dot(lefts[1], value, 0, 0).astype(BF16)
        made = send(
            r.wes.at[:, first : first + size], r.wer.at[:, first : first + size], to_plane(1, 0)
        )
        out[...] = dot(lefts[0], value, 0, 0)
        return made

    def cut_rows(which):
        return [r.xz[which, :, lax.rem(s + a, 2)].reshape(512, 128) for a in (0, 1)]

    arrive(got_sm)
    grad_all = r.sz[...].reshape(512, 512)
    arrive(got_ez)
    r.ps[...] = dot(r.ez[...].reshape(512, 256), grad_all, 0, 0).astype(BF16)
    got_p = [send(r.ps, r.pr, to_plane(1, 0))]

    r.ga[...] = dot(grad_all, r.v_w_proj[...], 1, 1).astype(BF16)
    grad_upper = (dot(r.ga[...], r.v_w_down[...], 1, 0) * r.sa[...].astype(F32)).astype(BF16)
    columns = []
    for a in (0, 1):
        block = lax.rem(s + a, 2) * 4 + d
        columns.append(pl.ds(pl.multiple_of(block * 128, 128), 128))
    lefts = [r.ga[:, at] for at in columns]
    arrive(got_p)
    half_rows = pl.ds(pl.multiple_of(s * 128, 128), 128)
    r.pa[m, s] = (r.ps[half_rows, :].astype(F32) + r.pr[half_rows, :].astype(F32)).astype(BF16)
    got_pa = [send(r.pa.at[m, s], r.pa.at[m, s], {"mp": model(k)}) for k in (1, 2, 3)]
    got_w = [enc_weights(lefts, r.ha[...], 2048, r.v_o_down)]
    lefts = [r.nz[:, :, :, :, at].reshape(512, 128) for at in columns]
    got_w.append(enc_weights(lefts, grad_upper, 1024, r.v_o_up))

    arrive(got_z1)
    mine64 = pl.ds(pl.multiple_of(d * 64, 64), 64)
    total = r.w1o[mine64, :]
    for k in range(3):
        total = total + r.z1r[k].astype(F32)
    r.v_o_dup[...] = total[:, :512]
    r.v_o_ddown[...] = total[:, 512:]
    store("o_dup", "o_ddown")
    arrive(got_z2)
    total = r.w2o[mine64, :]
    for k in range(3):
        total = total + r.z2r[k].astype(F32)
    for c in range(3):
        r.v_o_dqkv[c] = total[:, c * 128 : (c + 1) * 128]
    r.v_o_dout[...] = total[:, 384:]
    store("o_dqkv", "o_dout")
    arrive(got_v)
    total = r.vr[0]
    for k in range(1, 8):
        total = total + r.vr[k]
    r.vz[d] = total
    got_vz = along(r.vz)
    arrive(got_pa)
    got_ps = [send(r.pa.at[:, s], r.pa.at[:, s], to_plane(1, 0))]
    arrive(got_dec)
    token_at = padded_row(lax.broadcasted_iota(jnp.int32, (1024, 196), 1))
    row_at = lax.rem(lax.broadcasted_iota(jnp.int32, (1024, 1), 0), 256)
    kept = (row_at == token_at).astype(F32).astype(BF16)
    for a in (0, 1):
        total = dot(r.dr[4 * a : 4 * a + 4].reshape(1024, 128), kept, 0, 0)
        for i in pair:
            r.v_o_dec[PAIR * a + i] = total[i * 64 : (i + 1) * 64]
    store("o_dec")
    arrive(got_f)
    for a in (0, 1):
        total = r.fr[4 * a].astype(F32)
        for k in (1, 2, 3):
            total = total + r.fr[4 * a + k].astype(F32)
        for i in pair:
            r.o_pat[:, PAIR * a + i, :] = total[i]
    arrive(got_ps)
    for a in range(4):
        for b in range(2):
            at = a * 256 + b * 128
            r.v_o_proj[at : at + 128, :] = r.pa[a, b].astype(F32)
    store("o_proj")
    arrive(got_c)
    arrive(got_x4)
    got_w.append(enc_weights(cut_rows(1), r.cz[...].reshape(512, 256), 768, r.v_o_out))
    arrive(got_x1)
    arrive(got_q)
    got_w.append(enc_weights(cut_rows(0), r.qz[...].reshape(512, 768), 0, r.own_qkv))
    arrive(got_vz)
    total = r.vz[0] + r.vz[1] + r.vz[2] + r.vz[3]
    r.o_v1[...] = jnp.concatenate([total[0:1], total[1:2]], axis=1).reshape(WIDTH)
    r.o_v2[...] = jnp.concatenate([total[2:3], total[3:4]], axis=1).reshape(WIDTH)
    for at, out in ((4, r.o_v3), (5, r.o_v4), (6, r.o_v5)):
        out[...] = total[at : at + 1].reshape(DEC_WIDTH)
    firsts = [(2048, 1024), (1024, 1024), (768, 256), (0, 768)]
    names = ["o_down", "o_up", "o_out", "o_qkv"]
    for made, (first, size), name in zip(got_w, firsts, names):
        made.wait_recv()
        more = r.wer[:, first : first + size].astype(F32)
        if name == "o_qkv":
            for c in range(3):
                at = slice(c * 256, (c + 1) * 256)
                r.v_o_qkv[c] = r.own_qkv[:, at] + more[:, at]
        else:
            out = getattr(r, "v_" + name)
            out[...] = out[...] + more
        store(name)
    for made in started:
        made.wait_send()
    for leave in (info, sent, back):
        leave.left()
    for made in stores:
        made.wait()
    assert used[0] <= COPIES


def with_kernel(
    patches,
    counts,
    patch_index,
    scale_level,
    enc_gain_one,
    enc_qkv,
    enc_out,
    enc_gain_two,
    enc_up,
    enc_down,
    w_proj,
    mask_token,
    pos_table,
    dec_gain_one,
    dec_qkv,
    dec_out,
    dec_gain_two,
    dec_up,
    dec_down,
    decoded_grad,
):
    inputs = (
        patches,
        counts,
        patch_index.T,
        scale_level,
        enc_gain_one,
        enc_gain_two,
        dec_gain_one,
        dec_gain_two,
        mask_token,
        decoded_grad,
        jnp.swapaxes(enc_qkv, 0, 1),
        enc_out,
        enc_up,
        enc_down,
        w_proj,
        jnp.swapaxes(pos_table, 0, 1),
        jnp.swapaxes(dec_qkv, 0, 1),
        dec_out,
        dec_up,
        dec_down,
    )
    shapes = dict(STORED, o_pat=(SLOTS, 4, 128), o_v1=(WIDTH,), o_v2=(WIDTH,))
    shapes.update(o_v3=(DEC_WIDTH,), o_v4=(DEC_WIDTH,), o_v5=(DEC_WIDTH,))
    shapes = [jax.ShapeDtypeStruct(shapes[name], F32) for name in OUT_NAMES]
    vmem = pl.BlockSpec(memory_space=pltpu.VMEM)
    smem = pl.BlockSpec(memory_space=pltpu.SMEM)
    hbm = pl.BlockSpec(memory_space=pl.ANY)
    outs = pl.pallas_call(
        kernel,
        out_shape=shapes,
        in_specs=[vmem, smem, vmem, smem] + [vmem] * 6 + [hbm] * len(LOADED),
        out_specs=[hbm if name in STORED else vmem for name in OUT_NAMES],
        scratch_shapes=[pltpu.VMEM(shape, kind) for shape, kind in BUFFERS.values()]
        + [pltpu.VMEM(shape, BF16) for shape in LOADED.values()]
        + [pltpu.VMEM(shape, F32) for shape in STORED.values()]
        + [
            pltpu.SemaphoreType.DMA((len(LOADED) + 4,)),
            pltpu.SemaphoreType.DMA((len(STORED),)),
            pltpu.SemaphoreType.DMA((COPIES,)),
            pltpu.SemaphoreType.DMA((COPIES,)),
        ],
        compiler_params=pltpu.CompilerParams(
            collective_id=0, has_side_effects=True, vmem_limit_bytes=60 * 2**20
        ),
        name="layer_pair",
    )(*inputs)
    outs = list(
        pl.pallas_call(
            hand_over,
            out_shape=shapes,
            in_specs=[hbm] * len(shapes),
            out_specs=[hbm] * len(shapes),
            scratch_shapes=[pltpu.VMEM(shape.shape, F32) for shape in shapes]
            + [pltpu.SemaphoreType.DMA((len(shapes),))] * 2,
            compiler_params=pltpu.CompilerParams(vmem_limit_bytes=60 * 2**20),
            name="hand_over",
        )(*outs)
    )
    outs[0] = jnp.transpose(outs[0], (2, 0, 1))
    outs[2] = jnp.swapaxes(outs[2], 0, 1)
    outs[6] = jnp.swapaxes(outs[6], 0, 1)
    return tuple(outs)


def hand_over(*refs):
    count = len(OUT_NAMES)
    given, returned, held = (refs[i * count : (i + 1) * count] for i in range(3))
    come, go = refs[3 * count :]
    arriving = [pltpu.make_async_copy(given[i], held[i], come.at[i]) for i in range(count)]
    leaving = [pltpu.make_async_copy(held[i], returned[i], go.at[i]) for i in range(count)]
    for made in arriving:
        made.start()
    for first, second in zip(arriving, leaving):
        first.wait()
        second.start()
    for made in leaving:
        made.wait()


def fits_kernel(mesh, shapes):
    ways = (mesh.shape["section"], mesh.shape["dp"], mesh.shape["mp"])
    wanted = {0: (64, 16, 1024), 5: (1024, 3, 1024), 8: (1024, 4096), 10: (1024, 512)}
    wanted.update({12: (8, 196, 512), 14: (512, 3, 512), 17: (512, 2048), 19: (196, 16, 512)})
    return ways == (2, 4, 4) and all(shapes[i] == shape for i, shape in wanted.items())


def solution(mesh):
    def program(*arrays):
        shapes = [array.shape for array in arrays]
        body = with_kernel if fits_kernel(mesh, shapes) else on_device
        return placed_on(mesh, body)(*arrays)

    return program
```

```python
import functools
import math

import jax
import jax.numpy as jnp
from jax import lax
from jax.experimental import pallas as pl
from jax.experimental.pallas import tpu as pltpu
from jax.sharding import PartitionSpec as P

HEAD = 64
DEC_HEAD = 32


eps = 1e-06


def norm_rows(values):
    average = jnp.mean(values, axis=-1, keepdims=True)
    centered = values - average
    variance = jnp.mean(centered * centered, axis=-1, keepdims=True)
    inverse = lax.rsqrt(variance + eps)
    return (centered * inverse, inverse)


def norm_back(normal, inverse, gain_vec, gradient):
    weighted = gradient * gain_vec
    first_term = jnp.mean(weighted, axis=-1, keepdims=True)
    second_term = jnp.mean(weighted * normal, axis=-1, keepdims=True)
    return (
        inverse * (weighted - first_term - normal * second_term),
        jnp.sum(gradient * normal, axis=(0, 1)),
    )


def spread(values):
    return lax.all_gather(values, "mp", axis=0, tiled=True)


def collect(values):
    return lax.psum_scatter(values, "mp", scatter_dimension=0, tiled=True)


def spare_of(work):
    return lambda: jax.tree.map(jnp.zeros_like, work())


def head_view(qkv_rows, head_size):
    return qkv_rows.reshape(
        qkv_rows.shape[0], qkv_rows.shape[1], 3, qkv_rows.shape[3] // head_size, head_size
    )


def score_rows(queries, key_rows, visible, head_size):
    scores = jnp.einsum(
        "sbhe,tbhe->bhst", queries, key_rows, preferred_element_type=jnp.float32
    ) * (1.0 / math.sqrt(head_size))
    return jnp.where(visible[:, None, None, :], scores, -1e30)


def attend(qkv_rows, visible, head_size):
    heads_view = head_view(qkv_rows, head_size)
    scores = score_rows(heads_view[:, :, 0], heads_view[:, :, 1], visible, head_size)
    highest = jnp.max(scores, axis=-1, keepdims=True)
    weights = jnp.exp(scores - highest)
    denominator = jnp.sum(weights, axis=-1, keepdims=True)
    probability = (weights / denominator).astype(jnp.bfloat16)
    context = jnp.einsum(
        "bhst,tbhe->sbhe", probability, heads_view[:, :, 2], preferred_element_type=jnp.float32
    )
    context = context.reshape(qkv_rows.shape[0], qkv_rows.shape[1], qkv_rows.shape[3]).astype(
        jnp.bfloat16
    )
    return (context, highest + jnp.log(denominator))


def attend_back(qkv_rows, visible, logsum, grad_context, head_size):
    heads_view = head_view(qkv_rows, head_size)
    queries = heads_view[:, :, 0]
    key_rows = heads_view[:, :, 1]
    value_rows = heads_view[:, :, 2]
    probability = jnp.exp(score_rows(queries, key_rows, visible, head_size) - logsum)
    grad_heads = grad_context.reshape(queries.shape)
    grad_values = jnp.einsum(
        "bhst,sbhe->tbhe",
        probability.astype(jnp.bfloat16),
        grad_heads,
        preferred_element_type=jnp.float32,
    )
    grad_probs = jnp.einsum(
        "sbhe,tbhe->bhst", grad_heads, value_rows, preferred_element_type=jnp.float32
    )
    row_inner = jnp.sum(grad_probs * probability, axis=-1, keepdims=True)
    grad_scores = (probability * (grad_probs - row_inner)).astype(jnp.bfloat16)
    score_scale = 1.0 / math.sqrt(head_size)
    grad_queries = (
        jnp.einsum("bhst,tbhe->sbhe", grad_scores, key_rows, preferred_element_type=jnp.float32)
        * score_scale
    )
    grad_keys = (
        jnp.einsum("bhst,sbhe->tbhe", grad_scores, queries, preferred_element_type=jnp.float32)
        * score_scale
    )
    stacked = jnp.stack([grad_queries, grad_keys, grad_values], axis=2)
    return stacked.reshape(qkv_rows.shape).astype(jnp.bfloat16)


def attention_local(normed_one, visible, w_qkv, w_out, head_size):
    qkv_rows = jnp.einsum(
        "sbw,wcf->sbcf", normed_one, w_qkv, preferred_element_type=jnp.float32
    ).astype(jnp.bfloat16)
    context, logsum = attend(qkv_rows, visible, head_size)
    mixed_terms = jnp.einsum("sbf,wf->sbw", context, w_out, preferred_element_type=jnp.float32)
    return (qkv_rows, context, logsum, mixed_terms)


def feed_local(normed_two, w_up, w_down):
    upper_in = jnp.einsum("sbw,wf->sbf", normed_two, w_up, preferred_element_type=jnp.float32)
    hidden = jax.nn.gelu(upper_in, approximate=False).astype(jnp.bfloat16)
    return (upper_in, jnp.einsum("sbf,wf->sbw", hidden, w_down, preferred_element_type=jnp.float32))


def feed_back_local(grad_full, normed_two, upper_in, w_up, w_down):
    value_out, gelu_pull = jax.vjp(
        lambda argument: jax.nn.gelu(argument, approximate=False), upper_in
    )
    hidden = value_out.astype(jnp.bfloat16)
    grad_down_w = jnp.einsum("sbw,sbf->wf", grad_full, hidden, preferred_element_type=jnp.float32)
    grad_hidden = jnp.einsum("sbw,wf->sbf", grad_full, w_down, preferred_element_type=jnp.float32)
    grad_upper = gelu_pull(grad_hidden)[0].astype(jnp.bfloat16)
    grad_up_w = jnp.einsum(
        "sbw,sbf->wf", normed_two, grad_upper, preferred_element_type=jnp.float32
    )
    grad_terms = jnp.einsum("sbf,wf->sbw", grad_upper, w_up, preferred_element_type=jnp.float32)
    return (grad_up_w, grad_down_w, grad_terms)


def attention_back_local(
    grad_full, qkv_rows, context, logsum, visible, normed_one, w_qkv, w_out, head_size
):
    grad_out_w = jnp.einsum("sbw,sbf->wf", grad_full, context, preferred_element_type=jnp.float32)
    grad_context = jnp.einsum(
        "sbw,wf->sbf", grad_full, w_out, preferred_element_type=jnp.float32
    ).astype(jnp.bfloat16)
    grad_qkv = attend_back(qkv_rows, visible, logsum, grad_context, head_size)
    grad_qkv_w = jnp.einsum(
        "sbw,sbcf->wcf", normed_one, grad_qkv, preferred_element_type=jnp.float32
    )
    grad_normed = jnp.einsum("sbcf,wcf->sbw", grad_qkv, w_qkv, preferred_element_type=jnp.float32)
    return (grad_qkv_w, grad_out_w, grad_normed)


def on_device(
    patches,
    counts,
    patch_index,
    scale_level,
    enc_gain_one,
    enc_qkv,
    enc_out,
    enc_gain_two,
    enc_up,
    enc_down,
    w_proj,
    mask_token,
    pos_table,
    dec_gain_one,
    dec_qkv,
    dec_out,
    dec_gain_two,
    dec_up,
    dec_down,
    decoded_grad,
):
    data_ways = lax.axis_size("dp")
    model_ways = lax.axis_size("mp")
    slot_rows = patches.shape[0]
    images = patches.shape[1]
    grid_rows = decoded_grad.shape[0]
    dec_width = decoded_grad.shape[2]
    slot_count = slot_rows * model_ways
    grid_count = grid_rows * model_ways
    per_peer = images // data_ways
    slot_start = lax.axis_index("mp") * slot_rows
    grid_start = lax.axis_index("mp") * grid_rows
    is_encoder = lax.axis_index("section") == 0
    visible = jnp.arange(slot_count, dtype=jnp.int32)[None, :] < counts[:, None]
    all_visible = jnp.ones((images, grid_count), dtype=bool)
    enc_g1 = enc_gain_one.astype(jnp.float32)
    enc_g2 = enc_gain_two.astype(jnp.float32)
    dec_g1 = dec_gain_one.astype(jnp.float32)
    dec_g2 = dec_gain_two.astype(jnp.float32)
    token_vec = mask_token.astype(jnp.float32)

    def on_encoder(work):
        return lax.cond(is_encoder, work, spare_of(work))

    def on_decoder(work):
        return lax.cond(is_encoder, spare_of(work), work)

    full_in = spread(patches)

    def enc_attention():
        normal_one, inverse_one = norm_rows(full_in.astype(jnp.float32))
        normed_one = (normal_one * enc_g1).astype(jnp.bfloat16)
        return attention_local(normed_one, visible, enc_qkv, enc_out, HEAD)

    enc_qkv_rows, enc_context, enc_logsum, enc_mixed_terms = on_encoder(enc_attention)
    enc_middle = patches.astype(jnp.float32) + collect(enc_mixed_terms)
    enc_normal_two, enc_inverse_two = norm_rows(enc_middle)
    enc_normed_two = spread((enc_normal_two * enc_g2).astype(jnp.bfloat16))
    enc_upper, enc_down_terms = on_encoder(lambda: feed_local(enc_normed_two, enc_up, enc_down))
    enc_out_low = (enc_middle + collect(enc_down_terms)).astype(jnp.bfloat16)

    def enc_send():
        sent_rows = jnp.einsum(
            "sbw,wf->sbf", enc_out_low, w_proj, preferred_element_type=jnp.float32
        ).astype(jnp.bfloat16)
        live_slot = (slot_start + jnp.arange(slot_rows, dtype=jnp.int32))[:, None] < counts[None, :]
        sent_index = jnp.where(live_slot, patch_index, grid_count)
        packed = (
            sent_rows.reshape(slot_rows, per_peer, data_ways, dec_width),
            sent_index.reshape(slot_rows, per_peer, data_ways),
            scale_level.reshape(1, per_peer, data_ways),
        )
        packed = tuple(
            (jnp.concatenate([jnp.zeros_like(member), member], axis=2) for member in packed)
        )
        return packed

    packed = on_encoder(enc_send)
    received = (
        lax.all_to_all(packed[0], ("section", "dp"), split_axis=2, concat_axis=1, tiled=True),
        lax.all_to_all(packed[1], ("section", "dp"), split_axis=2, concat_axis=1, tiled=True),
        lax.all_to_all(packed[2], ("section", "dp"), split_axis=2, concat_axis=1, tiled=True),
    )
    arrived = (received[0][:, :images, 0], received[1][:, :images, 0], received[2][0, :images, 0])
    arrived_rows, arrived_index, arrived_level = arrived

    def make_onehot():
        return (
            arrived_index[:, :, None] == jnp.arange(grid_count, dtype=jnp.int32)[None, None, :]
        ).astype(jnp.bfloat16)

    def dec_place():
        onehot_low = make_onehot()
        covered = jnp.transpose(jnp.sum(onehot_low.astype(jnp.float32), axis=0))
        placed = jnp.einsum(
            "sbp,sbf->pbf", onehot_low, arrived_rows, preferred_element_type=jnp.float32
        )
        return (placed - covered[:, :, None] * token_vec, covered)

    placed_terms, covered_terms = on_decoder(dec_place)
    placed_rows, covered_rows = collect((placed_terms, covered_terms))
    table_rows = lax.dynamic_slice_in_dim(pos_table, grid_start, grid_rows, 1)
    level_hot = (
        arrived_level[:, None] == jnp.arange(pos_table.shape[0], dtype=jnp.int32)[None, :]
    ).astype(jnp.bfloat16)
    position = jnp.einsum("bl,lpf->pbf", level_hot, table_rows, preferred_element_type=jnp.float32)
    grid_values = placed_rows + token_vec + position
    dec_normal_one, dec_inverse_one = norm_rows(grid_values)
    dec_normed_one = spread((dec_normal_one * dec_g1).astype(jnp.bfloat16))
    dec_qkv_rows, dec_context, dec_logsum, dec_mixed_terms = on_decoder(
        lambda: attention_local(dec_normed_one, all_visible, dec_qkv, dec_out, DEC_HEAD)
    )
    dec_middle = grid_values + collect(dec_mixed_terms)
    dec_normal_two, dec_inverse_two = norm_rows(dec_middle)
    dec_normed_two = spread((dec_normal_two * dec_g2).astype(jnp.bfloat16))

    def dec_feed():
        upper_in, down_terms = feed_local(dec_normed_two, dec_up, dec_down)
        own_rows = lax.dynamic_slice_in_dim(down_terms, grid_start, grid_rows, 0) + dec_middle
        return (upper_in, lax.dynamic_update_slice_in_dim(down_terms, own_rows, grid_start, 0))

    dec_upper, dec_summand = on_decoder(dec_feed)
    decoded = lax.psum_scatter(
        dec_summand.astype(jnp.bfloat16), ("section", "mp"), scatter_dimension=2, tiled=True
    ).astype(jnp.float32)
    dec_grad_full = spread(decoded_grad)
    dec_up_grad, dec_down_grad, dec_two_terms = on_decoder(
        lambda: feed_back_local(dec_grad_full, dec_normed_two, dec_upper, dec_up, dec_down)
    )
    dec_through, dec_gain_two_grad = norm_back(
        dec_normal_two, dec_inverse_two, dec_g2, collect(dec_two_terms)
    )
    dec_grad_middle = decoded_grad.astype(jnp.float32) + dec_through
    dec_middle_full = spread(dec_grad_middle.astype(jnp.bfloat16))
    dec_qkv_grad, dec_out_grad, dec_one_terms = on_decoder(
        lambda: attention_back_local(
            dec_middle_full,
            dec_qkv_rows,
            dec_context,
            dec_logsum,
            all_visible,
            dec_normed_one,
            dec_qkv,
            dec_out,
            DEC_HEAD,
        )
    )
    dec_inner, dec_gain_one_grad = norm_back(
        dec_normal_one, dec_inverse_one, dec_g1, collect(dec_one_terms)
    )
    grad_grid = dec_grad_middle + dec_inner
    grad_token = jnp.sum(grad_grid * (1.0 - covered_rows)[:, :, None], axis=(0, 1))
    grad_grid_full = spread(grad_grid.astype(jnp.bfloat16))

    def dec_return():
        grad_sent = jnp.einsum(
            "sbp,pbf->sbf", make_onehot(), grad_grid_full, preferred_element_type=jnp.float32
        ).astype(jnp.bfloat16)
        return jnp.concatenate([grad_sent, jnp.zeros_like(grad_sent)], axis=1)[:, :, None, :]

    back_rows = on_decoder(dec_return)
    returned = lax.all_to_all(
        back_rows, ("section", "dp"), split_axis=1, concat_axis=2, tiled=True
    )[:, :, data_ways:]
    grad_arrived = returned.reshape(slot_rows, images, dec_width)

    def enc_project_back():
        grad_proj_w = jnp.einsum(
            "sbw,sbf->wf", enc_out_low, grad_arrived, preferred_element_type=jnp.float32
        )
        grad_block = jnp.einsum(
            "sbf,wf->sbw", grad_arrived, w_proj, preferred_element_type=jnp.float32
        )
        return (grad_proj_w, grad_block)

    proj_grad, enc_grad_block = on_encoder(enc_project_back)
    enc_grad_full = spread(enc_grad_block.astype(jnp.bfloat16))
    enc_up_grad, enc_down_grad, enc_two_terms = on_encoder(
        lambda: feed_back_local(enc_grad_full, enc_normed_two, enc_upper, enc_up, enc_down)
    )
    enc_through, enc_gain_two_grad = norm_back(
        enc_normal_two, enc_inverse_two, enc_g2, collect(enc_two_terms)
    )
    enc_grad_middle = enc_grad_block + enc_through
    enc_middle_full = spread(enc_grad_middle.astype(jnp.bfloat16))

    def enc_attention_back():
        normal_one, inverse_one = norm_rows(full_in.astype(jnp.float32))
        normed_one = (normal_one * enc_g1).astype(jnp.bfloat16)
        grad_qkv_w, grad_out_w, grad_normed = attention_back_local(
            enc_middle_full,
            enc_qkv_rows,
            enc_context,
            enc_logsum,
            visible,
            normed_one,
            enc_qkv,
            enc_out,
            HEAD,
        )
        grad_inner, grad_gain_one = norm_back(normal_one, inverse_one, enc_g1, grad_normed)
        own_rows = lax.dynamic_slice_in_dim(grad_inner, slot_start, slot_rows, 0) + enc_grad_middle
        summand = lax.dynamic_update_slice_in_dim(grad_inner, own_rows, slot_start, 0)
        return (grad_qkv_w, grad_out_w, grad_gain_one, summand)

    enc_qkv_grad, enc_out_grad, enc_gain_one_grad, in_summand = on_encoder(enc_attention_back)
    patches_grad = lax.psum_scatter(
        in_summand.astype(jnp.bfloat16), ("section", "mp"), scatter_dimension=2, tiled=True
    ).astype(jnp.float32)
    enc_gain_two_grad = jnp.where(is_encoder, enc_gain_two_grad, 0.0)
    dec_gain_one_grad = jnp.where(is_encoder, 0.0, dec_gain_one_grad)
    dec_gain_two_grad = jnp.where(is_encoder, 0.0, dec_gain_two_grad)
    grad_token = jnp.where(is_encoder, 0.0, grad_token)
    sharded = (
        lax.psum_scatter(enc_qkv_grad, ("section", "dp"), scatter_dimension=0, tiled=True),
        lax.psum_scatter(enc_out_grad, ("section", "dp"), scatter_dimension=0, tiled=True),
        lax.psum_scatter(enc_up_grad, ("section", "dp"), scatter_dimension=0, tiled=True),
        lax.psum_scatter(enc_down_grad, ("section", "dp"), scatter_dimension=0, tiled=True),
        lax.psum_scatter(dec_qkv_grad, ("section", "dp"), scatter_dimension=0, tiled=True),
        lax.psum_scatter(dec_out_grad, ("section", "dp"), scatter_dimension=0, tiled=True),
        lax.psum_scatter(dec_up_grad, ("section", "dp"), scatter_dimension=0, tiled=True),
        lax.psum_scatter(dec_down_grad, ("section", "dp"), scatter_dimension=0, tiled=True),
    )
    shared = lax.psum(
        (
            proj_grad,
            enc_gain_one_grad,
            enc_gain_two_grad,
            dec_gain_one_grad,
            dec_gain_two_grad,
            grad_token,
        ),
        ("section", "dp", "mp"),
    )
    return (
        decoded,
        patches_grad,
        sharded[0],
        sharded[1],
        sharded[2],
        sharded[3],
        sharded[4],
        sharded[5],
        sharded[6],
        sharded[7],
        shared[0],
        shared[1],
        shared[2],
        shared[3],
        shared[4],
        shared[5],
    )


def placed_on(mesh, body):
    placed = (
        P("mp", "dp", None),
        P("dp"),
        P("mp", "dp"),
        P("dp"),
        P(),
        P(None, None, "mp"),
        P(None, "mp"),
        P(),
        P(None, "mp"),
        P(None, "mp"),
        P(),
        P(),
        P(),
        P(),
        P(None, None, "mp"),
        P(None, "mp"),
        P(),
        P(None, "mp"),
        P(None, "mp"),
        P("mp", "dp", None),
    )
    return jax.shard_map(
        body,
        mesh=mesh,
        in_specs=placed,
        out_specs=(
            P(None, "dp", ("section", "mp")),
            P(None, "dp", ("section", "mp")),
            P(("section", "dp"), None, "mp"),
            P(("section", "dp"), "mp"),
            P(("section", "dp"), "mp"),
            P(("section", "dp"), "mp"),
            P(("section", "dp"), None, "mp"),
            P(("section", "dp"), "mp"),
            P(("section", "dp"), "mp"),
            P(("section", "dp"), "mp"),
            P(),
            P(),
            P(),
            P(),
            P(),
            P(),
        ),
        check_vma=False,
    )


MESH = pl.DeviceIdType.MESH
F32 = jnp.float32
BF16 = jnp.bfloat16
WAYS = 4
PAIR = 2
SLOTS = 64
SHARD = 16
PATCHES = 49
ROWS = 64
WIDTH = 1024
DEC_WIDTH = 512
HEADS_HERE = 4
COPIES = 256


def padded_row(patch):
    shard = sum((patch >= k * PATCHES).astype(jnp.int32) for k in (1, 2, 3))
    return patch + (ROWS - PATCHES) * shard


def dot(left, right, left_dim, right_dim):
    return lax.dot_general(
        left, right, (((left_dim,), (right_dim,)), ((), ())), preferred_element_type=F32
    )


def rows_back(normal, inverse, gain, gradient):
    weighted = gradient * gain
    first = jnp.mean(weighted, axis=-1, keepdims=True)
    second = jnp.mean(weighted * normal, axis=-1, keepdims=True)
    return inverse * (weighted - first - normal * second)


def gelu_both(upper):
    phi = 0.5 * (1.0 + lax.erf(upper * math.sqrt(0.5)))
    density = jnp.exp(-0.5 * upper * upper) * (1.0 / math.sqrt(2.0 * math.pi))
    return upper * phi, phi + upper * density


def head_mask(width, head, kind):
    lane = lax.broadcasted_iota(jnp.int32, (1, width), 1)
    return [
        ((lane >= h * head) & (lane < (h + 1) * head)).astype(F32).astype(kind)
        for h in range(HEADS_HERE)
    ]


def stack_heads(values, masks):
    return jnp.concatenate([values * mask for mask in masks], axis=0)


def fold_heads(stacked, masks, rows):
    total = None
    for h, mask in enumerate(masks):
        part = stacked[h * rows : (h + 1) * rows] * mask
        total = part if total is None else total + part
    return total


def probabilities(qkv, keep, width, head, scale):
    queries = stack_heads(qkv[:, :width], head_mask(width, head, BF16))
    scores = dot(queries, qkv[:, width : 2 * width], 1, 1) * scale
    scores = jnp.where(keep, scores, -1e30)
    weights = jnp.exp(scores - jnp.max(scores, axis=-1, keepdims=True))
    return weights / jnp.sum(weights, axis=-1, keepdims=True)


def attention(qkv, keep, rows, width, head, scale):
    probs = probabilities(qkv, keep, width, head, scale)
    mixed = dot(probs.astype(BF16), qkv[:, 2 * width :], 1, 0)
    return probs, fold_heads(mixed, head_mask(width, head, F32), rows).astype(BF16)


def attention_back(qkv, probs, grad_context, rows, width, head, scale):
    low = head_mask(width, head, BF16)
    wide = head_mask(width, head, F32)
    queries = stack_heads(qkv[:, :width], low)
    grads = stack_heads(grad_context, low)
    grad_probs = dot(grads, qkv[:, 2 * width :], 1, 1)
    inner = jnp.sum(grad_probs * probs, axis=-1, keepdims=True)
    grad_scores = (probs * (grad_probs - inner)).astype(BF16)
    grad_queries = fold_heads(dot(grad_scores, qkv[:, width : 2 * width], 1, 0), wide, rows) * scale
    grad_keys = dot(grad_scores, queries, 0, 0) * scale
    grad_values = dot(probs.astype(BF16), grads, 0, 0)
    return jnp.concatenate([grad_queries, grad_keys, grad_values], axis=1).astype(BF16)


IN_NAMES = [
    "xs",
    "counts",
    "index",
    "levels",
    "g1",
    "g2",
    "g3",
    "g4",
    "g5",
    "dgrad",
    "w_qkv",
    "w_out",
    "w_up",
    "w_down",
    "w_proj",
    "table",
    "d_qkv",
    "d_out",
    "d_up",
    "d_down",
]
OUT_NAMES = [
    "o_dec",
    "o_pat",
    "o_qkv",
    "o_out",
    "o_up",
    "o_down",
    "o_dqkv",
    "o_dout",
    "o_dup",
    "o_ddown",
    "o_proj",
    "o_v1",
    "o_v2",
    "o_v3",
    "o_v4",
    "o_v5",
]
LOADED = dict(
    w_qkv=(WIDTH, 768),
    w_out=(WIDTH, 256),
    w_up=(WIDTH, 1024),
    w_down=(WIDTH, 1024),
    w_proj=(WIDTH, DEC_WIDTH),
    table=(196, 8, DEC_WIDTH),
    d_qkv=(DEC_WIDTH, 384),
    d_out=(DEC_WIDTH, 128),
    d_up=(DEC_WIDTH, 512),
    d_down=(DEC_WIDTH, 512),
)
STORED = dict(
    o_dec=(4, 64, 196),
    o_qkv=(3, 128, 256),
    o_out=(128, 256),
    o_up=(128, 1024),
    o_down=(128, 1024),
    o_dqkv=(3, 64, 128),
    o_dout=(64, 128),
    o_dup=(64, 512),
    o_ddown=(64, 512),
    o_proj=(1024, 512),
)
BUFFERS = dict(
    info=((2, 8, 128), jnp.int32),
    flat=((1568, 512), BF16),
    xf=((2, 64, 1024), BF16),
    probs=((2, 256, 64), F32),
    s1=((2, 64, 1024), BF16),
    r1=((2, 3, 16, 1024), BF16),
    mid=((2, 16, 1024), F32),
    n2=((2, 64, 1024), BF16),
    gp=((2, 64, 1024), F32),
    s2=((2, 64, 1024), BF16),
    r2=((2, 3, 16, 1024), BF16),
    eo=((2, 16, 1024), BF16),
    sent=((2, 16, 512), BF16),
    arr=((2, 64, 512), BF16),
    meta=((2, 4, 8, 128), jnp.int32),
    dgf=((2, 256, 512), BF16),
    hot=((2, 256, 64), BF16),
    free=((2, 256, 1), F32),
    grid=((2, 256, 512), F32),
    dn1=((512, 512), BF16),
    dqkv=((512, 384), BF16),
    dprobs=((2, 1024, 256), F32),
    dctx=((512, 128), BF16),
    s3=((2, 256, 512), BF16),
    r3=((2, 3, 64, 512), BF16),
    dmid=((2, 64, 512), F32),
    dn2=((2, 256, 512), BF16),
    dhid=((512, 512), BF16),
    dgh=((512, 512), F32),
    dgu=((512, 512), BF16),
    s4=((2, 256, 512), BF16),
    r4=((2, 3, 64, 512), BF16),
    ds=((8, 256, 128), BF16),
    dr=((8, 256, 128), BF16),
    dgm=((2, 256, 512), BF16),
    dgq=((512, 384), BF16),
    s5=((2, 64, 512), BF16),
    r5=((2, 3, 16, 512), BF16),
    sg=((2, 16, 512), BF16),
    w1s=((256, 1024), BF16),
    w1r=((256, 1024), BF16),
    w1o=((256, 1024), F32),
    z1s=((4, 64, 1024), BF16),
    z1r=((3, 64, 1024), BF16),
    w2s=((256, 512), BF16),
    w2r=((256, 512), BF16),
    w2o=((256, 512), F32),
    z2s=((4, 64, 512), BF16),
    z2r=((3, 64, 512), BF16),
    s6=((2, 64, 1024), BF16),
    r6=((2, 3, 16, 1024), BF16),
    gm=((2, 64, 1024), BF16),
    fs=((8, 2, 64, 128), BF16),
    fr=((8, 2, 64, 128), BF16),
    cz=((4, 2, 64, 256), BF16),
    nz=((4, 2, 4, 16, 1024), BF16),
    kz=((4, 2, 64, 768), BF16),
    gz=((4, 2, 64, 256), BF16),
    qa=((4, 2, 64, 768), BF16),
    pz=((3, 2, 256, 64), F32),
    seen=((4, 8, 128), jnp.int32),
    ez=((4, 2, 64, 256), BF16),
    sz=((4, 2, 4, 16, 512), BF16),
    xb=((2, 2, 4, 2, 64, 128), BF16),
    xz=((2, 4, 2, 2, 64, 128), BF16),
    ha=((4, 2, 64, 1024), BF16),
    sa=((4, 2, 64, 1024), BF16),
    ga=((512, 1024), BF16),
    wes=((128, 3072), BF16),
    wer=((128, 3072), BF16),
    own_qkv=((128, 768), F32),
    ps=((256, 512), BF16),
    pr=((256, 512), BF16),
    pa=((4, 2, 128, 512), BF16),
    vec=((8, 512), F32),
    vr=((8, 8, 512), F32),
    vz=((4, 8, 512), F32),
)


class Refs:
    pass


def kernel(*refs):
    r = Refs()
    names = IN_NAMES + OUT_NAMES + list(BUFFERS) + ["v_" + n for n in (*LOADED, *STORED)]
    for name, ref in zip(names, refs):
        setattr(r, name, ref)
    load_sem, store_sem, send_sem, recv_sem = refs[len(names) :]
    s, d, m = (lax.axis_index(a) for a in ("section", "dp", "mp"))
    used = [0]

    def take(count):
        used[0] += count
        return used[0] - count

    def copy(src, dst, device, at, land=None):
        return pltpu.make_async_remote_copy(
            src_ref=src,
            dst_ref=dst,
            send_sem=send_sem.at[at],
            recv_sem=recv_sem.at[at if land is None else land],
            device_id=device,
            device_id_type=MESH,
        )

    def send(src, dst, device):
        made = copy(src, dst, device, take(1))
        made.start()
        return made

    def arrive(copies):
        for made in copies:
            made.wait_send()
            made.wait_recv()

    def model(k):
        return lax.rem(m + k, WAYS)

    def data(k):
        return lax.rem(d + k, WAYS)

    def gather(ref, rows):
        own = ref.at[pl.ds(pl.multiple_of(m * rows, rows), rows)]
        return [send(own, own, {"mp": model(k)}) for k in (1, 2, 3)]

    def scatter(src, dst, rows):
        copies = []
        for k in (1, 2, 3):
            to = model(k)
            part = src.at[pl.ds(pl.multiple_of(to * rows, rows), rows)]
            copies.append(send(part, dst.at[k - 1], {"mp": to}))
        return copies

    def summed(src, dst, rows):
        total = src[pl.ds(pl.multiple_of(m * rows, rows), rows), :].astype(F32)
        for k in range(3):
            total = total + dst[k].astype(F32)
        return total

    def relay(ref, i):
        copies = []
        for k in (1, 2, 3):
            part = ref.at[data(k), i, m]
            copies += [send(part, part, {"mp": model(j)}) for j in (1, 2, 3)]
        return copies

    def along(ref):
        return [send(ref.at[d], ref.at[d], {"dp": data(k)}) for k in (1, 2, 3)]

    def block_columns(which, values):
        for i, value in enumerate(values):
            for block in range(8):
                at = slice(block * 128, (block + 1) * 128)
                r.xb[which, block // 4, block % 4, i] = value[:, at]
        r.xz[which, d] = r.xb[which, :, d]

    def send_columns(which):
        return [
            send(r.xb.at[which, :, data(k)], r.xz.at[which, d], {"dp": data(k)}) for k in (1, 2, 3)
        ]

    plane = [(a, k) for a in (0, 1) for k in range(4) if (a, k) != (0, 0)]

    def to_plane(a, k):
        return {"section": lax.rem(s + a, 2), "mp": model(k)}

    half = d // 2
    place = lax.rem(d, 2)

    def across(i, k):
        return {"section": half, "dp": 2 * s + i, "mp": model(k)}

    def mine(i):
        return (half == s) & (2 * s + i == d)

    def to_dp():
        return sending[0] if sending else d

    sending = []

    class exchange:
        def __init__(self, src_of, dst_of, own):
            self.src_of, self.dst_of, self.own = src_of, dst_of, own
            self.at = take(8)

        def out(self, i, k):
            sending.append(2 * s + i)
            land = self.dst_of(place, m)
            sending.clear()
            at = self.at
            return copy(self.src_of(i), land, across(i, k), at + 4 * i + k, at + 4 * place + k)

        def come(self, i, k):
            at = self.at + 4 * i + k
            return copy(self.src_of(i), self.dst_of(i, model(4 - k)), across(i, k), at)

        def start(self, i):
            for k in (1, 2, 3):
                self.out(i, k).start()
            pl.when(jnp.logical_not(mine(i)))(self.out(i, 0).start)
            pl.when(mine(i))(functools.partial(self.own, i))

        def landed(self, i):
            pl.when(jnp.logical_not(mine(i)))(self.come(i, 0).wait_recv)
            for k in (1, 2, 3):
                self.come(i, k).wait_recv()

        def left(self):
            for i in range(PAIR):
                for k in (1, 2, 3):
                    self.out(i, k).wait_send()
                pl.when(jnp.logical_not(mine(i)))(self.out(i, 0).wait_send)

    def slot_rows(ref):
        return lambda i, at: ref.at[i, pl.ds(pl.multiple_of(at * SHARD, SHARD), SHARD)]

    def put_info(i):
        r.meta[place, m] = r.info[i]

    def put_rows(ref):
        def put(i):
            ref[place, pl.ds(pl.multiple_of(m * SHARD, SHARD), SHARD), :] = r.sent[i]

        return put

    loads = {}

    def load(name, parts):
        src, dst = getattr(r, name), getattr(r, "v_" + name)
        if not parts:
            return [(src, dst)]
        width = dst.shape[1] // parts
        return [(src.at[c], dst.at[:, c * width : (c + 1) * width]) for c in range(parts)]

    at = 0
    for name in LOADED:
        loads[name] = []
        for src, dst in load(name, 3 if name in ("w_qkv", "d_qkv") else 0):
            loads[name].append(pltpu.make_async_copy(src, dst, load_sem.at[at]))
            at += 1
        for made in loads[name]:
            made.start()

    def loaded(*which):
        for name in which:
            for made in loads[name]:
                made.wait()

    stores = []

    def store(*which):
        for name in which:
            at = list(STORED).index(name)
            made = pltpu.make_async_copy(getattr(r, "v_" + name), getattr(r, name), store_sem.at[at])
            made.start()
            stores.append(made)

    barrier = pltpu.get_barrier_semaphore()
    for a, k in plane:
        pl.semaphore_signal(barrier, inc=1, device_id=to_plane(a, k), device_id_type=MESH)
    for k in (1, 2, 3):
        pl.semaphore_signal(barrier, inc=1, device_id={"dp": data(k)}, device_id_type=MESH)
    for i in range(PAIR):
        for k in range(4):
            signal = functools.partial(
                pl.semaphore_signal, barrier, inc=1, device_id=across(i, k), device_id_type=MESH
            )
            if k:
                signal()
            else:
                pl.when(jnp.logical_not(mine(i)))(signal)
    pl.semaphore_wait(barrier, 7 + 3 + 8 - (half == s).astype(jnp.int32))

    e_g1, e_g2 = (g[...].astype(F32).reshape(1, WIDTH) for g in (r.g1, r.g2))
    d_g1, d_g2, token = (g[...].astype(F32).reshape(1, DEC_WIDTH) for g in (r.g3, r.g4, r.g5))

    own16 = pl.ds(pl.multiple_of(m * SHARD, SHARD), SHARD)
    own64 = pl.ds(pl.multiple_of(m * ROWS, ROWS), ROWS)
    e_scale = 1.0 / math.sqrt(HEAD)
    d_scale = 1.0 / math.sqrt(DEC_HEAD)
    other = lax.rem(s + 1, 2)
    rank = s * 4 + m
    pair = range(PAIR)

    def own_images(ref):
        values = ref[...].astype(F32)
        return [jnp.where(s == 0, values[:, i], values[:, PAIR + i]) for i in pair]

    got = []
    for i, rows in enumerate(own_images(r.xs)):
        r.xf[i, own16, :] = rows.astype(BF16)
        got.append(gather(r.xf.at[i], SHARD))
    slot = m * SHARD + lax.broadcasted_iota(jnp.int32, (1, SHARD), 1)
    r.info[...] = jnp.zeros((2, 8, 128), jnp.int32)
    for i in pair:
        patch = r.index[pl.ds(PAIR * s + i, 1), :]
        live = slot < r.counts[PAIR * s + i]
        r.info[i, 0:1, 0:SHARD] = jnp.where(live, padded_row(patch), -1)
        r.info[i, 1:2, :] = jnp.zeros((1, 128), jnp.int32) + r.levels[PAIR * s + i]
        r.info[i, 2:3, :] = jnp.zeros((1, 128), jnp.int32) + r.counts[PAIR * s + i]
    r.seen[d] = jnp.concatenate([r.info[0, 2:3, :]] * 4 + [r.info[1, 2:3, :]] * 4, axis=0)
    got_seen = along(r.seen)
    info = exchange(lambda i: r.info.at[i], lambda i, at: r.meta.at[i, at], put_info)
    for i in pair:
        info.start(i)
    for i, rows in enumerate(own_images(r.dgrad)):
        rows = jnp.concatenate([rows, jnp.zeros((ROWS - PATCHES, DEC_WIDTH), F32)], axis=0)
        r.dgf[i, own64, :] = rows.astype(BF16)
    loaded("w_qkv")
    loaded("w_out")
    sent_on = []
    contexts, normeds = [], []
    for i in pair:
        arrive(got[i])
    got_dg = []
    for i in pair:
        got_dg += gather(r.dgf.at[i], ROWS)
        normal, _ = norm_rows(r.xf[i].astype(F32))
        normed = (normal * e_g1).astype(BF16)
        part = dot(normed, r.v_w_qkv[...], 1, 0).astype(BF16)
        r.kz[d, i] = part
        keep = lax.broadcasted_iota(jnp.int32, (1, SLOTS), 1) < r.counts[PAIR * s + i]
        probs, context = attention(part, keep, 64, 256, HEAD, e_scale)
        r.probs[i] = probs
        r.s1[i] = dot(context, r.v_w_out[...], 1, 1).astype(BF16)
        sent_on.append(scatter(r.s1.at[i], r.r1.at[i], SHARD))
        r.cz[d, i] = context
        normeds.append(normed)
    block_columns(0, normeds)
    got_c = along(r.cz)
    got_x1 = send_columns(0)

    row = lax.broadcasted_iota(jnp.int32, (256, 1), 0)
    is_real = lax.rem(row, ROWS) < PATCHES
    real = is_real.astype(F32)
    entry = jnp.where(is_real, (row - (ROWS - PATCHES) * (row // ROWS)) * 8, -8)

    def start_grid(i):
        info.landed(i)
        index = jnp.concatenate([r.meta[i, k, 0:1, 0:SHARD] for k in range(4)], axis=1)
        hot = (lax.broadcasted_iota(jnp.int32, (256, 64), 0) == index).astype(F32)
        free = real - jnp.sum(hot, axis=1, keepdims=True)
        r.hot[i] = hot.astype(BF16)
        r.free[i] = free
        level = r.meta[i, 0, 1:2, 0:1]
        chosen = lax.broadcasted_iota(jnp.int32, (256, 196 * 8), 1) == entry + level
        r.grid[i] = free * token + dot(chosen.astype(F32).astype(BF16), r.flat[...], 1, 0)

    loaded("table")
    r.flat[...] = r.v_table[...].astype(F32).reshape(196 * 8, DEC_WIDTH).astype(BF16)
    start_grid(0)

    got = []
    for i in pair:
        arrive(sent_on[i])
        middle = r.xf[i, own16, :].astype(F32) + summed(r.s1.at[i], r.r1.at[i], SHARD)
        r.mid[i] = middle
        normal, _ = norm_rows(middle)
        r.n2[i, own16, :] = (normal * e_g2).astype(BF16)
        got.append(gather(r.n2.at[i], SHARD))
    got_nz = [
        send(r.n2.at[:, own16], r.nz.at[d, :, m], {"dp": data(k)}) for k in (1, 2, 3)
    ]
    start_grid(1)
    loaded("w_up")
    loaded("w_down")
    loaded("w_proj")
    sent_on = []
    for i in pair:
        arrive(got[i])
        upper = dot(r.n2[i], r.v_w_up[...], 1, 0)
        hidden, slope = gelu_both(upper)
        r.gp[i] = slope
        r.s2[i] = dot(hidden.astype(BF16), r.v_w_down[...], 1, 1).astype(BF16)
        sent_on.append(scatter(r.s2.at[i], r.r2.at[i], SHARD))
    arrive(got_dg)
    loaded("d_down")
    r.dgh[...] = dot(r.dgf[...].reshape(512, 512), r.v_d_down[...], 1, 0)
    sent = exchange(lambda i: r.sent.at[i], slot_rows(r.arr), put_rows(r.arr))
    for i in pair:
        arrive(sent_on[i])
        out_low = (r.mid[i] + summed(r.s2.at[i], r.r2.at[i], SHARD)).astype(BF16)
        r.eo[i] = out_low
        r.sent[i] = dot(out_low, r.v_w_proj[...], 1, 0).astype(BF16)
        sent.start(i)
    r.ez[d, :, own16] = r.eo[:, :, pl.ds(pl.multiple_of(m * 256, 256), 256)]
    got_eo = []
    for k in (1, 2, 3):
        columns = pl.ds(pl.multiple_of(model(k) * 256, 256), 256)
        got_eo.append(send(r.eo.at[:, :, columns], r.ez.at[d, :, own16], {"mp": model(k)}))

    loaded("d_qkv")
    loaded("d_out")
    loaded("d_up")
    cols = lax.broadcasted_iota(jnp.int32, (1, 256), 1)
    d_keep = lax.rem(cols, ROWS) < PATCHES
    sent_on = []
    for i in pair:
        sent.landed(i)
    info.left()
    arrive(got_nz)
    got_nm = [relay(r.nz, 0)]
    for i in pair:
        values = r.grid[i] + dot(r.hot[i], r.arr[i], 1, 0)
        r.grid[i] = values
        normal, _ = norm_rows(values)
        normed = (normal * d_g1).astype(BF16)
        at = slice(i * 256, (i + 1) * 256)
        r.dn1[at, :] = normed
        part = dot(normed, r.v_d_qkv[...], 1, 0).astype(BF16)
        r.dqkv[at, :] = part
        probs, context = attention(part, d_keep, 256, 128, DEC_HEAD, d_scale)
        r.dprobs[i] = probs
        r.dctx[at, :] = context
        r.s3[i] = dot(context, r.v_d_out[...], 1, 1).astype(BF16)
        sent_on.append(scatter(r.s3.at[i], r.r3.at[i], ROWS))
    r.nz[d] = r.n2[...].reshape(2, 4, 16, WIDTH)
    arrive(got_eo)
    got_ez = along(r.ez)
    got_k = along(r.kz)
    got = []
    for i in pair:
        arrive(sent_on[i])
        middle = r.grid[i, own64, :] + summed(r.s3.at[i], r.r3.at[i], ROWS)
        r.dmid[i] = middle
        normal, _ = norm_rows(middle)
        r.dn2[i, own64, :] = (normal * d_g2).astype(BF16)
        got.append(gather(r.dn2.at[i], ROWS))

    sent.left()

    def upper_of(i):
        arrive(got_nm[i])
        rows = r.nz[:, i].reshape(256, WIDTH)
        hidden, slope = gelu_both(dot(rows, r.v_w_up[...], 1, 0))
        r.ha[:, i] = hidden.astype(BF16).reshape(4, 64, WIDTH)
        r.sa[:, i] = slope.astype(BF16).reshape(4, 64, WIDTH)

    upper_of(0)
    sent_on = []
    for i in pair:
        arrive(got[i])
        at = slice(i * 256, (i + 1) * 256)
        hidden, slope = gelu_both(dot(r.dn2[i], r.v_d_up[...], 1, 0))
        grad_upper = (r.dgh[at, :] * slope).astype(BF16)
        r.dhid[at, :] = hidden.astype(BF16)
        r.dgu[at, :] = grad_upper
        r.s4[i] = dot(grad_upper, r.v_d_up[...], 1, 1).astype(BF16)
        sent_on.append(scatter(r.s4.at[i], r.r4.at[i], ROWS))

    def dec_weights(left, right, own, away, first):
        size = right.shape[1]
        for a in (0, 1):
            rows = pl.ds(pl.multiple_of(lax.rem(s + a, 2) * 256, 256), 256)
            value = dot(left[:, rows], right[...], 0, 0)
            if a == 0:
                own[:, first : first + size] = value
            else:
                away[:, first : first + size] = value.astype(BF16)

    def dec_sums(own, arrived, away, landing):
        for block in range(4):
            at = slice(block * 64, (block + 1) * 64)
            own[at, :] = own[at, :] + arrived[at, :].astype(F32)
            away[block] = own[at, :].astype(BF16)
        return [send(away.at[data(k)], landing.at[k - 1], {"dp": data(k)}) for k in (1, 2, 3)]

    dec_weights(r.dn2.reshape(512, 512), r.dgu, r.w1o, r.w1s, 0)
    dec_weights(r.dgf.reshape(512, 512), r.dhid, r.w1o, r.w1s, 512)
    got_w1 = [send(r.w1s, r.w1r, to_plane(1, 0))]
    r.vec[...] = jnp.zeros((8, 512), F32)
    got = []
    gain_sum = jnp.zeros((1, 512), F32)
    for i in pair:
        arrive(sent_on[i])
        total = summed(r.s4.at[i], r.r4.at[i], ROWS)
        normal, inverse = norm_rows(r.dmid[i])
        grad = r.dgf[i, own64, :].astype(F32) + rows_back(normal, inverse, d_g2, total)
        gain_sum += jnp.sum(total * normal, axis=0, keepdims=True)
        r.dgm[i, own64, :] = grad.astype(BF16)
        got.append(gather(r.dgm.at[i], ROWS))
    r.vec[5:6, :] = gain_sum
    shard = lax.broadcasted_iota(jnp.int32, (256, 1), 0) // ROWS
    here = (shard == m).astype(F32)
    parts = []
    for i in pair:
        whole = jnp.concatenate([r.dmid[i]] * 4, axis=0)
        value = dot(r.dhid[i * 256 : (i + 1) * 256, :], r.v_d_down[...], 1, 1)
        parts.append(value + whole * here)
    for block in range(8):
        at = slice(block * 64, (block + 1) * 64)
        r.ds[block] = jnp.concatenate([parts[0][:, at], parts[1][:, at]], axis=1).astype(BF16)
    arrive(got_seen)
    arrive(got_k)

    def probs_of(k):
        for i in pair:
            keep = lax.broadcasted_iota(jnp.int32, (1, SLOTS), 1) < r.seen[data(k), 4 * i, 0:1].reshape(1, 1)
            r.pz[k - 1, i] = probabilities(r.kz[data(k), i], keep, 256, HEAD, e_scale)

    arrive(got_w1)
    got_z1 = dec_sums(r.w1o, r.w1r, r.z1s, r.z1r)

    gain_sum = jnp.zeros((1, 512), F32)
    token_sum = jnp.zeros((1, 512), F32)
    sent_on = []
    for i in pair:
        arrive(got[i])
        if i == 0:
            got_nm.append(relay(r.nz, 1))
        at = slice(i * 256, (i + 1) * 256)
        grad_low = r.dgm[i]
        grad_context = dot(grad_low, r.v_d_out[...], 1, 0).astype(BF16)
        part = attention_back(
            r.dqkv[at, :], r.dprobs[i], grad_context, 256, 128, DEC_HEAD, d_scale
        )
        r.dgq[at, :] = part
        terms = dot(part, r.v_d_qkv[...], 1, 1)
        normal, inverse = norm_rows(r.grid[i])
        gain_sum += jnp.sum(terms * normal, axis=0, keepdims=True)
        back = rows_back(normal, inverse, d_g1, terms) + 0.25 * grad_low.astype(F32)
        token_sum += jnp.sum(back * r.free[i], axis=0, keepdims=True)
        r.s5[i] = dot(r.hot[i], back.astype(BF16), 0, 0).astype(BF16)
        sent_on.append(scatter(r.s5.at[i], r.r5.at[i], SHARD))
    r.vec[4:5, :] = gain_sum
    r.vec[6:7, :] = token_sum

    def put_back(i):
        r.sz[d, place, m] = r.sg[i]

    back = exchange(
        lambda i: r.sg.at[i], lambda i, at: r.sz.at[to_dp(), i, at], put_back
    )
    for i in pair:
        arrive(sent_on[i])
        r.sg[i] = summed(r.s5.at[i], r.r5.at[i], SHARD).astype(BF16)
        back.start(i)
    got_dec = []
    for a, k in plane:
        to = lax.rem(s + a, 2) * 4 + model(k)
        got_dec.append(send(r.ds.at[to], r.dr.at[rank], to_plane(a, k)))
    r.dr[rank] = r.ds[rank]
    dec_weights(r.dn1, r.dgq, r.w2o, r.w2s, 0)
    dec_weights(r.dgm.reshape(512, 512), r.dctx, r.w2o, r.w2s, 384)
    got_w2 = [send(r.w2s, r.w2r, to_plane(1, 0))]
    upper_of(1)
    probs_of(1)

    sent_on = []
    for i in pair:
        back.landed(i)
        grad_low = dot(r.sz[d, i].reshape(64, 512), r.v_w_proj[...], 1, 1).astype(BF16)
        grad_upper = (dot(grad_low, r.v_w_down[...], 1, 0) * r.gp[i]).astype(BF16)
        r.s6[i] = dot(grad_upper, r.v_w_up[...], 1, 1).astype(BF16)
        sent_on.append(scatter(r.s6.at[i], r.r6.at[i], SHARD))
    got_sz = [
        send(r.sz.at[d, :, m], r.sz.at[d, :, m], {"dp": data(k)}) for k in (1, 2, 3)
    ]
    probs_of(2)
    arrive(got_w2)
    got_z2 = dec_sums(r.w2o, r.w2r, r.z2s, r.z2r)
    got = []
    gain_two = jnp.zeros((1, WIDTH), F32)
    for i in pair:
        arrive(sent_on[i])
        total = summed(r.s6.at[i], r.r6.at[i], SHARD)
        normal, inverse = norm_rows(r.mid[i])
        own_grad = dot(r.sz[d, i, m], r.v_w_proj[...], 1, 1)
        grad = own_grad + rows_back(normal, inverse, e_g2, total)
        gain_two += jnp.sum(total * normal, axis=0, keepdims=True)
        r.gm[i, own16, :] = grad.astype(BF16)
        got.append(gather(r.gm.at[i], SHARD))
    r.vec[2:3, :] = gain_two[:, :512]
    r.vec[3:4, :] = gain_two[:, 512:]
    probs_of(3)
    back.left()
    arrive(got_sz)
    got_sm = relay(r.sz, 0) + relay(r.sz, 1)
    gain_one = jnp.zeros((1, WIDTH), F32)
    got_f, got_q = [], []
    for i in pair:
        arrive(got[i])
        if i == 1:
            block_columns(1, [r.gm[0], r.gm[1]])
            got_x4 = send_columns(1)
        grad_low = r.gm[i]
        grad_context = dot(grad_low, r.v_w_out[...], 1, 0).astype(BF16)
        r.gz[d, i] = grad_context
        got_q += [send(r.gz.at[d, i], r.gz.at[d, i], {"dp": data(k)}) for k in (1, 2, 3)]
        part = attention_back(r.kz[d, i], r.probs[i], grad_context, 64, 256, HEAD, e_scale)
        r.qa[d, i] = part
        terms = dot(part, r.v_w_qkv[...], 1, 1)
        normal, inverse = norm_rows(r.xf[i].astype(F32))
        gain_one += jnp.sum(terms * normal, axis=0, keepdims=True)
        grad = rows_back(normal, inverse, e_g1, terms) + 0.25 * grad_low.astype(F32)
        for block in range(8):
            r.fs[block, i] = grad[:, block * 128 : (block + 1) * 128].astype(BF16)
        for a, k in plane:
            to = lax.rem(s + a, 2) * 4 + model(k)
            got_f.append(send(r.fs.at[to, i], r.fr.at[rank, i], to_plane(a, k)))
        r.fr[rank, i] = r.fs[rank, i]
    r.vec[0:1, :] = gain_one[:, :512]
    r.vec[1:2, :] = gain_one[:, 512:]
    r.vr[rank] = r.vec[...]
    got_v = [send(r.vec, r.vr.at[rank], to_plane(a, k)) for a, k in plane]

    def enc_weights(lefts, value, first, out):
        size = value.shape[1]
        r.wes[:, first : first + size] = dot(lefts[1], value, 0, 0).astype(BF16)
        made = send(
            r.wes.at[:, first : first + size], r.wer.at[:, first : first + size], to_plane(1, 0)
        )
        out[...] = dot(lefts[0], value, 0, 0)
        return made

    def cut_rows(which):
        return [r.xz[which, :, lax.rem(s + a, 2)].reshape(512, 128) for a in (0, 1)]

    arrive(got_sm)
    grad_all = r.sz[...].reshape(512, 512)
    arrive(got_ez)
    r.ps[...] = dot(r.ez[...].reshape(512, 256), grad_all, 0, 0).astype(BF16)
    got_p = [send(r.ps, r.pr, to_plane(1, 0))]

    r.ga[...] = dot(grad_all, r.v_w_proj[...], 1, 1).astype(BF16)
    grad_upper = (dot(r.ga[...], r.v_w_down[...], 1, 0) * r.sa[...].reshape(512, WIDTH).astype(F32)).astype(BF16)
    columns = []
    for a in (0, 1):
        block = lax.rem(s + a, 2) * 4 + d
        columns.append(pl.ds(pl.multiple_of(block * 128, 128), 128))
    lefts = [r.ga[:, at] for at in columns]
    arrive(got_p)
    half_rows = pl.ds(pl.multiple_of(s * 128, 128), 128)
    r.pa[m, s] = (r.ps[half_rows, :].astype(F32) + r.pr[half_rows, :].astype(F32)).astype(BF16)
    got_pa = [send(r.pa.at[m, s], r.pa.at[m, s], {"mp": model(k)}) for k in (1, 2, 3)]
    got_w = [enc_weights(lefts, r.ha[...].reshape(512, WIDTH), 2048, r.v_o_down)]
    lefts = [r.nz[:, :, :, :, at].reshape(512, 128) for at in columns]
    got_w.append(enc_weights(lefts, grad_upper, 1024, r.v_o_up))

    arrive(got_q)
    for k in (1, 2, 3):
        for i in pair:
            at = data(k)
            r.qa[at, i] = attention_back(
                r.kz[at, i], r.pz[k - 1, i], r.gz[at, i], 64, 256, HEAD, e_scale
            )
    arrive(got_z1)
    mine64 = pl.ds(pl.multiple_of(d * 64, 64), 64)
    total = r.w1o[mine64, :]
    for k in range(3):
        total = total + r.z1r[k].astype(F32)
    r.v_o_dup[...] = total[:, :512]
    r.v_o_ddown[...] = total[:, 512:]
    store("o_dup", "o_ddown")
    arrive(got_z2)
    total = r.w2o[mine64, :]
    for k in range(3):
        total = total + r.z2r[k].astype(F32)
    for c in range(3):
        r.v_o_dqkv[c] = total[:, c * 128 : (c + 1) * 128]
    r.v_o_dout[...] = total[:, 384:]
    store("o_dqkv", "o_dout")
    arrive(got_v)
    total = r.vr[0]
    for k in range(1, 8):
        total = total + r.vr[k]
    r.vz[d] = total
    got_vz = along(r.vz)
    arrive(got_pa)
    got_ps = [send(r.pa.at[:, s], r.pa.at[:, s], to_plane(1, 0))]
    arrive(got_dec)
    token_at = padded_row(lax.broadcasted_iota(jnp.int32, (1024, 196), 1))
    row_at = lax.rem(lax.broadcasted_iota(jnp.int32, (1024, 1), 0), 256)
    kept = (row_at == token_at).astype(F32).astype(BF16)
    for a in (0, 1):
        total = dot(r.dr[4 * a : 4 * a + 4].reshape(1024, 128), kept, 0, 0)
        for i in pair:
            r.v_o_dec[PAIR * a + i] = total[i * 64 : (i + 1) * 64]
    store("o_dec")
    arrive(got_f)
    for a in (0, 1):
        total = r.fr[4 * a].astype(F32)
        for k in (1, 2, 3):
            total = total + r.fr[4 * a + k].astype(F32)
        for i in pair:
            r.o_pat[:, PAIR * a + i, :] = total[i]
    arrive(got_ps)
    for a in range(4):
        for b in range(2):
            at = a * 256 + b * 128
            r.v_o_proj[at : at + 128, :] = r.pa[a, b].astype(F32)
    store("o_proj")
    arrive(got_c)
    arrive(got_x4)
    got_w.append(enc_weights(cut_rows(1), r.cz[...].reshape(512, 256), 768, r.v_o_out))
    arrive(got_x1)
    got_w.append(enc_weights(cut_rows(0), r.qa[...].reshape(512, 768), 0, r.own_qkv))
    arrive(got_vz)
    total = r.vz[0] + r.vz[1] + r.vz[2] + r.vz[3]
    r.o_v1[...] = jnp.concatenate([total[0:1], total[1:2]], axis=1).reshape(WIDTH)
    r.o_v2[...] = jnp.concatenate([total[2:3], total[3:4]], axis=1).reshape(WIDTH)
    for at, out in ((4, r.o_v3), (5, r.o_v4), (6, r.o_v5)):
        out[...] = total[at : at + 1].reshape(DEC_WIDTH)
    firsts = [(2048, 1024), (1024, 1024), (768, 256), (0, 768)]
    names = ["o_down", "o_up", "o_out", "o_qkv"]
    for made, (first, size), name in zip(got_w, firsts, names):
        arrive([made])
        more = r.wer[:, first : first + size].astype(F32)
        if name == "o_qkv":
            for c in range(3):
                at = slice(c * 256, (c + 1) * 256)
                r.v_o_qkv[c] = r.own_qkv[:, at] + more[:, at]
        else:
            out = getattr(r, "v_" + name)
            out[...] = out[...] + more
        store(name)
    for made in stores:
        made.wait()
    assert used[0] <= COPIES


def with_kernel(
    patches,
    counts,
    patch_index,
    scale_level,
    enc_gain_one,
    enc_qkv,
    enc_out,
    enc_gain_two,
    enc_up,
    enc_down,
    w_proj,
    mask_token,
    pos_table,
    dec_gain_one,
    dec_qkv,
    dec_out,
    dec_gain_two,
    dec_up,
    dec_down,
    decoded_grad,
):
    inputs = (
        patches,
        counts,
        patch_index.T,
        scale_level,
        enc_gain_one,
        enc_gain_two,
        dec_gain_one,
        dec_gain_two,
        mask_token,
        decoded_grad,
        jnp.swapaxes(enc_qkv, 0, 1),
        enc_out,
        enc_up,
        enc_down,
        w_proj,
        jnp.swapaxes(pos_table, 0, 1),
        jnp.swapaxes(dec_qkv, 0, 1),
        dec_out,
        dec_up,
        dec_down,
    )
    shapes = dict(STORED, o_pat=(SLOTS, 4, 128), o_v1=(WIDTH,), o_v2=(WIDTH,))
    shapes.update(o_v3=(DEC_WIDTH,), o_v4=(DEC_WIDTH,), o_v5=(DEC_WIDTH,))
    shapes = [jax.ShapeDtypeStruct(shapes[name], F32) for name in OUT_NAMES]
    vmem = pl.BlockSpec(memory_space=pltpu.VMEM)
    smem = pl.BlockSpec(memory_space=pltpu.SMEM)
    hbm = pl.BlockSpec(memory_space=pl.ANY)
    outs = pl.pallas_call(
        kernel,
        out_shape=shapes,
        in_specs=[vmem, smem, vmem, smem] + [vmem] * 6 + [hbm] * len(LOADED),
        out_specs=[hbm if name in STORED else vmem for name in OUT_NAMES],
        scratch_shapes=[pltpu.VMEM(shape, kind) for shape, kind in BUFFERS.values()]
        + [pltpu.VMEM(shape, BF16) for shape in LOADED.values()]
        + [pltpu.VMEM(shape, F32) for shape in STORED.values()]
        + [
            pltpu.SemaphoreType.DMA((len(LOADED) + 4,)),
            pltpu.SemaphoreType.DMA((len(STORED),)),
            pltpu.SemaphoreType.DMA((COPIES,)),
            pltpu.SemaphoreType.DMA((COPIES,)),
        ],
        compiler_params=pltpu.CompilerParams(
            collective_id=0, has_side_effects=True, vmem_limit_bytes=60 * 2**20
        ),
        name="layer_pair",
    )(*inputs)
    outs = list(
        pl.pallas_call(
            hand_over,
            out_shape=shapes,
            in_specs=[hbm] * len(shapes),
            out_specs=[hbm] * len(shapes),
            scratch_shapes=[pltpu.VMEM(shape.shape, F32) for shape in shapes]
            + [pltpu.SemaphoreType.DMA((len(shapes),))] * 2,
            compiler_params=pltpu.CompilerParams(vmem_limit_bytes=60 * 2**20),
            name="hand_over",
        )(*outs)
    )
    outs[0] = jnp.transpose(outs[0], (2, 0, 1))
    outs[2] = jnp.swapaxes(outs[2], 0, 1)
    outs[6] = jnp.swapaxes(outs[6], 0, 1)
    return tuple(outs)


def hand_over(*refs):
    count = len(OUT_NAMES)
    given, returned, held = (refs[i * count : (i + 1) * count] for i in range(3))
    come, go = refs[3 * count :]
    arriving = [pltpu.make_async_copy(given[i], held[i], come.at[i]) for i in range(count)]
    leaving = [pltpu.make_async_copy(held[i], returned[i], go.at[i]) for i in range(count)]
    for made in arriving:
        made.start()
    for first, second in zip(arriving, leaving):
        first.wait()
        second.start()
    for made in leaving:
        made.wait()


def fits_kernel(mesh, shapes):
    ways = (mesh.shape["section"], mesh.shape["dp"], mesh.shape["mp"])
    wanted = {0: (64, 16, 1024), 5: (1024, 3, 1024), 8: (1024, 4096), 10: (1024, 512)}
    wanted.update({12: (8, 196, 512), 14: (512, 3, 512), 17: (512, 2048), 19: (196, 16, 512)})
    return ways == (2, 4, 4) and all(shapes[i] == shape for i, shape in wanted.items())


def solution(mesh):
    def program(*arrays):
        shapes = [array.shape for array in arrays]
        body = with_kernel if fits_kernel(mesh, shapes) else on_device
        return placed_on(mesh, body)(*arrays)

    return program
```

```python
import functools
import math

import jax
import jax.numpy as jnp
from jax import lax
from jax.experimental import pallas as pl
from jax.experimental.pallas import tpu as pltpu
from jax.sharding import PartitionSpec as P

HEAD = 64
DEC_HEAD = 32


eps = 1e-06


def norm_rows(values):
    average = jnp.mean(values, axis=-1, keepdims=True)
    centered = values - average
    variance = jnp.mean(centered * centered, axis=-1, keepdims=True)
    inverse = lax.rsqrt(variance + eps)
    return (centered * inverse, inverse)


def norm_back(normal, inverse, gain_vec, gradient):
    weighted = gradient * gain_vec
    first_term = jnp.mean(weighted, axis=-1, keepdims=True)
    second_term = jnp.mean(weighted * normal, axis=-1, keepdims=True)
    return (
        inverse * (weighted - first_term - normal * second_term),
        jnp.sum(gradient * normal, axis=(0, 1)),
    )


def spread(values):
    return lax.all_gather(values, "mp", axis=0, tiled=True)


def collect(values):
    return lax.psum_scatter(values, "mp", scatter_dimension=0, tiled=True)


def spare_of(work):
    return lambda: jax.tree.map(jnp.zeros_like, work())


def head_view(qkv_rows, head_size):
    return qkv_rows.reshape(
        qkv_rows.shape[0], qkv_rows.shape[1], 3, qkv_rows.shape[3] // head_size, head_size
    )


def score_rows(queries, key_rows, visible, head_size):
    scores = jnp.einsum(
        "sbhe,tbhe->bhst", queries, key_rows, preferred_element_type=jnp.float32
    ) * (1.0 / math.sqrt(head_size))
    return jnp.where(visible[:, None, None, :], scores, -1e30)


def attend(qkv_rows, visible, head_size):
    heads_view = head_view(qkv_rows, head_size)
    scores = score_rows(heads_view[:, :, 0], heads_view[:, :, 1], visible, head_size)
    highest = jnp.max(scores, axis=-1, keepdims=True)
    weights = jnp.exp(scores - highest)
    denominator = jnp.sum(weights, axis=-1, keepdims=True)
    probability = (weights / denominator).astype(jnp.bfloat16)
    context = jnp.einsum(
        "bhst,tbhe->sbhe", probability, heads_view[:, :, 2], preferred_element_type=jnp.float32
    )
    context = context.reshape(qkv_rows.shape[0], qkv_rows.shape[1], qkv_rows.shape[3]).astype(
        jnp.bfloat16
    )
    return (context, highest + jnp.log(denominator))


def attend_back(qkv_rows, visible, logsum, grad_context, head_size):
    heads_view = head_view(qkv_rows, head_size)
    queries = heads_view[:, :, 0]
    key_rows = heads_view[:, :, 1]
    value_rows = heads_view[:, :, 2]
    probability = jnp.exp(score_rows(queries, key_rows, visible, head_size) - logsum)
    grad_heads = grad_context.reshape(queries.shape)
    grad_values = jnp.einsum(
        "bhst,sbhe->tbhe",
        probability.astype(jnp.bfloat16),
        grad_heads,
        preferred_element_type=jnp.float32,
    )
    grad_probs = jnp.einsum(
        "sbhe,tbhe->bhst", grad_heads, value_rows, preferred_element_type=jnp.float32
    )
    row_inner = jnp.sum(grad_probs * probability, axis=-1, keepdims=True)
    grad_scores = (probability * (grad_probs - row_inner)).astype(jnp.bfloat16)
    score_scale = 1.0 / math.sqrt(head_size)
    grad_queries = (
        jnp.einsum("bhst,tbhe->sbhe", grad_scores, key_rows, preferred_element_type=jnp.float32)
        * score_scale
    )
    grad_keys = (
        jnp.einsum("bhst,sbhe->tbhe", grad_scores, queries, preferred_element_type=jnp.float32)
        * score_scale
    )
    stacked = jnp.stack([grad_queries, grad_keys, grad_values], axis=2)
    return stacked.reshape(qkv_rows.shape).astype(jnp.bfloat16)


def attention_local(normed_one, visible, w_qkv, w_out, head_size):
    qkv_rows = jnp.einsum(
        "sbw,wcf->sbcf", normed_one, w_qkv, preferred_element_type=jnp.float32
    ).astype(jnp.bfloat16)
    context, logsum = attend(qkv_rows, visible, head_size)
    mixed_terms = jnp.einsum("sbf,wf->sbw", context, w_out, preferred_element_type=jnp.float32)
    return (qkv_rows, context, logsum, mixed_terms)


def feed_local(normed_two, w_up, w_down):
    upper_in = jnp.einsum("sbw,wf->sbf", normed_two, w_up, preferred_element_type=jnp.float32)
    hidden = jax.nn.gelu(upper_in, approximate=False).astype(jnp.bfloat16)
    return (upper_in, jnp.einsum("sbf,wf->sbw", hidden, w_down, preferred_element_type=jnp.float32))


def feed_back_local(grad_full, normed_two, upper_in, w_up, w_down):
    value_out, gelu_pull = jax.vjp(
        lambda argument: jax.nn.gelu(argument, approximate=False), upper_in
    )
    hidden = value_out.astype(jnp.bfloat16)
    grad_down_w = jnp.einsum("sbw,sbf->wf", grad_full, hidden, preferred_element_type=jnp.float32)
    grad_hidden = jnp.einsum("sbw,wf->sbf", grad_full, w_down, preferred_element_type=jnp.float32)
    grad_upper = gelu_pull(grad_hidden)[0].astype(jnp.bfloat16)
    grad_up_w = jnp.einsum(
        "sbw,sbf->wf", normed_two, grad_upper, preferred_element_type=jnp.float32
    )
    grad_terms = jnp.einsum("sbf,wf->sbw", grad_upper, w_up, preferred_element_type=jnp.float32)
    return (grad_up_w, grad_down_w, grad_terms)


def attention_back_local(
    grad_full, qkv_rows, context, logsum, visible, normed_one, w_qkv, w_out, head_size
):
    grad_out_w = jnp.einsum("sbw,sbf->wf", grad_full, context, preferred_element_type=jnp.float32)
    grad_context = jnp.einsum(
        "sbw,wf->sbf", grad_full, w_out, preferred_element_type=jnp.float32
    ).astype(jnp.bfloat16)
    grad_qkv = attend_back(qkv_rows, visible, logsum, grad_context, head_size)
    grad_qkv_w = jnp.einsum(
        "sbw,sbcf->wcf", normed_one, grad_qkv, preferred_element_type=jnp.float32
    )
    grad_normed = jnp.einsum("sbcf,wcf->sbw", grad_qkv, w_qkv, preferred_element_type=jnp.float32)
    return (grad_qkv_w, grad_out_w, grad_normed)


def on_device(
    patches,
    counts,
    patch_index,
    scale_level,
    enc_gain_one,
    enc_qkv,
    enc_out,
    enc_gain_two,
    enc_up,
    enc_down,
    w_proj,
    mask_token,
    pos_table,
    dec_gain_one,
    dec_qkv,
    dec_out,
    dec_gain_two,
    dec_up,
    dec_down,
    decoded_grad,
):
    data_ways = lax.axis_size("dp")
    model_ways = lax.axis_size("mp")
    slot_rows = patches.shape[0]
    images = patches.shape[1]
    grid_rows = decoded_grad.shape[0]
    dec_width = decoded_grad.shape[2]
    slot_count = slot_rows * model_ways
    grid_count = grid_rows * model_ways
    per_peer = images // data_ways
    slot_start = lax.axis_index("mp") * slot_rows
    grid_start = lax.axis_index("mp") * grid_rows
    is_encoder = lax.axis_index("section") == 0
    visible = jnp.arange(slot_count, dtype=jnp.int32)[None, :] < counts[:, None]
    all_visible = jnp.ones((images, grid_count), dtype=bool)
    enc_g1 = enc_gain_one.astype(jnp.float32)
    enc_g2 = enc_gain_two.astype(jnp.float32)
    dec_g1 = dec_gain_one.astype(jnp.float32)
    dec_g2 = dec_gain_two.astype(jnp.float32)
    token_vec = mask_token.astype(jnp.float32)

    def on_encoder(work):
        return lax.cond(is_encoder, work, spare_of(work))

    def on_decoder(work):
        return lax.cond(is_encoder, spare_of(work), work)

    full_in = spread(patches)

    def enc_attention():
        normal_one, inverse_one = norm_rows(full_in.astype(jnp.float32))
        normed_one = (normal_one * enc_g1).astype(jnp.bfloat16)
        return attention_local(normed_one, visible, enc_qkv, enc_out, HEAD)

    enc_qkv_rows, enc_context, enc_logsum, enc_mixed_terms = on_encoder(enc_attention)
    enc_middle = patches.astype(jnp.float32) + collect(enc_mixed_terms)
    enc_normal_two, enc_inverse_two = norm_rows(enc_middle)
    enc_normed_two = spread((enc_normal_two * enc_g2).astype(jnp.bfloat16))
    enc_upper, enc_down_terms = on_encoder(lambda: feed_local(enc_normed_two, enc_up, enc_down))
    enc_out_low = (enc_middle + collect(enc_down_terms)).astype(jnp.bfloat16)

    def enc_send():
        sent_rows = jnp.einsum(
            "sbw,wf->sbf", enc_out_low, w_proj, preferred_element_type=jnp.float32
        ).astype(jnp.bfloat16)
        live_slot = (slot_start + jnp.arange(slot_rows, dtype=jnp.int32))[:, None] < counts[None, :]
        sent_index = jnp.where(live_slot, patch_index, grid_count)
        packed = (
            sent_rows.reshape(slot_rows, per_peer, data_ways, dec_width),
            sent_index.reshape(slot_rows, per_peer, data_ways),
            scale_level.reshape(1, per_peer, data_ways),
        )
        packed = tuple(
            (jnp.concatenate([jnp.zeros_like(member), member], axis=2) for member in packed)
        )
        return packed

    packed = on_encoder(enc_send)
    received = (
        lax.all_to_all(packed[0], ("section", "dp"), split_axis=2, concat_axis=1, tiled=True),
        lax.all_to_all(packed[1], ("section", "dp"), split_axis=2, concat_axis=1, tiled=True),
        lax.all_to_all(packed[2], ("section", "dp"), split_axis=2, concat_axis=1, tiled=True),
    )
    arrived = (received[0][:, :images, 0], received[1][:, :images, 0], received[2][0, :images, 0])
    arrived_rows, arrived_index, arrived_level = arrived

    def make_onehot():
        return (
            arrived_index[:, :, None] == jnp.arange(grid_count, dtype=jnp.int32)[None, None, :]
        ).astype(jnp.bfloat16)

    def dec_place():
        onehot_low = make_onehot()
        covered = jnp.transpose(jnp.sum(onehot_low.astype(jnp.float32), axis=0))
        placed = jnp.einsum(
            "sbp,sbf->pbf", onehot_low, arrived_rows, preferred_element_type=jnp.float32
        )
        return (placed - covered[:, :, None] * token_vec, covered)

    placed_terms, covered_terms = on_decoder(dec_place)
    placed_rows, covered_rows = collect((placed_terms, covered_terms))
    table_rows = lax.dynamic_slice_in_dim(pos_table, grid_start, grid_rows, 1)
    level_hot = (
        arrived_level[:, None] == jnp.arange(pos_table.shape[0], dtype=jnp.int32)[None, :]
    ).astype(jnp.bfloat16)
    position = jnp.einsum("bl,lpf->pbf", level_hot, table_rows, preferred_element_type=jnp.float32)
    grid_values = placed_rows + token_vec + position
    dec_normal_one, dec_inverse_one = norm_rows(grid_values)
    dec_normed_one = spread((dec_normal_one * dec_g1).astype(jnp.bfloat16))
    dec_qkv_rows, dec_context, dec_logsum, dec_mixed_terms = on_decoder(
        lambda: attention_local(dec_normed_one, all_visible, dec_qkv, dec_out, DEC_HEAD)
    )
    dec_middle = grid_values + collect(dec_mixed_terms)
    dec_normal_two, dec_inverse_two = norm_rows(dec_middle)
    dec_normed_two = spread((dec_normal_two * dec_g2).astype(jnp.bfloat16))

    def dec_feed():
        upper_in, down_terms = feed_local(dec_normed_two, dec_up, dec_down)
        own_rows = lax.dynamic_slice_in_dim(down_terms, grid_start, grid_rows, 0) + dec_middle
        return (upper_in, lax.dynamic_update_slice_in_dim(down_terms, own_rows, grid_start, 0))

    dec_upper, dec_summand = on_decoder(dec_feed)
    decoded = lax.psum_scatter(
        dec_summand.astype(jnp.bfloat16), ("section", "mp"), scatter_dimension=2, tiled=True
    ).astype(jnp.float32)
    dec_grad_full = spread(decoded_grad)
    dec_up_grad, dec_down_grad, dec_two_terms = on_decoder(
        lambda: feed_back_local(dec_grad_full, dec_normed_two, dec_upper, dec_up, dec_down)
    )
    dec_through, dec_gain_two_grad = norm_back(
        dec_normal_two, dec_inverse_two, dec_g2, collect(dec_two_terms)
    )
    dec_grad_middle = decoded_grad.astype(jnp.float32) + dec_through
    dec_middle_full = spread(dec_grad_middle.astype(jnp.bfloat16))
    dec_qkv_grad, dec_out_grad, dec_one_terms = on_decoder(
        lambda: attention_back_local(
            dec_middle_full,
            dec_qkv_rows,
            dec_context,
            dec_logsum,
            all_visible,
            dec_normed_one,
            dec_qkv,
            dec_out,
            DEC_HEAD,
        )
    )
    dec_inner, dec_gain_one_grad = norm_back(
        dec_normal_one, dec_inverse_one, dec_g1, collect(dec_one_terms)
    )
    grad_grid = dec_grad_middle + dec_inner
    grad_token = jnp.sum(grad_grid * (1.0 - covered_rows)[:, :, None], axis=(0, 1))
    grad_grid_full = spread(grad_grid.astype(jnp.bfloat16))

    def dec_return():
        grad_sent = jnp.einsum(
            "sbp,pbf->sbf", make_onehot(), grad_grid_full, preferred_element_type=jnp.float32
        ).astype(jnp.bfloat16)
        return jnp.concatenate([grad_sent, jnp.zeros_like(grad_sent)], axis=1)[:, :, None, :]

    back_rows = on_decoder(dec_return)
    returned = lax.all_to_all(
        back_rows, ("section", "dp"), split_axis=1, concat_axis=2, tiled=True
    )[:, :, data_ways:]
    grad_arrived = returned.reshape(slot_rows, images, dec_width)

    def enc_project_back():
        grad_proj_w = jnp.einsum(
            "sbw,sbf->wf", enc_out_low, grad_arrived, preferred_element_type=jnp.float32
        )
        grad_block = jnp.einsum(
            "sbf,wf->sbw", grad_arrived, w_proj, preferred_element_type=jnp.float32
        )
        return (grad_proj_w, grad_block)

    proj_grad, enc_grad_block = on_encoder(enc_project_back)
    enc_grad_full = spread(enc_grad_block.astype(jnp.bfloat16))
    enc_up_grad, enc_down_grad, enc_two_terms = on_encoder(
        lambda: feed_back_local(enc_grad_full, enc_normed_two, enc_upper, enc_up, enc_down)
    )
    enc_through, enc_gain_two_grad = norm_back(
        enc_normal_two, enc_inverse_two, enc_g2, collect(enc_two_terms)
    )
    enc_grad_middle = enc_grad_block + enc_through
    enc_middle_full = spread(enc_grad_middle.astype(jnp.bfloat16))

    def enc_attention_back():
        normal_one, inverse_one = norm_rows(full_in.astype(jnp.float32))
        normed_one = (normal_one * enc_g1).astype(jnp.bfloat16)
        grad_qkv_w, grad_out_w, grad_normed = attention_back_local(
            enc_middle_full,
            enc_qkv_rows,
            enc_context,
            enc_logsum,
            visible,
            normed_one,
            enc_qkv,
            enc_out,
            HEAD,
        )
        grad_inner, grad_gain_one = norm_back(normal_one, inverse_one, enc_g1, grad_normed)
        own_rows = lax.dynamic_slice_in_dim(grad_inner, slot_start, slot_rows, 0) + enc_grad_middle
        summand = lax.dynamic_update_slice_in_dim(grad_inner, own_rows, slot_start, 0)
        return (grad_qkv_w, grad_out_w, grad_gain_one, summand)

    enc_qkv_grad, enc_out_grad, enc_gain_one_grad, in_summand = on_encoder(enc_attention_back)
    patches_grad = lax.psum_scatter(
        in_summand.astype(jnp.bfloat16), ("section", "mp"), scatter_dimension=2, tiled=True
    ).astype(jnp.float32)
    enc_gain_two_grad = jnp.where(is_encoder, enc_gain_two_grad, 0.0)
    dec_gain_one_grad = jnp.where(is_encoder, 0.0, dec_gain_one_grad)
    dec_gain_two_grad = jnp.where(is_encoder, 0.0, dec_gain_two_grad)
    grad_token = jnp.where(is_encoder, 0.0, grad_token)
    sharded = (
        lax.psum_scatter(enc_qkv_grad, ("section", "dp"), scatter_dimension=0, tiled=True),
        lax.psum_scatter(enc_out_grad, ("section", "dp"), scatter_dimension=0, tiled=True),
        lax.psum_scatter(enc_up_grad, ("section", "dp"), scatter_dimension=0, tiled=True),
        lax.psum_scatter(enc_down_grad, ("section", "dp"), scatter_dimension=0, tiled=True),
        lax.psum_scatter(dec_qkv_grad, ("section", "dp"), scatter_dimension=0, tiled=True),
        lax.psum_scatter(dec_out_grad, ("section", "dp"), scatter_dimension=0, tiled=True),
        lax.psum_scatter(dec_up_grad, ("section", "dp"), scatter_dimension=0, tiled=True),
        lax.psum_scatter(dec_down_grad, ("section", "dp"), scatter_dimension=0, tiled=True),
    )
    shared = lax.psum(
        (
            proj_grad,
            enc_gain_one_grad,
            enc_gain_two_grad,
            dec_gain_one_grad,
            dec_gain_two_grad,
            grad_token,
        ),
        ("section", "dp", "mp"),
    )
    return (
        decoded,
        patches_grad,
        sharded[0],
        sharded[1],
        sharded[2],
        sharded[3],
        sharded[4],
        sharded[5],
        sharded[6],
        sharded[7],
        shared[0],
        shared[1],
        shared[2],
        shared[3],
        shared[4],
        shared[5],
    )


def placed_on(mesh, body):
    placed = (
        P("mp", "dp", None),
        P("dp"),
        P("mp", "dp"),
        P("dp"),
        P(),
        P(None, None, "mp"),
        P(None, "mp"),
        P(),
        P(None, "mp"),
        P(None, "mp"),
        P(),
        P(),
        P(),
        P(),
        P(None, None, "mp"),
        P(None, "mp"),
        P(),
        P(None, "mp"),
        P(None, "mp"),
        P("mp", "dp", None),
    )
    return jax.shard_map(
        body,
        mesh=mesh,
        in_specs=placed,
        out_specs=(
            P(None, "dp", ("section", "mp")),
            P(None, "dp", ("section", "mp")),
            P(("section", "dp"), None, "mp"),
            P(("section", "dp"), "mp"),
            P(("section", "dp"), "mp"),
            P(("section", "dp"), "mp"),
            P(("section", "dp"), None, "mp"),
            P(("section", "dp"), "mp"),
            P(("section", "dp"), "mp"),
            P(("section", "dp"), "mp"),
            P(),
            P(),
            P(),
            P(),
            P(),
            P(),
        ),
        check_vma=False,
    )


MESH = pl.DeviceIdType.MESH
F32 = jnp.float32
BF16 = jnp.bfloat16
WAYS = 4
PAIR = 2
SLOTS = 64
SHARD = 16
PATCHES = 49
ROWS = 64
WIDTH = 1024
DEC_WIDTH = 512
HEADS_HERE = 4
COPIES = 256


def padded_row(patch):
    shard = sum((patch >= k * PATCHES).astype(jnp.int32) for k in (1, 2, 3))
    return patch + (ROWS - PATCHES) * shard


def dot(left, right, left_dim, right_dim):
    return lax.dot_general(
        left, right, (((left_dim,), (right_dim,)), ((), ())), preferred_element_type=F32
    )


def rows_back(normal, inverse, gain, gradient):
    weighted = gradient * gain
    first = jnp.mean(weighted, axis=-1, keepdims=True)
    second = jnp.mean(weighted * normal, axis=-1, keepdims=True)
    return inverse * (weighted - first - normal * second)


def gelu_both(upper):
    phi = 0.5 * (1.0 + lax.erf(upper * math.sqrt(0.5)))
    density = jnp.exp(-0.5 * upper * upper) * (1.0 / math.sqrt(2.0 * math.pi))
    return upper * phi, phi + upper * density


def head_mask(width, head, kind):
    lane = lax.broadcasted_iota(jnp.int32, (1, width), 1)
    return [
        ((lane >= h * head) & (lane < (h + 1) * head)).astype(F32).astype(kind)
        for h in range(HEADS_HERE)
    ]


def stack_heads(values, masks):
    return jnp.concatenate([values * mask for mask in masks], axis=0)


def fold_heads(stacked, masks, rows):
    total = None
    for h, mask in enumerate(masks):
        part = stacked[h * rows : (h + 1) * rows] * mask
        total = part if total is None else total + part
    return total


def probabilities(qkv, keep, width, head, scale):
    queries = stack_heads(qkv[:, :width], head_mask(width, head, BF16))
    scores = dot(queries, qkv[:, width : 2 * width], 1, 1) * scale
    scores = jnp.where(keep, scores, -1e30)
    weights = jnp.exp(scores - jnp.max(scores, axis=-1, keepdims=True))
    return weights * (1.0 / jnp.sum(weights, axis=-1, keepdims=True))


def attention(qkv, keep, rows, width, head, scale):
    probs = probabilities(qkv, keep, width, head, scale)
    mixed = dot(probs.astype(BF16), qkv[:, 2 * width :], 1, 0)
    return probs, fold_heads(mixed, head_mask(width, head, F32), rows).astype(BF16)


def attention_back(qkv, probs, grad_context, rows, width, head, scale):
    low = head_mask(width, head, BF16)
    wide = head_mask(width, head, F32)
    queries = stack_heads(qkv[:, :width], low)
    grads = stack_heads(grad_context, low)
    grad_probs = dot(grads, qkv[:, 2 * width :], 1, 1)
    inner = jnp.sum(grad_probs * probs, axis=-1, keepdims=True)
    grad_scores = (probs * (grad_probs - inner)).astype(BF16)
    grad_queries = fold_heads(dot(grad_scores, qkv[:, width : 2 * width], 1, 0), wide, rows) * scale
    grad_keys = dot(grad_scores, queries, 0, 0) * scale
    grad_values = dot(probs.astype(BF16), grads, 0, 0)
    return jnp.concatenate([grad_queries, grad_keys, grad_values], axis=1).astype(BF16)


IN_NAMES = [
    "xs",
    "counts",
    "index",
    "levels",
    "g1",
    "g2",
    "g3",
    "g4",
    "g5",
    "dgrad",
    "w_qkv",
    "w_out",
    "w_up",
    "w_down",
    "w_proj",
    "table",
    "d_qkv",
    "d_out",
    "d_up",
    "d_down",
]
OUT_NAMES = [
    "o_dec",
    "o_pat",
    "o_qkv",
    "o_out",
    "o_up",
    "o_down",
    "o_dqkv",
    "o_dout",
    "o_dup",
    "o_ddown",
    "o_proj",
    "o_v1",
    "o_v2",
    "o_v3",
    "o_v4",
    "o_v5",
]
LOADED = dict(
    w_qkv=(WIDTH, 768),
    w_out=(WIDTH, 256),
    w_up=(WIDTH, 1024),
    w_down=(WIDTH, 1024),
    w_proj=(WIDTH, DEC_WIDTH),
    table=(196, 8, DEC_WIDTH),
    d_qkv=(DEC_WIDTH, 384),
    d_out=(DEC_WIDTH, 128),
    d_up=(DEC_WIDTH, 512),
    d_down=(DEC_WIDTH, 512),
)
STORED = dict(
    o_dec=(4, 64, 196),
    o_qkv=(3, 128, 256),
    o_out=(128, 256),
    o_up=(128, 1024),
    o_down=(128, 1024),
    o_dqkv=(3, 64, 128),
    o_dout=(64, 128),
    o_dup=(64, 512),
    o_ddown=(64, 512),
    o_proj=(1024, 512),
)
BUFFERS = dict(
    info=((2, 8, 128), jnp.int32),
    flat=((1568, 512), BF16),
    xf=((2, 64, 1024), BF16),
    probs=((2, 256, 64), F32),
    s1=((2, 64, 1024), BF16),
    r1=((2, 3, 16, 1024), BF16),
    mid=((2, 16, 1024), F32),
    n2=((2, 64, 1024), BF16),
    gp=((2, 64, 1024), F32),
    s2=((2, 64, 1024), BF16),
    r2=((2, 3, 16, 1024), BF16),
    eo=((2, 16, 1024), BF16),
    sent=((2, 16, 512), BF16),
    arr=((2, 64, 512), BF16),
    meta=((2, 4, 8, 128), jnp.int32),
    dgf=((2, 256, 512), BF16),
    hot=((2, 256, 64), BF16),
    free=((2, 256, 1), F32),
    grid=((2, 256, 512), F32),
    dn1=((512, 512), BF16),
    dqkv=((512, 384), BF16),
    dprobs=((2, 1024, 256), F32),
    dctx=((512, 128), BF16),
    s3=((2, 256, 512), BF16),
    r3=((2, 3, 64, 512), BF16),
    dmid=((2, 64, 512), F32),
    dn2=((2, 256, 512), BF16),
    dhid=((512, 512), BF16),
    dgh=((512, 512), F32),
    dgu=((512, 512), BF16),
    s4=((2, 256, 512), BF16),
    r4=((2, 3, 64, 512), BF16),
    ds=((8, 256, 128), BF16),
    dr=((8, 256, 128), BF16),
    dgm=((2, 256, 512), BF16),
    dgq=((512, 384), BF16),
    s5=((2, 64, 512), BF16),
    r5=((2, 3, 16, 512), BF16),
    sg=((2, 16, 512), BF16),
    w1s=((256, 1024), BF16),
    w1r=((256, 1024), BF16),
    w1o=((256, 1024), F32),
    z1s=((4, 64, 1024), BF16),
    z1r=((3, 64, 1024), BF16),
    w2s=((256, 512), BF16),
    w2r=((256, 512), BF16),
    w2o=((256, 512), F32),
    z2s=((4, 64, 512), BF16),
    z2r=((3, 64, 512), BF16),
    s6=((2, 64, 1024), BF16),
    r6=((2, 3, 16, 1024), BF16),
    gm=((2, 64, 1024), BF16),
    fs=((8, 2, 64, 128), BF16),
    fr=((8, 2, 64, 128), BF16),
    cz=((4, 2, 64, 256), BF16),
    nz=((4, 2, 4, 16, 1024), BF16),
    kz=((4, 2, 64, 768), BF16),
    gz=((4, 2, 64, 256), BF16),
    qa=((4, 2, 64, 768), BF16),
    pz=((3, 2, 256, 64), F32),
    seen=((4, 8, 128), jnp.int32),
    ez=((4, 2, 64, 256), BF16),
    sz=((4, 2, 4, 16, 512), BF16),
    xb=((2, 2, 4, 2, 64, 128), BF16),
    xz=((2, 4, 2, 2, 64, 128), BF16),
    ha=((4, 2, 64, 1024), BF16),
    sa=((4, 2, 64, 1024), BF16),
    ga=((512, 1024), BF16),
    wes=((128, 3072), BF16),
    wer=((128, 3072), BF16),
    own_qkv=((128, 768), F32),
    ps=((256, 512), BF16),
    pr=((256, 512), BF16),
    pa=((4, 2, 128, 512), BF16),
    vec=((8, 512), F32),
    vr=((8, 8, 512), F32),
    vz=((4, 8, 512), F32),
)


def kind_of(name):
    return BF16 if name == "o_proj" else F32


class Refs:
    pass


def kernel(*refs):
    r = Refs()
    names = IN_NAMES + OUT_NAMES + list(BUFFERS) + ["v_" + n for n in (*LOADED, *STORED)]
    for name, ref in zip(names, refs):
        setattr(r, name, ref)
    load_sem, store_sem, send_sem, recv_sem = refs[len(names) :]
    s, d, m = (lax.axis_index(a) for a in ("section", "dp", "mp"))
    used = [0]

    def take(count):
        used[0] += count
        return used[0] - count

    def copy(src, dst, device, at, land=None):
        return pltpu.make_async_remote_copy(
            src_ref=src,
            dst_ref=dst,
            send_sem=send_sem.at[at],
            recv_sem=recv_sem.at[at if land is None else land],
            device_id=device,
            device_id_type=MESH,
        )

    def send(src, dst, device):
        made = copy(src, dst, device, take(1))
        made.start()
        return made

    def arrive(copies):
        for made in copies:
            made.wait_send()
            made.wait_recv()

    def model(k):
        return lax.rem(m + k, WAYS)

    def data(k):
        return lax.rem(d + k, WAYS)

    def gather(ref, rows):
        own = ref.at[pl.ds(pl.multiple_of(m * rows, rows), rows)]
        return [send(own, own, {"mp": model(k)}) for k in (1, 2, 3)]

    def scatter(src, dst, rows):
        copies = []
        for k in (1, 2, 3):
            to = model(k)
            part = src.at[pl.ds(pl.multiple_of(to * rows, rows), rows)]
            copies.append(send(part, dst.at[k - 1], {"mp": to}))
        return copies

    def summed(src, dst, rows):
        total = src[pl.ds(pl.multiple_of(m * rows, rows), rows), :].astype(F32)
        for k in range(3):
            total = total + dst[k].astype(F32)
        return total

    def relay(ref, i):
        copies = []
        for k in (1, 2, 3):
            part = ref.at[data(k), i, m]
            copies += [send(part, part, {"mp": model(j)}) for j in (1, 2, 3)]
        return copies

    def along(ref):
        return [send(ref.at[d], ref.at[d], {"dp": data(k)}) for k in (1, 2, 3)]

    def block_columns(which, values):
        for i, value in enumerate(values):
            for block in range(8):
                at = slice(block * 128, (block + 1) * 128)
                r.xb[which, block // 4, block % 4, i] = value[:, at]
        r.xz[which, d] = r.xb[which, :, d]

    def send_columns(which):
        return [
            send(r.xb.at[which, :, data(k)], r.xz.at[which, d], {"dp": data(k)}) for k in (1, 2, 3)
        ]

    plane = [(a, k) for a in (0, 1) for k in range(4) if (a, k) != (0, 0)]

    def to_plane(a, k):
        return {"section": lax.rem(s + a, 2), "mp": model(k)}

    half = d // 2
    place = lax.rem(d, 2)

    def across(i, k):
        return {"section": half, "dp": 2 * s + i, "mp": model(k)}

    def mine(i):
        return (half == s) & (2 * s + i == d)

    def to_dp():
        return sending[0] if sending else d

    sending = []

    class exchange:
        def __init__(self, src_of, dst_of, own):
            self.src_of, self.dst_of, self.own = src_of, dst_of, own
            self.at = take(8)

        def out(self, i, k):
            sending.append(2 * s + i)
            land = self.dst_of(place, m)
            sending.clear()
            at = self.at
            return copy(self.src_of(i), land, across(i, k), at + 4 * i + k, at + 4 * place + k)

        def come(self, i, k):
            at = self.at + 4 * i + k
            return copy(self.src_of(i), self.dst_of(i, model(4 - k)), across(i, k), at)

        def start(self, i):
            for k in (1, 2, 3):
                self.out(i, k).start()
            pl.when(jnp.logical_not(mine(i)))(self.out(i, 0).start)
            pl.when(mine(i))(functools.partial(self.own, i))

        def landed(self, i):
            pl.when(jnp.logical_not(mine(i)))(self.come(i, 0).wait_recv)
            for k in (1, 2, 3):
                self.come(i, k).wait_recv()

        def left(self):
            for i in range(PAIR):
                for k in (1, 2, 3):
                    self.out(i, k).wait_send()
                pl.when(jnp.logical_not(mine(i)))(self.out(i, 0).wait_send)

    def slot_rows(ref):
        return lambda i, at: ref.at[i, pl.ds(pl.multiple_of(at * SHARD, SHARD), SHARD)]

    def put_info(i):
        r.meta[place, m] = r.info[i]

    def put_rows(ref):
        def put(i):
            ref[place, pl.ds(pl.multiple_of(m * SHARD, SHARD), SHARD), :] = r.sent[i]

        return put

    loads = {}

    def load(name, parts):
        src, dst = getattr(r, name), getattr(r, "v_" + name)
        if not parts:
            return [(src, dst)]
        width = dst.shape[1] // parts
        return [(src.at[c], dst.at[:, c * width : (c + 1) * width]) for c in range(parts)]

    at = 0
    for name in LOADED:
        loads[name] = []
        for src, dst in load(name, 3 if name in ("w_qkv", "d_qkv") else 0):
            loads[name].append(pltpu.make_async_copy(src, dst, load_sem.at[at]))
            at += 1
        for made in loads[name]:
            made.start()

    def loaded(*which):
        for name in which:
            for made in loads[name]:
                made.wait()

    stores = []

    def store(*which):
        for name in which:
            at = list(STORED).index(name)
            made = pltpu.make_async_copy(getattr(r, "v_" + name), getattr(r, name), store_sem.at[at])
            made.start()
            stores.append(made)

    barrier = pltpu.get_barrier_semaphore()
    for a, k in plane:
        pl.semaphore_signal(barrier, inc=1, device_id=to_plane(a, k), device_id_type=MESH)
    for k in (1, 2, 3):
        pl.semaphore_signal(barrier, inc=1, device_id={"dp": data(k)}, device_id_type=MESH)
    for i in range(PAIR):
        for k in range(4):
            signal = functools.partial(
                pl.semaphore_signal, barrier, inc=1, device_id=across(i, k), device_id_type=MESH
            )
            if k:
                signal()
            else:
                pl.when(jnp.logical_not(mine(i)))(signal)
    pl.semaphore_wait(barrier, 7 + 3 + 8 - (half == s).astype(jnp.int32))

    e_g1, e_g2 = (g[...].astype(F32).reshape(1, WIDTH) for g in (r.g1, r.g2))
    d_g1, d_g2, token = (g[...].astype(F32).reshape(1, DEC_WIDTH) for g in (r.g3, r.g4, r.g5))

    own16 = pl.ds(pl.multiple_of(m * SHARD, SHARD), SHARD)
    own64 = pl.ds(pl.multiple_of(m * ROWS, ROWS), ROWS)
    e_scale = 1.0 / math.sqrt(HEAD)
    d_scale = 1.0 / math.sqrt(DEC_HEAD)
    other = lax.rem(s + 1, 2)
    rank = s * 4 + m
    pair = range(PAIR)

    def own_images(ref):
        values = ref[...].astype(F32)
        return [jnp.where(s == 0, values[:, i], values[:, PAIR + i]) for i in pair]

    got = []
    for i, rows in enumerate(own_images(r.xs)):
        r.xf[i, own16, :] = rows.astype(BF16)
        got.append(gather(r.xf.at[i], SHARD))
    slot = m * SHARD + lax.broadcasted_iota(jnp.int32, (1, SHARD), 1)
    r.info[...] = jnp.zeros((2, 8, 128), jnp.int32)
    for i in pair:
        patch = r.index[pl.ds(PAIR * s + i, 1), :]
        live = slot < r.counts[PAIR * s + i]
        r.info[i, 0:1, 0:SHARD] = jnp.where(live, padded_row(patch), -1)
        r.info[i, 1:2, :] = jnp.zeros((1, 128), jnp.int32) + r.levels[PAIR * s + i]
        r.info[i, 2:3, :] = jnp.zeros((1, 128), jnp.int32) + r.counts[PAIR * s + i]
    r.seen[d] = jnp.concatenate([r.info[0, 2:3, :]] * 4 + [r.info[1, 2:3, :]] * 4, axis=0)
    got_seen = along(r.seen)
    info = exchange(lambda i: r.info.at[i], lambda i, at: r.meta.at[i, at], put_info)
    for i in pair:
        info.start(i)
    for i, rows in enumerate(own_images(r.dgrad)):
        rows = jnp.concatenate([rows, jnp.zeros((ROWS - PATCHES, DEC_WIDTH), F32)], axis=0)
        r.dgf[i, own64, :] = rows.astype(BF16)
    loaded("w_qkv")
    loaded("w_out")
    sent_on = []
    contexts, normeds = [], []
    for i in pair:
        arrive(got[i])
    for i in pair:
        normal, _ = norm_rows(r.xf[i].astype(F32))
        normed = (normal * e_g1).astype(BF16)
        part = dot(normed, r.v_w_qkv[...], 1, 0).astype(BF16)
        r.kz[d, i] = part
        keep = lax.broadcasted_iota(jnp.int32, (1, SLOTS), 1) < r.counts[PAIR * s + i]
        probs, context = attention(part, keep, 64, 256, HEAD, e_scale)
        r.probs[i] = probs
        r.s1[i] = dot(context, r.v_w_out[...], 1, 1).astype(BF16)
        sent_on.append(scatter(r.s1.at[i], r.r1.at[i], SHARD))
        r.cz[d, i] = context
        normeds.append(normed)
    block_columns(0, normeds)
    got_c = along(r.cz)
    got_x1 = send_columns(0)

    row = lax.broadcasted_iota(jnp.int32, (256, 1), 0)
    is_real = lax.rem(row, ROWS) < PATCHES
    real = is_real.astype(F32)
    entry = jnp.where(is_real, (row - (ROWS - PATCHES) * (row // ROWS)) * 8, -8)

    def start_grid(i):
        info.landed(i)
        index = jnp.concatenate([r.meta[i, k, 0:1, 0:SHARD] for k in range(4)], axis=1)
        hot = (lax.broadcasted_iota(jnp.int32, (256, 64), 0) == index).astype(F32)
        free = real - jnp.sum(hot, axis=1, keepdims=True)
        r.hot[i] = hot.astype(BF16)
        r.free[i] = free
        level = r.meta[i, 0, 1:2, 0:1]
        chosen = lax.broadcasted_iota(jnp.int32, (256, 196 * 8), 1) == entry + level
        r.grid[i] = free * token + dot(chosen.astype(F32).astype(BF16), r.flat[...], 1, 0)

    loaded("table")
    r.flat[...] = r.v_table[...].astype(F32).reshape(196 * 8, DEC_WIDTH).astype(BF16)
    start_grid(0)

    got = []
    for i in pair:
        arrive(sent_on[i])
        middle = r.xf[i, own16, :].astype(F32) + summed(r.s1.at[i], r.r1.at[i], SHARD)
        r.mid[i] = middle
        normal, _ = norm_rows(middle)
        r.n2[i, own16, :] = (normal * e_g2).astype(BF16)
        got.append(gather(r.n2.at[i], SHARD))
    got_nz = [
        send(r.n2.at[:, own16], r.nz.at[d, :, m], {"dp": data(k)}) for k in (1, 2, 3)
    ]
    start_grid(1)
    loaded("w_up")
    loaded("w_down")
    loaded("w_proj")
    sent_on = []
    for i in pair:
        arrive(got[i])
        upper = dot(r.n2[i], r.v_w_up[...], 1, 0)
        hidden, slope = gelu_both(upper)
        r.gp[i] = slope
        r.s2[i] = dot(hidden.astype(BF16), r.v_w_down[...], 1, 1).astype(BF16)
        sent_on.append(scatter(r.s2.at[i], r.r2.at[i], SHARD))
    sent = exchange(lambda i: r.sent.at[i], slot_rows(r.arr), put_rows(r.arr))
    for i in pair:
        arrive(sent_on[i])
        out_low = (r.mid[i] + summed(r.s2.at[i], r.r2.at[i], SHARD)).astype(BF16)
        r.eo[i] = out_low
        r.sent[i] = dot(out_low, r.v_w_proj[...], 1, 0).astype(BF16)
        sent.start(i)
    got_dg = gather(r.dgf.at[0], ROWS) + gather(r.dgf.at[1], ROWS)
    r.ez[d, :, own16] = r.eo[:, :, pl.ds(pl.multiple_of(m * 256, 256), 256)]
    got_eo = []
    for k in (1, 2, 3):
        columns = pl.ds(pl.multiple_of(model(k) * 256, 256), 256)
        got_eo.append(send(r.eo.at[:, :, columns], r.ez.at[d, :, own16], {"mp": model(k)}))

    loaded("d_qkv")
    loaded("d_out")
    loaded("d_up")
    cols = lax.broadcasted_iota(jnp.int32, (1, 256), 1)
    d_keep = lax.rem(cols, ROWS) < PATCHES
    sent_on = []
    for i in pair:
        sent.landed(i)
    info.left()
    arrive(got_nz)
    got_nm = [relay(r.nz, 0)]
    for i in pair:
        values = r.grid[i] + dot(r.hot[i], r.arr[i], 1, 0)
        r.grid[i] = values
        normal, _ = norm_rows(values)
        normed = (normal * d_g1).astype(BF16)
        at = slice(i * 256, (i + 1) * 256)
        r.dn1[at, :] = normed
        part = dot(normed, r.v_d_qkv[...], 1, 0).astype(BF16)
        r.dqkv[at, :] = part
        probs, context = attention(part, d_keep, 256, 128, DEC_HEAD, d_scale)
        r.dprobs[i] = probs
        r.dctx[at, :] = context
        r.s3[i] = dot(context, r.v_d_out[...], 1, 1).astype(BF16)
        sent_on.append(scatter(r.s3.at[i], r.r3.at[i], ROWS))
    r.nz[d] = r.n2[...].reshape(2, 4, 16, WIDTH)
    arrive(got_eo)
    got_ez = along(r.ez)
    got_k = along(r.kz)
    got = []
    for i in pair:
        arrive(sent_on[i])
        middle = r.grid[i, own64, :] + summed(r.s3.at[i], r.r3.at[i], ROWS)
        r.dmid[i] = middle
        normal, _ = norm_rows(middle)
        r.dn2[i, own64, :] = (normal * d_g2).astype(BF16)
        got.append(gather(r.dn2.at[i], ROWS))

    sent.left()

    def upper_of(i):
        arrive(got_nm[i])
        rows = r.nz[:, i].reshape(256, WIDTH)
        hidden, slope = gelu_both(dot(rows, r.v_w_up[...], 1, 0))
        r.ha[:, i] = hidden.astype(BF16).reshape(4, 64, WIDTH)
        r.sa[:, i] = slope.astype(BF16).reshape(4, 64, WIDTH)

    arrive(got_dg)
    loaded("d_down")
    r.dgh[...] = dot(r.dgf[...].reshape(512, 512), r.v_d_down[...], 1, 0)
    upper_of(0)
    sent_on = []
    for i in pair:
        arrive(got[i])
        at = slice(i * 256, (i + 1) * 256)
        hidden, slope = gelu_both(dot(r.dn2[i], r.v_d_up[...], 1, 0))
        grad_upper = (r.dgh[at, :] * slope).astype(BF16)
        r.dhid[at, :] = hidden.astype(BF16)
        r.dgu[at, :] = grad_upper
        r.s4[i] = dot(grad_upper, r.v_d_up[...], 1, 1).astype(BF16)
        sent_on.append(scatter(r.s4.at[i], r.r4.at[i], ROWS))

    def dec_weights(left, right, own, away, first):
        size = right.shape[1]
        for a in (0, 1):
            rows = pl.ds(pl.multiple_of(lax.rem(s + a, 2) * 256, 256), 256)
            value = dot(left[:, rows], right[...], 0, 0)
            if a == 0:
                own[:, first : first + size] = value
            else:
                away[:, first : first + size] = value.astype(BF16)

    def dec_sums(own, arrived, away, landing):
        for block in range(4):
            at = slice(block * 64, (block + 1) * 64)
            own[at, :] = own[at, :] + arrived[at, :].astype(F32)
            away[block] = own[at, :].astype(BF16)
        return [send(away.at[data(k)], landing.at[k - 1], {"dp": data(k)}) for k in (1, 2, 3)]

    dec_weights(r.dn2.reshape(512, 512), r.dgu, r.w1o, r.w1s, 0)
    dec_weights(r.dgf.reshape(512, 512), r.dhid, r.w1o, r.w1s, 512)
    got_w1 = [send(r.w1s, r.w1r, to_plane(1, 0))]
    r.vec[...] = jnp.zeros((8, 512), F32)
    got = []
    gain_sum = jnp.zeros((1, 512), F32)
    for i in pair:
        arrive(sent_on[i])
        total = summed(r.s4.at[i], r.r4.at[i], ROWS)
        normal, inverse = norm_rows(r.dmid[i])
        grad = r.dgf[i, own64, :].astype(F32) + rows_back(normal, inverse, d_g2, total)
        gain_sum += jnp.sum(total * normal, axis=0, keepdims=True)
        r.dgm[i, own64, :] = grad.astype(BF16)
        got.append(gather(r.dgm.at[i], ROWS))
    r.vec[5:6, :] = gain_sum
    shard = lax.broadcasted_iota(jnp.int32, (256, 1), 0) // ROWS
    here = (shard == m).astype(F32)
    parts = []
    for i in pair:
        whole = jnp.concatenate([r.dmid[i]] * 4, axis=0)
        value = dot(r.dhid[i * 256 : (i + 1) * 256, :], r.v_d_down[...], 1, 1)
        parts.append(value + whole * here)
    for block in range(8):
        at = slice(block * 64, (block + 1) * 64)
        r.ds[block] = jnp.concatenate([parts[0][:, at], parts[1][:, at]], axis=1).astype(BF16)
    arrive(got_seen)
    arrive(got_k)

    def probs_of(k):
        for i in pair:
            keep = lax.broadcasted_iota(jnp.int32, (1, SLOTS), 1) < r.seen[data(k), 4 * i, 0:1].reshape(1, 1)
            r.pz[k - 1, i] = probabilities(r.kz[data(k), i], keep, 256, HEAD, e_scale)

    arrive(got_w1)
    got_z1 = dec_sums(r.w1o, r.w1r, r.z1s, r.z1r)

    gain_sum = jnp.zeros((1, 512), F32)
    token_sum = jnp.zeros((1, 512), F32)
    sent_on = []
    for i in pair:
        arrive(got[i])
        if i == 0:
            got_nm.append(relay(r.nz, 1))
        at = slice(i * 256, (i + 1) * 256)
        grad_low = r.dgm[i]
        grad_context = dot(grad_low, r.v_d_out[...], 1, 0).astype(BF16)
        part = attention_back(
            r.dqkv[at, :], r.dprobs[i], grad_context, 256, 128, DEC_HEAD, d_scale
        )
        r.dgq[at, :] = part
        terms = dot(part, r.v_d_qkv[...], 1, 1)
        normal, inverse = norm_rows(r.grid[i])
        back = rows_back(normal, inverse, d_g1, terms) + 0.25 * grad_low.astype(F32)
        r.s5[i] = dot(r.hot[i], back.astype(BF16), 0, 0).astype(BF16)
        sent_on.append(scatter(r.s5.at[i], r.r5.at[i], SHARD))
        gain_sum += jnp.sum(terms * normal, axis=0, keepdims=True)
        token_sum += jnp.sum(back * r.free[i], axis=0, keepdims=True)
    r.vec[4:5, :] = gain_sum
    r.vec[6:7, :] = token_sum

    def put_back(i):
        r.sz[d, place, m] = r.sg[i]

    back = exchange(
        lambda i: r.sg.at[i], lambda i, at: r.sz.at[to_dp(), i, at], put_back
    )
    for i in pair:
        arrive(sent_on[i])
        r.sg[i] = summed(r.s5.at[i], r.r5.at[i], SHARD).astype(BF16)
        back.start(i)
    got_dec = []
    for a, k in plane:
        to = lax.rem(s + a, 2) * 4 + model(k)
        got_dec.append(send(r.ds.at[to], r.dr.at[rank], to_plane(a, k)))
    r.dr[rank] = r.ds[rank]
    dec_weights(r.dn1, r.dgq, r.w2o, r.w2s, 0)
    dec_weights(r.dgm.reshape(512, 512), r.dctx, r.w2o, r.w2s, 384)
    got_w2 = [send(r.w2s, r.w2r, to_plane(1, 0))]
    upper_of(1)
    probs_of(1)

    sent_on = []
    for i in pair:
        back.landed(i)
        grad_low = dot(r.sz[d, i].reshape(64, 512), r.v_w_proj[...], 1, 1).astype(BF16)
        grad_upper = (dot(grad_low, r.v_w_down[...], 1, 0) * r.gp[i]).astype(BF16)
        r.s6[i] = dot(grad_upper, r.v_w_up[...], 1, 1).astype(BF16)
        sent_on.append(scatter(r.s6.at[i], r.r6.at[i], SHARD))
    got_sz = [
        send(r.sz.at[d, :, m], r.sz.at[d, :, m], {"dp": data(k)}) for k in (1, 2, 3)
    ]
    probs_of(2)
    arrive(got_w2)
    got_z2 = dec_sums(r.w2o, r.w2r, r.z2s, r.z2r)
    got = []
    gain_two = jnp.zeros((1, WIDTH), F32)
    for i in pair:
        arrive(sent_on[i])
        total = summed(r.s6.at[i], r.r6.at[i], SHARD)
        normal, inverse = norm_rows(r.mid[i])
        own_grad = dot(r.sz[d, i, m], r.v_w_proj[...], 1, 1)
        grad = own_grad + rows_back(normal, inverse, e_g2, total)
        gain_two += jnp.sum(total * normal, axis=0, keepdims=True)
        r.gm[i, own16, :] = grad.astype(BF16)
        got.append(gather(r.gm.at[i], SHARD))
    r.vec[2:3, :] = gain_two[:, :512]
    r.vec[3:4, :] = gain_two[:, 512:]
    probs_of(3)
    back.left()
    arrive(got_sz)
    got_sm = relay(r.sz, 0) + relay(r.sz, 1)
    arrive(got_dec)
    token_at = padded_row(lax.broadcasted_iota(jnp.int32, (1024, 196), 1))
    row_at = lax.rem(lax.broadcasted_iota(jnp.int32, (1024, 1), 0), 256)
    kept = (row_at == token_at).astype(F32).astype(BF16)
    for a in (0, 1):
        total = dot(r.dr[4 * a : 4 * a + 4].reshape(1024, 128), kept, 0, 0)
        for i in pair:
            r.v_o_dec[PAIR * a + i] = total[i * 64 : (i + 1) * 64]
    store("o_dec")
    gain_one = jnp.zeros((1, WIDTH), F32)
    got_f, got_q = [], []
    for i in pair:
        arrive(got[i])
        grad_low = r.gm[i]
        grad_context = dot(grad_low, r.v_w_out[...], 1, 0).astype(BF16)
        r.gz[d, i] = grad_context
        got_q.append([send(r.gz.at[d, i], r.gz.at[d, i], {"dp": data(k)}) for k in (1, 2, 3)])
        if i == 1:
            block_columns(1, [r.gm[0], r.gm[1]])
            got_x4 = send_columns(1)
        part = attention_back(r.kz[d, i], r.probs[i], grad_context, 64, 256, HEAD, e_scale)
        r.qa[d, i] = part
        terms = dot(part, r.v_w_qkv[...], 1, 1)
        normal, inverse = norm_rows(r.xf[i].astype(F32))
        gain_one += jnp.sum(terms * normal, axis=0, keepdims=True)
        grad = rows_back(normal, inverse, e_g1, terms) + 0.25 * grad_low.astype(F32)
        for block in range(8):
            r.fs[block, i] = grad[:, block * 128 : (block + 1) * 128].astype(BF16)
        for a, k in plane:
            to = lax.rem(s + a, 2) * 4 + model(k)
            got_f.append(send(r.fs.at[to, i], r.fr.at[rank, i], to_plane(a, k)))
        r.fr[rank, i] = r.fs[rank, i]
    r.vec[0:1, :] = gain_one[:, :512]
    r.vec[1:2, :] = gain_one[:, 512:]
    r.vr[rank] = r.vec[...]
    got_v = [send(r.vec, r.vr.at[rank], to_plane(a, k)) for a, k in plane]

    def enc_weights(lefts, value, first, out):
        size = value.shape[1]
        r.wes[:, first : first + size] = dot(lefts[1], value, 0, 0).astype(BF16)
        made = send(
            r.wes.at[:, first : first + size], r.wer.at[:, first : first + size], to_plane(1, 0)
        )
        out[...] = dot(lefts[0], value, 0, 0)
        return made

    def cut_rows(which):
        return [r.xz[which, :, lax.rem(s + a, 2)].reshape(512, 128) for a in (0, 1)]

    arrive(got_sm)
    grad_all = r.sz[...].reshape(512, 512)
    arrive(got_ez)
    r.ps[...] = dot(r.ez[...].reshape(512, 256), grad_all, 0, 0).astype(BF16)
    got_p = [send(r.ps, r.pr, to_plane(1, 0))]

    r.ga[...] = dot(grad_all, r.v_w_proj[...], 1, 1).astype(BF16)
    grad_upper = (dot(r.ga[...], r.v_w_down[...], 1, 0) * r.sa[...].reshape(512, WIDTH).astype(F32)).astype(BF16)
    columns = []
    for a in (0, 1):
        block = lax.rem(s + a, 2) * 4 + d
        columns.append(pl.ds(pl.multiple_of(block * 128, 128), 128))
    lefts = [r.ga[:, at] for at in columns]
    arrive(got_p)
    half_rows = pl.ds(pl.multiple_of(s * 128, 128), 128)
    r.pa[m, s] = (r.ps[half_rows, :].astype(F32) + r.pr[half_rows, :].astype(F32)).astype(BF16)
    got_pa = [send(r.pa.at[m, s], r.pa.at[m, s], {"mp": model(k)}) for k in (1, 2, 3)]
    got_w = [enc_weights(lefts, r.ha[...].reshape(512, WIDTH), 2048, r.v_o_down)]
    lefts = [r.nz[:, :, :, :, at].reshape(512, 128) for at in columns]
    got_w.append(enc_weights(lefts, grad_upper, 1024, r.v_o_up))

    for i in pair:
        arrive(got_q[i])
        for k in (1, 2, 3):
            at = data(k)
            r.qa[at, i] = attention_back(
                r.kz[at, i], r.pz[k - 1, i], r.gz[at, i], 64, 256, HEAD, e_scale
            )
    arrive(got_z1)
    mine64 = pl.ds(pl.multiple_of(d * 64, 64), 64)
    total = r.w1o[mine64, :]
    for k in range(3):
        total = total + r.z1r[k].astype(F32)
    r.v_o_dup[...] = total[:, :512]
    r.v_o_ddown[...] = total[:, 512:]
    store("o_dup", "o_ddown")
    arrive(got_z2)
    total = r.w2o[mine64, :]
    for k in range(3):
        total = total + r.z2r[k].astype(F32)
    for c in range(3):
        r.v_o_dqkv[c] = total[:, c * 128 : (c + 1) * 128]
    r.v_o_dout[...] = total[:, 384:]
    store("o_dqkv", "o_dout")
    arrive(got_v)
    total = r.vr[0]
    for k in range(1, 8):
        total = total + r.vr[k]
    r.vz[d] = total
    got_vz = along(r.vz)
    arrive(got_pa)
    got_ps = [send(r.pa.at[:, s], r.pa.at[:, s], to_plane(1, 0))]
    arrive(got_f)
    for a in (0, 1):
        total = r.fr[4 * a].astype(F32)
        for k in (1, 2, 3):
            total = total + r.fr[4 * a + k].astype(F32)
        for i in pair:
            r.o_pat[:, PAIR * a + i, :] = total[i]
    arrive(got_ps)
    for a in range(4):
        for b in range(2):
            at = a * 256 + b * 128
            r.v_o_proj[at : at + 128, :] = r.pa[a, b]
    store("o_proj")
    arrive(got_c)
    arrive(got_x4)
    got_w.append(enc_weights(cut_rows(1), r.cz[...].reshape(512, 256), 768, r.v_o_out))
    arrive(got_x1)
    got_w.append(enc_weights(cut_rows(0), r.qa[...].reshape(512, 768), 0, r.own_qkv))
    arrive(got_vz)
    total = r.vz[0] + r.vz[1] + r.vz[2] + r.vz[3]
    r.o_v1[...] = jnp.concatenate([total[0:1], total[1:2]], axis=1).reshape(WIDTH)
    r.o_v2[...] = jnp.concatenate([total[2:3], total[3:4]], axis=1).reshape(WIDTH)
    for at, out in ((4, r.o_v3), (5, r.o_v4), (6, r.o_v5)):
        out[...] = total[at : at + 1].reshape(DEC_WIDTH)
    firsts = [(2048, 1024), (1024, 1024), (768, 256), (0, 768)]
    names = ["o_down", "o_up", "o_out", "o_qkv"]
    for made, (first, size), name in zip(got_w, firsts, names):
        arrive([made])
        more = r.wer[:, first : first + size].astype(F32)
        if name == "o_qkv":
            for c in range(3):
                at = slice(c * 256, (c + 1) * 256)
                r.v_o_qkv[c] = r.own_qkv[:, at] + more[:, at]
        else:
            out = getattr(r, "v_" + name)
            out[...] = out[...] + more
        store(name)
    for made in stores:
        made.wait()
    assert used[0] <= COPIES


def with_kernel(
    patches,
    counts,
    patch_index,
    scale_level,
    enc_gain_one,
    enc_qkv,
    enc_out,
    enc_gain_two,
    enc_up,
    enc_down,
    w_proj,
    mask_token,
    pos_table,
    dec_gain_one,
    dec_qkv,
    dec_out,
    dec_gain_two,
    dec_up,
    dec_down,
    decoded_grad,
):
    inputs = (
        patches,
        counts,
        patch_index.T,
        scale_level,
        enc_gain_one,
        enc_gain_two,
        dec_gain_one,
        dec_gain_two,
        mask_token,
        decoded_grad,
        jnp.swapaxes(enc_qkv, 0, 1),
        enc_out,
        enc_up,
        enc_down,
        w_proj,
        jnp.swapaxes(pos_table, 0, 1),
        jnp.swapaxes(dec_qkv, 0, 1),
        dec_out,
        dec_up,
        dec_down,
    )
    shapes = dict(STORED, o_pat=(SLOTS, 4, 128), o_v1=(WIDTH,), o_v2=(WIDTH,))
    shapes.update(o_v3=(DEC_WIDTH,), o_v4=(DEC_WIDTH,), o_v5=(DEC_WIDTH,))
    given = [jax.ShapeDtypeStruct(shapes[name], kind_of(name)) for name in OUT_NAMES]
    shapes = [jax.ShapeDtypeStruct(shapes[name], F32) for name in OUT_NAMES]
    vmem = pl.BlockSpec(memory_space=pltpu.VMEM)
    smem = pl.BlockSpec(memory_space=pltpu.SMEM)
    hbm = pl.BlockSpec(memory_space=pl.ANY)
    outs = pl.pallas_call(
        kernel,
        out_shape=given,
        in_specs=[vmem, smem, vmem, smem] + [vmem] * 6 + [hbm] * len(LOADED),
        out_specs=[hbm if name in STORED else vmem for name in OUT_NAMES],
        scratch_shapes=[pltpu.VMEM(shape, kind) for shape, kind in BUFFERS.values()]
        + [pltpu.VMEM(shape, BF16) for shape in LOADED.values()]
        + [pltpu.VMEM(shape, kind_of(name)) for name, shape in STORED.items()]
        + [
            pltpu.SemaphoreType.DMA((len(LOADED) + 4,)),
            pltpu.SemaphoreType.DMA((len(STORED),)),
            pltpu.SemaphoreType.DMA((COPIES,)),
            pltpu.SemaphoreType.DMA((COPIES,)),
        ],
        compiler_params=pltpu.CompilerParams(
            collective_id=0, has_side_effects=True, vmem_limit_bytes=60 * 2**20
        ),
        name="layer_pair",
    )(*inputs)
    outs = list(
        pl.pallas_call(
            hand_over,
            out_shape=shapes,
            in_specs=[hbm] * len(shapes),
            out_specs=[hbm] * len(shapes),
            scratch_shapes=[pltpu.VMEM(shape.shape, F32) for shape in shapes]
            + [pltpu.VMEM((WIDTH, DEC_WIDTH), BF16)]
            + [pltpu.SemaphoreType.DMA((len(shapes),))] * 2,
            compiler_params=pltpu.CompilerParams(vmem_limit_bytes=60 * 2**20),
            name="hand_over",
        )(*outs)
    )
    outs[0] = jnp.transpose(outs[0], (2, 0, 1))
    outs[2] = jnp.swapaxes(outs[2], 0, 1)
    outs[6] = jnp.swapaxes(outs[6], 0, 1)
    return tuple(outs)


def hand_over(*refs):
    count = len(OUT_NAMES)
    given, returned, held = (refs[i * count : (i + 1) * count] for i in range(3))
    low, come, go = refs[3 * count :]
    wide = OUT_NAMES.index("o_proj")
    order = [wide] + [i for i in range(count) if i != wide]
    arriving, leaving = {}, {}
    for i in order:
        landing = low if i == wide else held[i]
        arriving[i] = pltpu.make_async_copy(given[i], landing, come.at[i])
        leaving[i] = pltpu.make_async_copy(held[i], returned[i], go.at[i])
        arriving[i].start()
    for i in order:
        arriving[i].wait()
        if i == wide:
            held[i][...] = low[...].astype(F32)
        leaving[i].start()
    for i in order:
        leaving[i].wait()


def fits_kernel(mesh, shapes):
    ways = (mesh.shape["section"], mesh.shape["dp"], mesh.shape["mp"])
    wanted = {0: (64, 16, 1024), 5: (1024, 3, 1024), 8: (1024, 4096), 10: (1024, 512)}
    wanted.update({12: (8, 196, 512), 14: (512, 3, 512), 17: (512, 2048), 19: (196, 16, 512)})
    return ways == (2, 4, 4) and all(shapes[i] == shape for i, shape in wanted.items())


def solution(mesh):
    def program(*arrays):
        shapes = [array.shape for array in arrays]
        body = with_kernel if fits_kernel(mesh, shapes) else on_device
        return placed_on(mesh, body)(*arrays)

    return program
```

```python
import functools
import math

import jax
import jax.numpy as jnp
from jax import lax
from jax.experimental import pallas as pl
from jax.experimental.pallas import tpu as pltpu
from jax.sharding import PartitionSpec as P

HEAD = 64
DEC_HEAD = 32


eps = 1e-06


def norm_rows(values):
    average = jnp.mean(values, axis=-1, keepdims=True)
    centered = values - average
    variance = jnp.mean(centered * centered, axis=-1, keepdims=True)
    inverse = lax.rsqrt(variance + eps)
    return (centered * inverse, inverse)


def norm_back(normal, inverse, gain_vec, gradient):
    weighted = gradient * gain_vec
    first_term = jnp.mean(weighted, axis=-1, keepdims=True)
    second_term = jnp.mean(weighted * normal, axis=-1, keepdims=True)
    return (
        inverse * (weighted - first_term - normal * second_term),
        jnp.sum(gradient * normal, axis=(0, 1)),
    )


def spread(values):
    return lax.all_gather(values, "mp", axis=0, tiled=True)


def collect(values):
    return lax.psum_scatter(values, "mp", scatter_dimension=0, tiled=True)


def spare_of(work):
    return lambda: jax.tree.map(jnp.zeros_like, work())


def head_view(qkv_rows, head_size):
    return qkv_rows.reshape(
        qkv_rows.shape[0], qkv_rows.shape[1], 3, qkv_rows.shape[3] // head_size, head_size
    )


def score_rows(queries, key_rows, visible, head_size):
    scores = jnp.einsum(
        "sbhe,tbhe->bhst", queries, key_rows, preferred_element_type=jnp.float32
    ) * (1.0 / math.sqrt(head_size))
    return jnp.where(visible[:, None, None, :], scores, -1e30)


def attend(qkv_rows, visible, head_size):
    heads_view = head_view(qkv_rows, head_size)
    scores = score_rows(heads_view[:, :, 0], heads_view[:, :, 1], visible, head_size)
    highest = jnp.max(scores, axis=-1, keepdims=True)
    weights = jnp.exp(scores - highest)
    denominator = jnp.sum(weights, axis=-1, keepdims=True)
    probability = (weights / denominator).astype(jnp.bfloat16)
    context = jnp.einsum(
        "bhst,tbhe->sbhe", probability, heads_view[:, :, 2], preferred_element_type=jnp.float32
    )
    context = context.reshape(qkv_rows.shape[0], qkv_rows.shape[1], qkv_rows.shape[3]).astype(
        jnp.bfloat16
    )
    return (context, highest + jnp.log(denominator))


def attend_back(qkv_rows, visible, logsum, grad_context, head_size):
    heads_view = head_view(qkv_rows, head_size)
    queries = heads_view[:, :, 0]
    key_rows = heads_view[:, :, 1]
    value_rows = heads_view[:, :, 2]
    probability = jnp.exp(score_rows(queries, key_rows, visible, head_size) - logsum)
    grad_heads = grad_context.reshape(queries.shape)
    grad_values = jnp.einsum(
        "bhst,sbhe->tbhe",
        probability.astype(jnp.bfloat16),
        grad_heads,
        preferred_element_type=jnp.float32,
    )
    grad_probs = jnp.einsum(
        "sbhe,tbhe->bhst", grad_heads, value_rows, preferred_element_type=jnp.float32
    )
    row_inner = jnp.sum(grad_probs * probability, axis=-1, keepdims=True)
    grad_scores = (probability * (grad_probs - row_inner)).astype(jnp.bfloat16)
    score_scale = 1.0 / math.sqrt(head_size)
    grad_queries = (
        jnp.einsum("bhst,tbhe->sbhe", grad_scores, key_rows, preferred_element_type=jnp.float32)
        * score_scale
    )
    grad_keys = (
        jnp.einsum("bhst,sbhe->tbhe", grad_scores, queries, preferred_element_type=jnp.float32)
        * score_scale
    )
    stacked = jnp.stack([grad_queries, grad_keys, grad_values], axis=2)
    return stacked.reshape(qkv_rows.shape).astype(jnp.bfloat16)


def attention_local(normed_one, visible, w_qkv, w_out, head_size):
    qkv_rows = jnp.einsum(
        "sbw,wcf->sbcf", normed_one, w_qkv, preferred_element_type=jnp.float32
    ).astype(jnp.bfloat16)
    context, logsum = attend(qkv_rows, visible, head_size)
    mixed_terms = jnp.einsum("sbf,wf->sbw", context, w_out, preferred_element_type=jnp.float32)
    return (qkv_rows, context, logsum, mixed_terms)


def feed_local(normed_two, w_up, w_down):
    upper_in = jnp.einsum("sbw,wf->sbf", normed_two, w_up, preferred_element_type=jnp.float32)
    hidden = jax.nn.gelu(upper_in, approximate=False).astype(jnp.bfloat16)
    return (upper_in, jnp.einsum("sbf,wf->sbw", hidden, w_down, preferred_element_type=jnp.float32))


def feed_back_local(grad_full, normed_two, upper_in, w_up, w_down):
    value_out, gelu_pull = jax.vjp(
        lambda argument: jax.nn.gelu(argument, approximate=False), upper_in
    )
    hidden = value_out.astype(jnp.bfloat16)
    grad_down_w = jnp.einsum("sbw,sbf->wf", grad_full, hidden, preferred_element_type=jnp.float32)
    grad_hidden = jnp.einsum("sbw,wf->sbf", grad_full, w_down, preferred_element_type=jnp.float32)
    grad_upper = gelu_pull(grad_hidden)[0].astype(jnp.bfloat16)
    grad_up_w = jnp.einsum(
        "sbw,sbf->wf", normed_two, grad_upper, preferred_element_type=jnp.float32
    )
    grad_terms = jnp.einsum("sbf,wf->sbw", grad_upper, w_up, preferred_element_type=jnp.float32)
    return (grad_up_w, grad_down_w, grad_terms)


def attention_back_local(
    grad_full, qkv_rows, context, logsum, visible, normed_one, w_qkv, w_out, head_size
):
    grad_out_w = jnp.einsum("sbw,sbf->wf", grad_full, context, preferred_element_type=jnp.float32)
    grad_context = jnp.einsum(
        "sbw,wf->sbf", grad_full, w_out, preferred_element_type=jnp.float32
    ).astype(jnp.bfloat16)
    grad_qkv = attend_back(qkv_rows, visible, logsum, grad_context, head_size)
    grad_qkv_w = jnp.einsum(
        "sbw,sbcf->wcf", normed_one, grad_qkv, preferred_element_type=jnp.float32
    )
    grad_normed = jnp.einsum("sbcf,wcf->sbw", grad_qkv, w_qkv, preferred_element_type=jnp.float32)
    return (grad_qkv_w, grad_out_w, grad_normed)


def on_device(
    patches,
    counts,
    patch_index,
    scale_level,
    enc_gain_one,
    enc_qkv,
    enc_out,
    enc_gain_two,
    enc_up,
    enc_down,
    w_proj,
    mask_token,
    pos_table,
    dec_gain_one,
    dec_qkv,
    dec_out,
    dec_gain_two,
    dec_up,
    dec_down,
    decoded_grad,
):
    data_ways = lax.axis_size("dp")
    model_ways = lax.axis_size("mp")
    slot_rows = patches.shape[0]
    images = patches.shape[1]
    grid_rows = decoded_grad.shape[0]
    dec_width = decoded_grad.shape[2]
    slot_count = slot_rows * model_ways
    grid_count = grid_rows * model_ways
    per_peer = images // data_ways
    slot_start = lax.axis_index("mp") * slot_rows
    grid_start = lax.axis_index("mp") * grid_rows
    is_encoder = lax.axis_index("section") == 0
    visible = jnp.arange(slot_count, dtype=jnp.int32)[None, :] < counts[:, None]
    all_visible = jnp.ones((images, grid_count), dtype=bool)
    enc_g1 = enc_gain_one.astype(jnp.float32)
    enc_g2 = enc_gain_two.astype(jnp.float32)
    dec_g1 = dec_gain_one.astype(jnp.float32)
    dec_g2 = dec_gain_two.astype(jnp.float32)
    token_vec = mask_token.astype(jnp.float32)

    def on_encoder(work):
        return lax.cond(is_encoder, work, spare_of(work))

    def on_decoder(work):
        return lax.cond(is_encoder, spare_of(work), work)

    full_in = spread(patches)

    def enc_attention():
        normal_one, inverse_one = norm_rows(full_in.astype(jnp.float32))
        normed_one = (normal_one * enc_g1).astype(jnp.bfloat16)
        return attention_local(normed_one, visible, enc_qkv, enc_out, HEAD)

    enc_qkv_rows, enc_context, enc_logsum, enc_mixed_terms = on_encoder(enc_attention)
    enc_middle = patches.astype(jnp.float32) + collect(enc_mixed_terms)
    enc_normal_two, enc_inverse_two = norm_rows(enc_middle)
    enc_normed_two = spread((enc_normal_two * enc_g2).astype(jnp.bfloat16))
    enc_upper, enc_down_terms = on_encoder(lambda: feed_local(enc_normed_two, enc_up, enc_down))
    enc_out_low = (enc_middle + collect(enc_down_terms)).astype(jnp.bfloat16)

    def enc_send():
        sent_rows = jnp.einsum(
            "sbw,wf->sbf", enc_out_low, w_proj, preferred_element_type=jnp.float32
        ).astype(jnp.bfloat16)
        live_slot = (slot_start + jnp.arange(slot_rows, dtype=jnp.int32))[:, None] < counts[None, :]
        sent_index = jnp.where(live_slot, patch_index, grid_count)
        packed = (
            sent_rows.reshape(slot_rows, per_peer, data_ways, dec_width),
            sent_index.reshape(slot_rows, per_peer, data_ways),
            scale_level.reshape(1, per_peer, data_ways),
        )
        packed = tuple(
            (jnp.concatenate([jnp.zeros_like(member), member], axis=2) for member in packed)
        )
        return packed

    packed = on_encoder(enc_send)
    received = (
        lax.all_to_all(packed[0], ("section", "dp"), split_axis=2, concat_axis=1, tiled=True),
        lax.all_to_all(packed[1], ("section", "dp"), split_axis=2, concat_axis=1, tiled=True),
        lax.all_to_all(packed[2], ("section", "dp"), split_axis=2, concat_axis=1, tiled=True),
    )
    arrived = (received[0][:, :images, 0], received[1][:, :images, 0], received[2][0, :images, 0])
    arrived_rows, arrived_index, arrived_level = arrived

    def make_onehot():
        return (
            arrived_index[:, :, None] == jnp.arange(grid_count, dtype=jnp.int32)[None, None, :]
        ).astype(jnp.bfloat16)

    def dec_place():
        onehot_low = make_onehot()
        covered = jnp.transpose(jnp.sum(onehot_low.astype(jnp.float32), axis=0))
        placed = jnp.einsum(
            "sbp,sbf->pbf", onehot_low, arrived_rows, preferred_element_type=jnp.float32
        )
        return (placed - covered[:, :, None] * token_vec, covered)

    placed_terms, covered_terms = on_decoder(dec_place)
    placed_rows, covered_rows = collect((placed_terms, covered_terms))
    table_rows = lax.dynamic_slice_in_dim(pos_table, grid_start, grid_rows, 1)
    level_hot = (
        arrived_level[:, None] == jnp.arange(pos_table.shape[0], dtype=jnp.int32)[None, :]
    ).astype(jnp.bfloat16)
    position = jnp.einsum("bl,lpf->pbf", level_hot, table_rows, preferred_element_type=jnp.float32)
    grid_values = placed_rows + token_vec + position
    dec_normal_one, dec_inverse_one = norm_rows(grid_values)
    dec_normed_one = spread((dec_normal_one * dec_g1).astype(jnp.bfloat16))
    dec_qkv_rows, dec_context, dec_logsum, dec_mixed_terms = on_decoder(
        lambda: attention_local(dec_normed_one, all_visible, dec_qkv, dec_out, DEC_HEAD)
    )
    dec_middle = grid_values + collect(dec_mixed_terms)
    dec_normal_two, dec_inverse_two = norm_rows(dec_middle)
    dec_normed_two = spread((dec_normal_two * dec_g2).astype(jnp.bfloat16))

    def dec_feed():
        upper_in, down_terms = feed_local(dec_normed_two, dec_up, dec_down)
        own_rows = lax.dynamic_slice_in_dim(down_terms, grid_start, grid_rows, 0) + dec_middle
        return (upper_in, lax.dynamic_update_slice_in_dim(down_terms, own_rows, grid_start, 0))

    dec_upper, dec_summand = on_decoder(dec_feed)
    decoded = lax.psum_scatter(
        dec_summand.astype(jnp.bfloat16), ("section", "mp"), scatter_dimension=2, tiled=True
    ).astype(jnp.float32)
    dec_grad_full = spread(decoded_grad)
    dec_up_grad, dec_down_grad, dec_two_terms = on_decoder(
        lambda: feed_back_local(dec_grad_full, dec_normed_two, dec_upper, dec_up, dec_down)
    )
    dec_through, dec_gain_two_grad = norm_back(
        dec_normal_two, dec_inverse_two, dec_g2, collect(dec_two_terms)
    )
    dec_grad_middle = decoded_grad.astype(jnp.float32) + dec_through
    dec_middle_full = spread(dec_grad_middle.astype(jnp.bfloat16))
    dec_qkv_grad, dec_out_grad, dec_one_terms = on_decoder(
        lambda: attention_back_local(
            dec_middle_full,
            dec_qkv_rows,
            dec_context,
            dec_logsum,
            all_visible,
            dec_normed_one,
            dec_qkv,
            dec_out,
            DEC_HEAD,
        )
    )
    dec_inner, dec_gain_one_grad = norm_back(
        dec_normal_one, dec_inverse_one, dec_g1, collect(dec_one_terms)
    )
    grad_grid = dec_grad_middle + dec_inner
    grad_token = jnp.sum(grad_grid * (1.0 - covered_rows)[:, :, None], axis=(0, 1))
    grad_grid_full = spread(grad_grid.astype(jnp.bfloat16))

    def dec_return():
        grad_sent = jnp.einsum(
            "sbp,pbf->sbf", make_onehot(), grad_grid_full, preferred_element_type=jnp.float32
        ).astype(jnp.bfloat16)
        return jnp.concatenate([grad_sent, jnp.zeros_like(grad_sent)], axis=1)[:, :, None, :]

    back_rows = on_decoder(dec_return)
    returned = lax.all_to_all(
        back_rows, ("section", "dp"), split_axis=1, concat_axis=2, tiled=True
    )[:, :, data_ways:]
    grad_arrived = returned.reshape(slot_rows, images, dec_width)

    def enc_project_back():
        grad_proj_w = jnp.einsum(
            "sbw,sbf->wf", enc_out_low, grad_arrived, preferred_element_type=jnp.float32
        )
        grad_block = jnp.einsum(
            "sbf,wf->sbw", grad_arrived, w_proj, preferred_element_type=jnp.float32
        )
        return (grad_proj_w, grad_block)

    proj_grad, enc_grad_block = on_encoder(enc_project_back)
    enc_grad_full = spread(enc_grad_block.astype(jnp.bfloat16))
    enc_up_grad, enc_down_grad, enc_two_terms = on_encoder(
        lambda: feed_back_local(enc_grad_full, enc_normed_two, enc_upper, enc_up, enc_down)
    )
    enc_through, enc_gain_two_grad = norm_back(
        enc_normal_two, enc_inverse_two, enc_g2, collect(enc_two_terms)
    )
    enc_grad_middle = enc_grad_block + enc_through
    enc_middle_full = spread(enc_grad_middle.astype(jnp.bfloat16))

    def enc_attention_back():
        normal_one, inverse_one = norm_rows(full_in.astype(jnp.float32))
        normed_one = (normal_one * enc_g1).astype(jnp.bfloat16)
        grad_qkv_w, grad_out_w, grad_normed = attention_back_local(
            enc_middle_full,
            enc_qkv_rows,
            enc_context,
            enc_logsum,
            visible,
            normed_one,
            enc_qkv,
            enc_out,
            HEAD,
        )
        grad_inner, grad_gain_one = norm_back(normal_one, inverse_one, enc_g1, grad_normed)
        own_rows = lax.dynamic_slice_in_dim(grad_inner, slot_start, slot_rows, 0) + enc_grad_middle
        summand = lax.dynamic_update_slice_in_dim(grad_inner, own_rows, slot_start, 0)
        return (grad_qkv_w, grad_out_w, grad_gain_one, summand)

    enc_qkv_grad, enc_out_grad, enc_gain_one_grad, in_summand = on_encoder(enc_attention_back)
    patches_grad = lax.psum_scatter(
        in_summand.astype(jnp.bfloat16), ("section", "mp"), scatter_dimension=2, tiled=True
    ).astype(jnp.float32)
    enc_gain_two_grad = jnp.where(is_encoder, enc_gain_two_grad, 0.0)
    dec_gain_one_grad = jnp.where(is_encoder, 0.0, dec_gain_one_grad)
    dec_gain_two_grad = jnp.where(is_encoder, 0.0, dec_gain_two_grad)
    grad_token = jnp.where(is_encoder, 0.0, grad_token)
    sharded = (
        lax.psum_scatter(enc_qkv_grad, ("section", "dp"), scatter_dimension=0, tiled=True),
        lax.psum_scatter(enc_out_grad, ("section", "dp"), scatter_dimension=0, tiled=True),
        lax.psum_scatter(enc_up_grad, ("section", "dp"), scatter_dimension=0, tiled=True),
        lax.psum_scatter(enc_down_grad, ("section", "dp"), scatter_dimension=0, tiled=True),
        lax.psum_scatter(dec_qkv_grad, ("section", "dp"), scatter_dimension=0, tiled=True),
        lax.psum_scatter(dec_out_grad, ("section", "dp"), scatter_dimension=0, tiled=True),
        lax.psum_scatter(dec_up_grad, ("section", "dp"), scatter_dimension=0, tiled=True),
        lax.psum_scatter(dec_down_grad, ("section", "dp"), scatter_dimension=0, tiled=True),
    )
    shared = lax.psum(
        (
            proj_grad,
            enc_gain_one_grad,
            enc_gain_two_grad,
            dec_gain_one_grad,
            dec_gain_two_grad,
            grad_token,
        ),
        ("section", "dp", "mp"),
    )
    return (
        decoded,
        patches_grad,
        sharded[0],
        sharded[1],
        sharded[2],
        sharded[3],
        sharded[4],
        sharded[5],
        sharded[6],
        sharded[7],
        shared[0],
        shared[1],
        shared[2],
        shared[3],
        shared[4],
        shared[5],
    )


def placed_on(mesh, body):
    placed = (
        P("mp", "dp", None),
        P("dp"),
        P("mp", "dp"),
        P("dp"),
        P(),
        P(None, None, "mp"),
        P(None, "mp"),
        P(),
        P(None, "mp"),
        P(None, "mp"),
        P(),
        P(),
        P(),
        P(),
        P(None, None, "mp"),
        P(None, "mp"),
        P(),
        P(None, "mp"),
        P(None, "mp"),
        P("mp", "dp", None),
    )
    return jax.shard_map(
        body,
        mesh=mesh,
        in_specs=placed,
        out_specs=(
            P(None, "dp", ("section", "mp")),
            P(None, "dp", ("section", "mp")),
            P(("section", "dp"), None, "mp"),
            P(("section", "dp"), "mp"),
            P(("section", "dp"), "mp"),
            P(("section", "dp"), "mp"),
            P(("section", "dp"), None, "mp"),
            P(("section", "dp"), "mp"),
            P(("section", "dp"), "mp"),
            P(("section", "dp"), "mp"),
            P(),
            P(),
            P(),
            P(),
            P(),
            P(),
        ),
        check_vma=False,
    )


MESH = pl.DeviceIdType.MESH
F32 = jnp.float32
BF16 = jnp.bfloat16
WAYS = 4
PAIR = 2
SLOTS = 64
SHARD = 16
PATCHES = 49
ROWS = 64
WIDTH = 1024
DEC_WIDTH = 512
HEADS_HERE = 4
COPIES = 256


def padded_row(patch):
    shard = sum((patch >= k * PATCHES).astype(jnp.int32) for k in (1, 2, 3))
    return patch + (ROWS - PATCHES) * shard


def dot(left, right, left_dim, right_dim):
    return lax.dot_general(
        left, right, (((left_dim,), (right_dim,)), ((), ())), preferred_element_type=F32
    )


def rows_back(normal, inverse, gain, gradient):
    weighted = gradient * gain
    first = jnp.mean(weighted, axis=-1, keepdims=True)
    second = jnp.mean(weighted * normal, axis=-1, keepdims=True)
    return inverse * (weighted - first - normal * second)


def gelu_both(upper):
    phi = 0.5 * (1.0 + lax.erf(upper * math.sqrt(0.5)))
    density = jnp.exp(-0.5 * upper * upper) * (1.0 / math.sqrt(2.0 * math.pi))
    return upper * phi, phi + upper * density


def head_mask(width, head, kind):
    lane = lax.broadcasted_iota(jnp.int32, (1, width), 1)
    return [
        ((lane >= h * head) & (lane < (h + 1) * head)).astype(F32).astype(kind)
        for h in range(HEADS_HERE)
    ]


def stack_heads(values, masks):
    return jnp.concatenate([values * mask for mask in masks], axis=0)


def fold_heads(stacked, masks, rows):
    total = None
    for h, mask in enumerate(masks):
        part = stacked[h * rows : (h + 1) * rows] * mask
        total = part if total is None else total + part
    return total


def probabilities(qkv, keep, width, head, scale):
    queries = stack_heads(qkv[:, :width], head_mask(width, head, BF16))
    scores = dot(queries, qkv[:, width : 2 * width], 1, 1) * scale
    scores = jnp.where(keep, scores, -1e30)
    weights = jnp.exp(scores - jnp.max(scores, axis=-1, keepdims=True))
    return weights * (1.0 / jnp.sum(weights, axis=-1, keepdims=True))


def attention(qkv, keep, rows, width, head, scale):
    probs = probabilities(qkv, keep, width, head, scale)
    mixed = dot(probs.astype(BF16), qkv[:, 2 * width :], 1, 0)
    return probs, fold_heads(mixed, head_mask(width, head, F32), rows).astype(BF16)


def attention_back(qkv, probs, grad_context, rows, width, head, scale):
    low = head_mask(width, head, BF16)
    wide = head_mask(width, head, F32)
    queries = stack_heads(qkv[:, :width], low)
    grads = stack_heads(grad_context, low)
    grad_probs = dot(grads, qkv[:, 2 * width :], 1, 1)
    inner = jnp.sum(grad_probs * probs, axis=-1, keepdims=True)
    grad_scores = (probs * (grad_probs - inner)).astype(BF16)
    grad_queries = fold_heads(dot(grad_scores, qkv[:, width : 2 * width], 1, 0), wide, rows) * scale
    grad_keys = dot(grad_scores, queries, 0, 0) * scale
    grad_values = dot(probs.astype(BF16), grads, 0, 0)
    return jnp.concatenate([grad_queries, grad_keys, grad_values], axis=1).astype(BF16)


IN_NAMES = [
    "xs",
    "counts",
    "index",
    "levels",
    "g1",
    "g2",
    "g3",
    "g4",
    "g5",
    "dgrad",
    "w_qkv",
    "w_out",
    "w_up",
    "w_down",
    "w_proj",
    "table",
    "d_qkv",
    "d_out",
    "d_up",
    "d_down",
]
OUT_NAMES = [
    "o_dec",
    "o_pat",
    "o_qkv",
    "o_out",
    "o_up",
    "o_down",
    "o_dqkv",
    "o_dout",
    "o_dup",
    "o_ddown",
    "o_proj",
    "o_v1",
    "o_v2",
    "o_v3",
    "o_v4",
    "o_v5",
]
LOADED = dict(
    w_qkv=(WIDTH, 768),
    w_out=(WIDTH, 256),
    w_up=(WIDTH, 1024),
    w_down=(WIDTH, 1024),
    w_proj=(WIDTH, DEC_WIDTH),
    table=(196, 8, DEC_WIDTH),
    d_qkv=(DEC_WIDTH, 384),
    d_out=(DEC_WIDTH, 128),
    d_up=(DEC_WIDTH, 512),
    d_down=(DEC_WIDTH, 512),
)
STORED = dict(
    o_dec=(4, 64, 196),
    o_qkv=(3, 128, 256),
    o_out=(128, 256),
    o_up=(128, 1024),
    o_down=(128, 1024),
    o_dqkv=(3, 64, 128),
    o_dout=(64, 128),
    o_dup=(64, 512),
    o_ddown=(64, 512),
    o_proj=(1024, 512),
)
BUFFERS = dict(
    info=((2, 8, 128), jnp.int32),
    flat=((1568, 512), BF16),
    xf=((2, 64, 1024), BF16),
    probs=((2, 256, 64), F32),
    s1=((2, 64, 1024), BF16),
    r1=((2, 3, 16, 1024), BF16),
    mid=((2, 16, 1024), F32),
    n2=((2, 64, 1024), BF16),
    gp=((2, 64, 1024), F32),
    s2=((2, 64, 1024), BF16),
    r2=((2, 3, 16, 1024), BF16),
    eo=((2, 16, 1024), BF16),
    sent=((2, 16, 512), BF16),
    arr=((2, 64, 512), BF16),
    meta=((2, 4, 8, 128), jnp.int32),
    dgf=((2, 256, 512), BF16),
    hot=((2, 256, 64), BF16),
    free=((2, 256, 1), F32),
    grid=((2, 256, 512), F32),
    dn1=((512, 512), BF16),
    dqkv=((512, 384), BF16),
    dprobs=((2, 1024, 256), F32),
    dctx=((512, 128), BF16),
    s3=((2, 256, 512), BF16),
    r3=((2, 3, 64, 512), BF16),
    dmid=((2, 64, 512), F32),
    dn2=((2, 256, 512), BF16),
    dhid=((512, 512), BF16),
    dgh=((512, 512), F32),
    dgu=((512, 512), BF16),
    s4=((2, 256, 512), BF16),
    r4=((2, 3, 64, 512), BF16),
    ds=((8, 256, 128), BF16),
    dr=((8, 256, 128), BF16),
    dgm=((2, 256, 512), BF16),
    dgq=((512, 384), BF16),
    s5=((2, 64, 512), BF16),
    r5=((2, 3, 16, 512), BF16),
    sg=((2, 16, 512), BF16),
    w1s=((256, 1024), BF16),
    w1r=((256, 1024), BF16),
    w1o=((256, 1024), F32),
    z1s=((4, 64, 1024), BF16),
    z1r=((3, 64, 1024), BF16),
    w2s=((256, 512), BF16),
    w2r=((256, 512), BF16),
    w2o=((256, 512), F32),
    z2s=((4, 64, 512), BF16),
    z2r=((3, 64, 512), BF16),
    s6=((2, 64, 1024), BF16),
    r6=((2, 3, 16, 1024), BF16),
    gm=((2, 64, 1024), BF16),
    fs=((8, 2, 64, 128), BF16),
    fr=((8, 2, 64, 128), BF16),
    cz=((4, 2, 64, 256), BF16),
    nz=((4, 2, 4, 16, 1024), BF16),
    kz=((4, 2, 64, 768), BF16),
    gz=((4, 2, 64, 256), BF16),
    qa=((4, 2, 64, 768), BF16),
    pz=((3, 2, 256, 64), F32),
    seen=((4, 8, 128), jnp.int32),
    ez=((4, 2, 64, 256), BF16),
    sz=((4, 2, 4, 16, 512), BF16),
    xb=((2, 2, 4, 2, 64, 128), BF16),
    xz=((2, 4, 2, 2, 64, 128), BF16),
    ha=((4, 2, 64, 1024), BF16),
    sa=((4, 2, 64, 1024), BF16),
    ga=((512, 1024), BF16),
    wes=((128, 3072), BF16),
    wer=((128, 3072), BF16),
    own_qkv=((128, 768), F32),
    ps=((256, 512), BF16),
    pr=((256, 512), BF16),
    pa=((4, 2, 128, 512), BF16),
    vec=((8, 512), F32),
    vr=((8, 8, 512), F32),
    vz=((4, 8, 512), F32),
)


def kind_of(name):
    return BF16 if name == "o_proj" else F32


class Refs:
    pass


def kernel(*refs):
    r = Refs()
    names = IN_NAMES + OUT_NAMES + list(BUFFERS) + ["v_" + n for n in (*LOADED, *STORED)]
    for name, ref in zip(names, refs):
        setattr(r, name, ref)
    load_sem, store_sem, send_sem, recv_sem = refs[len(names) :]
    s, d, m = (lax.axis_index(a) for a in ("section", "dp", "mp"))
    used = [0]

    def take(count):
        used[0] += count
        return used[0] - count

    def copy(src, dst, device, at, land=None):
        return pltpu.make_async_remote_copy(
            src_ref=src,
            dst_ref=dst,
            send_sem=send_sem.at[at],
            recv_sem=recv_sem.at[at if land is None else land],
            device_id=device,
            device_id_type=MESH,
        )

    def send(src, dst, device):
        made = copy(src, dst, device, take(1))
        made.start()
        return made

    def arrive(copies):
        for made in copies:
            made.wait_send()
            made.wait_recv()

    def model(k):
        return lax.rem(m + k, WAYS)

    def data(k):
        return lax.rem(d + k, WAYS)

    def gather(ref, rows):
        own = ref.at[pl.ds(pl.multiple_of(m * rows, rows), rows)]
        return [send(own, own, {"mp": model(k)}) for k in (1, 2, 3)]

    def scatter(src, dst, rows):
        copies = []
        for k in (1, 2, 3):
            to = model(k)
            part = src.at[pl.ds(pl.multiple_of(to * rows, rows), rows)]
            copies.append(send(part, dst.at[k - 1], {"mp": to}))
        return copies

    def summed(src, dst, rows):
        total = src[pl.ds(pl.multiple_of(m * rows, rows), rows), :].astype(F32)
        for k in range(3):
            total = total + dst[k].astype(F32)
        return total

    def relay(ref, i):
        copies = []
        for k in (1, 2, 3):
            part = ref.at[data(k), i, m]
            copies += [send(part, part, {"mp": model(j)}) for j in (1, 2, 3)]
        return copies

    def along(ref):
        return [send(ref.at[d], ref.at[d], {"dp": data(k)}) for k in (1, 2, 3)]

    def block_columns(which, values):
        for i, value in enumerate(values):
            for block in range(8):
                at = slice(block * 128, (block + 1) * 128)
                r.xb[which, block // 4, block % 4, i] = value[:, at]
        r.xz[which, d] = r.xb[which, :, d]

    def send_columns(which):
        return [
            send(r.xb.at[which, :, data(k)], r.xz.at[which, d], {"dp": data(k)}) for k in (1, 2, 3)
        ]

    plane = [(a, k) for a in (0, 1) for k in range(4) if (a, k) != (0, 0)]

    def to_plane(a, k):
        return {"section": lax.rem(s + a, 2), "mp": model(k)}

    half = d // 2
    place = lax.rem(d, 2)

    def across(i, k):
        return {"section": half, "dp": 2 * s + i, "mp": model(k)}

    def mine(i):
        return (half == s) & (2 * s + i == d)

    def to_dp():
        return sending[0] if sending else d

    sending = []

    class exchange:
        def __init__(self, src_of, dst_of, own):
            self.src_of, self.dst_of, self.own = src_of, dst_of, own
            self.at = take(8)

        def out(self, i, k):
            sending.append(2 * s + i)
            land = self.dst_of(place, m)
            sending.clear()
            at = self.at
            return copy(self.src_of(i), land, across(i, k), at + 4 * i + k, at + 4 * place + k)

        def come(self, i, k):
            at = self.at + 4 * i + k
            return copy(self.src_of(i), self.dst_of(i, model(4 - k)), across(i, k), at)

        def start(self, i):
            for k in (1, 2, 3):
                self.out(i, k).start()
            pl.when(jnp.logical_not(mine(i)))(self.out(i, 0).start)
            pl.when(mine(i))(functools.partial(self.own, i))

        def landed(self, i):
            pl.when(jnp.logical_not(mine(i)))(self.come(i, 0).wait_recv)
            for k in (1, 2, 3):
                self.come(i, k).wait_recv()

        def left(self):
            for i in range(PAIR):
                for k in (1, 2, 3):
                    self.out(i, k).wait_send()
                pl.when(jnp.logical_not(mine(i)))(self.out(i, 0).wait_send)

    def slot_rows(ref):
        return lambda i, at: ref.at[i, pl.ds(pl.multiple_of(at * SHARD, SHARD), SHARD)]

    def put_info(i):
        r.meta[place, m] = r.info[i]

    def put_rows(ref):
        def put(i):
            ref[place, pl.ds(pl.multiple_of(m * SHARD, SHARD), SHARD), :] = r.sent[i]

        return put

    loads = {}

    def load(name, parts):
        src, dst = getattr(r, name), getattr(r, "v_" + name)
        if not parts:
            return [(src, dst)]
        width = dst.shape[1] // parts
        return [(src.at[c], dst.at[:, c * width : (c + 1) * width]) for c in range(parts)]

    at = 0
    for name in LOADED:
        loads[name] = []
        for src, dst in load(name, 3 if name in ("w_qkv", "d_qkv") else 0):
            loads[name].append(pltpu.make_async_copy(src, dst, load_sem.at[at]))
            at += 1
        for made in loads[name]:
            made.start()

    def loaded(*which):
        for name in which:
            for made in loads[name]:
                made.wait()

    stores = []

    def store(*which):
        for name in which:
            at = list(STORED).index(name)
            made = pltpu.make_async_copy(getattr(r, "v_" + name), getattr(r, name), store_sem.at[at])
            made.start()
            stores.append(made)

    barrier = pltpu.get_barrier_semaphore()
    for a, k in plane:
        pl.semaphore_signal(barrier, inc=1, device_id=to_plane(a, k), device_id_type=MESH)
    for k in (1, 2, 3):
        pl.semaphore_signal(barrier, inc=1, device_id={"dp": data(k)}, device_id_type=MESH)
    for i in range(PAIR):
        for k in range(4):
            signal = functools.partial(
                pl.semaphore_signal, barrier, inc=1, device_id=across(i, k), device_id_type=MESH
            )
            if k:
                signal()
            else:
                pl.when(jnp.logical_not(mine(i)))(signal)
    pl.semaphore_wait(barrier, 7 + 3 + 8 - (half == s).astype(jnp.int32))

    e_g1, e_g2 = (g[...].astype(F32).reshape(1, WIDTH) for g in (r.g1, r.g2))
    d_g1, d_g2, token = (g[...].astype(F32).reshape(1, DEC_WIDTH) for g in (r.g3, r.g4, r.g5))

    own16 = pl.ds(pl.multiple_of(m * SHARD, SHARD), SHARD)
    own64 = pl.ds(pl.multiple_of(m * ROWS, ROWS), ROWS)
    e_scale = 1.0 / math.sqrt(HEAD)
    d_scale = 1.0 / math.sqrt(DEC_HEAD)
    other = lax.rem(s + 1, 2)
    rank = s * 4 + m
    pair = range(PAIR)

    def own_images(ref):
        values = ref[...].astype(F32)
        return [jnp.where(s == 0, values[:, i], values[:, PAIR + i]) for i in pair]

    got = []
    for i, rows in enumerate(own_images(r.xs)):
        r.xf[i, own16, :] = rows.astype(BF16)
        got.append(gather(r.xf.at[i], SHARD))
    slot = m * SHARD + lax.broadcasted_iota(jnp.int32, (1, SHARD), 1)
    r.info[...] = jnp.zeros((2, 8, 128), jnp.int32)
    for i in pair:
        patch = r.index[pl.ds(PAIR * s + i, 1), :]
        live = slot < r.counts[PAIR * s + i]
        r.info[i, 0:1, 0:SHARD] = jnp.where(live, padded_row(patch), -1)
        r.info[i, 1:2, :] = jnp.zeros((1, 128), jnp.int32) + r.levels[PAIR * s + i]
        r.info[i, 2:3, :] = jnp.zeros((1, 128), jnp.int32) + r.counts[PAIR * s + i]
    r.seen[d] = jnp.concatenate([r.info[0, 2:3, :]] * 4 + [r.info[1, 2:3, :]] * 4, axis=0)
    got_seen = along(r.seen)
    info = exchange(lambda i: r.info.at[i], lambda i, at: r.meta.at[i, at], put_info)
    for i in pair:
        info.start(i)
    for i, rows in enumerate(own_images(r.dgrad)):
        rows = jnp.concatenate([rows, jnp.zeros((ROWS - PATCHES, DEC_WIDTH), F32)], axis=0)
        r.dgf[i, own64, :] = rows.astype(BF16)
    loaded("w_qkv")
    loaded("w_out")
    sent_on = []
    contexts, normeds = [], []
    for i in pair:
        arrive(got[i])
    for i in pair:
        normal, _ = norm_rows(r.xf[i].astype(F32))
        normed = (normal * e_g1).astype(BF16)
        part = dot(normed, r.v_w_qkv[...], 1, 0).astype(BF16)
        r.kz[d, i] = part
        keep = lax.broadcasted_iota(jnp.int32, (1, SLOTS), 1) < r.counts[PAIR * s + i]
        probs, context = attention(part, keep, 64, 256, HEAD, e_scale)
        r.probs[i] = probs
        r.s1[i] = dot(context, r.v_w_out[...], 1, 1).astype(BF16)
        sent_on.append(scatter(r.s1.at[i], r.r1.at[i], SHARD))
        r.cz[d, i] = context
        normeds.append(normed)
    block_columns(0, normeds)
    got_c = along(r.cz)
    got_x1 = send_columns(0)

    row = lax.broadcasted_iota(jnp.int32, (256, 1), 0)
    is_real = lax.rem(row, ROWS) < PATCHES
    real = is_real.astype(F32)
    entry = jnp.where(is_real, (row - (ROWS - PATCHES) * (row // ROWS)) * 8, -8)

    def start_grid(i):
        info.landed(i)
        index = jnp.concatenate([r.meta[i, k, 0:1, 0:SHARD] for k in range(4)], axis=1)
        hot = (lax.broadcasted_iota(jnp.int32, (256, 64), 0) == index).astype(F32)
        free = real - jnp.sum(hot, axis=1, keepdims=True)
        r.hot[i] = hot.astype(BF16)
        r.free[i] = free
        level = r.meta[i, 0, 1:2, 0:1]
        chosen = lax.broadcasted_iota(jnp.int32, (256, 196 * 8), 1) == entry + level
        r.grid[i] = free * token + dot(chosen.astype(F32).astype(BF16), r.flat[...], 1, 0)

    loaded("table")
    r.flat[...] = r.v_table[...].astype(F32).reshape(196 * 8, DEC_WIDTH).astype(BF16)
    start_grid(0)

    got = []
    for i in pair:
        arrive(sent_on[i])
        middle = r.xf[i, own16, :].astype(F32) + summed(r.s1.at[i], r.r1.at[i], SHARD)
        r.mid[i] = middle
        normal, _ = norm_rows(middle)
        r.n2[i, own16, :] = (normal * e_g2).astype(BF16)
        got.append(gather(r.n2.at[i], SHARD))
    got_nz = [
        send(r.n2.at[:, own16], r.nz.at[d, :, m], {"dp": data(k)}) for k in (1, 2, 3)
    ]
    start_grid(1)
    loaded("w_up")
    loaded("w_down")
    loaded("w_proj")
    sent_on = []
    for i in pair:
        arrive(got[i])
        upper = dot(r.n2[i], r.v_w_up[...], 1, 0)
        hidden, slope = gelu_both(upper)
        r.gp[i] = slope
        r.s2[i] = dot(hidden.astype(BF16), r.v_w_down[...], 1, 1).astype(BF16)
        sent_on.append(scatter(r.s2.at[i], r.r2.at[i], SHARD))
    sent = exchange(lambda i: r.sent.at[i], slot_rows(r.arr), put_rows(r.arr))
    for i in pair:
        arrive(sent_on[i])
        out_low = (r.mid[i] + summed(r.s2.at[i], r.r2.at[i], SHARD)).astype(BF16)
        r.eo[i] = out_low
        r.sent[i] = dot(out_low, r.v_w_proj[...], 1, 0).astype(BF16)
        sent.start(i)
    got_dg = gather(r.dgf.at[0], ROWS) + gather(r.dgf.at[1], ROWS)
    r.ez[d, :, own16] = r.eo[:, :, pl.ds(pl.multiple_of(m * 256, 256), 256)]
    got_eo = []
    for k in (1, 2, 3):
        columns = pl.ds(pl.multiple_of(model(k) * 256, 256), 256)
        got_eo.append(send(r.eo.at[:, :, columns], r.ez.at[d, :, own16], {"mp": model(k)}))

    loaded("d_qkv")
    loaded("d_out")
    loaded("d_up")
    cols = lax.broadcasted_iota(jnp.int32, (1, 256), 1)
    d_keep = lax.rem(cols, ROWS) < PATCHES
    sent_on = []
    for i in pair:
        sent.landed(i)
    info.left()
    arrive(got_nz)
    got_nm = [relay(r.nz, 0)]
    for i in pair:
        values = r.grid[i] + dot(r.hot[i], r.arr[i], 1, 0)
        r.grid[i] = values
        normal, _ = norm_rows(values)
        normed = (normal * d_g1).astype(BF16)
        at = slice(i * 256, (i + 1) * 256)
        r.dn1[at, :] = normed
        part = dot(normed, r.v_d_qkv[...], 1, 0).astype(BF16)
        r.dqkv[at, :] = part
        probs, context = attention(part, d_keep, 256, 128, DEC_HEAD, d_scale)
        r.dprobs[i] = probs
        r.dctx[at, :] = context
        r.s3[i] = dot(context, r.v_d_out[...], 1, 1).astype(BF16)
        sent_on.append(scatter(r.s3.at[i], r.r3.at[i], ROWS))
    r.nz[d] = r.n2[...].reshape(2, 4, 16, WIDTH)
    arrive(got_eo)
    got_ez = along(r.ez)
    got_k = along(r.kz)
    got = []
    for i in pair:
        arrive(sent_on[i])
        middle = r.grid[i, own64, :] + summed(r.s3.at[i], r.r3.at[i], ROWS)
        r.dmid[i] = middle
        normal, _ = norm_rows(middle)
        r.dn2[i, own64, :] = (normal * d_g2).astype(BF16)
        got.append(gather(r.dn2.at[i], ROWS))

    sent.left()

    def upper_of(i):
        arrive(got_nm[i])
        rows = r.nz[:, i].reshape(256, WIDTH)
        hidden, slope = gelu_both(dot(rows, r.v_w_up[...], 1, 0))
        r.ha[:, i] = hidden.astype(BF16).reshape(4, 64, WIDTH)
        r.sa[:, i] = slope.astype(BF16).reshape(4, 64, WIDTH)

    arrive(got_dg)
    loaded("d_down")
    r.dgh[...] = dot(r.dgf[...].reshape(512, 512), r.v_d_down[...], 1, 0)
    upper_of(0)
    sent_on = []
    for i in pair:
        arrive(got[i])
        at = slice(i * 256, (i + 1) * 256)
        hidden, slope = gelu_both(dot(r.dn2[i], r.v_d_up[...], 1, 0))
        grad_upper = (r.dgh[at, :] * slope).astype(BF16)
        r.dhid[at, :] = hidden.astype(BF16)
        r.dgu[at, :] = grad_upper
        r.s4[i] = dot(grad_upper, r.v_d_up[...], 1, 1).astype(BF16)
        sent_on.append(scatter(r.s4.at[i], r.r4.at[i], ROWS))

    def dec_weights(left, right, own, away, first):
        size = right.shape[1]
        for a in (0, 1):
            rows = pl.ds(pl.multiple_of(lax.rem(s + a, 2) * 256, 256), 256)
            value = dot(left[:, rows], right[...], 0, 0)
            if a == 0:
                own[:, first : first + size] = value
            else:
                away[:, first : first + size] = value.astype(BF16)

    def dec_sums(own, arrived, away, landing):
        for block in range(4):
            at = slice(block * 64, (block + 1) * 64)
            own[at, :] = own[at, :] + arrived[at, :].astype(F32)
            away[block] = own[at, :].astype(BF16)
        return [send(away.at[data(k)], landing.at[k - 1], {"dp": data(k)}) for k in (1, 2, 3)]

    dec_weights(r.dn2.reshape(512, 512), r.dgu, r.w1o, r.w1s, 0)
    dec_weights(r.dgf.reshape(512, 512), r.dhid, r.w1o, r.w1s, 512)
    got_w1 = [send(r.w1s, r.w1r, to_plane(1, 0))]
    r.vec[...] = jnp.zeros((8, 512), F32)
    got = []
    gain_sum = jnp.zeros((1, 512), F32)
    for i in pair:
        arrive(sent_on[i])
        total = summed(r.s4.at[i], r.r4.at[i], ROWS)
        normal, inverse = norm_rows(r.dmid[i])
        grad = r.dgf[i, own64, :].astype(F32) + rows_back(normal, inverse, d_g2, total)
        gain_sum += jnp.sum(total * normal, axis=0, keepdims=True)
        r.dgm[i, own64, :] = grad.astype(BF16)
        got.append(gather(r.dgm.at[i], ROWS))
    r.vec[5:6, :] = gain_sum
    shard = lax.broadcasted_iota(jnp.int32, (256, 1), 0) // ROWS
    here = (shard == m).astype(F32)
    parts = []
    for i in pair:
        whole = jnp.concatenate([r.dmid[i]] * 4, axis=0)
        value = dot(r.dhid[i * 256 : (i + 1) * 256, :], r.v_d_down[...], 1, 1)
        parts.append(value + whole * here)
    for block in range(8):
        at = slice(block * 64, (block + 1) * 64)
        r.ds[block] = jnp.concatenate([parts[0][:, at], parts[1][:, at]], axis=1).astype(BF16)
    arrive(got_seen)
    arrive(got_k)

    def probs_of(k):
        for i in pair:
            keep = lax.broadcasted_iota(jnp.int32, (1, SLOTS), 1) < r.seen[data(k), 4 * i, 0:1].reshape(1, 1)
            r.pz[k - 1, i] = probabilities(r.kz[data(k), i], keep, 256, HEAD, e_scale)

    arrive(got_w1)
    got_z1 = dec_sums(r.w1o, r.w1r, r.z1s, r.z1r)

    gain_sum = jnp.zeros((1, 512), F32)
    token_sum = jnp.zeros((1, 512), F32)
    sent_on = []
    for i in pair:
        arrive(got[i])
        if i == 0:
            got_nm.append(relay(r.nz, 1))
        at = slice(i * 256, (i + 1) * 256)
        grad_low = r.dgm[i]
        grad_context = dot(grad_low, r.v_d_out[...], 1, 0).astype(BF16)
        part = attention_back(
            r.dqkv[at, :], r.dprobs[i], grad_context, 256, 128, DEC_HEAD, d_scale
        )
        r.dgq[at, :] = part
        terms = dot(part, r.v_d_qkv[...], 1, 1)
        normal, inverse = norm_rows(r.grid[i])
        back = rows_back(normal, inverse, d_g1, terms) + 0.25 * grad_low.astype(F32)
        r.s5[i] = dot(r.hot[i], back.astype(BF16), 0, 0).astype(BF16)
        sent_on.append(scatter(r.s5.at[i], r.r5.at[i], SHARD))
        gain_sum += jnp.sum(terms * normal, axis=0, keepdims=True)
        token_sum += jnp.sum(back * r.free[i], axis=0, keepdims=True)
    r.vec[4:5, :] = gain_sum
    r.vec[6:7, :] = token_sum

    def put_back(i):
        r.sz[d, place, m] = r.sg[i]

    back = exchange(
        lambda i: r.sg.at[i], lambda i, at: r.sz.at[to_dp(), i, at], put_back
    )
    for i in pair:
        arrive(sent_on[i])
        r.sg[i] = summed(r.s5.at[i], r.r5.at[i], SHARD).astype(BF16)
        back.start(i)
    got_dec = []
    for a, k in plane:
        to = lax.rem(s + a, 2) * 4 + model(k)
        got_dec.append(send(r.ds.at[to], r.dr.at[rank], to_plane(a, k)))
    r.dr[rank] = r.ds[rank]
    dec_weights(r.dn1, r.dgq, r.w2o, r.w2s, 0)
    dec_weights(r.dgm.reshape(512, 512), r.dctx, r.w2o, r.w2s, 384)
    got_w2 = [send(r.w2s, r.w2r, to_plane(1, 0))]
    upper_of(1)
    probs_of(1)

    sent_on = []
    for i in pair:
        back.landed(i)
        grad_low = dot(r.sz[d, i].reshape(64, 512), r.v_w_proj[...], 1, 1).astype(BF16)
        grad_upper = (dot(grad_low, r.v_w_down[...], 1, 0) * r.gp[i]).astype(BF16)
        r.s6[i] = dot(grad_upper, r.v_w_up[...], 1, 1).astype(BF16)
        sent_on.append(scatter(r.s6.at[i], r.r6.at[i], SHARD))
    got_sz = [
        send(r.sz.at[d, :, m], r.sz.at[d, :, m], {"dp": data(k)}) for k in (1, 2, 3)
    ]
    probs_of(2)
    arrive(got_w2)
    got_z2 = dec_sums(r.w2o, r.w2r, r.z2s, r.z2r)
    got = []
    gain_two = jnp.zeros((1, WIDTH), F32)
    for i in pair:
        arrive(sent_on[i])
        total = summed(r.s6.at[i], r.r6.at[i], SHARD)
        normal, inverse = norm_rows(r.mid[i])
        own_grad = dot(r.sz[d, i, m], r.v_w_proj[...], 1, 1)
        grad = own_grad + rows_back(normal, inverse, e_g2, total)
        gain_two += jnp.sum(total * normal, axis=0, keepdims=True)
        r.gm[i, own16, :] = grad.astype(BF16)
        got.append(gather(r.gm.at[i], SHARD))
    r.vec[2:3, :] = gain_two[:, :512]
    r.vec[3:4, :] = gain_two[:, 512:]
    probs_of(3)
    back.left()
    arrive(got_sz)
    got_sm = relay(r.sz, 0) + relay(r.sz, 1)
    arrive(got_dec)
    token_at = padded_row(lax.broadcasted_iota(jnp.int32, (1024, 196), 1))
    row_at = lax.rem(lax.broadcasted_iota(jnp.int32, (1024, 1), 0), 256)
    kept = (row_at == token_at).astype(F32).astype(BF16)
    for a in (0, 1):
        total = dot(r.dr[4 * a : 4 * a + 4].reshape(1024, 128), kept, 0, 0)
        for i in pair:
            r.v_o_dec[PAIR * a + i] = total[i * 64 : (i + 1) * 64]
    store("o_dec")
    gain_one = jnp.zeros((1, WIDTH), F32)
    got_f, got_q = [], []
    for i in pair:
        arrive(got[i])
        grad_low = r.gm[i]
        grad_context = dot(grad_low, r.v_w_out[...], 1, 0).astype(BF16)
        r.gz[d, i] = grad_context
        got_q.append([send(r.gz.at[d, i], r.gz.at[d, i], {"dp": data(k)}) for k in (1, 2, 3)])
        if i == 1:
            block_columns(1, [r.gm[0], r.gm[1]])
            got_x4 = send_columns(1)
        part = attention_back(r.kz[d, i], r.probs[i], grad_context, 64, 256, HEAD, e_scale)
        r.qa[d, i] = part
        terms = dot(part, r.v_w_qkv[...], 1, 1)
        normal, inverse = norm_rows(r.xf[i].astype(F32))
        gain_one += jnp.sum(terms * normal, axis=0, keepdims=True)
        grad = rows_back(normal, inverse, e_g1, terms) + 0.25 * grad_low.astype(F32)
        for block in range(8):
            r.fs[block, i] = grad[:, block * 128 : (block + 1) * 128].astype(BF16)
        for a, k in plane:
            to = lax.rem(s + a, 2) * 4 + model(k)
            got_f.append(send(r.fs.at[to, i], r.fr.at[rank, i], to_plane(a, k)))
        r.fr[rank, i] = r.fs[rank, i]
    r.vec[0:1, :] = gain_one[:, :512]
    r.vec[1:2, :] = gain_one[:, 512:]
    r.vr[rank] = r.vec[...]
    got_v = [send(r.vec, r.vr.at[rank], to_plane(a, k)) for a, k in plane]

    def enc_weights(lefts, value, first, out):
        size = value.shape[1]
        r.wes[:, first : first + size] = dot(lefts[1], value, 0, 0).astype(BF16)
        made = send(
            r.wes.at[:, first : first + size], r.wer.at[:, first : first + size], to_plane(1, 0)
        )
        out[...] = dot(lefts[0], value, 0, 0)
        return made

    def cut_rows(which):
        return [r.xz[which, :, lax.rem(s + a, 2)].reshape(512, 128) for a in (0, 1)]

    arrive(got_sm)
    grad_all = r.sz[...].reshape(512, 512)
    arrive(got_ez)
    r.ps[...] = dot(r.ez[...].reshape(512, 256), grad_all, 0, 0).astype(BF16)
    got_p = [send(r.ps, r.pr, to_plane(1, 0))]

    r.ga[...] = dot(grad_all, r.v_w_proj[...], 1, 1).astype(BF16)
    grad_upper = (dot(r.ga[...], r.v_w_down[...], 1, 0) * r.sa[...].reshape(512, WIDTH).astype(F32)).astype(BF16)
    columns = []
    for a in (0, 1):
        block = lax.rem(s + a, 2) * 4 + d
        columns.append(pl.ds(pl.multiple_of(block * 128, 128), 128))
    lefts = [r.ga[:, at] for at in columns]
    arrive(got_p)
    half_rows = pl.ds(pl.multiple_of(s * 128, 128), 128)
    r.pa[m, s] = (r.ps[half_rows, :].astype(F32) + r.pr[half_rows, :].astype(F32)).astype(BF16)
    got_pa = [send(r.pa.at[m, s], r.pa.at[m, s], {"mp": model(k)}) for k in (1, 2, 3)]
    got_w = [enc_weights(lefts, r.ha[...].reshape(512, WIDTH), 2048, r.v_o_down)]
    lefts = [r.nz[:, :, :, :, at].reshape(512, 128) for at in columns]
    got_w.append(enc_weights(lefts, grad_upper, 1024, r.v_o_up))

    for i in pair:
        arrive(got_q[i])
        for k in (1, 2, 3):
            at = data(k)
            r.qa[at, i] = attention_back(
                r.kz[at, i], r.pz[k - 1, i], r.gz[at, i], 64, 256, HEAD, e_scale
            )
    arrive(got_z1)
    mine64 = pl.ds(pl.multiple_of(d * 64, 64), 64)
    total = r.w1o[mine64, :]
    for k in range(3):
        total = total + r.z1r[k].astype(F32)
    r.v_o_dup[...] = total[:, :512]
    r.v_o_ddown[...] = total[:, 512:]
    store("o_dup", "o_ddown")
    arrive(got_z2)
    total = r.w2o[mine64, :]
    for k in range(3):
        total = total + r.z2r[k].astype(F32)
    for c in range(3):
        r.v_o_dqkv[c] = total[:, c * 128 : (c + 1) * 128]
    r.v_o_dout[...] = total[:, 384:]
    store("o_dqkv", "o_dout")
    arrive(got_v)
    total = r.vr[0]
    for k in range(1, 8):
        total = total + r.vr[k]
    r.vz[d] = total
    got_vz = along(r.vz)
    arrive(got_pa)
    got_ps = [send(r.pa.at[:, s], r.pa.at[:, s], to_plane(1, 0))]
    arrive(got_f)
    for a in (0, 1):
        total = r.fr[4 * a].astype(F32)
        for k in (1, 2, 3):
            total = total + r.fr[4 * a + k].astype(F32)
        for i in pair:
            r.o_pat[:, PAIR * a + i, :] = total[i]
    arrive(got_ps)
    for a in range(4):
        for b in range(2):
            at = a * 256 + b * 128
            r.v_o_proj[at : at + 128, :] = r.pa[a, b]
    store("o_proj")
    arrive(got_c)
    arrive(got_x4)
    got_w.append(enc_weights(cut_rows(1), r.cz[...].reshape(512, 256), 768, r.v_o_out))
    arrive(got_x1)
    got_w.append(enc_weights(cut_rows(0), r.qa[...].reshape(512, 768), 0, r.own_qkv))
    arrive(got_vz)
    total = r.vz[0] + r.vz[1] + r.vz[2] + r.vz[3]
    r.o_v1[...] = jnp.concatenate([total[0:1], total[1:2]], axis=1).reshape(WIDTH)
    r.o_v2[...] = jnp.concatenate([total[2:3], total[3:4]], axis=1).reshape(WIDTH)
    for at, out in ((4, r.o_v3), (5, r.o_v4), (6, r.o_v5)):
        out[...] = total[at : at + 1].reshape(DEC_WIDTH)
    firsts = [(2048, 1024), (1024, 1024), (768, 256), (0, 768)]
    names = ["o_down", "o_up", "o_out", "o_qkv"]
    for made, (first, size), name in zip(got_w, firsts, names):
        arrive([made])
        more = r.wer[:, first : first + size].astype(F32)
        if name == "o_qkv":
            for c in range(3):
                at = slice(c * 256, (c + 1) * 256)
                r.v_o_qkv[c] = r.own_qkv[:, at] + more[:, at]
        else:
            out = getattr(r, "v_" + name)
            out[...] = out[...] + more
        store(name)
    for made in stores:
        made.wait()
    assert used[0] <= COPIES


def with_kernel(
    patches,
    counts,
    patch_index,
    scale_level,
    enc_gain_one,
    enc_qkv,
    enc_out,
    enc_gain_two,
    enc_up,
    enc_down,
    w_proj,
    mask_token,
    pos_table,
    dec_gain_one,
    dec_qkv,
    dec_out,
    dec_gain_two,
    dec_up,
    dec_down,
    decoded_grad,
):
    inputs = (
        patches,
        counts,
        patch_index.T,
        scale_level,
        enc_gain_one,
        enc_gain_two,
        dec_gain_one,
        dec_gain_two,
        mask_token,
        decoded_grad,
        jnp.swapaxes(enc_qkv, 0, 1),
        enc_out,
        enc_up,
        enc_down,
        w_proj,
        jnp.swapaxes(pos_table, 0, 1),
        jnp.swapaxes(dec_qkv, 0, 1),
        dec_out,
        dec_up,
        dec_down,
    )
    shapes = dict(STORED, o_pat=(SLOTS, 4, 128), o_v1=(WIDTH,), o_v2=(WIDTH,))
    shapes.update(o_v3=(DEC_WIDTH,), o_v4=(DEC_WIDTH,), o_v5=(DEC_WIDTH,))
    given = [jax.ShapeDtypeStruct(shapes[name], kind_of(name)) for name in OUT_NAMES]
    shapes = [jax.ShapeDtypeStruct(shapes[name], F32) for name in OUT_NAMES]
    vmem = pl.BlockSpec(memory_space=pltpu.VMEM)
    smem = pl.BlockSpec(memory_space=pltpu.SMEM)
    hbm = pl.BlockSpec(memory_space=pl.ANY)
    outs = pl.pallas_call(
        kernel,
        out_shape=given,
        in_specs=[vmem, smem, vmem, smem] + [vmem] * 6 + [hbm] * len(LOADED),
        out_specs=[hbm if name in STORED else vmem for name in OUT_NAMES],
        scratch_shapes=[pltpu.VMEM(shape, kind) for shape, kind in BUFFERS.values()]
        + [pltpu.VMEM(shape, BF16) for shape in LOADED.values()]
        + [pltpu.VMEM(shape, kind_of(name)) for name, shape in STORED.items()]
        + [
            pltpu.SemaphoreType.DMA((len(LOADED) + 4,)),
            pltpu.SemaphoreType.DMA((len(STORED),)),
            pltpu.SemaphoreType.DMA((COPIES,)),
            pltpu.SemaphoreType.DMA((COPIES,)),
        ],
        compiler_params=pltpu.CompilerParams(
            collective_id=0, has_side_effects=True, vmem_limit_bytes=60 * 2**20
        ),
        name="layer_pair",
    )(*inputs)
    outs = list(
        pl.pallas_call(
            hand_over,
            out_shape=shapes,
            in_specs=[hbm] * len(shapes),
            out_specs=[hbm] * len(shapes),
            scratch_shapes=[pltpu.VMEM(shape.shape, F32) for shape in shapes]
            + [pltpu.VMEM((WIDTH, DEC_WIDTH), BF16)]
            + [pltpu.SemaphoreType.DMA((len(shapes) + 3,))] * 2,
            compiler_params=pltpu.CompilerParams(vmem_limit_bytes=60 * 2**20),
            name="hand_over",
        )(*outs)
    )
    outs[0] = jnp.transpose(outs[0], (2, 0, 1))
    outs[2] = jnp.swapaxes(outs[2], 0, 1)
    outs[6] = jnp.swapaxes(outs[6], 0, 1)
    return tuple(outs)


def hand_over(*refs):
    count = len(OUT_NAMES)
    given, returned, held = (refs[i * count : (i + 1) * count] for i in range(3))
    low, come, go = refs[3 * count :]
    wide = OUT_NAMES.index("o_proj")
    order = [wide] + [i for i in range(count) if i != wide]
    arriving, leaving = {}, {}
    for i in order:
        landing = low if i == wide else held[i]
        arriving[i] = pltpu.make_async_copy(given[i], landing, come.at[i])
        leaving[i] = pltpu.make_async_copy(held[i], returned[i], go.at[i])
        arriving[i].start()
    arriving[wide].wait()
    parts = []
    for part in range(4):
        rows = pl.ds(part * 256, 256)
        held[wide][rows, :] = low[rows, :].astype(F32)
        at = go.at[wide] if part == 0 else go.at[count + part - 1]
        made = pltpu.make_async_copy(held[wide].at[rows], returned[wide].at[rows], at)
        made.start()
        parts.append(made)
    for i in order[1:]:
        arriving[i].wait()
        leaving[i].start()
    for made in parts:
        made.wait()
    for i in order[1:]:
        leaving[i].wait()


def fits_kernel(mesh, shapes):
    ways = (mesh.shape["section"], mesh.shape["dp"], mesh.shape["mp"])
    wanted = {0: (64, 16, 1024), 5: (1024, 3, 1024), 8: (1024, 4096), 10: (1024, 512)}
    wanted.update({12: (8, 196, 512), 14: (512, 3, 512), 17: (512, 2048), 19: (196, 16, 512)})
    return ways == (2, 4, 4) and all(shapes[i] == shape for i, shape in wanted.items())


def solution(mesh):
    def program(*arrays):
        shapes = [array.shape for array in arrays]
        body = with_kernel if fits_kernel(mesh, shapes) else on_device
        return placed_on(mesh, body)(*arrays)

    return program
```
